32 devices in a mesh: fsdp: 4 (over y, core), ctx: 8 (over z, x).
Axes of the slice: x: 2, y: 2, z: 4, core: 2. Of those that a mesh axis runs over, the one named last changes fastest.
Arguments:
- tokens: bfloat16 [4, 2048, 1024], P('fsdp', 'ctx'), may hold values from -6 to 6
- positions: int32 [4, 2048], P('fsdp'), may hold values from 0 to 2047, as said below
- w_query: bfloat16 [1024, 2048], P(('fsdp', 'ctx')), may hold values from -0.1875 to 0.1875
- w_key: bfloat16 [1024, 1024], P(('fsdp', 'ctx')), may hold values from -0.1875 to 0.1875
- w_value: bfloat16 [1024, 1024], P(('fsdp', 'ctx')), may hold values from -0.1875 to 0.1875
- w_output: bfloat16 [2048, 1024], P(None, ('fsdp', 'ctx')), may hold values from -2 to 2
- w_gate: bfloat16 [1024, 3072], P(('fsdp', 'ctx')), may hold values from -0.1875 to 0.1875
- w_up: bfloat16 [1024, 3072], P(('fsdp', 'ctx')), may hold values from -0.1875 to 0.1875
- w_down: bfloat16 [3072, 1024], P(('fsdp', 'ctx')), may hold values from -0.109375 to 0.109375
- first_gain: bfloat16 [1024], P(('fsdp', 'ctx')), may hold values from 0.099609375 to 1.8984375
- second_gain: bfloat16 [1024], P(('fsdp', 'ctx')), may hold values from 0.099609375 to 1.8984375
- head_gain: bfloat16 [256], P(('fsdp', 'ctx')), may hold values from 0.099609375 to 1.8984375
- cotangent: bfloat16 [4, 2048, 1024], P('fsdp', 'ctx'), may hold values from -6 to 6
Outputs:
- layer_out: bfloat16 [4, 2048, 1024], P('fsdp', 'ctx')
- grad_tokens: bfloat16 [4, 2048, 1024], P('fsdp', 'ctx')
- grad_query: float32 [1024, 2048], P(('fsdp', 'ctx'))
- grad_key: float32 [1024, 1024], P(('fsdp', 'ctx'))
- grad_value: float32 [1024, 1024], P(('fsdp', 'ctx'))
- grad_output: float32 [2048, 1024], P(None, ('fsdp', 'ctx'))
- grad_gate: float32 [1024, 3072], P(('fsdp', 'ctx'))
- grad_up: float32 [1024, 3072], P(('fsdp', 'ctx'))
- grad_down: float32 [3072, 1024], P(('fsdp', 'ctx'))
- grad_first: float32 [1024], P(('fsdp', 'ctx'))
- grad_second: float32 [1024], P(('fsdp', 'ctx'))
- grad_head: float32 [256], P(('fsdp', 'ctx'))
The draws below stay inside these ranges and needn't reach their ends.
Inputs may be any that keep to these rules, and one draw needn't show every extreme that they name: In each sequence, each aligned run of 256 rows holds two runs of 128 consecutive ascending positions: block p and block 15 - p of 128 positions, with p differing between runs, so that every position appears once.
All inputs are finite; a program needn't handle non-finite values.
Results may differ from the reference program's by a relative error of at most 0.025.
Values may be sent and summed in bfloat16 or wider, within the bound.
A program may use at most 256 MiB of HBM per device.

```python
import jax
import jax.numpy as jnp
from jax import lax

D = 1024
HEADS = 16
KV_HEADS = 8
HEAD_DIM = 128
FF = 3072
TOK_DEV = 256
SEQS = 4
LENGTH = 2048
QW = 2048
KW = 1024


def draw_positions(key, part):
    key = jax.random.fold_in(key, 7)
    half_block = TOK_DEV // 2
    rank_count = LENGTH // TOK_DEV
    seq_keys = jax.random.split(key, SEQS)
    pair_order = jax.vmap(lambda seq_key: jax.random.permutation(seq_key, rank_count))(seq_keys).astype(jnp.int32)
    offsets = jnp.arange(half_block, dtype=jnp.int32)
    front_rows = pair_order[:, :, None] * half_block + offsets[None, None, :]
    back_rows = (2 * rank_count - 1 - pair_order[:, :, None]) * half_block + offsets[None, None, :]
    return jnp.concatenate([front_rows, back_rows], axis=2).reshape(SEQS, LENGTH).astype(jnp.int32)


def block_levels(stream_key, extent, shards, least, largest):
    def one(dim, shards_of):
        heights = jax.random.uniform(jax.random.fold_in(jax.random.fold_in(stream_key, 6), dim), (shards_of,), jnp.float32, least / len(shards), largest / len(shards))
        return jnp.repeat(jnp.exp(heights), extent[dim] // shards_of).reshape((-1,) + (1,) * (len(extent) - dim - 1))

    level = one(*shards[0])
    for cut in shards[1:]:
        level = level * one(*cut)
    return level


def centred(rng, extent, scale, reach, cuts=(), kind=jnp.bfloat16):
    entries = scale * jax.random.normal(rng, extent, jnp.float32)
    if cuts:
        entries = entries * block_levels(rng, extent, cuts, -0.22, 0.18)
    return jnp.clip(entries, -reach, reach).astype(kind)


def setup_inputs(seed: int = 0) -> dict:
    splits = jax.random.split(jax.random.key(seed), 14)
    return {
        "tokens": centred(splits[0], (SEQS, LENGTH, D), 1.0, 6.0, ((0, 4), (1, 8))),
        "positions": draw_positions(jax.random.fold_in(splits[13], 71), 0),
        "w_query": centred(splits[2], (D, QW), D ** -0.5, 0.1875, ((0, 32),)),
        "w_key": centred(splits[3], (D, KW), D ** -0.5, 0.1875, ((0, 32),)),
        "w_value": centred(splits[4], (D, KW), D ** -0.5, 0.1875, ((0, 32),)),
        "w_output": centred(splits[5], (QW, D), (max(1, HEADS * HEAD_DIM // 256)) ** -0.5, 2.0, ((1, 32),)),
        "w_gate": centred(splits[6], (D, FF), D ** -0.5, 0.1875, ((0, 32),)),
        "w_up": centred(splits[7], (D, FF), D ** -0.5, 0.1875, ((0, 32),)),
        "w_down": centred(splits[8], (FF, D), FF ** -0.5, 0.109375, ((0, 32),)),
        "first_gain": jnp.clip(1.0 + 0.18 * jax.random.normal(splits[9], (D,), jnp.float32), 0.099609375, 1.8984375).astype(jnp.bfloat16),
        "second_gain": jnp.clip(1.0 + 0.18 * jax.random.normal(splits[10], (D,), jnp.float32), 0.099609375, 1.8984375).astype(jnp.bfloat16),
        "head_gain": jnp.clip(1.0 + 0.18 * jax.random.normal(splits[11], (2 * HEAD_DIM,), jnp.float32), 0.099609375, 1.8984375).astype(jnp.bfloat16),
        "cotangent": centred(splits[12], (SEQS, LENGTH, D), 1.0, 6.0, ((0, 4), (1, 8))),
    }


@jax.custom_vjp
def low(v):
    return lax.optimization_barrier(v.astype(jnp.bfloat16)).astype(jnp.float32)

@jax.custom_vjp
def low_back(v):
    return v

def low_keep(v):
    return (low(v), None)

def low_pass(kept, grad):
    return (grad,)

def back_keep(v):
    return (v, None)

def back_low(kept, grad):
    return (low(grad),)
low.defvjp(low_keep, low_pass)
low_back.defvjp(back_keep, back_low)

def normed(operand, gain_in):
    return operand * lax.rsqrt(lax.optimization_barrier(jnp.mean(operand * operand, axis=-1, keepdims=True)) + 1e-06) * gain_in

def rotary(operand, places):
    head_width = operand.shape[-1]
    half_width = head_width // 2
    inverse = 1000000.0 ** (-2.0 * jnp.arange(half_width, dtype=jnp.float32) / head_width)
    angles = places.astype(jnp.float32)[:, None] * inverse[None, :]
    cosine = jnp.concatenate([jnp.cos(angles), jnp.cos(angles)], axis=-1)[:, None, :]
    sine_table = jnp.concatenate([jnp.sin(angles), jnp.sin(angles)], axis=-1)[:, None, :]
    turned = jnp.concatenate([-operand[..., half_width:], operand[..., :half_width]], axis=-1)
    return operand * cosine + turned * sine_table

def matmul(left_side, right_side):
    return jnp.dot(left_side, right_side, precision=lax.Precision.HIGHEST)

def block_forward(inputs, places, w_query, w_key, w_value, w_output, w_gate, w_up, w_down, first_gain, second_gain, head_gain):
    length = inputs.shape[0]
    group_size = HEADS // KV_HEADS
    score_scale = HEAD_DIM ** (-0.5)
    hidden_one = low(normed(inputs, first_gain))
    query_raw = low_back(matmul(hidden_one, w_query)).reshape(length, HEADS, HEAD_DIM)
    key_raw = low_back(matmul(hidden_one, w_key)).reshape(length, KV_HEADS, HEAD_DIM)
    value_rows = low(low_back(matmul(hidden_one, w_value))).reshape(length, KV_HEADS, HEAD_DIM)
    queries = low(rotary(normed(query_raw, head_gain[:HEAD_DIM]), places))
    key_rows = low(rotary(normed(key_raw, head_gain[HEAD_DIM:]), places))
    query_block = min(512, length)
    block_count = length // query_block
    query_parts = queries.reshape(block_count, query_block, KV_HEADS, group_size, HEAD_DIM)
    place_parts = places.reshape(block_count, query_block)

    def attend(block_item):
        query_part, place_part = block_item
        scores = jnp.einsum('qhge,khe->hgqk', query_part, key_rows, precision=lax.Precision.HIGHEST) * score_scale
        scores = low_back(scores)
        visible = places[None, None, None, :] <= place_part[None, None, :, None]
        scores = jnp.where(visible, scores, -1e+30)
        weights = low(jax.nn.softmax(scores, axis=-1))
        mixed = jnp.einsum('hgqk,khe->qhge', weights, value_rows, precision=lax.Precision.HIGHEST)
        return mixed.reshape(query_block, HEADS * HEAD_DIM)
    attention = lax.map(jax.checkpoint(attend), (query_parts, place_parts)).reshape(length, HEADS * HEAD_DIM)
    attention = low(low_back(attention))
    middle = inputs + low_back(matmul(attention, w_output))
    hidden_two = low(normed(middle, second_gain))
    gate_raw = low_back(matmul(hidden_two, w_gate))
    up_raw = low_back(matmul(hidden_two, w_up))
    activated = low(jax.nn.silu(gate_raw) * up_raw)
    return middle + low_back(matmul(activated, w_down))

def reference(tokens, positions, w_query, w_key, w_value, w_output, w_gate, w_up, w_down, first_gain, second_gain, head_gain, cotangent):
    weights = tuple((w.astype(jnp.float32) for w in (w_query, w_key, w_value, w_output, w_gate, w_up, w_down, first_gain, second_gain, head_gain)))

    def forward_all(inputs, params):
        return lax.map(lambda block_item: block_forward(block_item[0], block_item[1], *params), (inputs, positions))
    result, pullback = jax.vjp(forward_all, tokens.astype(jnp.float32), weights)
    grad_inputs, gradients = pullback(cotangent.astype(jnp.float32))
    return (result.astype(jnp.bfloat16), grad_inputs.astype(jnp.bfloat16), gradients[0], gradients[1], gradients[2], gradients[3], gradients[4], gradients[5], gradients[6], gradients[7], gradients[8], gradients[9])
```

```python
from functools import partial

import jax
import jax.numpy as jnp
import numpy as np
from jax import lax
from jax.experimental import pallas as pl
from jax.experimental.pallas import tpu as pltpu
from jax.sharding import PartitionSpec as P

MESH = pl.DeviceIdType.MESH

HEADS = 16
KV_HEADS = 8
HEAD_DIM = 128


def normed(operand, gain_in):
    return (
        operand * lax.rsqrt(jnp.mean(operand * operand, axis=-1, keepdims=True) + 1e-06) * gain_in
    )


def rotary(operand, places):
    head_width = operand.shape[-1]
    half_width = head_width // 2
    inverse = 1000000.0 ** (-2.0 * jnp.arange(half_width, dtype=jnp.float32) / head_width)
    angles = places.astype(jnp.float32)[:, None] * inverse[None, :]
    cosine = jnp.concatenate([jnp.cos(angles), jnp.cos(angles)], axis=-1)[:, None, :]
    sine_table = jnp.concatenate([jnp.sin(angles), jnp.sin(angles)], axis=-1)[:, None, :]
    turned = jnp.concatenate([-operand[..., half_width:], operand[..., :half_width]], axis=-1)
    return operand * cosine + turned * sine_table


def head_prep(raw_proj, gain_in, places, head_count):
    row_count = raw_proj.shape[0]
    shaped = raw_proj.reshape(row_count, head_count, HEAD_DIM)
    return rotary(normed(shaped, gain_in), places).reshape(row_count, head_count * HEAD_DIM)


def gated(gate_raw, up_raw):
    return jax.nn.silu(gate_raw) * up_raw


def project(left_side, right_side):
    return jnp.dot(left_side, right_side, preferred_element_type=jnp.float32)


def project_back(left_side, right_side):
    return lax.dot_general(
        left_side, right_side, (((1,), (1,)), ((), ())), preferred_element_type=jnp.float32
    )


def outer_sum(left_side, right_side):
    return lax.dot_general(
        left_side, right_side, (((0,), (0,)), ((), ())), preferred_element_type=jnp.float32
    )


def halves_apart(rows_in, shard_count):
    shape_in = rows_in.shape
    split = rows_in.reshape((shard_count, 2, shape_in[0] // (2 * shard_count)) + shape_in[1:])
    return jnp.swapaxes(split, 0, 1).reshape(shape_in)


def halves_back(rows_in, shard_count):
    shape_in = rows_in.shape
    split = rows_in.reshape((2, shard_count, shape_in[0] // (2 * shard_count)) + shape_in[1:])
    return jnp.swapaxes(split, 0, 1).reshape(shape_in)


def key_layout(key_rows, value_rows, place_all):
    key_count = key_rows.shape[0]
    key_block = min(512, key_count)
    block_count = key_count // key_block
    key_parts = key_rows.reshape(block_count, key_block, KV_HEADS, HEAD_DIM)
    value_parts = value_rows.reshape(block_count, key_block, KV_HEADS, HEAD_DIM)
    place_parts = place_all.reshape(block_count, key_block)
    return (key_parts, value_parts, place_parts)


def attend_forward(queries, key_rows, value_rows, place_here, place_all):
    row_count = queries.shape[0]
    group_size = HEADS // KV_HEADS
    score_scale = HEAD_DIM ** (-0.5)
    grouped = queries.reshape(row_count, KV_HEADS, group_size, HEAD_DIM)
    layout = key_layout(key_rows, value_rows, place_all)
    top_place = jnp.max(place_here)

    def attend_step(state_now, block_item):
        key_part, value_part, place_part = block_item

        def attend_compute(state_in):
            run_max, run_sum, run_out = state_in
            scores = (
                jnp.einsum("qhge,khe->hgqk", grouped, key_part, preferred_element_type=jnp.float32)
                * score_scale
            )
            visible = place_part[None, None, None, :] <= place_here[None, None, :, None]
            scores = jnp.where(visible, scores, -1e30)
            new_max = jnp.maximum(run_max, jnp.max(scores, axis=-1))
            weights = jnp.where(visible, jnp.exp(scores - new_max[..., None]), 0.0)
            rescale = jnp.exp(run_max - new_max)
            run_sum = run_sum * rescale + jnp.sum(weights, axis=-1)
            mixed = jnp.einsum(
                "hgqk,khe->hgqe",
                weights.astype(jnp.bfloat16),
                value_part,
                preferred_element_type=jnp.float32,
            )
            run_out = run_out * rescale[..., None] + mixed
            return (new_max, run_sum, run_out)

        state_next = lax.cond(
            jnp.min(place_part) > top_place, lambda state_in: state_in, attend_compute, state_now
        )
        return (state_next, None)

    start_state = (
        jnp.full((KV_HEADS, group_size, row_count), -1e30, jnp.float32),
        jnp.zeros((KV_HEADS, group_size, row_count), jnp.float32),
        jnp.zeros((KV_HEADS, group_size, row_count, HEAD_DIM), jnp.float32),
    )
    (run_max, run_sum, run_out), _ = lax.scan(attend_step, start_state, layout)
    attention = (
        (run_out / run_sum[..., None]).transpose(2, 0, 1, 3).reshape(row_count, HEADS * HEAD_DIM)
    )
    return (attention, run_max + jnp.log(run_sum))


def row_dot_table(grad_attn, attention):
    row_count = grad_attn.shape[0]
    group_size = HEADS // KV_HEADS
    grad_grouped = grad_attn.reshape(row_count, KV_HEADS, group_size, HEAD_DIM)
    return jnp.sum(
        grad_grouped.astype(jnp.float32)
        * attention.reshape(row_count, KV_HEADS, group_size, HEAD_DIM),
        axis=-1,
    ).transpose(1, 2, 0)


def attend_backward(
    queries, key_rows, value_rows, grad_attn, row_dots, log_total, place_here, place_all
):
    row_count = queries.shape[0]
    key_count = key_rows.shape[0]
    group_size = HEADS // KV_HEADS
    score_scale = HEAD_DIM ** (-0.5)
    grouped = queries.reshape(row_count, KV_HEADS, group_size, HEAD_DIM)
    grad_grouped = grad_attn.reshape(row_count, KV_HEADS, group_size, HEAD_DIM)
    layout = key_layout(key_rows, value_rows, place_all)
    top_place = jnp.max(place_here)

    def back_step(grad_query, block_item):
        key_part, value_part, place_part = block_item
        key_block = key_part.shape[0]

        def back_compute(grad_in):
            scores = (
                jnp.einsum("qhge,khe->hgqk", grouped, key_part, preferred_element_type=jnp.float32)
                * score_scale
            )
            visible = place_part[None, None, None, :] <= place_here[None, None, :, None]
            weights = jnp.where(
                visible, jnp.exp(jnp.where(visible, scores, -1e30) - log_total[..., None]), 0.0
            )
            grad_probs = jnp.einsum(
                "qhge,khe->hgqk", grad_grouped, value_part, preferred_element_type=jnp.float32
            )
            grad_scores = (weights * (grad_probs - row_dots[..., None])).astype(jnp.bfloat16)
            grad_out = (
                grad_in
                + jnp.einsum(
                    "hgqk,khe->qhge", grad_scores, key_part, preferred_element_type=jnp.float32
                )
                * score_scale
            )
            grad_keys = (
                jnp.einsum(
                    "hgqk,qhge->khe", grad_scores, grouped, preferred_element_type=jnp.float32
                )
                * score_scale
            )
            grad_values = jnp.einsum(
                "hgqk,qhge->khe",
                weights.astype(jnp.bfloat16),
                grad_grouped,
                preferred_element_type=jnp.float32,
            )
            return (
                grad_out,
                (
                    grad_keys.reshape(key_block, KV_HEADS * HEAD_DIM),
                    grad_values.reshape(key_block, KV_HEADS * HEAD_DIM),
                ),
            )

        def skipped(grad_in):
            empty_terms = jnp.zeros((key_block, KV_HEADS * HEAD_DIM), jnp.float32)
            return (grad_in, (empty_terms, empty_terms))

        return lax.cond(jnp.min(place_part) > top_place, skipped, back_compute, grad_query)

    start_grad = jnp.zeros((row_count, KV_HEADS, group_size, HEAD_DIM), jnp.float32)
    grad_query, key_terms = lax.scan(back_step, start_grad, layout)
    grad_query = grad_query.reshape(row_count, HEADS * HEAD_DIM)
    return (
        grad_query,
        key_terms[0].reshape(key_count, KV_HEADS * HEAD_DIM),
        key_terms[1].reshape(key_count, KV_HEADS * HEAD_DIM),
    )


def per_device(
    tokens,
    positions,
    w_query,
    w_key,
    w_value,
    w_output,
    w_gate,
    w_up,
    w_down,
    first_gain,
    second_gain,
    head_gain,
    cotangent,
):
    inputs = tokens[0].astype(jnp.float32)
    row_count = inputs.shape[0]
    shard_count = lax.axis_size("ctx")
    place_stored = positions[0]
    place_here = lax.dynamic_slice_in_dim(
        place_stored, lax.axis_index("ctx") * row_count, row_count
    )
    place_all = halves_apart(place_stored, shard_count)
    query_full, key_full, value_full, output_full, gain_first, gain_head = (
        lax.all_gather(w_query, ("fsdp", "ctx"), axis=0, tiled=True),
        lax.all_gather(w_key, ("fsdp", "ctx"), axis=0, tiled=True),
        lax.all_gather(w_value, ("fsdp", "ctx"), axis=0, tiled=True),
        lax.all_gather(w_output, ("fsdp", "ctx"), axis=1, tiled=True),
        lax.all_gather(first_gain, ("fsdp", "ctx"), axis=0, tiled=True),
        lax.all_gather(head_gain, ("fsdp", "ctx"), axis=0, tiled=True),
    )
    gain_one = gain_first.astype(jnp.float32)
    gain_query = gain_head[:HEAD_DIM].astype(jnp.float32)
    gain_key = gain_head[HEAD_DIM:].astype(jnp.float32)
    hidden_one = normed(inputs, gain_one).astype(jnp.bfloat16)
    query_raw = project(hidden_one, query_full)
    key_raw = project(hidden_one, key_full)
    value_rows = project(hidden_one, value_full).astype(jnp.bfloat16)
    query_prep = partial(head_prep, places=place_here, head_count=HEADS)
    key_prep = partial(head_prep, places=place_here, head_count=KV_HEADS)
    queries, query_back = jax.vjp(query_prep, query_raw, gain_query)
    key_local, key_back = jax.vjp(key_prep, key_raw, gain_key)
    queries = queries.astype(jnp.bfloat16)
    key_local = key_local.astype(jnp.bfloat16)
    key_stored, value_stored = (
        lax.all_gather(key_local, "ctx", axis=0, tiled=True),
        lax.all_gather(value_rows, "ctx", axis=0, tiled=True),
    )
    key_all = halves_apart(key_stored, shard_count)
    value_all = halves_apart(value_stored, shard_count)
    attention, log_total = attend_forward(queries, key_all, value_all, place_here, place_all)
    attn_low = attention.astype(jnp.bfloat16)
    middle = inputs + project(attn_low, output_full)
    gate_full, up_full, down_full, gain_second = (
        lax.all_gather(w_gate, ("fsdp", "ctx"), axis=0, tiled=True),
        lax.all_gather(w_up, ("fsdp", "ctx"), axis=0, tiled=True),
        lax.all_gather(w_down, ("fsdp", "ctx"), axis=0, tiled=True),
        lax.all_gather(second_gain, ("fsdp", "ctx"), axis=0, tiled=True),
    )
    gain_two = gain_second.astype(jnp.float32)
    hidden_two = normed(middle, gain_two).astype(jnp.bfloat16)
    gate_raw = project(hidden_two, gate_full)
    up_raw = project(hidden_two, up_full)
    activated, gated_back = jax.vjp(gated, gate_raw, up_raw)
    act_low = activated.astype(jnp.bfloat16)
    layer_out = (middle + project(act_low, down_full)).astype(jnp.bfloat16)
    grad_out = cotangent[0].astype(jnp.float32)
    gate_full, up_full, down_full, gain_second = (
        lax.all_gather(w_gate, ("fsdp", "ctx"), axis=0, tiled=True),
        lax.all_gather(w_up, ("fsdp", "ctx"), axis=0, tiled=True),
        lax.all_gather(w_down, ("fsdp", "ctx"), axis=0, tiled=True),
        lax.all_gather(second_gain, ("fsdp", "ctx"), axis=0, tiled=True),
    )
    gain_two = gain_second.astype(jnp.float32)
    out_low = grad_out.astype(jnp.bfloat16)
    down_terms = outer_sum(act_low, out_low)
    grad_act = project_back(out_low, down_full)
    grad_gate_raw, grad_up_raw = gated_back(grad_act)
    gate_low = grad_gate_raw.astype(jnp.bfloat16)
    up_low = grad_up_raw.astype(jnp.bfloat16)
    gate_terms = outer_sum(hidden_two, gate_low)
    up_terms = outer_sum(hidden_two, up_low)
    grad_hidden_two = project_back(gate_low, gate_full) + project_back(up_low, up_full)
    _, norm_two_back = jax.vjp(normed, middle, gain_two)
    middle_part, gain_two_terms = norm_two_back(grad_hidden_two)
    grad_gate, grad_up, grad_down, grad_second = (
        lax.psum_scatter(gate_terms, ("fsdp", "ctx"), scatter_dimension=0, tiled=True),
        lax.psum_scatter(up_terms, ("fsdp", "ctx"), scatter_dimension=0, tiled=True),
        lax.psum_scatter(down_terms, ("fsdp", "ctx"), scatter_dimension=0, tiled=True),
        lax.psum_scatter(gain_two_terms, ("fsdp", "ctx"), scatter_dimension=0, tiled=True),
    )
    grad_middle = grad_out + middle_part
    query_full, key_full, value_full, output_full, gain_first, gain_head = (
        lax.all_gather(w_query, ("fsdp", "ctx"), axis=0, tiled=True),
        lax.all_gather(w_key, ("fsdp", "ctx"), axis=0, tiled=True),
        lax.all_gather(w_value, ("fsdp", "ctx"), axis=0, tiled=True),
        lax.all_gather(w_output, ("fsdp", "ctx"), axis=1, tiled=True),
        lax.all_gather(first_gain, ("fsdp", "ctx"), axis=0, tiled=True),
        lax.all_gather(head_gain, ("fsdp", "ctx"), axis=0, tiled=True),
    )
    gain_one = gain_first.astype(jnp.float32)
    middle_low = grad_middle.astype(jnp.bfloat16)
    output_terms = outer_sum(attn_low, middle_low)
    grad_attn = project_back(middle_low, output_full).astype(jnp.bfloat16)
    row_dots = row_dot_table(grad_attn, attention)
    grad_queries, key_terms, value_terms = attend_backward(
        queries, key_all, value_all, grad_attn, row_dots, log_total, place_here, place_all
    )
    key_terms = halves_back(key_terms, shard_count)
    value_terms = halves_back(value_terms, shard_count)
    grad_key_local, grad_value_local = (
        lax.psum_scatter(
            key_terms.astype(jnp.bfloat16), "ctx", scatter_dimension=0, tiled=True
        ).astype(jnp.float32),
        lax.psum_scatter(
            value_terms.astype(jnp.bfloat16), "ctx", scatter_dimension=0, tiled=True
        ).astype(jnp.float32),
    )
    grad_query_raw, gain_query_terms = query_back(grad_queries)
    grad_key_raw, gain_key_terms = key_back(grad_key_local)
    query_low = grad_query_raw.astype(jnp.bfloat16)
    keyraw_low = grad_key_raw.astype(jnp.bfloat16)
    value_low = grad_value_local.astype(jnp.bfloat16)
    query_terms = outer_sum(hidden_one, query_low)
    key_weight_terms = outer_sum(hidden_one, keyraw_low)
    value_weight_terms = outer_sum(hidden_one, value_low)
    grad_hidden_one = (
        project_back(query_low, query_full)
        + project_back(keyraw_low, key_full)
        + project_back(value_low, value_full)
    )
    _, norm_one_back = jax.vjp(normed, inputs, gain_one)
    input_part, gain_one_terms = norm_one_back(grad_hidden_one)
    head_terms = jnp.concatenate([gain_query_terms, gain_key_terms])
    grad_query, grad_key, grad_value, grad_output, grad_first, grad_head = (
        lax.psum_scatter(query_terms, ("fsdp", "ctx"), scatter_dimension=0, tiled=True),
        lax.psum_scatter(key_weight_terms, ("fsdp", "ctx"), scatter_dimension=0, tiled=True),
        lax.psum_scatter(value_weight_terms, ("fsdp", "ctx"), scatter_dimension=0, tiled=True),
        lax.psum_scatter(output_terms, ("fsdp", "ctx"), scatter_dimension=1, tiled=True),
        lax.psum_scatter(gain_one_terms, ("fsdp", "ctx"), scatter_dimension=0, tiled=True),
        lax.psum_scatter(head_terms, ("fsdp", "ctx"), scatter_dimension=0, tiled=True),
    )
    grad_tokens = (grad_middle + input_part).astype(jnp.bfloat16)
    return (
        layer_out[None],
        grad_tokens[None],
        grad_query,
        grad_key,
        grad_value,
        grad_output,
        grad_gate,
        grad_up,
        grad_down,
        grad_first,
        grad_second,
        grad_head,
    )


ROWS = 256
QROWS = 512
EPS = 1e-06
LOG2E = 1.4426950408889634
SCALE = HEAD_DIM**-0.5
VMEM_LIMIT = 60 * 1024 * 1024
BF16 = jnp.bfloat16
F32 = jnp.float32


def dot_nn(a, b):
    return lax.dot_general(a, b, (((1,), (0,)), ((), ())), preferred_element_type=F32)


def dot_nt(a, b):
    return lax.dot_general(a, b, (((1,), (1,)), ((), ())), preferred_element_type=F32)


def dot_tn(a, b):
    return lax.dot_general(a, b, (((0,), (0,)), ((), ())), preferred_element_type=F32)


def whereabouts():
    f, c = lax.axis_index("fsdp"), lax.axis_index("ctx")
    return f, c, f // 2, f % 2, c // 2, c % 2


def plane_of(s):
    return (s % 2) * 2 + s // 2


def remote(src, dst, send, recv, fsdp, ctx):
    return pltpu.make_async_remote_copy(
        src_ref=src, dst_ref=dst, send_sem=send, recv_sem=recv, device_id=(fsdp, ctx), device_id_type=MESH
    )


def await_bytes(ref, sem):
    pltpu.make_async_copy(ref, ref, sem).wait()


def greet_all():
    f, c, y, core, z, x = whereabouts()
    barrier = pltpu.get_barrier_semaphore()
    me = f * 8 + c

    def greet(j, carry):
        dev = (me + j) % 32
        pl.semaphore_signal(barrier, inc=1, device_id=(dev // 8, dev % 8), device_id_type=MESH)
        return carry

    lax.fori_loop(1, 32, greet, 0)
    pl.semaphore_wait(barrier, 31)


def greet_plane():
    f, c, y, core, z, x = whereabouts()
    barrier = pltpu.get_barrier_semaphore()
    me = f * 2 + x

    def greet(j, carry):
        t = (me + j) % 8
        pl.semaphore_signal(barrier, inc=1, device_id=(t // 2, z * 2 + t % 2), device_id_type=MESH)
        return carry

    lax.fori_loop(1, 8, greet, 0)
    pl.semaphore_wait(barrier, 7)


def chip_peer(r):
    f, c, y, core, z, x = whereabouts()
    y2 = 1 - y if r & 2 else y
    x2 = 1 - x if r & 1 else x
    return y2, x2


def chunk_of(r, core):
    y2, x2 = chip_peer(r)
    return (y2 * 2 + core) * 2 + x2


def rows_of(ref, chunk):
    return ref.at[pl.ds(pl.multiple_of(chunk * ROWS, ROWS), ROWS)]


def gather_kernel(
    tok, cot, pos, wq, wk, wv, wo, wg, wu, wd, gains,
    x_all, g_all, pos_all, w_attn, w_ffn, w_down, gains_all,
    pack_a, pack_f,
    x_recv, g_recv, hop_send, x_send, g_send, pos_sem, gain_sem, wa_sem, wf_sem, wd_sem,
):
    f, c, y, core, z, x = whereabouts()
    me = f * 8 + c
    for t in range(8):
        pack_a[t, :, 0:256] = wq[:, t * 256 : t * 256 + 256]
        pack_a[t, :, 256:384] = wk[:, t * 128 : t * 128 + 128]
        pack_a[t, :, 384:512] = wv[:, t * 128 : t * 128 + 128]
        pack_a[t, :, 512:768] = wo[:, t * 256 : t * 256 + 256]
        pack_f[t, :, 0:384] = wg[:, t * 384 : t * 384 + 384]
        pack_f[t, :, 384:768] = wu[:, t * 384 : t * 384 + 384]
    greet_all()

    home = plane_of(f)
    for src, dst, recv, k in ((tok, x_all, x_recv, 0), (cot, g_all, g_recv, 1)):

        @pl.when(home != z)
        def _():
            remote(src, rows_of(dst, c), hop_send.at[k], recv.at[c], f, home * 2 + x).start()

        @pl.when(home == z)
        def _():
            pltpu.make_async_copy(src, rows_of(dst, c), recv.at[c]).start()

    pltpu.make_async_copy(pos, pos_all.at[f], pos_sem.at[1]).start()
    pltpu.make_async_copy(gains, gains_all.at[me], gain_sem.at[1]).start()
    for j in range(1, 4):
        remote(pos, pos_all.at[f], pos_sem.at[0], pos_sem.at[1], (f + j) % 4, c).start()

    def my_rows(ref):
        return ref.at[pl.ds(pl.multiple_of(me * 32, 32), 32)]

    def send_attn(j, carry):
        dev = (me + j) % 32
        df, dc = dev // 8, dev % 8
        remote(pack_a.at[df * 2 + dc % 2], my_rows(w_attn), wa_sem.at[0], wa_sem.at[1], df, dc).start()
        remote(gains, gains_all.at[me], gain_sem.at[0], gain_sem.at[1], df, dc).start()
        return carry

    lax.fori_loop(1, 32, send_attn, 0)
    pltpu.make_async_copy(pack_a.at[f * 2 + x], my_rows(w_attn), wa_sem.at[1]).start()

    def relay(buf, recv, send):
        s = plane_of(z)
        ys, cs = s // 2, s % 2

        @pl.when(core == cs)
        def _():
            for k in range(4):
                ch = k * 2 + x
                part = rows_of(buf, ch)
                await_bytes(part, recv.at[ch])
                remote(part, part, send.at[1], recv.at[ch], f, z * 2 + 1 - x).start()

                @pl.when(y == ys)
                def _():
                    remote(part, part, send.at[2], recv.at[ch], (1 - y) * 2 + core, c).start()

                remote(part, part, send.at[0], recv.at[ch], y * 2 + 1 - core, c).start()
            for k in range(4):
                ch = k * 2 + 1 - x
                part = rows_of(buf, ch)
                await_bytes(part, recv.at[ch])
                remote(part, part, send.at[0], recv.at[ch], y * 2 + 1 - core, c).start()

        @pl.when(core != cs)
        def _():
            for ch in range(8):
                await_bytes(buf.at[pl.ds(ch * ROWS, ROWS)], recv.at[ch])

    def relay_done(buf, send):
        s = plane_of(z)
        ys, cs = s // 2, s % 2

        @pl.when(core == cs)
        def _():
            await_bytes(buf, send.at[0])
            await_bytes(buf.at[pl.ds(0, 4 * ROWS)], send.at[1])

            @pl.when(y == ys)
            def _():
                await_bytes(buf.at[pl.ds(0, 4 * ROWS)], send.at[2])

    relay(x_all, x_recv, x_send)

    def send_ffn(j, carry):
        dev = (me + j) % 32
        df, dc = dev // 8, dev % 8
        remote(pack_f.at[df * 2 + dc % 2], my_rows(w_ffn), wf_sem.at[0], wf_sem.at[1], df, dc).start()
        return carry

    lax.fori_loop(1, 32, send_ffn, 0)
    pltpu.make_async_copy(pack_f.at[f * 2 + x], my_rows(w_ffn), wf_sem.at[1]).start()

    t_down = me // 4
    down_rows = w_down.at[pl.ds(pl.multiple_of((me % 4) * 96, 32), 96)]
    self_down = t_down == f * 2 + x
    for k in range(4):
        here = self_down & (z == k)

        @pl.when(here)
        def _():
            pltpu.make_async_copy(wd, down_rows, wd_sem.at[1]).start()

        @pl.when(jnp.logical_not(here))
        def _():
            remote(wd, down_rows, wd_sem.at[0], wd_sem.at[1], t_down // 2, k * 2 + t_down % 2).start()

    relay(g_all, g_recv, g_send)

    await_bytes(pos_all, pos_sem.at[1])
    await_bytes(gains_all, gain_sem.at[1])
    await_bytes(w_attn, wa_sem.at[1])
    await_bytes(w_ffn, wf_sem.at[1])
    await_bytes(w_down, wd_sem.at[1])

    @pl.when(home != z)
    def _():
        await_bytes(tok, hop_send.at[0])
        await_bytes(cot, hop_send.at[1])

    relay_done(x_all, x_send)
    relay_done(g_all, g_send)
    await_bytes(pos_all.at[pl.ds(0, 3)], pos_sem.at[0])
    await_bytes(gains_all.at[pl.ds(0, 31)], gain_sem.at[0])
    await_bytes(w_attn.at[pl.ds(0, 31 * 32)], wa_sem.at[0])
    await_bytes(w_ffn.at[pl.ds(0, 31 * 32)], wf_sem.at[0])
    for k in range(4):

        @pl.when(jnp.logical_not(self_down & (z == k)))
        def _():
            await_bytes(wd, wd_sem.at[0])


def gather(tok, cot, pos, wq, wk, wv, wo, wg, wu, wd, gains):
    any_spec, vmem = pl.BlockSpec(memory_space=pl.ANY), pl.BlockSpec(memory_space=pltpu.VMEM)
    dma = pltpu.SemaphoreType.DMA
    return pl.pallas_call(
        gather_kernel,
        out_shape=(
            jax.ShapeDtypeStruct((2048, 1024), BF16),
            jax.ShapeDtypeStruct((2048, 1024), BF16),
            jax.ShapeDtypeStruct((4, 1, 2048), jnp.int32),
            jax.ShapeDtypeStruct((1024, 768), BF16),
            jax.ShapeDtypeStruct((1024, 768), BF16),
            jax.ShapeDtypeStruct((384, 1024), BF16),
            jax.ShapeDtypeStruct((32, 1, 128), F32),
        ),
        in_specs=[any_spec] * 3 + [vmem] * 6 + [any_spec] * 2,
        out_specs=(any_spec,) * 7,
        scratch_shapes=[
            pltpu.VMEM((8, 32, 768), BF16),
            pltpu.VMEM((8, 32, 768), BF16),
            dma((8,)), dma((8,)), dma((2,)), dma((3,)), dma((3,)),
            dma((2,)), dma((2,)), dma((2,)), dma((2,)), dma((2,)),
        ],
        compiler_params=pltpu.CompilerParams(collective_id=0, has_side_effects=True, vmem_limit_bytes=VMEM_LIMIT),
        name="gather",
    )(tok, cot, pos, wq, wk, wv, wo, wg, wu, wd, gains)


def head_norm_rope(raw, gain, cos, sin):
    r = lax.rsqrt(jnp.mean(raw * raw, axis=-1, keepdims=True) + EPS)
    u = raw * r * gain
    return u * cos + pltpu.roll(u, HEAD_DIM // 2, 1) * sin


def sorted_rows(ref, perm, first, count):
    return jnp.concatenate(
        [ref[pl.ds(pl.multiple_of(perm[first + k] * 128, 128), 128), :] for k in range(count)], axis=0
    )


def norm_rows(values, gain):
    v = values.astype(F32)
    return v * lax.rsqrt(jnp.mean(v * v, axis=-1, keepdims=True) + EPS) * gain


def attend_kernel(
    perm, x_ref, w_ref, gain_ref, hgain_ref, cos_ref, sin_ref,
    p_ref, q_ref, k_ref, v_ref, o_ref, lse_ref,
    vt, acc, total,
):
    def prepare(b, carry):
        rows = pl.ds(pl.multiple_of(b * QROWS, QROWS), QROWS)
        h = norm_rows(sorted_rows(x_ref, perm, b * 4, 4), gain_ref[...]).astype(BF16)
        raw = dot_nn(h, w_ref[:, 0:512])
        cos, sin = cos_ref[rows, :], sin_ref[rows, :]
        gq, gk = hgain_ref[0:1, :], hgain_ref[1:2, :]
        for k in range(2):
            q_ref[rows, k * 128 : k * 128 + 128] = head_norm_rope(
                raw[:, k * 128 : k * 128 + 128], gq, cos, sin
            ).astype(BF16)
        k_ref[rows, :] = head_norm_rope(raw[:, 256:384], gk, cos, sin).astype(BF16)
        v = raw[:, 384:512].astype(BF16)
        v_ref[rows, :] = v
        vt[b] = v.T
        return carry

    lax.fori_loop(0, 4, prepare, 0)

    def query_tile(qt, carry):
        def step(kt, diagonal):
            kb = k_ref[pl.ds(pl.multiple_of(kt * QROWS, QROWS), QROWS), :]
            vb = vt[kt]
            for g in range(4):
                head, half = g // 2, g % 2
                start = pl.multiple_of(qt * QROWS + half * 256, 256)
                qb = q_ref[pl.ds(start, 256), head * 128 : head * 128 + 128]
                depth = 256 * (half + 1) if diagonal else QROWS
                s = dot_nt(kb[:depth], qb)
                p = jnp.exp2(s * (SCALE * LOG2E))
                if diagonal:
                    ki = lax.broadcasted_iota(jnp.int32, (depth, 256), 0)
                    qi = lax.broadcasted_iota(jnp.int32, (depth, 256), 1) + half * 256
                    p = jnp.where(ki <= qi, p, 0.0)
                cols = slice(g * 256, g * 256 + 256)
                total[:, cols] += jnp.sum(p, axis=0, keepdims=True)
                acc[:, cols] += dot_nn(vb[:, :depth], p.astype(BF16))

        total[...] = jnp.zeros_like(total)
        acc[...] = jnp.zeros_like(acc)

        def off(kt, inner):
            step(kt, False)
            return inner

        lax.fori_loop(0, qt, off, 0)
        step(qt, True)
        sums = total[...]
        lse_ref[qt] = jnp.log2(sums)
        out = acc[...] * (1.0 / sums)
        for g in range(4):
            head, half = g // 2, g % 2
            start = pl.multiple_of(qt * QROWS + half * 256, 256)
            o_ref[pl.ds(start, 256), head * 128 : head * 128 + 128] = out[:, g * 256 : g * 256 + 256].T.astype(BF16)
        rows = pl.ds(pl.multiple_of(qt * QROWS, QROWS), QROWS)
        part = dot_nt(o_ref[rows, :], w_ref[:, 512:768]).astype(BF16)
        for k in range(4):
            p_ref[pl.ds(pl.multiple_of(perm[qt * 4 + k] * 128, 128), 128), :] = part[k * 128 : k * 128 + 128]
        return carry

    lax.fori_loop(0, 4, query_tile, 0)


def attend(perm, x_all, w_attn, gain, hgain, cos, sin):
    smem, vmem = pl.BlockSpec(memory_space=pltpu.SMEM), pl.BlockSpec(memory_space=pltpu.VMEM)
    return pl.pallas_call(
        attend_kernel,
        out_shape=(
            jax.ShapeDtypeStruct((2048, 1024), BF16),
            jax.ShapeDtypeStruct((2048, 256), BF16),
            jax.ShapeDtypeStruct((2048, 128), BF16),
            jax.ShapeDtypeStruct((2048, 128), BF16),
            jax.ShapeDtypeStruct((2048, 256), BF16),
            jax.ShapeDtypeStruct((4, 1, 1024), F32),
        ),
        in_specs=[smem] + [vmem] * 6,
        out_specs=(vmem,) * 6,
        scratch_shapes=[
            pltpu.VMEM((4, 128, QROWS), BF16),
            pltpu.VMEM((128, 1024), F32),
            pltpu.VMEM((1, 1024), F32),
        ],
        compiler_params=pltpu.CompilerParams(vmem_limit_bytes=VMEM_LIMIT),
        name="attend",
    )(perm, x_all, w_attn, gain, hgain, cos, sin)


def sum_begin(part, from_core, send, core_recv):
    f, c, y, core, z, x = whereabouts()
    for r in (3, 1, 2, 0):
        remote(
            rows_of(part, chunk_of(r, 1 - core)), from_core.at[r], send.at[0], core_recv.at[r], y * 2 + 1 - core, c
        ).start()


def sum_middle(part, from_core, out_buf, in_buf, send, core_recv, recv):
    f, c, y, core, z, x = whereabouts()
    for r in (3, 1, 2):
        await_bytes(from_core.at[r], core_recv.at[r])
        first = pl.multiple_of(chunk_of(r, core) * ROWS, ROWS)
        out_buf[r - 1] = (part[pl.ds(first, ROWS), :].astype(F32) + from_core[r].astype(F32)).astype(BF16)
        y2, x2 = chip_peer(r)
        remote(out_buf.at[r - 1], in_buf.at[r - 1], send.at[r], recv.at[r - 1], y2 * 2 + core, z * 2 + x2).start()


def sum_end(part, from_core, in_buf, core_recv, recv):
    f, c, y, core, z, x = whereabouts()
    await_bytes(from_core.at[0], core_recv.at[0])
    for r in (1, 2, 3):
        await_bytes(in_buf.at[r - 1], recv.at[r - 1])
    first = pl.multiple_of(chunk_of(0, core) * ROWS, ROWS)
    total = part[pl.ds(first, ROWS), :].astype(F32) + from_core[0].astype(F32)
    return total + in_buf[0].astype(F32) + in_buf[1].astype(F32) + in_buf[2].astype(F32)


def sum_sent(from_core, out_buf, send):
    await_bytes(from_core, send.at[0])
    for r in (1, 2, 3):
        await_bytes(out_buf.at[r - 1], send.at[r])


def spread(every, send, recv):
    f, c, y, core, z, x = whereabouts()
    mine = rows_of(every, f * 2 + x)
    for r in (3, 1, 2):
        y2, x2 = chip_peer(r)
        remote(mine, mine, send.at[r], recv.at[f * 2 + x], y2 * 2 + core, z * 2 + x2).start()
    remote(mine, mine, send.at[0], recv.at[f * 2 + x], y * 2 + 1 - core, c).start()
    for r in (1, 2, 3):
        ch = chunk_of(r, core)
        part = rows_of(every, ch)
        await_bytes(part, recv.at[ch])
        remote(part, part, send.at[0], recv.at[ch], y * 2 + 1 - core, c).start()
    for r in range(4):
        ch = chunk_of(r, 1 - core)
        await_bytes(rows_of(every, ch), recv.at[ch])
    for r in (1, 2, 3):
        await_bytes(mine, send.at[r])
    await_bytes(every.at[pl.ds(0, 4 * ROWS)], send.at[0])


SUM_SCRATCH = [
    pltpu.VMEM((4, ROWS, 1024), BF16),
    pltpu.VMEM((3, ROWS, 1024), BF16),
    pltpu.VMEM((3, ROWS, 1024), BF16),
    pltpu.SemaphoreType.DMA((4,)),
    pltpu.SemaphoreType.DMA((4,)),
    pltpu.SemaphoreType.DMA((3,)),
]
SPREAD_SCRATCH = [pltpu.SemaphoreType.DMA((4,)), pltpu.SemaphoreType.DMA((8,))]


def middle_kernel(
    part, x_all, gain, mid, h2_all, x_own, x_sem, from_core, out_buf, in_buf, send, core_recv, recv, sp_send, sp_recv
):
    f, c, y, core, z, x = whereabouts()
    own = pltpu.make_async_copy(rows_of(x_all, f * 2 + x), x_own, x_sem)
    own.start()
    greet_plane()
    sum_begin(part, from_core, send, core_recv)
    sum_middle(part, from_core, out_buf, in_buf, send, core_recv, recv)
    own.wait()
    mid[...] = x_own[...].astype(F32) + sum_end(part, from_core, in_buf, core_recv, recv)
    first = pl.multiple_of((f * 2 + x) * ROWS, ROWS)
    h2_all[pl.ds(first, ROWS), :] = norm_rows(mid[...], gain[...]).astype(BF16)
    spread(h2_all, sp_send, sp_recv)
    sum_sent(from_core, out_buf, send)


def middle(part, x_all, gain):
    any_spec, vmem = pl.BlockSpec(memory_space=pl.ANY), pl.BlockSpec(memory_space=pltpu.VMEM)
    return pl.pallas_call(
        middle_kernel,
        out_shape=(jax.ShapeDtypeStruct((ROWS, 1024), F32), jax.ShapeDtypeStruct((2048, 1024), BF16)),
        in_specs=[vmem, any_spec, vmem],
        out_specs=(vmem, vmem),
        scratch_shapes=[pltpu.VMEM((ROWS, 1024), BF16), pltpu.SemaphoreType.DMA] + SUM_SCRATCH + SPREAD_SCRATCH,
        compiler_params=pltpu.CompilerParams(collective_id=1, has_side_effects=True, vmem_limit_bytes=VMEM_LIMIT),
        name="middle",
    )(part, x_all, gain)


def feed_kernel(h_ref, d_ref, w_ref, wd_ref, p_ref, dh_ref, gw_ref, gd_ref, act_s, dgu_s):
    def tile(b, carry):
        rows = pl.ds(pl.multiple_of(b * ROWS, ROWS), ROWS)
        gu = dot_nn(h_ref[rows, :], w_ref[...])
        gate, up = gu[:, 0:384], gu[:, 384:768]
        sig = 1.0 / (1.0 + jnp.exp(-gate))
        sil = gate * sig
        act = (sil * up).astype(BF16)
        act_s[rows, :] = act
        p_ref[rows, :] = dot_nn(act, wd_ref[...]).astype(BF16)
        dact = dot_nt(d_ref[rows, :], wd_ref[...])
        dgu_s[rows, 0:384] = (dact * up * sig * (1.0 + gate * (1.0 - sig))).astype(BF16)
        dgu_s[rows, 384:768] = (dact * sil).astype(BF16)
        dh_ref[rows, :] = dot_nt(dgu_s[rows, :], w_ref[...]).astype(BF16)
        return carry

    lax.fori_loop(0, 8, tile, 0)

    def grad_w(b, carry):
        cols = pl.ds(pl.multiple_of(b * 256, 256), 256)
        gw_ref[cols, :] = dot_tn(h_ref[:, cols], dgu_s[...]).astype(BF16)
        return carry

    lax.fori_loop(0, 4, grad_w, 0)
    for b in range(3):
        gd_ref[b * 128 : b * 128 + 128, :] = dot_tn(act_s[:, b * 128 : b * 128 + 128], d_ref[...]).astype(BF16)


def feed(h_all, g_all, w_ffn, w_down):
    vmem = pl.BlockSpec(memory_space=pltpu.VMEM)
    return pl.pallas_call(
        feed_kernel,
        out_shape=(
            jax.ShapeDtypeStruct((2048, 1024), BF16),
            jax.ShapeDtypeStruct((2048, 1024), BF16),
            jax.ShapeDtypeStruct((1024, 768), BF16),
            jax.ShapeDtypeStruct((384, 1024), BF16),
        ),
        in_specs=[vmem] * 4,
        out_specs=(vmem,) * 4,
        scratch_shapes=[pltpu.VMEM((2048, 384), BF16), pltpu.VMEM((2048, 768), BF16)],
        compiler_params=pltpu.CompilerParams(vmem_limit_bytes=VMEM_LIMIT),
        name="feed",
    )(h_all, g_all, w_ffn, w_down)


def norm_back(values, gain, dy):
    r = lax.rsqrt(jnp.mean(values * values, axis=-1, keepdims=True) + EPS)
    cdy = gain * dy
    back = r * cdy - values * (r * r * r) * jnp.mean(cdy * values, axis=-1, keepdims=True)
    return back, dy * values * r


def turn_kernel(
    part, lpart, mid, g_all, gain, dmid, da_all, layer, gsecond,
    g_own, g_sem, from_core, out_buf, in_buf, send, core_recv, recv,
    from_core2, out_buf2, in_buf2, send2, core_recv2, recv2, sp_send, sp_recv,
):
    f, c, y, core, z, x = whereabouts()
    own = pltpu.make_async_copy(rows_of(g_all, f * 2 + x), g_own, g_sem)
    own.start()
    greet_plane()
    sum_begin(part, from_core, send, core_recv)
    sum_middle(part, from_core, out_buf, in_buf, send, core_recv, recv)
    sum_begin(lpart, from_core2, send2, core_recv2)
    own.wait()
    back, dgain = norm_back(mid[...], gain[...], sum_end(part, from_core, in_buf, core_recv, recv))
    dmid[...] = g_own[...].astype(F32) + back
    gsecond[...] = jnp.sum(dgain, axis=0, keepdims=True)
    first = pl.multiple_of((f * 2 + x) * ROWS, ROWS)
    da_all[pl.ds(first, ROWS), :] = dmid[...].astype(BF16)
    spread(da_all, sp_send, sp_recv)
    sum_middle(lpart, from_core2, out_buf2, in_buf2, send2, core_recv2, recv2)
    layer[...] = (mid[...] + sum_end(lpart, from_core2, in_buf2, core_recv2, recv2)).astype(BF16)
    sum_sent(from_core, out_buf, send)
    sum_sent(from_core2, out_buf2, send2)


def turn(part, lpart, mid, g_all, gain):
    any_spec, vmem = pl.BlockSpec(memory_space=pl.ANY), pl.BlockSpec(memory_space=pltpu.VMEM)
    return pl.pallas_call(
        turn_kernel,
        out_shape=(
            jax.ShapeDtypeStruct((ROWS, 1024), F32),
            jax.ShapeDtypeStruct((2048, 1024), BF16),
            jax.ShapeDtypeStruct((ROWS, 1024), BF16),
            jax.ShapeDtypeStruct((1, 1024), F32),
        ),
        in_specs=[vmem, vmem, vmem, any_spec, vmem],
        out_specs=(vmem,) * 4,
        scratch_shapes=[pltpu.VMEM((ROWS, 1024), BF16), pltpu.SemaphoreType.DMA]
        + SUM_SCRATCH
        + SUM_SCRATCH
        + SPREAD_SCRATCH,
        compiler_params=pltpu.CompilerParams(collective_id=2, has_side_effects=True, vmem_limit_bytes=VMEM_LIMIT),
        name="turn",
    )(part, lpart, mid, g_all, gain)


def unturn(d, cos, sin):
    return d * cos - pltpu.roll(d, HEAD_DIM // 2, 1) * sin


def attend_back_kernel(
    perm, x_ref, da_ref, w_ref, gain_ref, hgain_ref, cos_ref, sin_ref, q_ref, k_ref, v_ref, o_ref, lse_ref,
    p_ref, gw_ref, small_ref,
    h_s, da_s, do_s, delta_s, kt_s, dqt_s, dk_s, dv_s, dqkv_s,
):
    def prepare(b, carry):
        rows = pl.ds(pl.multiple_of(b * QROWS, QROWS), QROWS)
        h_s[rows, :] = norm_rows(sorted_rows(x_ref, perm, b * 4, 4), gain_ref[...]).astype(BF16)
        da = sorted_rows(da_ref, perm, b * 4, 4)
        da_s[rows, :] = da
        do = dot_nn(da, w_ref[:, 512:768]).astype(BF16)
        do_s[rows, :] = do
        ones = jnp.ones((8, 128), BF16)
        for head in range(2):
            cols = slice(head * 128, head * 128 + 128)
            prod = do[:, cols].astype(F32) * o_ref[rows, cols].astype(F32)
            high = prod.astype(BF16)
            low = (prod - high.astype(F32)).astype(BF16)
            delta = dot_nt(ones, high) + dot_nt(ones, low)
            delta_s[b, :, head * QROWS : head * QROWS + QROWS] = delta[0:1]
        kt_s[b] = k_ref[rows, :].T
        return carry

    lax.fori_loop(0, 4, prepare, 0)
    dqt_s[...] = jnp.zeros_like(dqt_s)

    def key_tile(kt, carry):
        krows = pl.ds(pl.multiple_of(kt * QROWS, QROWS), QROWS)
        dk_s[...] = jnp.zeros_like(dk_s)
        dv_s[...] = jnp.zeros_like(dv_s)

        def step(qt, diagonal):
            kb, vb, ktb = k_ref[krows, :], v_ref[krows, :], kt_s[kt]
            for g in range(4):
                head, half = g // 2, g % 2
                start = pl.multiple_of(qt * QROWS + half * 256, 256)
                cols = slice(head * 128, head * 128 + 128)
                lanes = slice(g * 256, g * 256 + 256)
                qb = q_ref[pl.ds(start, 256), cols]
                dob = do_s[pl.ds(start, 256), cols]
                depth = 256 * (half + 1) if diagonal else QROWS
                s = dot_nt(kb[:depth], qb)
                p = jnp.exp2(s * (SCALE * LOG2E) - lse_ref[qt, :, lanes])
                if diagonal:
                    ki = lax.broadcasted_iota(jnp.int32, (depth, 256), 0)
                    qi = lax.broadcasted_iota(jnp.int32, (depth, 256), 1) + half * 256
                    p = jnp.where(ki <= qi, p, 0.0)
                dp = dot_nt(vb[:depth], dob)
                ds = (p * (dp - delta_s[qt, :, lanes])).astype(BF16)
                dv_s[0:depth, :] += dot_nn(p.astype(BF16), dob)
                dk_s[0:depth, :] += dot_nn(ds, qb)
                dqt_s[qt, :, lanes] += dot_nn(ktb[:, :depth], ds)

        step(kt, True)

        def off(qt, inner):
            step(qt, False)
            return inner

        lax.fori_loop(kt + 1, 4, off, 0)
        cos, sin = cos_ref[krows, :], sin_ref[krows, :]
        gk = hgain_ref[1:2, :]
        raw = dot_nn(h_s[krows, :], w_ref[:, 256:384])
        back, dgain = norm_back(raw, gk, unturn(dk_s[...] * SCALE, cos, sin))
        dqkv_s[krows, 256:384] = back.astype(BF16)
        dqkv_s[krows, 384:512] = dv_s[...].astype(BF16)
        small_ref[2:3, 128:256] += jnp.sum(dgain, axis=0, keepdims=True)
        return carry

    small_ref[...] = jnp.zeros_like(small_ref)
    lax.fori_loop(0, 4, key_tile, 0)

    def finish(b, carry):
        rows = pl.ds(pl.multiple_of(b * QROWS, QROWS), QROWS)
        cos, sin = cos_ref[rows, :], sin_ref[rows, :]
        gq = hgain_ref[0:1, :]
        h = h_s[rows, :]
        for head in range(2):
            cols = slice(head * 128, head * 128 + 128)
            dq = dqt_s[b, :, head * QROWS : head * QROWS + QROWS].T * SCALE
            raw = dot_nn(h, w_ref[:, cols])
            back, dgain = norm_back(raw, gq, unturn(dq, cos, sin))
            dqkv_s[rows, cols] = back.astype(BF16)
            small_ref[2:3, 0:128] += jnp.sum(dgain, axis=0, keepdims=True)
        dh = dot_nt(dqkv_s[rows, :], w_ref[:, 0:512])
        x = sorted_rows(x_ref, perm, b * 4, 4).astype(F32)
        r = lax.rsqrt(jnp.mean(x * x, axis=-1, keepdims=True) + EPS)
        small_ref[0:1, :] += jnp.sum(dh * x * r, axis=0, keepdims=True)
        low = dh.astype(BF16)
        for k in range(4):
            p_ref[pl.ds(pl.multiple_of(perm[b * 4 + k] * 128, 128), 128), :] = low[k * 128 : k * 128 + 128]
        return carry

    lax.fori_loop(0, 4, finish, 0)

    def grads(b, carry):
        cols = pl.ds(pl.multiple_of(b * 256, 256), 256)
        gw_ref[cols, 0:512] = dot_tn(h_s[:, cols], dqkv_s[...]).astype(BF16)
        gw_ref[cols, 512:768] = dot_tn(da_s[:, cols], o_ref[...]).astype(BF16)
        return carry

    lax.fori_loop(0, 4, grads, 0)


def attend_back(perm, x_all, da_all, w_attn, gain, hgain, cos, sin, q, k, v, o, lse):
    smem, vmem = pl.BlockSpec(memory_space=pltpu.SMEM), pl.BlockSpec(memory_space=pltpu.VMEM)
    return pl.pallas_call(
        attend_back_kernel,
        out_shape=(
            jax.ShapeDtypeStruct((2048, 1024), BF16),
            jax.ShapeDtypeStruct((1024, 768), BF16),
            jax.ShapeDtypeStruct((8, 1024), F32),
        ),
        in_specs=[smem] + [vmem] * 12,
        out_specs=(vmem,) * 3,
        scratch_shapes=[
            pltpu.VMEM((2048, 1024), BF16),
            pltpu.VMEM((2048, 1024), BF16),
            pltpu.VMEM((2048, 256), BF16),
            pltpu.VMEM((4, 1, 1024), F32),
            pltpu.VMEM((4, 128, QROWS), BF16),
            pltpu.VMEM((4, 128, 1024), F32),
            pltpu.VMEM((QROWS, 128), F32),
            pltpu.VMEM((QROWS, 128), F32),
            pltpu.VMEM((2048, 512), BF16),
        ],
        compiler_params=pltpu.CompilerParams(vmem_limit_bytes=VMEM_LIMIT),
        name="attend_back",
    )(perm, x_all, da_all, w_attn, gain, hgain, cos, sin, q, k, v, o, lse)


def finish_kernel(
    part, x_all, gain, dmid, layer, g_attn, g_ffn, g_down, small,
    layer_out, grad_tokens, o_q, o_k, o_v, o_o, o_g, o_u, o_d, small_out,
    x_own, tok_own, ra, rf, rd, sbuf, s_in, p_in,
    x_sem, from_core, out_buf, in_buf, send, core_recv, recv,
    out_sem, ra_sem, rf_sem, rd_sem, s_sem, p_sem,
):
    f, c, y, core, z, x = whereabouts()
    me, t = f * 8 + c, f * 2 + x
    own = pltpu.make_async_copy(rows_of(x_all, t), x_own, x_sem)
    own.start()
    greet_all()
    sum_begin(part, from_core, send, core_recv)

    s_in[t] = small[...]
    for j in range(1, 8):
        t2 = (t + j) % 8
        remote(small, s_in.at[t], s_sem.at[0], s_sem.at[1], t2 // 2, z * 2 + t2 % 2).start()

    home_f, home_c = plane_of(z), f * 2 + x
    stays = (home_f == f) & (home_c == c)

    def deliver(src, dst, k):
        @pl.when(jnp.logical_not(stays))
        def _():
            remote(src, dst, out_sem.at[k], out_sem.at[k + 1], home_f, home_c).start()

        @pl.when(stays)
        def _():
            pltpu.make_async_copy(src, dst, out_sem.at[k + 1]).start()

    deliver(layer, layer_out, 0)
    sum_middle(part, from_core, out_buf, in_buf, send, core_recv, recv)

    def blocks(ref, dev):
        return ref.at[pl.ds(pl.multiple_of(dev * 32, 32), 32)]

    def send_grads(j, carry):
        dev = (me + j) % 32
        df, dc = dev // 8, dev % 8
        remote(blocks(g_ffn, dev), rf.at[z, t], rf_sem.at[0], rf_sem.at[1], df, dc).start()
        remote(blocks(g_attn, dev), ra.at[z, t], ra_sem.at[0], ra_sem.at[1], df, dc).start()
        return carry

    lax.fori_loop(1, 32, send_grads, 0)
    pltpu.make_async_copy(blocks(g_ffn, me), rf.at[z, t], rf_sem.at[1]).start()
    pltpu.make_async_copy(blocks(g_attn, me), ra.at[z, t], ra_sem.at[1]).start()
    for k in range(4):
        dev = t * 4 + k
        rows = g_down.at[pl.ds(k * 96, 96)]

        @pl.when(dev == me)
        def _():
            pltpu.make_async_copy(rows, rd.at[z], rd_sem.at[1]).start()

        @pl.when(dev != me)
        def _():
            remote(rows, rd.at[z], rd_sem.at[0], rd_sem.at[1], dev // 8, dev % 8).start()

    own.wait()
    back, _ = norm_back(x_own[...].astype(F32), gain[...], sum_end(part, from_core, in_buf, core_recv, recv))
    tok_own[...] = (dmid[...] + back).astype(BF16)
    deliver(tok_own, grad_tokens, 2)

    await_bytes(s_in.at[pl.ds(0, 7)], s_sem.at[1])
    sbuf[...] = jnp.sum(s_in[...], axis=0)
    p_in[z] = sbuf[...]
    for j in range(1, 4):
        remote(sbuf, p_in.at[z], p_sem.at[0], p_sem.at[1], f, ((z + j) % 4) * 2 + x).start()

    await_bytes(rf, rf_sem.at[1])
    for k in range(8):
        total = rf[0, k].astype(F32) + rf[1, k].astype(F32) + rf[2, k].astype(F32) + rf[3, k].astype(F32)
        o_g[:, k * 384 : k * 384 + 384] = total[:, 0:384]
        o_u[:, k * 384 : k * 384 + 384] = total[:, 384:768]
    await_bytes(rd, rd_sem.at[1])
    o_d[...] = rd[0].astype(F32) + rd[1].astype(F32) + rd[2].astype(F32) + rd[3].astype(F32)
    await_bytes(ra, ra_sem.at[1])
    for k in range(8):
        total = ra[0, k].astype(F32) + ra[1, k].astype(F32) + ra[2, k].astype(F32) + ra[3, k].astype(F32)
        o_q[:, k * 256 : k * 256 + 256] = total[:, 0:256]
        o_k[:, k * 128 : k * 128 + 128] = total[:, 256:384]
        o_v[:, k * 128 : k * 128 + 128] = total[:, 384:512]
        o_o[:, k * 256 : k * 256 + 256] = total[:, 512:768]
    await_bytes(p_in.at[pl.ds(0, 3)], p_sem.at[1])
    small_out[...] = jnp.sum(p_in[...], axis=0)

    await_bytes(layer_out, out_sem.at[1])
    await_bytes(grad_tokens, out_sem.at[3])

    @pl.when(jnp.logical_not(stays))
    def _():
        await_bytes(layer_out, out_sem.at[0])
        await_bytes(grad_tokens, out_sem.at[2])

    sum_sent(from_core, out_buf, send)
    await_bytes(s_in.at[pl.ds(0, 7)], s_sem.at[0])
    await_bytes(p_in.at[pl.ds(0, 3)], p_sem.at[0])
    await_bytes(g_ffn.at[pl.ds(0, 31 * 32)], rf_sem.at[0])
    await_bytes(g_attn.at[pl.ds(0, 31 * 32)], ra_sem.at[0])
    for k in range(4):

        @pl.when(t * 4 + k != me)
        def _():
            await_bytes(g_down.at[pl.ds(0, 96)], rd_sem.at[0])


def finish(part, x_all, gain, dmid, layer, g_attn, g_ffn, g_down, small):
    any_spec, vmem = pl.BlockSpec(memory_space=pl.ANY), pl.BlockSpec(memory_space=pltpu.VMEM)
    dma = pltpu.SemaphoreType.DMA
    return pl.pallas_call(
        finish_kernel,
        out_shape=(
            jax.ShapeDtypeStruct((ROWS, 1024), BF16),
            jax.ShapeDtypeStruct((ROWS, 1024), BF16),
            jax.ShapeDtypeStruct((32, 2048), F32),
            jax.ShapeDtypeStruct((32, 1024), F32),
            jax.ShapeDtypeStruct((32, 1024), F32),
            jax.ShapeDtypeStruct((32, 2048), F32),
            jax.ShapeDtypeStruct((32, 3072), F32),
            jax.ShapeDtypeStruct((32, 3072), F32),
            jax.ShapeDtypeStruct((96, 1024), F32),
            jax.ShapeDtypeStruct((8, 1024), F32),
        ),
        in_specs=[vmem, any_spec, vmem, vmem, any_spec, any_spec, any_spec, any_spec, vmem],
        out_specs=(any_spec, any_spec) + (vmem,) * 8,
        scratch_shapes=[
            pltpu.VMEM((ROWS, 1024), BF16),
            pltpu.VMEM((ROWS, 1024), BF16),
            pltpu.VMEM((4, 8, 32, 768), BF16),
            pltpu.VMEM((4, 8, 32, 768), BF16),
            pltpu.VMEM((4, 96, 1024), BF16),
            pltpu.VMEM((8, 1024), F32),
            pltpu.VMEM((8, 8, 1024), F32),
            pltpu.VMEM((4, 8, 1024), F32),
            dma,
        ]
        + SUM_SCRATCH
        + [dma((4,)), dma((2,)), dma((2,)), dma((2,)), dma((2,)), dma((2,))],
        compiler_params=pltpu.CompilerParams(collective_id=3, has_side_effects=True, vmem_limit_bytes=VMEM_LIMIT),
        name="finish",
    )(part, x_all, gain, dmid, layer, g_attn, g_ffn, g_down, small)


def rope_tables(length):
    inverse = 1000000.0 ** (-2.0 * np.arange(HEAD_DIM // 2, dtype=np.float64) / HEAD_DIM)
    angles = np.arange(length, dtype=np.float32)[:, None] * inverse.astype(np.float32)[None, :]
    angles = angles.astype(np.float32).astype(np.float64)
    cos, sin = np.cos(angles), np.sin(angles)
    return (
        np.concatenate([cos, cos], axis=1).astype(np.float32),
        np.concatenate([-sin, sin], axis=1).astype(np.float32),
    )


def per_device_planes(
    tokens, positions, w_query, w_key, w_value, w_output, w_gate, w_up, w_down, first_gain, second_gain, head_gain,
    cotangent,
):
    z = lax.axis_index("ctx") // 2
    me = lax.axis_index("fsdp") * 8 + lax.axis_index("ctx")
    gains = jnp.concatenate([first_gain, second_gain, head_gain, jnp.zeros((56,), BF16)]).astype(F32)[None]
    x_all, g_all, pos_all, w_attn, w_ffn, down, gains_all = gather(
        tokens[0], cotangent[0], positions, w_query, w_key, w_value, w_output.T, w_gate, w_up, w_down, gains
    )
    gains_all = gains_all[:, 0]
    gain_one = gains_all[:, 0:32].reshape(1, 1024)
    gain_two = gains_all[:, 32:64].reshape(1, 1024)
    gain_head = gains_all[:, 64:72].reshape(2, 128)
    starts = pos_all[plane_of(z), 0].reshape(16, 128)[:, 0] // 128
    blocks = jnp.arange(16, dtype=jnp.int32)
    perm = jnp.sum(jnp.where(starts[None, :] == blocks[:, None], blocks[None, :], 0), axis=1)
    cos, sin = rope_tables(2048)

    part, q, k, v, o, lse = attend(perm, x_all, w_attn, gain_one, gain_head, cos, sin)
    mid, h2_all = middle(part, x_all, gain_two)
    lpart, hpart, g_ffn, g_down = feed(h2_all, g_all, w_ffn, down)
    dmid, da_all, layer, gsecond = turn(hpart, lpart, mid, g_all, gain_two)
    tpart, g_attn, small = attend_back(
        perm, x_all, da_all, w_attn, gain_one, gain_head, cos, sin, q, k, v, o, lse
    )
    small = lax.dynamic_update_slice(small, gsecond, (1, 0))
    layer_out, grad_tokens, o_q, o_k, o_v, o_o, o_g, o_u, o_d, small = finish(
        tpart, x_all, gain_one, dmid, layer, g_attn, g_ffn, g_down, small
    )
    return (
        layer_out[None],
        grad_tokens[None],
        o_q,
        o_k,
        o_v,
        o_o.T,
        o_g,
        o_u,
        o_d,
        lax.dynamic_slice(small, (0, me * 32), (1, 32))[0],
        lax.dynamic_slice(small, (1, me * 32), (1, 32))[0],
        lax.dynamic_slice(small, (2, me * 8), (1, 8))[0],
    )


def solution(mesh):
    planes = mesh.shape["fsdp"] == 4 and mesh.shape["ctx"] == 8
    body = per_device_planes if planes else per_device
    return jax.shard_map(
        body,
        mesh=mesh,
        in_specs=(
            P("fsdp", "ctx", None),
            P("fsdp", None),
            P(("fsdp", "ctx"), None),
            P(("fsdp", "ctx"), None),
            P(("fsdp", "ctx"), None),
            P(None, ("fsdp", "ctx")),
            P(("fsdp", "ctx"), None),
            P(("fsdp", "ctx"), None),
            P(("fsdp", "ctx"), None),
            P(("fsdp", "ctx")),
            P(("fsdp", "ctx")),
            P(("fsdp", "ctx")),
            P("fsdp", "ctx", None),
        ),
        out_specs=(
            P("fsdp", "ctx", None),
            P("fsdp", "ctx", None),
            P(("fsdp", "ctx"), None),
            P(("fsdp", "ctx"), None),
            P(("fsdp", "ctx"), None),
            P(None, ("fsdp", "ctx")),
            P(("fsdp", "ctx"), None),
            P(("fsdp", "ctx"), None),
            P(("fsdp", "ctx"), None),
            P(("fsdp", "ctx")),
            P(("fsdp", "ctx")),
            P(("fsdp", "ctx")),
        ),
        check_vma=False,
    )
```

```python
from functools import partial

import jax
import jax.numpy as jnp
import numpy as np
from jax import lax
from jax.experimental import pallas as pl
from jax.experimental.pallas import tpu as pltpu
from jax.sharding import PartitionSpec as P

MESH = pl.DeviceIdType.MESH

HEADS = 16
KV_HEADS = 8
HEAD_DIM = 128


def normed(operand, gain_in):
    return (
        operand * lax.rsqrt(jnp.mean(operand * operand, axis=-1, keepdims=True) + 1e-06) * gain_in
    )


def rotary(operand, places):
    head_width = operand.shape[-1]
    half_width = head_width // 2
    inverse = 1000000.0 ** (-2.0 * jnp.arange(half_width, dtype=jnp.float32) / head_width)
    angles = places.astype(jnp.float32)[:, None] * inverse[None, :]
    cosine = jnp.concatenate([jnp.cos(angles), jnp.cos(angles)], axis=-1)[:, None, :]
    sine_table = jnp.concatenate([jnp.sin(angles), jnp.sin(angles)], axis=-1)[:, None, :]
    turned = jnp.concatenate([-operand[..., half_width:], operand[..., :half_width]], axis=-1)
    return operand * cosine + turned * sine_table


def head_prep(raw_proj, gain_in, places, head_count):
    row_count = raw_proj.shape[0]
    shaped = raw_proj.reshape(row_count, head_count, HEAD_DIM)
    return rotary(normed(shaped, gain_in), places).reshape(row_count, head_count * HEAD_DIM)


def gated(gate_raw, up_raw):
    return jax.nn.silu(gate_raw) * up_raw


def project(left_side, right_side):
    return jnp.dot(left_side, right_side, preferred_element_type=jnp.float32)


def project_back(left_side, right_side):
    return lax.dot_general(
        left_side, right_side, (((1,), (1,)), ((), ())), preferred_element_type=jnp.float32
    )


def outer_sum(left_side, right_side):
    return lax.dot_general(
        left_side, right_side, (((0,), (0,)), ((), ())), preferred_element_type=jnp.float32
    )


def halves_apart(rows_in, shard_count):
    shape_in = rows_in.shape
    split = rows_in.reshape((shard_count, 2, shape_in[0] // (2 * shard_count)) + shape_in[1:])
    return jnp.swapaxes(split, 0, 1).reshape(shape_in)


def halves_back(rows_in, shard_count):
    shape_in = rows_in.shape
    split = rows_in.reshape((2, shard_count, shape_in[0] // (2 * shard_count)) + shape_in[1:])
    return jnp.swapaxes(split, 0, 1).reshape(shape_in)


def key_layout(key_rows, value_rows, place_all):
    key_count = key_rows.shape[0]
    key_block = min(512, key_count)
    block_count = key_count // key_block
    key_parts = key_rows.reshape(block_count, key_block, KV_HEADS, HEAD_DIM)
    value_parts = value_rows.reshape(block_count, key_block, KV_HEADS, HEAD_DIM)
    place_parts = place_all.reshape(block_count, key_block)
    return (key_parts, value_parts, place_parts)


def attend_forward(queries, key_rows, value_rows, place_here, place_all):
    row_count = queries.shape[0]
    group_size = HEADS // KV_HEADS
    score_scale = HEAD_DIM ** (-0.5)
    grouped = queries.reshape(row_count, KV_HEADS, group_size, HEAD_DIM)
    layout = key_layout(key_rows, value_rows, place_all)
    top_place = jnp.max(place_here)

    def attend_step(state_now, block_item):
        key_part, value_part, place_part = block_item

        def attend_compute(state_in):
            run_max, run_sum, run_out = state_in
            scores = (
                jnp.einsum("qhge,khe->hgqk", grouped, key_part, preferred_element_type=jnp.float32)
                * score_scale
            )
            visible = place_part[None, None, None, :] <= place_here[None, None, :, None]
            scores = jnp.where(visible, scores, -1e30)
            new_max = jnp.maximum(run_max, jnp.max(scores, axis=-1))
            weights = jnp.where(visible, jnp.exp(scores - new_max[..., None]), 0.0)
            rescale = jnp.exp(run_max - new_max)
            run_sum = run_sum * rescale + jnp.sum(weights, axis=-1)
            mixed = jnp.einsum(
                "hgqk,khe->hgqe",
                weights.astype(jnp.bfloat16),
                value_part,
                preferred_element_type=jnp.float32,
            )
            run_out = run_out * rescale[..., None] + mixed
            return (new_max, run_sum, run_out)

        state_next = lax.cond(
            jnp.min(place_part) > top_place, lambda state_in: state_in, attend_compute, state_now
        )
        return (state_next, None)

    start_state = (
        jnp.full((KV_HEADS, group_size, row_count), -1e30, jnp.float32),
        jnp.zeros((KV_HEADS, group_size, row_count), jnp.float32),
        jnp.zeros((KV_HEADS, group_size, row_count, HEAD_DIM), jnp.float32),
    )
    (run_max, run_sum, run_out), _ = lax.scan(attend_step, start_state, layout)
    attention = (
        (run_out / run_sum[..., None]).transpose(2, 0, 1, 3).reshape(row_count, HEADS * HEAD_DIM)
    )
    return (attention, run_max + jnp.log(run_sum))


def row_dot_table(grad_attn, attention):
    row_count = grad_attn.shape[0]
    group_size = HEADS // KV_HEADS
    grad_grouped = grad_attn.reshape(row_count, KV_HEADS, group_size, HEAD_DIM)
    return jnp.sum(
        grad_grouped.astype(jnp.float32)
        * attention.reshape(row_count, KV_HEADS, group_size, HEAD_DIM),
        axis=-1,
    ).transpose(1, 2, 0)


def attend_backward(
    queries, key_rows, value_rows, grad_attn, row_dots, log_total, place_here, place_all
):
    row_count = queries.shape[0]
    key_count = key_rows.shape[0]
    group_size = HEADS // KV_HEADS
    score_scale = HEAD_DIM ** (-0.5)
    grouped = queries.reshape(row_count, KV_HEADS, group_size, HEAD_DIM)
    grad_grouped = grad_attn.reshape(row_count, KV_HEADS, group_size, HEAD_DIM)
    layout = key_layout(key_rows, value_rows, place_all)
    top_place = jnp.max(place_here)

    def back_step(grad_query, block_item):
        key_part, value_part, place_part = block_item
        key_block = key_part.shape[0]

        def back_compute(grad_in):
            scores = (
                jnp.einsum("qhge,khe->hgqk", grouped, key_part, preferred_element_type=jnp.float32)
                * score_scale
            )
            visible = place_part[None, None, None, :] <= place_here[None, None, :, None]
            weights = jnp.where(
                visible, jnp.exp(jnp.where(visible, scores, -1e30) - log_total[..., None]), 0.0
            )
            grad_probs = jnp.einsum(
                "qhge,khe->hgqk", grad_grouped, value_part, preferred_element_type=jnp.float32
            )
            grad_scores = (weights * (grad_probs - row_dots[..., None])).astype(jnp.bfloat16)
            grad_out = (
                grad_in
                + jnp.einsum(
                    "hgqk,khe->qhge", grad_scores, key_part, preferred_element_type=jnp.float32
                )
                * score_scale
            )
            grad_keys = (
                jnp.einsum(
                    "hgqk,qhge->khe", grad_scores, grouped, preferred_element_type=jnp.float32
                )
                * score_scale
            )
            grad_values = jnp.einsum(
                "hgqk,qhge->khe",
                weights.astype(jnp.bfloat16),
                grad_grouped,
                preferred_element_type=jnp.float32,
            )
            return (
                grad_out,
                (
                    grad_keys.reshape(key_block, KV_HEADS * HEAD_DIM),
                    grad_values.reshape(key_block, KV_HEADS * HEAD_DIM),
                ),
            )

        def skipped(grad_in):
            empty_terms = jnp.zeros((key_block, KV_HEADS * HEAD_DIM), jnp.float32)
            return (grad_in, (empty_terms, empty_terms))

        return lax.cond(jnp.min(place_part) > top_place, skipped, back_compute, grad_query)

    start_grad = jnp.zeros((row_count, KV_HEADS, group_size, HEAD_DIM), jnp.float32)
    grad_query, key_terms = lax.scan(back_step, start_grad, layout)
    grad_query = grad_query.reshape(row_count, HEADS * HEAD_DIM)
    return (
        grad_query,
        key_terms[0].reshape(key_count, KV_HEADS * HEAD_DIM),
        key_terms[1].reshape(key_count, KV_HEADS * HEAD_DIM),
    )


def per_device(
    tokens,
    positions,
    w_query,
    w_key,
    w_value,
    w_output,
    w_gate,
    w_up,
    w_down,
    first_gain,
    second_gain,
    head_gain,
    cotangent,
):
    inputs = tokens[0].astype(jnp.float32)
    row_count = inputs.shape[0]
    shard_count = lax.axis_size("ctx")
    place_stored = positions[0]
    place_here = lax.dynamic_slice_in_dim(
        place_stored, lax.axis_index("ctx") * row_count, row_count
    )
    place_all = halves_apart(place_stored, shard_count)
    query_full, key_full, value_full, output_full, gain_first, gain_head = (
        lax.all_gather(w_query, ("fsdp", "ctx"), axis=0, tiled=True),
        lax.all_gather(w_key, ("fsdp", "ctx"), axis=0, tiled=True),
        lax.all_gather(w_value, ("fsdp", "ctx"), axis=0, tiled=True),
        lax.all_gather(w_output, ("fsdp", "ctx"), axis=1, tiled=True),
        lax.all_gather(first_gain, ("fsdp", "ctx"), axis=0, tiled=True),
        lax.all_gather(head_gain, ("fsdp", "ctx"), axis=0, tiled=True),
    )
    gain_one = gain_first.astype(jnp.float32)
    gain_query = gain_head[:HEAD_DIM].astype(jnp.float32)
    gain_key = gain_head[HEAD_DIM:].astype(jnp.float32)
    hidden_one = normed(inputs, gain_one).astype(jnp.bfloat16)
    query_raw = project(hidden_one, query_full)
    key_raw = project(hidden_one, key_full)
    value_rows = project(hidden_one, value_full).astype(jnp.bfloat16)
    query_prep = partial(head_prep, places=place_here, head_count=HEADS)
    key_prep = partial(head_prep, places=place_here, head_count=KV_HEADS)
    queries, query_back = jax.vjp(query_prep, query_raw, gain_query)
    key_local, key_back = jax.vjp(key_prep, key_raw, gain_key)
    queries = queries.astype(jnp.bfloat16)
    key_local = key_local.astype(jnp.bfloat16)
    key_stored, value_stored = (
        lax.all_gather(key_local, "ctx", axis=0, tiled=True),
        lax.all_gather(value_rows, "ctx", axis=0, tiled=True),
    )
    key_all = halves_apart(key_stored, shard_count)
    value_all = halves_apart(value_stored, shard_count)
    attention, log_total = attend_forward(queries, key_all, value_all, place_here, place_all)
    attn_low = attention.astype(jnp.bfloat16)
    middle = inputs + project(attn_low, output_full)
    gate_full, up_full, down_full, gain_second = (
        lax.all_gather(w_gate, ("fsdp", "ctx"), axis=0, tiled=True),
        lax.all_gather(w_up, ("fsdp", "ctx"), axis=0, tiled=True),
        lax.all_gather(w_down, ("fsdp", "ctx"), axis=0, tiled=True),
        lax.all_gather(second_gain, ("fsdp", "ctx"), axis=0, tiled=True),
    )
    gain_two = gain_second.astype(jnp.float32)
    hidden_two = normed(middle, gain_two).astype(jnp.bfloat16)
    gate_raw = project(hidden_two, gate_full)
    up_raw = project(hidden_two, up_full)
    activated, gated_back = jax.vjp(gated, gate_raw, up_raw)
    act_low = activated.astype(jnp.bfloat16)
    layer_out = (middle + project(act_low, down_full)).astype(jnp.bfloat16)
    grad_out = cotangent[0].astype(jnp.float32)
    gate_full, up_full, down_full, gain_second = (
        lax.all_gather(w_gate, ("fsdp", "ctx"), axis=0, tiled=True),
        lax.all_gather(w_up, ("fsdp", "ctx"), axis=0, tiled=True),
        lax.all_gather(w_down, ("fsdp", "ctx"), axis=0, tiled=True),
        lax.all_gather(second_gain, ("fsdp", "ctx"), axis=0, tiled=True),
    )
    gain_two = gain_second.astype(jnp.float32)
    out_low = grad_out.astype(jnp.bfloat16)
    down_terms = outer_sum(act_low, out_low)
    grad_act = project_back(out_low, down_full)
    grad_gate_raw, grad_up_raw = gated_back(grad_act)
    gate_low = grad_gate_raw.astype(jnp.bfloat16)
    up_low = grad_up_raw.astype(jnp.bfloat16)
    gate_terms = outer_sum(hidden_two, gate_low)
    up_terms = outer_sum(hidden_two, up_low)
    grad_hidden_two = project_back(gate_low, gate_full) + project_back(up_low, up_full)
    _, norm_two_back = jax.vjp(normed, middle, gain_two)
    middle_part, gain_two_terms = norm_two_back(grad_hidden_two)
    grad_gate, grad_up, grad_down, grad_second = (
        lax.psum_scatter(gate_terms, ("fsdp", "ctx"), scatter_dimension=0, tiled=True),
        lax.psum_scatter(up_terms, ("fsdp", "ctx"), scatter_dimension=0, tiled=True),
        lax.psum_scatter(down_terms, ("fsdp", "ctx"), scatter_dimension=0, tiled=True),
        lax.psum_scatter(gain_two_terms, ("fsdp", "ctx"), scatter_dimension=0, tiled=True),
    )
    grad_middle = grad_out + middle_part
    query_full, key_full, value_full, output_full, gain_first, gain_head = (
        lax.all_gather(w_query, ("fsdp", "ctx"), axis=0, tiled=True),
        lax.all_gather(w_key, ("fsdp", "ctx"), axis=0, tiled=True),
        lax.all_gather(w_value, ("fsdp", "ctx"), axis=0, tiled=True),
        lax.all_gather(w_output, ("fsdp", "ctx"), axis=1, tiled=True),
        lax.all_gather(first_gain, ("fsdp", "ctx"), axis=0, tiled=True),
        lax.all_gather(head_gain, ("fsdp", "ctx"), axis=0, tiled=True),
    )
    gain_one = gain_first.astype(jnp.float32)
    middle_low = grad_middle.astype(jnp.bfloat16)
    output_terms = outer_sum(attn_low, middle_low)
    grad_attn = project_back(middle_low, output_full).astype(jnp.bfloat16)
    row_dots = row_dot_table(grad_attn, attention)
    grad_queries, key_terms, value_terms = attend_backward(
        queries, key_all, value_all, grad_attn, row_dots, log_total, place_here, place_all
    )
    key_terms = halves_back(key_terms, shard_count)
    value_terms = halves_back(value_terms, shard_count)
    grad_key_local, grad_value_local = (
        lax.psum_scatter(
            key_terms.astype(jnp.bfloat16), "ctx", scatter_dimension=0, tiled=True
        ).astype(jnp.float32),
        lax.psum_scatter(
            value_terms.astype(jnp.bfloat16), "ctx", scatter_dimension=0, tiled=True
        ).astype(jnp.float32),
    )
    grad_query_raw, gain_query_terms = query_back(grad_queries)
    grad_key_raw, gain_key_terms = key_back(grad_key_local)
    query_low = grad_query_raw.astype(jnp.bfloat16)
    keyraw_low = grad_key_raw.astype(jnp.bfloat16)
    value_low = grad_value_local.astype(jnp.bfloat16)
    query_terms = outer_sum(hidden_one, query_low)
    key_weight_terms = outer_sum(hidden_one, keyraw_low)
    value_weight_terms = outer_sum(hidden_one, value_low)
    grad_hidden_one = (
        project_back(query_low, query_full)
        + project_back(keyraw_low, key_full)
        + project_back(value_low, value_full)
    )
    _, norm_one_back = jax.vjp(normed, inputs, gain_one)
    input_part, gain_one_terms = norm_one_back(grad_hidden_one)
    head_terms = jnp.concatenate([gain_query_terms, gain_key_terms])
    grad_query, grad_key, grad_value, grad_output, grad_first, grad_head = (
        lax.psum_scatter(query_terms, ("fsdp", "ctx"), scatter_dimension=0, tiled=True),
        lax.psum_scatter(key_weight_terms, ("fsdp", "ctx"), scatter_dimension=0, tiled=True),
        lax.psum_scatter(value_weight_terms, ("fsdp", "ctx"), scatter_dimension=0, tiled=True),
        lax.psum_scatter(output_terms, ("fsdp", "ctx"), scatter_dimension=1, tiled=True),
        lax.psum_scatter(gain_one_terms, ("fsdp", "ctx"), scatter_dimension=0, tiled=True),
        lax.psum_scatter(head_terms, ("fsdp", "ctx"), scatter_dimension=0, tiled=True),
    )
    grad_tokens = (grad_middle + input_part).astype(jnp.bfloat16)
    return (
        layer_out[None],
        grad_tokens[None],
        grad_query,
        grad_key,
        grad_value,
        grad_output,
        grad_gate,
        grad_up,
        grad_down,
        grad_first,
        grad_second,
        grad_head,
    )


ROWS = 256
QROWS = 512
EPS = 1e-06
LOG2E = 1.4426950408889634
SCALE = HEAD_DIM**-0.5
VMEM_LIMIT = 60 * 1024 * 1024
BF16 = jnp.bfloat16
F32 = jnp.float32


def dot_nn(a, b):
    return lax.dot_general(a, b, (((1,), (0,)), ((), ())), preferred_element_type=F32)


def dot_nt(a, b):
    return lax.dot_general(a, b, (((1,), (1,)), ((), ())), preferred_element_type=F32)


def dot_tn(a, b):
    return lax.dot_general(a, b, (((0,), (0,)), ((), ())), preferred_element_type=F32)


def whereabouts():
    f, c = lax.axis_index("fsdp"), lax.axis_index("ctx")
    return f, c, f // 2, f % 2, c // 2, c % 2


def plane_of(s):
    return (s % 2) * 2 + s // 2


def remote(src, dst, send, recv, fsdp, ctx):
    return pltpu.make_async_remote_copy(
        src_ref=src, dst_ref=dst, send_sem=send, recv_sem=recv, device_id=(fsdp, ctx), device_id_type=MESH
    )


def await_bytes(ref, sem):
    pltpu.make_async_copy(ref, ref, sem).wait()


def greet_all():
    f, c, y, core, z, x = whereabouts()
    barrier = pltpu.get_barrier_semaphore()
    me = f * 8 + c

    def greet(j, carry):
        dev = (me + j) % 32
        pl.semaphore_signal(barrier, inc=1, device_id=(dev // 8, dev % 8), device_id_type=MESH)
        return carry

    lax.fori_loop(1, 32, greet, 0)
    pl.semaphore_wait(barrier, 31)


def chip_peer(r):
    f, c, y, core, z, x = whereabouts()
    y2 = 1 - y if r & 2 else y
    x2 = 1 - x if r & 1 else x
    return y2, x2


def chunk_of(r, core):
    y2, x2 = chip_peer(r)
    return (y2 * 2 + core) * 2 + x2


def rows_of(ref, chunk):
    return ref.at[pl.ds(pl.multiple_of(chunk * ROWS, ROWS), ROWS)]


def head_norm_rope(raw, gain, cos, sin):
    r = lax.rsqrt(jnp.mean(raw * raw, axis=-1, keepdims=True) + EPS)
    u = raw * r * gain
    return u * cos + pltpu.roll(u, HEAD_DIM // 2, 1) * sin


def norm_rows(values, gain):
    v = values.astype(F32)
    return v * lax.rsqrt(jnp.mean(v * v, axis=-1, keepdims=True) + EPS) * gain


def sum_begin(part, from_core, send, core_recv):
    f, c, y, core, z, x = whereabouts()
    for r in (3, 1, 2, 0):
        remote(
            rows_of(part, chunk_of(r, 1 - core)), from_core.at[r], send.at[0], core_recv.at[r], y * 2 + 1 - core, c
        ).start()


def sum_middle(part, from_core, out_buf, in_buf, send, core_recv, recv):
    f, c, y, core, z, x = whereabouts()
    for r in (3, 1, 2):
        await_bytes(from_core.at[r], core_recv.at[r])
        first = pl.multiple_of(chunk_of(r, core) * ROWS, ROWS)
        out_buf[r - 1] = (part[pl.ds(first, ROWS), :].astype(F32) + from_core[r].astype(F32)).astype(BF16)
        y2, x2 = chip_peer(r)
        remote(out_buf.at[r - 1], in_buf.at[r - 1], send.at[r], recv.at[r - 1], y2 * 2 + core, z * 2 + x2).start()


def sum_end(part, from_core, in_buf, core_recv, recv):
    f, c, y, core, z, x = whereabouts()
    await_bytes(from_core.at[0], core_recv.at[0])
    for r in (1, 2, 3):
        await_bytes(in_buf.at[r - 1], recv.at[r - 1])
    first = pl.multiple_of(chunk_of(0, core) * ROWS, ROWS)
    total = part[pl.ds(first, ROWS), :].astype(F32) + from_core[0].astype(F32)
    return total + in_buf[0].astype(F32) + in_buf[1].astype(F32) + in_buf[2].astype(F32)


def sum_sent(from_core, out_buf, send):
    await_bytes(from_core, send.at[0])
    for r in (1, 2, 3):
        await_bytes(out_buf.at[r - 1], send.at[r])


def norm_back(values, gain, dy):
    r = lax.rsqrt(jnp.mean(values * values, axis=-1, keepdims=True) + EPS)
    cdy = gain * dy
    back = r * cdy - values * (r * r * r) * jnp.mean(cdy * values, axis=-1, keepdims=True)
    return back, dy * values * r


def unturn(d, cos, sin):
    return d * cos - pltpu.roll(d, HEAD_DIM // 2, 1) * sin


def order_z(n, z):
    upper = z // 2
    low = (z + upper) % 2
    base = (low, 1 - low, 2, 3)[n]
    return base + upper * (3 - 2 * base)


def split_sum(partial, core_out, from_core, out_buf, in_buf, keep, send, core_recv, recv):
    f, c, y, core, z, x = whereabouts()
    half = ROWS // 2

    def to_core(k, carry):
        r = 3 - k
        y2, x2 = (y + r // 2) % 2, (x + r % 2) % 2
        chunk = (y2 * 2 + 1 - core) * 2 + x2
        core_out[r] = partial(chunk).astype(BF16)
        remote(core_out.at[r], from_core.at[r], send.at[6], core_recv.at[r], y * 2 + 1 - core, c).start()
        return carry

    lax.fori_loop(0, 4, to_core, 0)

    def both(r):
        await_bytes(from_core.at[r], core_recv.at[r])
        return partial(chunk_of(r, core)) + from_core[r].astype(F32)

    def over_x(k):
        remote(out_buf.at[k], in_buf.at[k], send.at[k], recv.at[k], f, z * 2 + 1 - x).start()

    def over_y(k):
        remote(out_buf.at[k], in_buf.at[k], send.at[k], recv.at[k], (1 - y) * 2 + core, c).start()

    total = both(3)
    out_buf[0] = total[:half].astype(BF16)
    over_x(0)
    out_buf[1] = total[half:].astype(BF16)
    over_y(1)
    total = both(1)
    out_buf[2] = total[:half].astype(BF16)
    over_x(2)
    keep[0] = total[half:]
    total = both(2)
    out_buf[3] = total[half:].astype(BF16)
    over_y(3)
    keep[1] = total[:half]
    await_bytes(in_buf.at[0], recv.at[0])
    out_buf[5] = (keep[1] + in_buf[0].astype(F32)).astype(BF16)
    over_y(5)
    await_bytes(in_buf.at[1], recv.at[1])
    out_buf[4] = (keep[0] + in_buf[1].astype(F32)).astype(BF16)
    over_x(4)
    total = both(0)
    keep[0] = total[:half]
    keep[1] = total[half:]


def split_sum_end(in_buf, keep, recv):
    for k in (2, 3, 4, 5):
        await_bytes(in_buf.at[k], recv.at[k])
    return (
        keep[0] + in_buf[2].astype(F32) + in_buf[5].astype(F32),
        keep[1] + in_buf[3].astype(F32) + in_buf[4].astype(F32),
    )


def split_sum_sent(from_core, out_buf, send):
    await_bytes(from_core, send.at[6])
    for k in range(6):
        await_bytes(out_buf.at[k], send.at[k])


SPLIT_SUM_SCRATCH = [
    pltpu.VMEM((4, ROWS, 1024), BF16),
    pltpu.VMEM((4, ROWS, 1024), BF16),
    pltpu.VMEM((6, ROWS // 2, 1024), BF16),
    pltpu.VMEM((6, ROWS // 2, 1024), BF16),
    pltpu.VMEM((2, ROWS // 2, 1024), F32),
    pltpu.SemaphoreType.DMA((7,)),
    pltpu.SemaphoreType.DMA((4,)),
    pltpu.SemaphoreType.DMA((6,)),
]


def rows_in_order(pos_s, ids_s, perm_s):
    ids = [lax.div(pos_s[0, j * 128], jnp.int32(128)) for j in range(16)]
    for b in range(16):
        ids_s[b] = ids[b]
        place = jnp.int32(0)
        for j in range(16):
            place = place + j * (1 - lax.min(lax.abs(ids[j] - b), jnp.int32(1)))
        perm_s[b] = lax.min(place, jnp.int32(15))


def turns(table):
    cos, sin = table[:, 0 : HEAD_DIM // 2], table[:, HEAD_DIM // 2 :]
    return jnp.concatenate([cos, cos], axis=1), jnp.concatenate([-sin, sin], axis=1)


def two_blocks(ref, chunk, cols):
    return ref[pl.ds(chunk * 2, 2), :, cols].reshape(ROWS, -1)


def put_two(ref, chunk, cols, value):
    for k in range(2):
        ref[chunk * 2 + k, :, cols] = value[k * 128 : k * 128 + 128]


def gain_rows(gains_all):
    one = [jnp.sum(gains_all[4 * m : 4 * m + 4, 0:1, :], axis=0) for m in range(8)]
    two = [jnp.sum(gains_all[4 * m : 4 * m + 4, 1:2, :], axis=0) for m in range(8)]
    query = jnp.sum(gains_all[0:16, 2:3, :], axis=0)
    key = jnp.sum(gains_all[16:32, 3:4, :], axis=0)
    return jnp.concatenate(one, axis=1), jnp.concatenate(two, axis=1), query, key


def first_kernel(
    tok, cot, pos, wq, wk, wv, wo, wg, wu, wd, gains, table_h,
    g_all, w_down, h_out, q_out, k_out, v_out, o_out, lse_ref, w1, w2, mid, x_out, pos_v, gains_out,
    x_all, pack1, pack2, gains_all, table_s, h_s, q_st, k_st, v_st, q_s, k_s, v_s, o_s, vt, acc, total,
    gain_s, pos_s, ids_s, perm_s,
    x_recv, g_recv, hop_send, x_send, g_send, pos_sem, gain_sem, w1_sem, w2_sem, wd_sem, tab_sem, out_sem, perm_sem,
    core_out, from_core, out_buf, in_buf, keep, send, core_recv, recv,
):
    f, c, y, core, z, x = whereabouts()
    me, t = f * 8 + c, f * 2 + x
    table = pltpu.make_async_copy(table_h, table_s, tab_sem)
    table.start()
    for k in range(8):
        pack1[k, :, 0:256] = wq[:, k * 256 : k * 256 + 256]
        pack1[k, :, 256:384] = wk[:, k * 128 : k * 128 + 128]
        pack1[k, :, 384:512] = wv[:, k * 128 : k * 128 + 128]
    greet_all()

    home = plane_of(f)
    seq = plane_of(z)
    ys, cs = seq // 2, seq % 2

    def hop(src, dst, recv_, k):
        @pl.when(home != z)
        def _():
            remote(src, rows_of(dst, c), hop_send.at[k], recv_.at[c], f, home * 2 + x).start()

        @pl.when(home == z)
        def _():
            pltpu.make_async_copy(src, rows_of(dst, c), recv_.at[c]).start()

    def relay_first(buf, recv_, send_, n):
        ch = order_z(n, z) * 2 + x
        part = rows_of(buf, ch)

        @pl.when(core == cs)
        def _():
            await_bytes(part, recv_.at[ch])

            @pl.when(y == ys)
            def _():
                remote(part, part, send_.at[2], recv_.at[ch], (1 - y) * 2 + core, c).start()

            remote(part, part, send_.at[1], recv_.at[ch], f, z * 2 + 1 - x).start()
            remote(part, part, send_.at[0], recv_.at[ch], y * 2 + 1 - core, c).start()

    def relay_second(buf, recv_, send_, n):
        ch = order_z(n, z) * 2 + 1 - x
        part = rows_of(buf, ch)

        @pl.when(core == cs)
        def _():
            await_bytes(part, recv_.at[ch])
            remote(part, part, send_.at[0], recv_.at[ch], y * 2 + 1 - core, c).start()

    def relay_done(buf, send_):
        @pl.when(core == cs)
        def _():
            await_bytes(buf, send_.at[0])
            await_bytes(buf.at[pl.ds(0, 4 * ROWS)], send_.at[1])

            @pl.when(y == ys)
            def _():
                await_bytes(buf.at[pl.ds(0, 4 * ROWS)], send_.at[2])

    def my_rows(ref):
        return ref.at[pl.ds(pl.multiple_of(me * 32, 32), 32)]

    def plane_rows(ref, k):
        return ref.at[pl.ds(pl.multiple_of((k * 8 + z * 2) * 32, 64), 64)]

    def weights_in_plane(pack, w, sem):
        pltpu.make_async_copy(pack.at[t], my_rows(w), sem.at[1]).start()
        for j in range(1, 8):
            t2 = (t + j) % 8
            remote(pack.at[t2], my_rows(w), sem.at[0], sem.at[1], t2 // 2, z * 2 + t2 % 2).start()

    def weights_across(w, sem):
        await_bytes(w.at[pl.ds(0, 256)], sem.at[1])
        for j in (1, 3, 2):
            for k in range(4):
                remote(plane_rows(w, k), plane_rows(w, k), sem.at[2], sem.at[3], f, ((z + j) % 4) * 2 + x).start()

    def weights_done(pack, w, sem):
        await_bytes(pack.at[pl.ds(0, 7)], sem.at[0])
        await_bytes(w.at[pl.ds(0, 768)], sem.at[2])

    hop(tok, x_all, x_recv, 0)
    weights_in_plane(pack1, w1, w1_sem)

    @pl.when(f == seq)
    def _():
        pltpu.make_async_copy(pos, pos_v, pos_sem.at[1]).start()
        for j in range(1, 4):
            remote(pos, pos_v, pos_sem.at[0], pos_sem.at[1], (f + j) % 4, c).start()

    pltpu.make_async_copy(gains, gains_all.at[me], gain_sem.at[1]).start()

    def send_gains(j, carry):
        dev = (me + j) % 32
        remote(gains, gains_all.at[me], gain_sem.at[0], gain_sem.at[1], dev // 8, dev % 8).start()
        return carry

    lax.fori_loop(1, 32, send_gains, 0)
    relay_first(x_all, x_recv, x_send, 0)
    weights_across(w1, w1_sem)
    for k in range(8):
        pack2[k, :, 0:256] = wo[:, k * 256 : k * 256 + 256]
        pack2[k, :, 256:640] = wg[:, k * 384 : k * 384 + 384]
        pack2[k, :, 640:1024] = wu[:, k * 384 : k * 384 + 384]
    await_bytes(gains_all, gain_sem.at[1])
    one, two, gain_q, gain_k = gain_rows(gains_all)
    gain_s[...] = jnp.zeros_like(gain_s)
    gain_s[0:1, :] = one
    gain_s[1:2, :] = two
    gain_s[2:3, 0:128] = gain_q
    gain_s[3:4, 0:128] = gain_k
    await_bytes(pos_v, pos_sem.at[1])
    pos_copy = pltpu.make_async_copy(pos_v, pos_s, perm_sem)
    pos_copy.start()
    pos_copy.wait()
    rows_in_order(pos_s, ids_s, perm_s)

    def norm_chunk(ch):
        rows = pl.ds(pl.multiple_of(ch * ROWS, ROWS), ROWS)
        h_s[rows, :] = norm_rows(x_all[rows, :], gain_s[0:1, :]).astype(BF16)
        pltpu.make_async_copy(rows_of(h_s, ch), rows_of(h_out, ch), out_sem.at[0]).start()

    def secondary_wait(ch):
        @pl.when(core != cs)
        def _():
            await_bytes(rows_of(x_all, ch), x_recv.at[ch])

    for n in range(4):
        if n:
            relay_first(x_all, x_recv, x_send, n)
        secondary_wait(order_z(n, z) * 2 + x)
        norm_chunk(order_z(n, z) * 2 + x)
    hop(cot, g_all, g_recv, 1)
    for n in range(4):
        relay_second(x_all, x_recv, x_send, n)
        secondary_wait(order_z(n, z) * 2 + 1 - x)
        norm_chunk(order_z(n, z) * 2 + 1 - x)

    weights_in_plane(pack2, w2, w2_sem)
    t_down = me // 4
    down_rows = w_down.at[pl.ds(pl.multiple_of((me % 4) * 96, 32), 96)]
    self_down = t_down == t
    for k in range(4):
        here = self_down & (z == k)

        @pl.when(here)
        def _():
            pltpu.make_async_copy(wd, down_rows, wd_sem.at[1]).start()

        @pl.when(jnp.logical_not(here))
        def _():
            remote(wd, down_rows, wd_sem.at[0], wd_sem.at[1], t_down // 2, k * 2 + t_down % 2).start()

    table.wait()
    await_bytes(w1.at[pl.ds(0, 768)], w1_sem.at[3])
    own_x = pltpu.make_async_copy(rows_of(x_all, t), x_out, out_sem.at[1])
    own_x.start()

    def project(ch, carry):
        rows = pl.ds(pl.multiple_of(ch * ROWS, ROWS), ROWS)
        raw = dot_nn(h_s[rows, :], w1[...])
        cos, sin = turns(jnp.concatenate([table_s[ids_s[ch * 2 + k]] for k in range(2)], axis=0))
        gq, gk = gain_s[2:3, 0:128], gain_s[3:4, 0:128]
        for k in range(2):
            cols = slice(k * 128, k * 128 + 128)
            put_two(q_st, ch, cols, head_norm_rope(raw[:, cols], gq, cos, sin).astype(BF16))
        put_two(k_st, ch, slice(0, 128), head_norm_rope(raw[:, 256:384], gk, cos, sin).astype(BF16))
        put_two(v_st, ch, slice(0, 128), raw[:, 384:512].astype(BF16))
        return carry

    lax.fori_loop(0, 8, project, 0)
    weights_across(w2, w2_sem)

    def arrange(b, carry):
        for k in range(4):
            rows = pl.ds(pl.multiple_of(b * QROWS + k * 128, 128), 128)
            stored = perm_s[b * 4 + k]
            q_s[rows, :] = q_st[stored]
            k_s[rows, :] = k_st[stored]
            v_s[rows, :] = v_st[stored]
        vt[b] = v_s[pl.ds(pl.multiple_of(b * QROWS, QROWS), QROWS), :].T
        return carry

    lax.fori_loop(0, 4, arrange, 0)
    outs = [
        pltpu.make_async_copy(a, b, out_sem.at[k])
        for a, b, k in ((q_s, q_out, 2), (k_s, k_out, 3), (v_s, v_out, 4))
    ]
    for copy in outs:
        copy.start()

    def query_tile(qt):
        def step(kt, diagonal):
            kb = k_s[pl.ds(pl.multiple_of(kt * QROWS, QROWS), QROWS), :]
            vb = vt[kt]
            for g in range(4):
                head, part = g // 2, g % 2
                qb = q_s[pl.ds(qt * QROWS + part * 256, 256), head * 128 : head * 128 + 128]
                depth = 256 * (part + 1) if diagonal else QROWS
                s = dot_nt(kb[:depth], qb)
                p = jnp.exp2(s * (SCALE * LOG2E))
                if diagonal:
                    ki = lax.broadcasted_iota(jnp.int32, (depth, 256), 0)
                    qi = lax.broadcasted_iota(jnp.int32, (depth, 256), 1) + part * 256
                    p = jnp.where(ki <= qi, p, 0.0)
                cols = slice(g * 256, g * 256 + 256)
                total[:, cols] += jnp.sum(p, axis=0, keepdims=True)
                acc[:, cols] += dot_nn(vb[:, :depth], p.astype(BF16))

        total[...] = jnp.zeros_like(total)
        acc[...] = jnp.zeros_like(acc)

        def off(kt, inner):
            step(kt, False)
            return inner

        lax.fori_loop(0, qt, off, 0)
        step(qt, True)
        sums = total[...]
        lse_ref[qt] = jnp.log2(sums)
        out = acc[...] * (1.0 / sums)
        for g in range(4):
            head, part = g // 2, g % 2
            value = out[:, g * 256 : g * 256 + 256].T.astype(BF16)
            put_two(o_s, qt * 2 + part, slice(head * 128, head * 128 + 128), value)

    for qt in range(4):
        query_tile(qt)
        relay_first(g_all, g_recv, g_send, qt)
    copy_o = pltpu.make_async_copy(o_s, o_out, out_sem.at[5])
    copy_o.start()
    await_bytes(w2.at[pl.ds(0, 768)], w2_sem.at[3])

    def partial(chunk):
        rows = jnp.concatenate([o_s[ids_s[chunk * 2 + k]] for k in range(2)], axis=0)
        return dot_nt(rows, w2[:, 0:256])

    split_sum(partial, core_out, from_core, out_buf, in_buf, keep, send, core_recv, recv)
    for n in range(4):
        relay_second(g_all, g_recv, g_send, n)
    low, high = split_sum_end(in_buf, keep, recv)
    half = ROWS // 2
    first = pl.multiple_of(t * ROWS, ROWS)
    mid[0:half, :] = x_all[pl.ds(first, half), :].astype(F32) + low
    mid[half:ROWS, :] = x_all[pl.ds(first + half, half), :].astype(F32) + high
    gains_out[...] = gain_s[...]

    for ch in range(8):

        @pl.when(core != cs)
        def _():
            await_bytes(g_all.at[pl.ds(ch * ROWS, ROWS)], g_recv.at[ch])

    await_bytes(w_down, wd_sem.at[1])
    split_sum_sent(from_core, out_buf, send)
    await_bytes(h_out, out_sem.at[0])
    own_x.wait()
    for copy in outs:
        copy.wait()
    copy_o.wait()

    @pl.when(home != z)
    def _():
        await_bytes(tok, hop_send.at[0])
        await_bytes(cot, hop_send.at[1])

    relay_done(x_all, x_send)
    relay_done(g_all, g_send)

    @pl.when(f == seq)
    def _():
        for j in range(3):
            await_bytes(pos_v, pos_sem.at[0])

    await_bytes(gains_all.at[pl.ds(0, 31)], gain_sem.at[0])
    weights_done(pack1, w1, w1_sem)
    weights_done(pack2, w2, w2_sem)
    for k in range(4):

        @pl.when(jnp.logical_not(self_down & (z == k)))
        def _():
            await_bytes(wd, wd_sem.at[0])


def first(tok, cot, pos, wq, wk, wv, wo, wg, wu, wd, gains, table):
    any_spec, vmem = pl.BlockSpec(memory_space=pl.ANY), pl.BlockSpec(memory_space=pltpu.VMEM)
    dma = pltpu.SemaphoreType.DMA
    bf = lambda *shape: jax.ShapeDtypeStruct(shape, BF16)
    fl = lambda *shape: jax.ShapeDtypeStruct(shape, F32)
    return pl.pallas_call(
        first_kernel,
        out_shape=(
            bf(2048, 1024), bf(384, 1024), bf(2048, 1024), bf(2048, 256), bf(2048, 128), bf(2048, 128), bf(16, 128, 256),
            fl(4, 1, 1024), bf(1024, 512), bf(1024, 1024), fl(ROWS, 1024), bf(ROWS, 1024),
            jax.ShapeDtypeStruct((1, 2048), jnp.int32), fl(8, 1024),
        ),
        in_specs=[any_spec] * 3 + [vmem] * 6 + [any_spec] * 3,
        out_specs=(any_spec,) * 7 + (vmem,) * 4 + (any_spec, vmem, vmem),
        scratch_shapes=[
            pltpu.VMEM((2048, 1024), BF16),
            pltpu.VMEM((8, 32, 512), BF16),
            pltpu.VMEM((8, 32, 1024), BF16),
            pltpu.VMEM((32, 4, 128), F32),
            pltpu.VMEM((16, 128, 128), F32),
            pltpu.VMEM((2048, 1024), BF16),
            pltpu.VMEM((16, 128, 256), BF16),
            pltpu.VMEM((16, 128, 128), BF16),
            pltpu.VMEM((16, 128, 128), BF16),
            pltpu.VMEM((2048, 256), BF16),
            pltpu.VMEM((2048, 128), BF16),
            pltpu.VMEM((2048, 128), BF16),
            pltpu.VMEM((16, 128, 256), BF16),
            pltpu.VMEM((4, 128, QROWS), BF16),
            pltpu.VMEM((128, 1024), F32),
            pltpu.VMEM((1, 1024), F32),
            pltpu.VMEM((8, 1024), F32),
            pltpu.SMEM((1, 2048), jnp.int32),
            pltpu.SMEM((16,), jnp.int32),
            pltpu.SMEM((16,), jnp.int32),
            dma((8,)), dma((8,)), dma((2,)), dma((3,)), dma((3,)), dma((2,)), dma((2,)),
            dma((4,)), dma((4,)), dma((2,)), dma, dma((6,)), dma,
        ]
        + SPLIT_SUM_SCRATCH,
        compiler_params=pltpu.CompilerParams(collective_id=0, has_side_effects=True, vmem_limit_bytes=VMEM_LIMIT),
        name="first",
    )(tok, cot, pos, wq, wk, wv, wo, wg, wu, wd, gains, table)


def second_kernel(
    mid, x_own, gains, g_h, w1_h, w2_h, wd_h, h_h, q_h, k_h, v_h, o_h, lse_h, table_h, pos_h,
    layer_out, grad_tokens, o_q, o_k, o_v, o_o, o_g, o_u, o_d, small_out,
    g_s, w1, w2, wd, q_s, k_s, v_s, o_s, lse_s, table_s, pos_s, ids_s, perm_s,
    hh, da_all, lpart, act_s, mix_s, kt_s, delta_s, dqt_s, dk_s, dv_s, dmid, small,
    core_out, from_core, out_buf, in_buf, keep,
    core_out2, from_core2, in_buf2,
    gf, go, rf, ro, ra, rd, sf, so, sa, pf, po, pa, s_in, sbuf, p_in,
    load, ag_send, ag_recv, ag_core, ag_recv2, ag_core2, send, core_recv, recv, recv_d, send2, core_recv2, recv2,
    f_sem, o_sem, a_sem, d_sem, fp_sem, op_sem, ap_sem, out_sem, s_sem, p_sem,
):
    f, c, y, core, z, x = whereabouts()
    me, t = f * 8 + c, f * 2 + x
    half = ROWS // 2
    pairs = (
        (w2_h, w2), (wd_h, wd), (g_h, g_s), (w1_h, w1), (q_h, q_s), (k_h, k_s), (v_h, v_s), (o_h, o_s),
        (lse_h, lse_s), (table_h, table_s), (pos_h, pos_s),
    )
    loads = [pltpu.make_async_copy(a, b, load.at[n]) for n, (a, b) in enumerate(pairs)]
    for copy in loads:
        copy.start()
    gain_one, gain_two = gains[0:1, :], gains[1:2, :]

    def piece(every, chunk, part):
        return every.at[pl.ds(pl.multiple_of(chunk * ROWS + part * half, half), half)]

    def gather_start(every, sem, core_sem):
        for part in (0, 1):
            a, b = piece(every, t, part), piece(every, t, 1 - part)
            remote(a, a, ag_send.at[0], sem.at[part], f, z * 2 + 1 - x).start()
            remote(b, b, ag_send.at[1], sem.at[2 + 1 - part], (1 - y) * 2 + core, c).start()
        for part in (0, 1):
            a = piece(every, t, part)
            remote(a, a, ag_send.at[2], core_sem.at[part], y * 2 + 1 - core, c).start()

    def gather_step(every, sem, core_sem, r, part):
        a = piece(every, chunk_of(r, core), part)
        k = (r - 1) * 2 + part
        await_bytes(a, sem.at[k])
        if r == 1 and part == 0:
            remote(a, a, ag_send.at[1], sem.at[4], (1 - y) * 2 + core, c).start()
        if r == 2 and part == 1:
            remote(a, a, ag_send.at[0], sem.at[5], f, z * 2 + 1 - x).start()
        remote(a, a, ag_send.at[2], core_sem.at[2 * r + part], y * 2 + 1 - core, c).start()

    def gather_core(every, core_sem, r):
        for part in (0, 1):
            await_bytes(piece(every, chunk_of(r, 1 - core), part), core_sem.at[2 * r + part])

    def gather_sent(every):
        await_bytes(every.at[pl.ds(0, 3 * half)], ag_send.at[0])
        await_bytes(every.at[pl.ds(0, 3 * half)], ag_send.at[1])
        await_bytes(every.at[pl.ds(0, 8 * half)], ag_send.at[2])

    hh[pl.ds(pl.multiple_of(t * ROWS, ROWS), ROWS), :] = norm_rows(mid[...], gain_two).astype(BF16)
    greet_all()
    gather_start(hh, ag_recv, ag_core)
    for n in range(3):
        loads[n].wait()

    def feed_chunk(r, same):
        chunk = chunk_of(r, core if same else 1 - core)
        rows = pl.ds(pl.multiple_of(chunk * ROWS, ROWS), ROWS)
        gu = dot_nn(hh[rows, :], w2[:, 256:1024])
        gate, up = gu[:, 0:384], gu[:, 384:768]
        sig = 1.0 / (1.0 + jnp.exp(-gate))
        sil = gate * sig
        act = (sil * up).astype(BF16)
        act_s[rows, :] = act
        layer = dot_nn(act, wd[...]).astype(BF16)
        if same:
            lpart[r] = layer
        else:
            slot = r % 2
            if r > 1:
                await_bytes(core_out2.at[slot], send2.at[slot])
            core_out2[slot] = layer
            remote(
                core_out2.at[slot], from_core2.at[r], send2.at[slot], core_recv2.at[r], y * 2 + 1 - core, c
            ).start()
        dact = dot_nt(g_s[rows, :], wd[...])
        put_two(mix_s, chunk, slice(0, 384), (dact * up * sig * (1.0 + gate * (1.0 - sig))).astype(BF16))
        put_two(mix_s, chunk, slice(384, 768), (dact * sil).astype(BF16))
        dh = dot_nt(two_blocks(mix_s, chunk, slice(0, 768)), w2[:, 256:1024])
        if not same:
            core_out[r] = dh.astype(BF16)
            remote(core_out.at[r], from_core.at[r], send.at[6], core_recv.at[r], y * 2 + 1 - core, c).start()
        elif r == 0:
            keep[0] = dh[:half]
            keep[1] = dh[half:]
        else:
            out_buf[2 * r - 2] = dh[:half].astype(BF16)
            out_buf[2 * r - 1] = dh[half:].astype(BF16)

    def sum_to_chip(r):
        await_bytes(from_core.at[r], core_recv.at[r])
        y2, x2 = chip_peer(r)
        for part in (0, 1):
            k = 2 * r - 2 + part
            out_buf[k] = (
                out_buf[k].astype(F32) + from_core[r, part * half : part * half + half].astype(F32)
            ).astype(BF16)
            remote(out_buf.at[k], in_buf.at[k], send.at[k], recv_d.at[k], y2 * 2 + core, z * 2 + x2).start()

    feed_chunk(0, True)
    gather_step(hh, ag_recv, ag_core, 1, 0)
    gather_step(hh, ag_recv, ag_core, 2, 1)
    gather_core(hh, ag_core, 0)
    feed_chunk(0, False)
    gather_step(hh, ag_recv, ag_core, 1, 1)
    gather_step(hh, ag_recv, ag_core, 2, 0)
    feed_chunk(1, True)
    feed_chunk(2, True)
    gather_core(hh, ag_core, 1)
    feed_chunk(1, False)
    gather_step(hh, ag_recv, ag_core, 3, 0)
    gather_step(hh, ag_recv, ag_core, 3, 1)
    gather_core(hh, ag_core, 2)
    feed_chunk(2, False)
    sum_to_chip(1)
    gather_core(hh, ag_core, 3)
    feed_chunk(3, False)
    sum_to_chip(2)
    feed_chunk(3, True)
    sum_to_chip(3)

    def scatter_rows(g, b, block, first, width):
        for k in range(4):
            g[k, b * 64 : b * 64 + 64, first : first + width] = block[k * 64 : k * 64 + 64].astype(BF16)

    def across(g, r_, sem):
        pltpu.make_async_copy(g.at[z], r_.at[z], sem.at[1]).start()
        for j in (2, 1, 3):
            z2 = (z + j) % 4
            remote(g.at[z2], r_.at[z], sem.at[0], sem.at[1], f, z2 * 2 + x).start()

    def in_plane(r_, s_, p_, sem, plane_sem):
        await_bytes(r_, sem.at[1])
        s_[...] = (r_[0].astype(F32) + r_[1].astype(F32) + r_[2].astype(F32) + r_[3].astype(F32)).astype(BF16)
        pltpu.make_async_copy(s_.at[pl.ds(pl.multiple_of(t * 32, 32), 32)], p_.at[t], plane_sem.at[1]).start()
        for j in range(1, 8):
            t2 = (t + j) % 8
            block = s_.at[pl.ds(pl.multiple_of(t2 * 32, 32), 32)]
            remote(block, p_.at[t], plane_sem.at[0], plane_sem.at[1], t2 // 2, z * 2 + t2 % 2).start()

    for b in range(4):
        scatter_rows(gf, b, dot_tn(hh[:, b * 256 : b * 256 + 256], mix_s[...].reshape(2048, 768)), 0, 768)
    across(gf, rf, f_sem)
    await_bytes(from_core, send.at[6])
    for b in range(3):
        block = dot_tn(act_s[:, b * 128 : b * 128 + 128], g_s[...]).astype(BF16)
        for k in range(4):
            low, high = max(b * 128, k * 96), min(b * 128 + 128, k * 96 + 96)
            if low < high:
                core_out[k, low - k * 96 : high - k * 96, :] = block[low - b * 128 : high - b * 128]
    for k in range(4):
        dev = t * 4 + k
        rows = core_out.at[k, pl.ds(0, 96)]

        @pl.when(dev == me)
        def _():
            pltpu.make_async_copy(rows, rd.at[z], d_sem.at[1]).start()

        @pl.when(dev != me)
        def _():
            remote(rows, rd.at[z], d_sem.at[0], d_sem.at[1], dev // 8, dev % 8).start()

    gather_sent(hh)
    h_load = pltpu.make_async_copy(h_h, hh, load.at[11])
    h_load.start()

    await_bytes(from_core.at[0], core_recv.at[0])
    for k in range(6):
        await_bytes(in_buf.at[k], recv_d.at[k])
    small[...] = jnp.zeros_like(small)
    for part in (0, 1):
        rows = slice(part * half, part * half + half)
        dh = keep[part] + from_core[0, rows].astype(F32)
        dh = dh + in_buf[part].astype(F32) + in_buf[2 + part].astype(F32) + in_buf[4 + part].astype(F32)
        back, dgain = norm_back(mid[rows, :], gain_two, dh)
        first = pl.multiple_of(t * ROWS + part * half, half)
        dm = g_s[pl.ds(first, half), :].astype(F32) + back
        dmid[rows, :] = dm
        da_all[pl.ds(first, half), :] = dm.astype(BF16)
        small[1:2, :] += jnp.sum(dgain, axis=0, keepdims=True)
    gather_start(da_all, ag_recv2, ag_core2)
    for k in range(6):
        await_bytes(out_buf.at[k], send.at[k])
    for copy in loads[3:]:
        copy.wait()

    rows_in_order(pos_s, ids_s, perm_s)
    for b in range(4):
        kt_s[b] = k_s[b * QROWS : b * QROWS + QROWS, :].T

    def back_out(r, same):
        chunk = chunk_of(r, core if same else 1 - core)
        rows = pl.ds(pl.multiple_of(chunk * ROWS, ROWS), ROWS)
        put_two(mix_s, chunk, slice(512, 768), dot_nn(da_all[rows, :], w2[:, 0:256]).astype(BF16))

    back_out(0, True)
    gather_step(da_all, ag_recv2, ag_core2, 1, 0)
    gather_step(da_all, ag_recv2, ag_core2, 2, 1)
    gather_core(da_all, ag_core2, 0)
    back_out(0, False)
    gather_step(da_all, ag_recv2, ag_core2, 1, 1)
    gather_step(da_all, ag_recv2, ag_core2, 2, 0)
    back_out(1, True)
    back_out(2, True)
    gather_core(da_all, ag_core2, 1)
    back_out(1, False)
    gather_core(da_all, ag_core2, 2)
    back_out(2, False)
    gather_step(da_all, ag_recv2, ag_core2, 3, 0)
    gather_step(da_all, ag_recv2, ag_core2, 3, 1)
    back_out(3, True)
    gather_core(da_all, ag_core2, 3)
    back_out(3, False)

    def layer_to_chips():
        for r in (3, 1, 2):
            await_bytes(from_core2.at[r], core_recv2.at[r])
            lpart[r] = (lpart[r].astype(F32) + from_core2[r].astype(F32)).astype(BF16)
            y2, x2 = chip_peer(r)
            remote(
                lpart.at[r], in_buf2.at[r - 1], send2.at[1 + r], recv2.at[r - 1], y2 * 2 + core, z * 2 + x2
            ).start()

    def prepare(b, carry):
        rows = pl.ds(pl.multiple_of(b * QROWS, QROWS), QROWS)
        do = jnp.concatenate(
            [mix_s[perm_s[b * 4 + k], :, 512:768] for k in range(4)], axis=0
        )
        act_s[rows, 0:256] = do
        ones = jnp.ones((8, 128), BF16)
        for head in range(2):
            cols = slice(head * 128, head * 128 + 128)
            prod = do[:, cols].astype(F32) * o_s[pl.ds(b * 4, 4), :, cols].reshape(QROWS, 128).astype(F32)
            high = prod.astype(BF16)
            low = (prod - high.astype(F32)).astype(BF16)
            delta = dot_nt(ones, high) + dot_nt(ones, low)
            delta_s[b, :, head * QROWS : head * QROWS + QROWS] = delta[0:1]
        return carry

    lax.fori_loop(0, 4, prepare, 0)
    for b in range(16):
        mix_s[b, :, 0:256] = o_s[ids_s[b]]
    for b in range(4):
        scatter_rows(go, b, dot_tn(da_all[:, b * 256 : b * 256 + 256], mix_s[:, :, 0:256].reshape(2048, 256)), 0, 256)
    across(go, ro, o_sem)
    dqt_s[...] = jnp.zeros_like(dqt_s)
    dk_s[...] = jnp.zeros_like(dk_s)
    dv_s[...] = jnp.zeros_like(dv_s)

    def key_tile(kt):
        krows = pl.ds(kt * QROWS, QROWS)

        def step(qt, diagonal):
            kb, vb, ktb = k_s[krows, :], v_s[krows, :], kt_s[kt]
            for g in range(4):
                head, part = g // 2, g % 2
                start = pl.multiple_of(qt * QROWS + part * 256, 256)
                cols = slice(head * 128, head * 128 + 128)
                lanes = slice(g * 256, g * 256 + 256)
                qb = q_s[pl.ds(start, 256), cols]
                dob = act_s[pl.ds(start, 256), cols]
                depth = 256 * (part + 1) if diagonal else QROWS
                s = dot_nt(kb[:depth], qb)
                p = jnp.exp2(s * (SCALE * LOG2E) - lse_s[qt, :, lanes])
                if diagonal:
                    ki = lax.broadcasted_iota(jnp.int32, (depth, 256), 0)
                    qi = lax.broadcasted_iota(jnp.int32, (depth, 256), 1) + part * 256
                    p = jnp.where(ki <= qi, p, 0.0)
                dp = dot_nt(vb[:depth], dob)
                ds = (p * (dp - delta_s[qt, :, lanes])).astype(BF16)
                out = pl.ds(kt * 4, depth // 128)
                dv_s[out] += dot_nn(p.astype(BF16), dob).reshape(depth // 128, 128, 128)
                dk_s[out] += dot_nn(ds, qb).reshape(depth // 128, 128, 128)
                dq = dot_nn(ktb[:, :depth], ds)
                dqt_s[qt * 4 + part * 2, cols, :] += dq[:, 0:128]
                dqt_s[qt * 4 + part * 2 + 1, cols, :] += dq[:, 128:256]

        step(kt, True)

        def off(qt, inner):
            step(qt, False)
            return inner

        lax.fori_loop(kt + 1, 4, off, 0)

    key_tile(0)
    layer_to_chips()
    key_tile(1)
    key_tile(2)
    in_plane(rf, sf, pf, f_sem, fp_sem)
    key_tile(3)

    home_f, home_c = plane_of(z), f * 2 + x
    stays = (home_f == f) & (home_c == c)

    def deliver(src, dst, k):
        @pl.when(jnp.logical_not(stays))
        def _():
            remote(src, dst, out_sem.at[k], out_sem.at[k + 1], home_f, home_c).start()

        @pl.when(stays)
        def _():
            pltpu.make_async_copy(src, dst, out_sem.at[k + 1]).start()

    await_bytes(from_core2.at[0], core_recv2.at[0])
    for r in (1, 2, 3):
        await_bytes(in_buf2.at[r - 1], recv2.at[r - 1])
    layer = mid[...] + lpart[0].astype(F32) + from_core2[0].astype(F32)
    layer = layer + in_buf2[0].astype(F32) + in_buf2[1].astype(F32) + in_buf2[2].astype(F32)
    in_buf2[0] = layer.astype(BF16)
    x_load = pltpu.make_async_copy(x_own, in_buf2.at[2], load.at[12])
    x_load.start()
    deliver(in_buf2.at[0], layer_out, 0)
    in_plane(ro, so, po, o_sem, op_sem)
    h_load.wait()

    def finish_chunk(chunk):
        rows = pl.ds(pl.multiple_of(chunk * ROWS, ROWS), ROWS)
        places = [ids_s[chunk * 2 + k] for k in range(2)]
        cos, sin = turns(jnp.concatenate([table_s[b] for b in places], axis=0))
        raw = dot_nn(hh[rows, :], w1[:, 0:384])
        for head in range(3):
            cols = slice(head * 128, head * 128 + 128)
            if head < 2:
                blocks = [dqt_s[b, cols, :].T for b in places]
                gain, lanes = gains[2:3, 0:128], slice(0, 128)
            else:
                blocks = [dk_s[b] for b in places]
                gain, lanes = gains[3:4, 0:128], slice(128, 256)
            d = jnp.concatenate(blocks, axis=0) * SCALE
            back, dgain = norm_back(raw[:, cols], gain, unturn(d, cos, sin))
            put_two(mix_s, chunk, cols, back.astype(BF16))
            small[2:3, lanes] += jnp.sum(dgain, axis=0, keepdims=True)
        for k in range(2):
            mix_s[chunk * 2 + k, :, 384:512] = dv_s[places[k]].astype(BF16)

    def partial(chunk):
        finish_chunk(chunk)
        return dot_nt(two_blocks(mix_s, chunk, slice(0, 512)), w1[...])

    gather_sent(da_all)
    await_bytes(gf.at[pl.ds(0, 3)], f_sem.at[0])
    await_bytes(rd, d_sem.at[1])
    for k in range(4):

        @pl.when(t * 4 + k != me)
        def _():
            await_bytes(core_out.at[k, pl.ds(0, 96)], d_sem.at[0])

    split_sum(partial, core_out, from_core, out_buf, in_buf, keep, send, core_recv, recv)
    for b in range(4):
        scatter_rows(gf, b, dot_tn(hh[:, b * 256 : b * 256 + 256], mix_s[:, :, 0:512].reshape(2048, 512)), 0, 512)
    across(gf.at[:, :, pl.ds(0, 512)], ra, a_sem)
    low, high = split_sum_end(in_buf, keep, recv)
    x_load.wait()
    for part, dh in ((0, low), (1, high)):
        rows = slice(part * half, part * half + half)
        back, dgain = norm_back(in_buf2[2, rows, :].astype(F32), gain_one, dh)
        in_buf2[1, rows, :] = (dmid[rows, :] + back).astype(BF16)
        small[0:1, :] += jnp.sum(dgain, axis=0, keepdims=True)
    deliver(in_buf2.at[1], grad_tokens, 2)

    s_in[t] = small[...]
    for j in range(1, 8):
        t2 = (t + j) % 8
        remote(small, s_in.at[t], s_sem.at[0], s_sem.at[1], t2 // 2, z * 2 + t2 % 2).start()

    await_bytes(pf, fp_sem.at[1])
    for k in range(8):
        o_g[:, k * 384 : k * 384 + 384] = pf[k, :, 0:384].astype(F32)
        o_u[:, k * 384 : k * 384 + 384] = pf[k, :, 384:768].astype(F32)
    await_bytes(po, op_sem.at[1])
    for k in range(8):
        o_o[:, k * 256 : k * 256 + 256] = po[k].astype(F32)
    o_d[...] = rd[0].astype(F32) + rd[1].astype(F32) + rd[2].astype(F32) + rd[3].astype(F32)

    await_bytes(s_in.at[pl.ds(0, 7)], s_sem.at[1])
    sbuf[...] = jnp.sum(s_in[...], axis=0)
    p_in[z] = sbuf[...]
    for j in range(1, 4):
        remote(sbuf, p_in.at[z], p_sem.at[0], p_sem.at[1], f, ((z + j) % 4) * 2 + x).start()
    in_plane(ra, sa, pa, a_sem, ap_sem)
    await_bytes(p_in.at[pl.ds(0, 3)], p_sem.at[1])
    small_out[...] = jnp.sum(p_in[...], axis=0)
    await_bytes(pa, ap_sem.at[1])
    for k in range(8):
        o_q[:, k * 256 : k * 256 + 256] = pa[k, :, 0:256].astype(F32)
        o_k[:, k * 128 : k * 128 + 128] = pa[k, :, 256:384].astype(F32)
        o_v[:, k * 128 : k * 128 + 128] = pa[k, :, 384:512].astype(F32)

    await_bytes(layer_out, out_sem.at[1])
    await_bytes(grad_tokens, out_sem.at[3])

    @pl.when(jnp.logical_not(stays))
    def _():
        await_bytes(layer_out, out_sem.at[0])
        await_bytes(grad_tokens, out_sem.at[2])

    split_sum_sent(from_core, out_buf, send)
    for k in range(2):
        await_bytes(core_out2.at[k], send2.at[k])
    for r in (1, 2, 3):
        await_bytes(lpart.at[r], send2.at[1 + r])
    await_bytes(s_in.at[pl.ds(0, 7)], s_sem.at[0])
    await_bytes(p_in.at[pl.ds(0, 3)], p_sem.at[0])
    await_bytes(go.at[pl.ds(0, 3)], o_sem.at[0])
    await_bytes(ra.at[pl.ds(0, 3)], a_sem.at[0])
    await_bytes(pf.at[pl.ds(0, 7)], fp_sem.at[0])
    await_bytes(po.at[pl.ds(0, 7)], op_sem.at[0])
    await_bytes(pa.at[pl.ds(0, 7)], ap_sem.at[0])


def second(mid, x_own, gains, *rest):
    any_spec, vmem = pl.BlockSpec(memory_space=pl.ANY), pl.BlockSpec(memory_space=pltpu.VMEM)
    dma = pltpu.SemaphoreType.DMA
    bf = lambda *shape: pltpu.VMEM(shape, BF16)
    fl = lambda *shape: pltpu.VMEM(shape, F32)
    out = lambda kind, *shape: jax.ShapeDtypeStruct(shape, kind)
    return pl.pallas_call(
        second_kernel,
        out_shape=(
            out(BF16, ROWS, 1024), out(BF16, ROWS, 1024), out(F32, 32, 2048), out(F32, 32, 1024), out(F32, 32, 1024),
            out(F32, 32, 2048), out(F32, 32, 3072), out(F32, 32, 3072), out(F32, 96, 1024), out(F32, 8, 1024),
        ),
        in_specs=[vmem, any_spec, vmem] + [any_spec] * 12,
        out_specs=(any_spec, any_spec) + (vmem,) * 8,
        scratch_shapes=[
            bf(2048, 1024), bf(1024, 512), bf(1024, 1024), bf(384, 1024), bf(2048, 256), bf(2048, 128), bf(2048, 128),
            bf(16, 128, 256), fl(4, 1, 1024), fl(16, 128, 128), pltpu.SMEM((1, 2048), jnp.int32),
            pltpu.SMEM((16,), jnp.int32), pltpu.SMEM((16,), jnp.int32),
            bf(2048, 1024), bf(2048, 1024), bf(4, ROWS, 1024), bf(2048, 384), bf(16, 128, 768), bf(4, 128, QROWS),
            fl(4, 1, 1024), fl(16, 256, 128), fl(16, 128, 128), fl(16, 128, 128), fl(ROWS, 1024), fl(8, 1024),
            bf(4, ROWS, 1024), bf(4, ROWS, 1024), bf(6, ROWS // 2, 1024), bf(6, ROWS // 2, 1024),
            fl(2, ROWS // 2, 1024),
            bf(2, ROWS, 1024), bf(4, ROWS, 1024), bf(3, ROWS, 1024),
            bf(4, 256, 768), bf(4, 256, 256),
            bf(4, 256, 768), bf(4, 256, 256), bf(4, 256, 512), bf(4, 96, 1024),
            bf(256, 768), bf(256, 256), bf(256, 512), bf(8, 32, 768), bf(8, 32, 256), bf(8, 32, 512),
            fl(8, 8, 1024), fl(8, 1024), fl(4, 8, 1024),
            dma((13,)), dma((3,)), dma((6,)), dma((8,)), dma((6,)), dma((8,)), dma((7,)), dma((4,)), dma((6,)), dma((6,)), dma((5,)),
            dma((4,)), dma((3,)),
            dma((2,)), dma((2,)), dma((2,)), dma((2,)), dma((2,)), dma((2,)), dma((2,)), dma((4,)), dma((2,)),
            dma((2,)),
        ],
        compiler_params=pltpu.CompilerParams(collective_id=1, has_side_effects=True, vmem_limit_bytes=VMEM_LIMIT),
        name="second",
    )(mid, x_own, gains, *rest)


def rope_table(length):
    inverse = 1000000.0 ** (-2.0 * np.arange(HEAD_DIM // 2, dtype=np.float64) / HEAD_DIM)
    angles = np.arange(length, dtype=np.float32)[:, None] * inverse.astype(np.float32)[None, :]
    angles = angles.astype(np.float64)
    return np.concatenate([np.cos(angles), np.sin(angles)], axis=1).astype(np.float32)


def per_device_planes(
    tokens, positions, w_query, w_key, w_value, w_output, w_gate, w_up, w_down, first_gain, second_gain, head_gain,
    cotangent,
):
    me = lax.axis_index("fsdp") * 8 + lax.axis_index("ctx")
    lane = jnp.arange(128, dtype=jnp.int32)
    head = jnp.where(lane // 8 == me % 16, jnp.tile(head_gain.astype(F32), 16), 0.0)
    gains = jnp.stack(
        [
            jnp.where(lane // 32 == me % 4, jnp.tile(first_gain.astype(F32), 4), 0.0),
            jnp.where(lane // 32 == me % 4, jnp.tile(second_gain.astype(F32), 4), 0.0),
            jnp.where(me < 16, head, 0.0),
            jnp.where(me >= 16, head, 0.0),
        ]
    )
    table = jnp.asarray(rope_table(2048)).reshape(16, 128, HEAD_DIM)
    g_all, w_down_t, h, q, k, v, o, lse, w1, w2, mid, x_own, pos, gains = first(
        tokens[0], cotangent[0], positions, w_query, w_key, w_value, w_output.T, w_gate, w_up, w_down, gains, table
    )
    layer_out, grad_tokens, o_q, o_k, o_v, o_o, o_g, o_u, o_d, small = second(
        mid, x_own, gains, g_all, w1, w2, w_down_t, h, q, k, v, o, lse, table, pos
    )
    return (
        layer_out[None],
        grad_tokens[None],
        o_q,
        o_k,
        o_v,
        o_o.T,
        o_g,
        o_u,
        o_d,
        lax.dynamic_slice(small, (0, me * 32), (1, 32))[0],
        lax.dynamic_slice(small, (1, me * 32), (1, 32))[0],
        lax.dynamic_slice(small, (2, me * 8), (1, 8))[0],
    )


def solution(mesh):
    planes = mesh.shape["fsdp"] == 4 and mesh.shape["ctx"] == 8
    body = per_device_planes if planes else per_device
    return jax.shard_map(
        body,
        mesh=mesh,
        in_specs=(
            P("fsdp", "ctx", None),
            P("fsdp", None),
            P(("fsdp", "ctx"), None),
            P(("fsdp", "ctx"), None),
            P(("fsdp", "ctx"), None),
            P(None, ("fsdp", "ctx")),
            P(("fsdp", "ctx"), None),
            P(("fsdp", "ctx"), None),
            P(("fsdp", "ctx"), None),
            P(("fsdp", "ctx")),
            P(("fsdp", "ctx")),
            P(("fsdp", "ctx")),
            P("fsdp", "ctx", None),
        ),
        out_specs=(
            P("fsdp", "ctx", None),
            P("fsdp", "ctx", None),
            P(("fsdp", "ctx"), None),
            P(("fsdp", "ctx"), None),
            P(("fsdp", "ctx"), None),
            P(None, ("fsdp", "ctx")),
            P(("fsdp", "ctx"), None),
            P(("fsdp", "ctx"), None),
            P(("fsdp", "ctx"), None),
            P(("fsdp", "ctx")),
            P(("fsdp", "ctx")),
            P(("fsdp", "ctx")),
        ),
        check_vma=False,
    )
```

```python
from functools import partial

import jax
import jax.numpy as jnp
import numpy as np
from jax import lax
from jax.experimental import pallas as pl
from jax.experimental.pallas import tpu as pltpu
from jax.sharding import PartitionSpec as P

MESH = pl.DeviceIdType.MESH

HEADS = 16
KV_HEADS = 8
HEAD_DIM = 128


def normed(operand, gain_in):
    return (
        operand * lax.rsqrt(jnp.mean(operand * operand, axis=-1, keepdims=True) + 1e-06) * gain_in
    )


def rotary(operand, places):
    head_width = operand.shape[-1]
    half_width = head_width // 2
    inverse = 1000000.0 ** (-2.0 * jnp.arange(half_width, dtype=jnp.float32) / head_width)
    angles = places.astype(jnp.float32)[:, None] * inverse[None, :]
    cosine = jnp.concatenate([jnp.cos(angles), jnp.cos(angles)], axis=-1)[:, None, :]
    sine_table = jnp.concatenate([jnp.sin(angles), jnp.sin(angles)], axis=-1)[:, None, :]
    turned = jnp.concatenate([-operand[..., half_width:], operand[..., :half_width]], axis=-1)
    return operand * cosine + turned * sine_table


def head_prep(raw_proj, gain_in, places, head_count):
    row_count = raw_proj.shape[0]
    shaped = raw_proj.reshape(row_count, head_count, HEAD_DIM)
    return rotary(normed(shaped, gain_in), places).reshape(row_count, head_count * HEAD_DIM)


def gated(gate_raw, up_raw):
    return jax.nn.silu(gate_raw) * up_raw


def project(left_side, right_side):
    return jnp.dot(left_side, right_side, preferred_element_type=jnp.float32)


def project_back(left_side, right_side):
    return lax.dot_general(
        left_side, right_side, (((1,), (1,)), ((), ())), preferred_element_type=jnp.float32
    )


def outer_sum(left_side, right_side):
    return lax.dot_general(
        left_side, right_side, (((0,), (0,)), ((), ())), preferred_element_type=jnp.float32
    )


def halves_apart(rows_in, shard_count):
    shape_in = rows_in.shape
    split = rows_in.reshape((shard_count, 2, shape_in[0] // (2 * shard_count)) + shape_in[1:])
    return jnp.swapaxes(split, 0, 1).reshape(shape_in)


def halves_back(rows_in, shard_count):
    shape_in = rows_in.shape
    split = rows_in.reshape((2, shard_count, shape_in[0] // (2 * shard_count)) + shape_in[1:])
    return jnp.swapaxes(split, 0, 1).reshape(shape_in)


def key_layout(key_rows, value_rows, place_all):
    key_count = key_rows.shape[0]
    key_block = min(512, key_count)
    block_count = key_count // key_block
    key_parts = key_rows.reshape(block_count, key_block, KV_HEADS, HEAD_DIM)
    value_parts = value_rows.reshape(block_count, key_block, KV_HEADS, HEAD_DIM)
    place_parts = place_all.reshape(block_count, key_block)
    return (key_parts, value_parts, place_parts)


def attend_forward(queries, key_rows, value_rows, place_here, place_all):
    row_count = queries.shape[0]
    group_size = HEADS // KV_HEADS
    score_scale = HEAD_DIM ** (-0.5)
    grouped = queries.reshape(row_count, KV_HEADS, group_size, HEAD_DIM)
    layout = key_layout(key_rows, value_rows, place_all)
    top_place = jnp.max(place_here)

    def attend_step(state_now, block_item):
        key_part, value_part, place_part = block_item

        def attend_compute(state_in):
            run_max, run_sum, run_out = state_in
            scores = (
                jnp.einsum("qhge,khe->hgqk", grouped, key_part, preferred_element_type=jnp.float32)
                * score_scale
            )
            visible = place_part[None, None, None, :] <= place_here[None, None, :, None]
            scores = jnp.where(visible, scores, -1e30)
            new_max = jnp.maximum(run_max, jnp.max(scores, axis=-1))
            weights = jnp.where(visible, jnp.exp(scores - new_max[..., None]), 0.0)
            rescale = jnp.exp(run_max - new_max)
            run_sum = run_sum * rescale + jnp.sum(weights, axis=-1)
            mixed = jnp.einsum(
                "hgqk,khe->hgqe",
                weights.astype(jnp.bfloat16),
                value_part,
                preferred_element_type=jnp.float32,
            )
            run_out = run_out * rescale[..., None] + mixed
            return (new_max, run_sum, run_out)

        state_next = lax.cond(
            jnp.min(place_part) > top_place, lambda state_in: state_in, attend_compute, state_now
        )
        return (state_next, None)

    start_state = (
        jnp.full((KV_HEADS, group_size, row_count), -1e30, jnp.float32),
        jnp.zeros((KV_HEADS, group_size, row_count), jnp.float32),
        jnp.zeros((KV_HEADS, group_size, row_count, HEAD_DIM), jnp.float32),
    )
    (run_max, run_sum, run_out), _ = lax.scan(attend_step, start_state, layout)
    attention = (
        (run_out / run_sum[..., None]).transpose(2, 0, 1, 3).reshape(row_count, HEADS * HEAD_DIM)
    )
    return (attention, run_max + jnp.log(run_sum))


def row_dot_table(grad_attn, attention):
    row_count = grad_attn.shape[0]
    group_size = HEADS // KV_HEADS
    grad_grouped = grad_attn.reshape(row_count, KV_HEADS, group_size, HEAD_DIM)
    return jnp.sum(
        grad_grouped.astype(jnp.float32)
        * attention.reshape(row_count, KV_HEADS, group_size, HEAD_DIM),
        axis=-1,
    ).transpose(1, 2, 0)


def attend_backward(
    queries, key_rows, value_rows, grad_attn, row_dots, log_total, place_here, place_all
):
    row_count = queries.shape[0]
    key_count = key_rows.shape[0]
    group_size = HEADS // KV_HEADS
    score_scale = HEAD_DIM ** (-0.5)
    grouped = queries.reshape(row_count, KV_HEADS, group_size, HEAD_DIM)
    grad_grouped = grad_attn.reshape(row_count, KV_HEADS, group_size, HEAD_DIM)
    layout = key_layout(key_rows, value_rows, place_all)
    top_place = jnp.max(place_here)

    def back_step(grad_query, block_item):
        key_part, value_part, place_part = block_item
        key_block = key_part.shape[0]

        def back_compute(grad_in):
            scores = (
                jnp.einsum("qhge,khe->hgqk", grouped, key_part, preferred_element_type=jnp.float32)
                * score_scale
            )
            visible = place_part[None, None, None, :] <= place_here[None, None, :, None]
            weights = jnp.where(
                visible, jnp.exp(jnp.where(visible, scores, -1e30) - log_total[..., None]), 0.0
            )
            grad_probs = jnp.einsum(
                "qhge,khe->hgqk", grad_grouped, value_part, preferred_element_type=jnp.float32
            )
            grad_scores = (weights * (grad_probs - row_dots[..., None])).astype(jnp.bfloat16)
            grad_out = (
                grad_in
                + jnp.einsum(
                    "hgqk,khe->qhge", grad_scores, key_part, preferred_element_type=jnp.float32
                )
                * score_scale
            )
            grad_keys = (
                jnp.einsum(
                    "hgqk,qhge->khe", grad_scores, grouped, preferred_element_type=jnp.float32
                )
                * score_scale
            )
            grad_values = jnp.einsum(
                "hgqk,qhge->khe",
                weights.astype(jnp.bfloat16),
                grad_grouped,
                preferred_element_type=jnp.float32,
            )
            return (
                grad_out,
                (
                    grad_keys.reshape(key_block, KV_HEADS * HEAD_DIM),
                    grad_values.reshape(key_block, KV_HEADS * HEAD_DIM),
                ),
            )

        def skipped(grad_in):
            empty_terms = jnp.zeros((key_block, KV_HEADS * HEAD_DIM), jnp.float32)
            return (grad_in, (empty_terms, empty_terms))

        return lax.cond(jnp.min(place_part) > top_place, skipped, back_compute, grad_query)

    start_grad = jnp.zeros((row_count, KV_HEADS, group_size, HEAD_DIM), jnp.float32)
    grad_query, key_terms = lax.scan(back_step, start_grad, layout)
    grad_query = grad_query.reshape(row_count, HEADS * HEAD_DIM)
    return (
        grad_query,
        key_terms[0].reshape(key_count, KV_HEADS * HEAD_DIM),
        key_terms[1].reshape(key_count, KV_HEADS * HEAD_DIM),
    )


def per_device(
    tokens,
    positions,
    w_query,
    w_key,
    w_value,
    w_output,
    w_gate,
    w_up,
    w_down,
    first_gain,
    second_gain,
    head_gain,
    cotangent,
):
    inputs = tokens[0].astype(jnp.float32)
    row_count = inputs.shape[0]
    shard_count = lax.axis_size("ctx")
    place_stored = positions[0]
    place_here = lax.dynamic_slice_in_dim(
        place_stored, lax.axis_index("ctx") * row_count, row_count
    )
    place_all = halves_apart(place_stored, shard_count)
    query_full, key_full, value_full, output_full, gain_first, gain_head = (
        lax.all_gather(w_query, ("fsdp", "ctx"), axis=0, tiled=True),
        lax.all_gather(w_key, ("fsdp", "ctx"), axis=0, tiled=True),
        lax.all_gather(w_value, ("fsdp", "ctx"), axis=0, tiled=True),
        lax.all_gather(w_output, ("fsdp", "ctx"), axis=1, tiled=True),
        lax.all_gather(first_gain, ("fsdp", "ctx"), axis=0, tiled=True),
        lax.all_gather(head_gain, ("fsdp", "ctx"), axis=0, tiled=True),
    )
    gain_one = gain_first.astype(jnp.float32)
    gain_query = gain_head[:HEAD_DIM].astype(jnp.float32)
    gain_key = gain_head[HEAD_DIM:].astype(jnp.float32)
    hidden_one = normed(inputs, gain_one).astype(jnp.bfloat16)
    query_raw = project(hidden_one, query_full)
    key_raw = project(hidden_one, key_full)
    value_rows = project(hidden_one, value_full).astype(jnp.bfloat16)
    query_prep = partial(head_prep, places=place_here, head_count=HEADS)
    key_prep = partial(head_prep, places=place_here, head_count=KV_HEADS)
    queries, query_back = jax.vjp(query_prep, query_raw, gain_query)
    key_local, key_back = jax.vjp(key_prep, key_raw, gain_key)
    queries = queries.astype(jnp.bfloat16)
    key_local = key_local.astype(jnp.bfloat16)
    key_stored, value_stored = (
        lax.all_gather(key_local, "ctx", axis=0, tiled=True),
        lax.all_gather(value_rows, "ctx", axis=0, tiled=True),
    )
    key_all = halves_apart(key_stored, shard_count)
    value_all = halves_apart(value_stored, shard_count)
    attention, log_total = attend_forward(queries, key_all, value_all, place_here, place_all)
    attn_low = attention.astype(jnp.bfloat16)
    middle = inputs + project(attn_low, output_full)
    gate_full, up_full, down_full, gain_second = (
        lax.all_gather(w_gate, ("fsdp", "ctx"), axis=0, tiled=True),
        lax.all_gather(w_up, ("fsdp", "ctx"), axis=0, tiled=True),
        lax.all_gather(w_down, ("fsdp", "ctx"), axis=0, tiled=True),
        lax.all_gather(second_gain, ("fsdp", "ctx"), axis=0, tiled=True),
    )
    gain_two = gain_second.astype(jnp.float32)
    hidden_two = normed(middle, gain_two).astype(jnp.bfloat16)
    gate_raw = project(hidden_two, gate_full)
    up_raw = project(hidden_two, up_full)
    activated, gated_back = jax.vjp(gated, gate_raw, up_raw)
    act_low = activated.astype(jnp.bfloat16)
    layer_out = (middle + project(act_low, down_full)).astype(jnp.bfloat16)
    grad_out = cotangent[0].astype(jnp.float32)
    gate_full, up_full, down_full, gain_second = (
        lax.all_gather(w_gate, ("fsdp", "ctx"), axis=0, tiled=True),
        lax.all_gather(w_up, ("fsdp", "ctx"), axis=0, tiled=True),
        lax.all_gather(w_down, ("fsdp", "ctx"), axis=0, tiled=True),
        lax.all_gather(second_gain, ("fsdp", "ctx"), axis=0, tiled=True),
    )
    gain_two = gain_second.astype(jnp.float32)
    out_low = grad_out.astype(jnp.bfloat16)
    down_terms = outer_sum(act_low, out_low)
    grad_act = project_back(out_low, down_full)
    grad_gate_raw, grad_up_raw = gated_back(grad_act)
    gate_low = grad_gate_raw.astype(jnp.bfloat16)
    up_low = grad_up_raw.astype(jnp.bfloat16)
    gate_terms = outer_sum(hidden_two, gate_low)
    up_terms = outer_sum(hidden_two, up_low)
    grad_hidden_two = project_back(gate_low, gate_full) + project_back(up_low, up_full)
    _, norm_two_back = jax.vjp(normed, middle, gain_two)
    middle_part, gain_two_terms = norm_two_back(grad_hidden_two)
    grad_gate, grad_up, grad_down, grad_second = (
        lax.psum_scatter(gate_terms, ("fsdp", "ctx"), scatter_dimension=0, tiled=True),
        lax.psum_scatter(up_terms, ("fsdp", "ctx"), scatter_dimension=0, tiled=True),
        lax.psum_scatter(down_terms, ("fsdp", "ctx"), scatter_dimension=0, tiled=True),
        lax.psum_scatter(gain_two_terms, ("fsdp", "ctx"), scatter_dimension=0, tiled=True),
    )
    grad_middle = grad_out + middle_part
    query_full, key_full, value_full, output_full, gain_first, gain_head = (
        lax.all_gather(w_query, ("fsdp", "ctx"), axis=0, tiled=True),
        lax.all_gather(w_key, ("fsdp", "ctx"), axis=0, tiled=True),
        lax.all_gather(w_value, ("fsdp", "ctx"), axis=0, tiled=True),
        lax.all_gather(w_output, ("fsdp", "ctx"), axis=1, tiled=True),
        lax.all_gather(first_gain, ("fsdp", "ctx"), axis=0, tiled=True),
        lax.all_gather(head_gain, ("fsdp", "ctx"), axis=0, tiled=True),
    )
    gain_one = gain_first.astype(jnp.float32)
    middle_low = grad_middle.astype(jnp.bfloat16)
    output_terms = outer_sum(attn_low, middle_low)
    grad_attn = project_back(middle_low, output_full).astype(jnp.bfloat16)
    row_dots = row_dot_table(grad_attn, attention)
    grad_queries, key_terms, value_terms = attend_backward(
        queries, key_all, value_all, grad_attn, row_dots, log_total, place_here, place_all
    )
    key_terms = halves_back(key_terms, shard_count)
    value_terms = halves_back(value_terms, shard_count)
    grad_key_local, grad_value_local = (
        lax.psum_scatter(
            key_terms.astype(jnp.bfloat16), "ctx", scatter_dimension=0, tiled=True
        ).astype(jnp.float32),
        lax.psum_scatter(
            value_terms.astype(jnp.bfloat16), "ctx", scatter_dimension=0, tiled=True
        ).astype(jnp.float32),
    )
    grad_query_raw, gain_query_terms = query_back(grad_queries)
    grad_key_raw, gain_key_terms = key_back(grad_key_local)
    query_low = grad_query_raw.astype(jnp.bfloat16)
    keyraw_low = grad_key_raw.astype(jnp.bfloat16)
    value_low = grad_value_local.astype(jnp.bfloat16)
    query_terms = outer_sum(hidden_one, query_low)
    key_weight_terms = outer_sum(hidden_one, keyraw_low)
    value_weight_terms = outer_sum(hidden_one, value_low)
    grad_hidden_one = (
        project_back(query_low, query_full)
        + project_back(keyraw_low, key_full)
        + project_back(value_low, value_full)
    )
    _, norm_one_back = jax.vjp(normed, inputs, gain_one)
    input_part, gain_one_terms = norm_one_back(grad_hidden_one)
    head_terms = jnp.concatenate([gain_query_terms, gain_key_terms])
    grad_query, grad_key, grad_value, grad_output, grad_first, grad_head = (
        lax.psum_scatter(query_terms, ("fsdp", "ctx"), scatter_dimension=0, tiled=True),
        lax.psum_scatter(key_weight_terms, ("fsdp", "ctx"), scatter_dimension=0, tiled=True),
        lax.psum_scatter(value_weight_terms, ("fsdp", "ctx"), scatter_dimension=0, tiled=True),
        lax.psum_scatter(output_terms, ("fsdp", "ctx"), scatter_dimension=1, tiled=True),
        lax.psum_scatter(gain_one_terms, ("fsdp", "ctx"), scatter_dimension=0, tiled=True),
        lax.psum_scatter(head_terms, ("fsdp", "ctx"), scatter_dimension=0, tiled=True),
    )
    grad_tokens = (grad_middle + input_part).astype(jnp.bfloat16)
    return (
        layer_out[None],
        grad_tokens[None],
        grad_query,
        grad_key,
        grad_value,
        grad_output,
        grad_gate,
        grad_up,
        grad_down,
        grad_first,
        grad_second,
        grad_head,
    )


ROWS = 256
QROWS = 512
EPS = 1e-06
LOG2E = 1.4426950408889634
SCALE = HEAD_DIM**-0.5
VMEM_LIMIT = 60 * 1024 * 1024
BF16 = jnp.bfloat16
F32 = jnp.float32


def dot_nn(a, b):
    return lax.dot_general(a, b, (((1,), (0,)), ((), ())), preferred_element_type=F32)


def dot_nt(a, b):
    return lax.dot_general(a, b, (((1,), (1,)), ((), ())), preferred_element_type=F32)


def dot_tn(a, b):
    return lax.dot_general(a, b, (((0,), (0,)), ((), ())), preferred_element_type=F32)


def whereabouts():
    f, c = lax.axis_index("fsdp"), lax.axis_index("ctx")
    return f, c, f // 2, f % 2, c // 2, c % 2


def plane_of(s):
    return (s % 2) * 2 + s // 2


def remote(src, dst, send, recv, fsdp, ctx):
    return pltpu.make_async_remote_copy(
        src_ref=src, dst_ref=dst, send_sem=send, recv_sem=recv, device_id=(fsdp, ctx), device_id_type=MESH
    )


def await_bytes(ref, sem):
    pltpu.make_async_copy(ref, ref, sem).wait()


def greet_all():
    f, c, y, core, z, x = whereabouts()
    barrier = pltpu.get_barrier_semaphore()
    me = f * 8 + c

    def greet(j, carry):
        dev = (me + j) % 32
        pl.semaphore_signal(barrier, inc=1, device_id=(dev // 8, dev % 8), device_id_type=MESH)
        return carry

    lax.fori_loop(1, 32, greet, 0)
    pl.semaphore_wait(barrier, 31)


def chip_peer(r):
    f, c, y, core, z, x = whereabouts()
    y2 = 1 - y if r & 2 else y
    x2 = 1 - x if r & 1 else x
    return y2, x2


def chunk_of(r, core):
    y2, x2 = chip_peer(r)
    return (core * 2 + y2) * 2 + x2


def rows_of(ref, chunk):
    return ref.at[pl.ds(pl.multiple_of(chunk * ROWS, ROWS), ROWS)]


def head_norm_rope(raw, gain, cos, sin):
    r = lax.rsqrt(jnp.mean(raw * raw, axis=-1, keepdims=True) + EPS)
    u = raw * r * gain
    return u * cos + pltpu.roll(u, HEAD_DIM // 2, 1) * sin


def norm_rows(values, gain):
    v = values.astype(F32)
    return v * lax.rsqrt(jnp.mean(v * v, axis=-1, keepdims=True) + EPS) * gain


def norm_back(values, gain, dy):
    r = lax.rsqrt(jnp.mean(values * values, axis=-1, keepdims=True) + EPS)
    cdy = gain * dy
    back = r * cdy - values * (r * r * r) * jnp.mean(cdy * values, axis=-1, keepdims=True)
    return back, dy * values * r


def unturn(d, cos, sin):
    return d * cos - pltpu.roll(d, HEAD_DIM // 2, 1) * sin


def order_z(n, z):
    upper = z // 2
    low = (z + upper) % 2
    base = (low, 1 - low, 2, 3)[n]
    return base + upper * (3 - 2 * base)


def split_sum(partial, core_out, from_core, out_buf, in_buf, keep, send, core_recv, recv):
    f, c, y, core, z, x = whereabouts()
    half = ROWS // 2

    def to_core(k, carry):
        r = 3 - k
        y2, x2 = (y + r // 2) % 2, (x + r % 2) % 2
        chunk = ((1 - core) * 2 + y2) * 2 + x2
        core_out[r] = partial(chunk).astype(BF16)
        remote(core_out.at[r], from_core.at[r], send.at[6], core_recv.at[r], y * 2 + 1 - core, c).start()
        return carry

    lax.fori_loop(0, 4, to_core, 0)

    def both(r):
        await_bytes(from_core.at[r], core_recv.at[r])
        return partial(chunk_of(r, core)) + from_core[r].astype(F32)

    def over_x(k):
        remote(out_buf.at[k], in_buf.at[k], send.at[k], recv.at[k], f, z * 2 + 1 - x).start()

    def over_y(k):
        remote(out_buf.at[k], in_buf.at[k], send.at[k], recv.at[k], (1 - y) * 2 + core, c).start()

    total = both(3)
    out_buf[0] = total[:half].astype(BF16)
    over_x(0)
    out_buf[1] = total[half:].astype(BF16)
    over_y(1)
    total = both(1)
    out_buf[2] = total[:half].astype(BF16)
    over_x(2)
    keep[0] = total[half:]
    total = both(2)
    out_buf[3] = total[half:].astype(BF16)
    over_y(3)
    keep[1] = total[:half]
    await_bytes(in_buf.at[0], recv.at[0])
    out_buf[5] = (keep[1] + in_buf[0].astype(F32)).astype(BF16)
    over_y(5)
    await_bytes(in_buf.at[1], recv.at[1])
    out_buf[4] = (keep[0] + in_buf[1].astype(F32)).astype(BF16)
    over_x(4)
    total = both(0)
    keep[0] = total[:half]
    keep[1] = total[half:]


def split_sum_end(in_buf, keep, recv):
    for k in (2, 3, 4, 5):
        await_bytes(in_buf.at[k], recv.at[k])
    return (
        keep[0] + in_buf[2].astype(F32) + in_buf[5].astype(F32),
        keep[1] + in_buf[3].astype(F32) + in_buf[4].astype(F32),
    )


def split_sum_sent(from_core, out_buf, send):
    await_bytes(from_core, send.at[6])
    for k in range(6):
        await_bytes(out_buf.at[k], send.at[k])


SPLIT_SUM_SCRATCH = [
    pltpu.VMEM((4, ROWS, 1024), BF16),
    pltpu.VMEM((4, ROWS, 1024), BF16),
    pltpu.VMEM((6, ROWS // 2, 1024), BF16),
    pltpu.VMEM((6, ROWS // 2, 1024), BF16),
    pltpu.VMEM((2, ROWS // 2, 1024), F32),
    pltpu.SemaphoreType.DMA((7,)),
    pltpu.SemaphoreType.DMA((4,)),
    pltpu.SemaphoreType.DMA((6,)),
]


def rows_in_order(pos_s, ids_s, perm_s):
    ids = [lax.div(pos_s[0, j * 128], jnp.int32(128)) for j in range(16)]
    for b in range(16):
        ids_s[b] = ids[b]
        place = jnp.int32(0)
        for j in range(16):
            place = place + j * (1 - lax.min(lax.abs(ids[j] - b), jnp.int32(1)))
        perm_s[b] = lax.min(place, jnp.int32(15))


def turns(table):
    cos, sin = table[:, 0 : HEAD_DIM // 2], table[:, HEAD_DIM // 2 :]
    return jnp.concatenate([cos, cos], axis=1), jnp.concatenate([-sin, sin], axis=1)


def two_blocks(ref, chunk, cols):
    return ref[pl.ds(chunk * 2, 2), :, cols].reshape(ROWS, -1)


def put_two(ref, chunk, cols, value):
    for k in range(2):
        ref[chunk * 2 + k, :, cols] = value[k * 128 : k * 128 + 128]


def gain_rows(gains_all):
    every = gains_all[...].reshape(32, 128)
    lane = lax.broadcasted_iota(jnp.int32, (32, 128), 1)

    def place(first, count, per_row):
        kept = jnp.where((lane >= first) & (lane < first + count), every, 0.0)
        turned = [pltpu.roll(kept, (count * seg - first) % 128, 1) for seg in range(per_row)]
        return [
            sum(turned[seg][m * per_row + seg : m * per_row + seg + 1] for seg in range(per_row))
            for m in range(32 // per_row)
        ]

    one, two = place(0, 32, 4), place(32, 32, 4)
    query, key = place(64, 8, 16)
    return jnp.concatenate(one, axis=1), jnp.concatenate(two, axis=1), query, key


PIECES = [
    ("o", 0), ("o", 1), ("x", 0), ("y", 0), ("o", 2), ("x", 1), ("y", 1), ("o", 3),
    ("x", 2), ("y", 2), ("d", 0), ("x", 3), ("y", 3), ("d", 1), ("d", 2), ("d", 3),
]


def layer_kernel(
    tok, cot, pos, wq, wk, wv, wo, wg, wu, wd_own, gains, table_h,
    layer_out, grad_tokens, pf, po, pa, rd, h_out, small_out,
    xx, hd, g_s, w1, w2, w3, wd, pack1, pack2, pack3, gains_all, table_s, gain_s,
    q_s, k_s, v_s, o_s, vt, acc, total, lse_s, x_keep, mid,
    mix_s, act_s, delta_s, dqt_s, dk_s, dv_s, dmid, small,
    core_out, from_core, out_buf, in_buf, keep, lpart, core_out2, from_core2, in_buf2,
    gf, go, rf, ro, ra, sf, so, sa, s_in, sbuf, p_in, stage, pos_v, pos_s, ids_s, perm_s,
    x_recv, g_recv, stage_recv, hop_send, x_send, g_send, pos_sem, gain_sem, w1_sem, w2_sem, w3_sem, w3_came, wd_sem,
    load, ag_send, ag_recv, ag_core, ag_recv2, ag_core2, send, core_recv, recv, recv_d, send2, core_recv2, recv2,
    f_sem, f_came, o_sem, a_sem, a_came, d_sem, fp_sem, op_sem, ap_sem, out_sem, s_sem, p_sem,
):
    f, c, y, core, z, x = whereabouts()
    me, t, own = f * 8 + c, f * 2 + x, (core * 2 + y) * 2 + x
    half = ROWS // 2
    upper = z // 2
    edge, inner, other_inner = 3 * upper, 1 + upper, 2 - upper
    table = pltpu.make_async_copy(table_h, table_s, load.at[0])
    table.start()
    for k in range(8):
        pack1[k, :, 0:256] = wq[:, k * 256 : k * 256 + 256]
        pack1[k, :, 256:384] = wk[:, k * 128 : k * 128 + 128]
        pack1[k, :, 384:512] = wv[:, k * 128 : k * 128 + 128]
    greet_all()

    home = plane_of(f)
    seq = plane_of(z)
    ys, cs = seq // 2, seq % 2
    side = (y + ys) % 2
    other_y = (1 - y) * 2 + core
    other_core = y * 2 + 1 - core
    other_x = z * 2 + 1 - x

    def piece(buf, chunk, part):
        return buf.at[pl.ds(pl.multiple_of(chunk * ROWS + part * half, half), half)]

    def hop(src, buf, recv_, k):
        low, high = src.at[pl.ds(0, half)], src.at[pl.ds(half, half)]

        @pl.when(home != z)
        def _():
            remote(low, piece(buf, c, 0), hop_send.at[3 * k], recv_.at[2 * c], f, home * 2 + x).start()
            remote(high, stage.at[k], hop_send.at[3 * k + 1], stage_recv.at[k], other_y, c).start()

        @pl.when(home == z)
        def _():
            pltpu.make_async_copy(low, piece(buf, c, 0), recv_.at[2 * c]).start()
            remote(high, piece(buf, c, 1), hop_send.at[3 * k + 1], recv_.at[2 * c + 1], other_y, c).start()

    beyond = plane_of(other_y)

    def hop_on(buf, recv_, k):
        @pl.when(beyond != z)
        def _():
            await_bytes(stage.at[k], stage_recv.at[k])
            remote(stage.at[k], piece(buf, c, 1), hop_send.at[3 * k + 2], recv_.at[2 * c + 1], f, beyond * 2 + x).start()

    def hop_done(k):
        @pl.when(home != z)
        def _():
            await_bytes(stage.at[k], hop_send.at[3 * k])

        await_bytes(stage.at[k], hop_send.at[3 * k + 1])

        @pl.when(beyond != z)
        def _():
            await_bytes(stage.at[k], hop_send.at[3 * k + 2])

    def whereof(kind, n):
        chunk = order_z(n, z) * 2 + (x if kind in "oy" else 1 - x)
        return chunk, (side if kind in "ox" else 1 - side)

    def relay(buf, recv_, send_, kind, n):
        chunk, part = whereof(kind, n)
        rows = piece(buf, chunk, part)
        sem = recv_.at[2 * chunk + part]

        @pl.when(core == cs)
        def _():
            await_bytes(rows, sem)
            if kind == "o" or kind == "y" and n % 2 == 1:
                remote(rows, rows, send_.at[1], sem, f, other_x).start()
            if kind == "o" or kind == "x" and n % 2 == 0:
                remote(rows, rows, send_.at[2], sem, other_y, c).start()
            remote(rows, rows, send_.at[0], sem, other_core, c).start()

    def relay_wait(buf, recv_, kind, n):
        chunk, part = whereof(kind, n)

        @pl.when(core != cs)
        def _():
            await_bytes(piece(buf, chunk, part), recv_.at[2 * chunk + part])

    def relay_done(buf, send_):
        @pl.when(core == cs)
        def _():
            await_bytes(buf, send_.at[0])
            await_bytes(buf.at[pl.ds(0, 6 * half)], send_.at[1])
            await_bytes(buf.at[pl.ds(0, 6 * half)], send_.at[2])

    def my_rows(w):
        return w.at[f, z, pl.ds(pl.multiple_of(x * 32, 32), 32)]

    def weights_in_plane(pack, w, sem):
        pltpu.make_async_copy(pack.at[t], my_rows(w), sem.at[1]).start()
        for j in range(1, 8):
            t2 = (t + j) % 8
            remote(pack.at[t2], my_rows(w), sem.at[0], sem.at[1], t2 // 2, z * 2 + t2 % 2).start()

    def weights_across(w, sem):
        await_bytes(w.at[:, z], sem.at[1])
        for j in (1, 3, 2):
            remote(w.at[:, z], w.at[:, z], sem.at[2], sem.at[3], f, ((z + j) % 4) * 2 + x).start()

    def weights_near(w, sem, came):
        await_bytes(w.at[:, z], sem.at[1])
        for to_z in (inner + edge - z, other_inner):
            remote(w.at[:, z], w.at[:, z], sem.at[2], came.at[z], f, to_z * 2 + x).start()

    def weights_relay(w, sem, came):
        @pl.when(z == inner)
        def _():
            for from_z in (other_inner, 3 - edge):
                await_bytes(w.at[:, from_z], came.at[from_z])
                remote(w.at[:, from_z], w.at[:, from_z], sem.at[2], came.at[from_z], f, edge * 2 + x).start()

    def weights_done(w, came):
        @pl.when(z == inner)
        def _():
            await_bytes(w.at[:, edge], came.at[edge])

        @pl.when(z == edge)
        def _():
            for from_z in (inner, other_inner, 3 - edge):
                await_bytes(w.at[:, from_z], came.at[from_z])

    def weights_sent(w, sem):
        await_bytes(w.at[:, pl.ds(0, 2)], sem.at[2])

        @pl.when(z == inner)
        def _():
            await_bytes(w.at[:, pl.ds(0, 2)], sem.at[2])

    hop(tok, xx, x_recv, 0)
    weights_in_plane(pack1, w1, w1_sem)

    @pl.when(f == seq)
    def _():
        pltpu.make_async_copy(pos, pos_v, pos_sem.at[1]).start()
        for j in range(1, 4):
            remote(pos, pos_v, pos_sem.at[0], pos_sem.at[1], (f + j) % 4, c).start()

    pltpu.make_async_copy(gains, gains_all.at[me], gain_sem.at[1]).start()

    def send_gains(j, carry):
        dev = (me + j) % 32
        remote(gains, gains_all.at[me], gain_sem.at[0], gain_sem.at[1], dev // 8, dev % 8).start()
        return carry

    lax.fori_loop(1, 32, send_gains, 0)
    relay(xx, x_recv, x_send, "o", 0)
    hop_on(xx, x_recv, 0)
    weights_across(w1, w1_sem)
    hop(cot, g_s, g_recv, 1)
    for k in range(8):
        pack2[k] = wo[:, k * 256 : k * 256 + 256]
        pack3[k, :, 0:384] = wg[:, k * 384 : k * 384 + 384]
        pack3[k, :, 384:768] = wu[:, k * 384 : k * 384 + 384]
    await_bytes(gains_all, gain_sem.at[1])
    one, two, gain_q, gain_k = gain_rows(gains_all)
    gain_s[...] = jnp.zeros_like(gain_s)
    gain_s[0:1, :] = one
    gain_s[1:2, :] = two
    gain_s[2:3, 0:128] = gain_q
    gain_s[3:4, 0:128] = gain_k
    await_bytes(pos_v, pos_sem.at[1])
    pos_copy = pltpu.make_async_copy(pos_v, pos_s, load.at[2])
    pos_copy.start()
    pos_copy.wait()
    rows_in_order(pos_s, ids_s, perm_s)

    def norm_piece(kind, n):
        chunk, part = whereof(kind, n)
        rows = pl.ds(pl.multiple_of(chunk * ROWS + part * half, half), half)
        hd[rows, :] = norm_rows(xx[rows, :], gain_s[0:1, :]).astype(BF16)

    for at, (kind, n) in enumerate(PIECES):
        if at:
            relay(xx, x_recv, x_send, kind, n)
        relay_wait(xx, x_recv, kind, n)
        norm_piece(kind, n)
        if at == 2:
            weights_in_plane(pack2, w2, w2_sem)
            hop_on(g_s, g_recv, 1)
        if at == 4:
            weights_in_plane(pack3, w3, w3_sem)
        if at == 6:
            weights_across(w2, w2_sem)
        if at == 10:
            weights_near(w3, w3_sem, w3_came)
    h_copy = pltpu.make_async_copy(hd, h_out, load.at[1])
    h_copy.start()
    x_keep[...] = xx[pl.ds(pl.multiple_of(own * ROWS, ROWS), ROWS), :]

    t_down = me // 4
    down_rows = wd.at[pl.ds(pl.multiple_of((me % 4) * 96, 32), 96)]
    self_down = t_down == t
    for k in range(4):
        here = self_down & (z == k)

        @pl.when(here)
        def _():
            pltpu.make_async_copy(wd_own, down_rows, wd_sem.at[1]).start()

        @pl.when(jnp.logical_not(here))
        def _():
            remote(wd_own, down_rows, wd_sem.at[0], wd_sem.at[1], t_down // 2, k * 2 + t_down % 2).start()

    table.wait()
    await_bytes(w1.at[pl.ds(0, 3)], w1_sem.at[3])

    def project(ch, carry):
        rows = pl.ds(pl.multiple_of(ch * ROWS, ROWS), ROWS)
        raw = dot_nn(hd[rows, :], w1[...].reshape(1024, 512))
        cos, sin = turns(jnp.concatenate([table_s[ids_s[ch * 2 + k]] for k in range(2)], axis=0))
        gq, gk = gain_s[2:3, 0:128], gain_s[3:4, 0:128]
        for k in range(2):
            cols = slice(k * 128, k * 128 + 128)
            put_two(mix_s, ch, cols, head_norm_rope(raw[:, cols], gq, cos, sin).astype(BF16))
        put_two(mix_s, ch, slice(256, 384), head_norm_rope(raw[:, 256:384], gk, cos, sin).astype(BF16))
        put_two(mix_s, ch, slice(384, 512), raw[:, 384:512].astype(BF16))
        return carry

    lax.fori_loop(0, 8, project, 0)
    for n in range(4):
        relay(g_s, g_recv, g_send, "o", n)

    def arrange(b, carry):
        for k in range(4):
            rows = pl.ds(pl.multiple_of(b * QROWS + k * 128, 128), 128)
            stored = perm_s[b * 4 + k]
            q_s[rows, :] = mix_s[stored, :, 0:256]
            k_s[rows, :] = mix_s[stored, :, 256:384]
            v_s[rows, :] = mix_s[stored, :, 384:512]
        vt[b] = v_s[pl.ds(pl.multiple_of(b * QROWS, QROWS), QROWS), :].T
        return carry

    lax.fori_loop(0, 4, arrange, 0)
    def query_tile(qt):
        def step(kt, diagonal):
            kb = k_s[pl.ds(pl.multiple_of(kt * QROWS, QROWS), QROWS), :]
            vb = vt[kt]
            for g in range(4):
                head, part = g // 2, g % 2
                qb = q_s[pl.ds(qt * QROWS + part * 256, 256), head * 128 : head * 128 + 128]
                depth = 256 * (part + 1) if diagonal else QROWS
                s = dot_nt(kb[:depth], qb)
                p = jnp.exp2(s * (SCALE * LOG2E))
                if diagonal:
                    ki = lax.broadcasted_iota(jnp.int32, (depth, 256), 0)
                    qi = lax.broadcasted_iota(jnp.int32, (depth, 256), 1) + part * 256
                    p = jnp.where(ki <= qi, p, 0.0)
                cols = slice(g * 256, g * 256 + 256)
                total[:, cols] += jnp.sum(p, axis=0, keepdims=True)
                acc[:, cols] += dot_nn(vb[:, :depth], p.astype(BF16))

        total[...] = jnp.zeros_like(total)
        acc[...] = jnp.zeros_like(acc)

        def off(kt, inner):
            step(kt, False)
            return inner

        lax.fori_loop(0, qt, off, 0)
        step(qt, True)
        sums = total[...]
        lse_s[qt] = jnp.log2(sums)
        out = acc[...] * (1.0 / sums)
        for g in range(4):
            head, part = g // 2, g % 2
            value = out[:, g * 256 : g * 256 + 256].T.astype(BF16)
            put_two(o_s, qt * 2 + part, slice(head * 128, head * 128 + 128), value)

    for qt in range(4):
        query_tile(qt)
        if qt == 1:
            for n in range(4):
                relay(g_s, g_recv, g_send, "x", n)
                relay(g_s, g_recv, g_send, "y", n)
        if qt == 3:
            for n in range(4):
                relay(g_s, g_recv, g_send, "d", n)
    await_bytes(w2.at[pl.ds(0, 3)], w2_sem.at[3])
    relay_done(xx, x_send)
    h_copy.wait()

    def attention_term(chunk):
        rows = jnp.concatenate([o_s[ids_s[chunk * 2 + k]] for k in range(2)], axis=0)
        return dot_nt(rows, w2[...].reshape(1024, 256))

    split_sum(attention_term, core_out, from_core, out_buf, in_buf, keep, send, core_recv, recv)
    weights_relay(w3, w3_sem, w3_came)
    low, high = split_sum_end(in_buf, keep, recv)
    gain_one, gain_two = gain_s[0:1, :], gain_s[1:2, :]
    mid[0:half, :] = x_keep[0:half, :].astype(F32) + low
    mid[half:ROWS, :] = x_keep[half:ROWS, :].astype(F32) + high
    xx[pl.ds(pl.multiple_of(own * ROWS, ROWS), ROWS), :] = norm_rows(mid[...], gain_two).astype(BF16)

    def gather_start(every, sem, core_sem):
        for part in (0, 1):
            a, b = piece(every, own, part), piece(every, own, 1 - part)
            remote(a, a, ag_send.at[0], sem.at[part], f, z * 2 + 1 - x).start()
            remote(b, b, ag_send.at[1], sem.at[2 + 1 - part], (1 - y) * 2 + core, c).start()
        for part in (0, 1):
            a = piece(every, own, part)
            remote(a, a, ag_send.at[2], core_sem.at[part], y * 2 + 1 - core, c).start()

    def gather_step(every, sem, core_sem, r, part):
        a = piece(every, chunk_of(r, core), part)
        k = (r - 1) * 2 + part
        await_bytes(a, sem.at[k])
        if r == 1 and part == 0:
            remote(a, a, ag_send.at[1], sem.at[4], (1 - y) * 2 + core, c).start()
        if r == 2 and part == 1:
            remote(a, a, ag_send.at[0], sem.at[5], f, z * 2 + 1 - x).start()
        remote(a, a, ag_send.at[2], core_sem.at[2 * r + part], y * 2 + 1 - core, c).start()

    def gather_core(every, core_sem, r):
        for part in (0, 1):
            await_bytes(piece(every, chunk_of(r, 1 - core), part), core_sem.at[2 * r + part])

    def gather_sent(every):
        await_bytes(every.at[pl.ds(0, 3 * half)], ag_send.at[0])
        await_bytes(every.at[pl.ds(0, 3 * half)], ag_send.at[1])
        await_bytes(every.at[pl.ds(0, 8 * half)], ag_send.at[2])

    gather_start(xx, ag_recv, ag_core)
    split_sum_sent(from_core, out_buf, send)
    weights_done(w3, w3_came)

    def feed_forward(r, same):
        chunk = chunk_of(r, core if same else 1 - core)
        rows = pl.ds(pl.multiple_of(chunk * ROWS, ROWS), ROWS)
        gu = dot_nn(xx[rows, :], w3[...].reshape(1024, 768))
        gate, up = gu[:, 0:384], gu[:, 384:768]
        sig = 1.0 / (1.0 + jnp.exp(-gate))
        sil = gate * sig
        act_s[rows, :] = (sil * up).astype(BF16)
        put_two(mix_s, chunk, slice(0, 384), (up * sig * (1.0 + gate * (1.0 - sig))).astype(BF16))
        put_two(mix_s, chunk, slice(384, 768), sil.astype(BF16))

    def feed_back(r, same):
        chunk = chunk_of(r, core if same else 1 - core)
        rows = pl.ds(pl.multiple_of(chunk * ROWS, ROWS), ROWS)
        layer = dot_nn(act_s[rows, :], wd[...]).astype(BF16)
        if same:
            lpart[r] = layer
        else:
            slot = r % 2
            if r in (3, 0):
                await_bytes(core_out2.at[slot], send2.at[slot])
            core_out2[slot] = layer
            remote(core_out2.at[slot], from_core2.at[r], send2.at[slot], core_recv2.at[r], other_core, c).start()
        dact = dot_nt(g_s[rows, :], wd[...])
        for cols in (slice(0, 384), slice(384, 768)):
            put_two(mix_s, chunk, cols, (dact * two_blocks(mix_s, chunk, cols).astype(F32)).astype(BF16))
        dh = dot_nt(two_blocks(mix_s, chunk, slice(0, 768)), w3[...].reshape(1024, 768))
        if not same:
            core_out[r] = dh.astype(BF16)
            remote(core_out.at[r], from_core.at[r], send.at[6], core_recv.at[r], other_core, c).start()
        elif r == 0:
            keep[0] = dh[:half]
            keep[1] = dh[half:]
        else:
            out_buf[2 * r - 2] = dh[:half].astype(BF16)
            out_buf[2 * r - 1] = dh[half:].astype(BF16)

    def sum_to_chip(r):
        await_bytes(from_core.at[r], core_recv.at[r])
        y2, x2 = chip_peer(r)
        for part in (0, 1):
            k = 2 * r - 2 + part
            out_buf[k] = (
                out_buf[k].astype(F32) + from_core[r, part * half : part * half + half].astype(F32)
            ).astype(BF16)
            remote(out_buf.at[k], in_buf.at[k], send.at[k], recv_d.at[k], y2 * 2 + core, z * 2 + x2).start()

    feed_forward(0, True)
    gather_step(xx, ag_recv, ag_core, 1, 0)
    gather_step(xx, ag_recv, ag_core, 2, 1)
    gather_core(xx, ag_core, 0)
    feed_forward(0, False)
    gather_step(xx, ag_recv, ag_core, 1, 1)
    gather_step(xx, ag_recv, ag_core, 2, 0)
    feed_forward(1, True)
    feed_forward(2, True)
    gather_core(xx, ag_core, 1)
    feed_forward(1, False)
    gather_core(xx, ag_core, 2)
    feed_forward(2, False)
    for kind, n in PIECES:
        relay_wait(g_s, g_recv, kind, n)
    await_bytes(wd, wd_sem.at[1])
    feed_back(1, False)
    feed_back(1, True)
    gather_step(xx, ag_recv, ag_core, 3, 0)
    gather_step(xx, ag_recv, ag_core, 3, 1)
    feed_back(2, False)
    sum_to_chip(1)
    feed_back(2, True)
    feed_forward(3, True)
    gather_core(xx, ag_core, 3)
    feed_forward(3, False)
    sum_to_chip(2)
    feed_back(3, False)
    feed_back(3, True)
    sum_to_chip(3)
    feed_back(0, False)
    feed_back(0, True)

    def scatter_rows(g, b, block, first, width):
        for k in range(4):
            g[k, b * 64 : b * 64 + 64, first : first + width] = block[k * 64 : k * 64 + 64].astype(BF16)

    def across(g, r_, sem):
        pltpu.make_async_copy(g.at[z], r_.at[z], sem.at[1]).start()
        for j in (2, 1, 3):
            z2 = (z + j) % 4
            remote(g.at[z2], r_.at[z], sem.at[0], sem.at[1], f, z2 * 2 + x).start()

    def across_near(g, r_, sem, came):
        @pl.when(z == edge)
        def _():
            for e in range(2):
                remote(
                    g.at[2 * (1 - upper) + e], r_.at[2 + e], sem.at[0], came.at[2 + e], f, inner * 2 + x
                ).start()

        remote(
            g.at[inner + edge - z], r_.at[upper], sem.at[0], came.at[upper], f, (inner + edge - z) * 2 + x
        ).start()

    def across_relay(g, r_, sem, came):
        @pl.when(z == inner)
        def _():
            for e in range(2):
                to_z = 2 * (1 - upper) + e
                await_bytes(r_.at[2 + e], came.at[2 + e])
                g[to_z] = (g[to_z].astype(F32) + r_[2 + e].astype(F32)).astype(BF16)
                remote(g.at[to_z], r_.at[upper], sem.at[0], came.at[upper], f, to_z * 2 + x).start()

    def across_sent(g, sem):
        await_bytes(g.at[pl.ds(0, 3)], sem.at[0])

    def to_plane(s_, p_, plane_sem):
        pltpu.make_async_copy(s_.at[pl.ds(pl.multiple_of(t * 32, 32), 32)], p_.at[t], plane_sem.at[1]).start()
        for j in range(1, 8):
            t2 = (t + j) % 8
            block = s_.at[pl.ds(pl.multiple_of(t2 * 32, 32), 32)]
            remote(block, p_.at[t], plane_sem.at[0], plane_sem.at[1], t2 // 2, z * 2 + t2 % 2).start()

    def in_plane(r_, s_, p_, sem, plane_sem):
        await_bytes(r_, sem.at[1])
        s_[...] = (r_[0].astype(F32) + r_[1].astype(F32) + r_[2].astype(F32) + r_[3].astype(F32)).astype(BF16)
        to_plane(s_, p_, plane_sem)

    def in_plane_near(g, r_, s_, p_, came, plane_sem):
        for k in range(2):
            await_bytes(r_.at[k], came.at[k])
        s_[...] = (g[z].astype(F32) + r_[0].astype(F32) + r_[1].astype(F32)).astype(BF16)
        to_plane(s_, p_, plane_sem)

    for b in range(4):
        scatter_rows(gf, b, dot_tn(xx[:, b * 256 : b * 256 + 256], mix_s[...].reshape(2048, 768)), 0, 768)
    across_near(gf, rf, f_sem, f_came)
    await_bytes(from_core, send.at[6])
    for b in range(3):
        block = dot_tn(act_s[:, b * 128 : b * 128 + 128], g_s[...]).astype(BF16)
        for k in range(4):
            low, high = max(b * 128, k * 96), min(b * 128 + 128, k * 96 + 96)
            if low < high:
                core_out[k, low - k * 96 : high - k * 96, :] = block[low - b * 128 : high - b * 128]
    for k in range(4):
        dev = t * 4 + k
        rows = core_out.at[k, pl.ds(0, 96)]

        @pl.when(dev == me)
        def _():
            pltpu.make_async_copy(rows, rd.at[z], d_sem.at[1]).start()

        @pl.when(dev != me)
        def _():
            remote(rows, rd.at[z], d_sem.at[0], d_sem.at[1], dev // 8, dev % 8).start()

    gather_sent(xx)
    h_load = pltpu.make_async_copy(h_out, xx, load.at[3])
    h_load.start()

    await_bytes(from_core.at[0], core_recv.at[0])
    for k in range(6):
        await_bytes(in_buf.at[k], recv_d.at[k])
    small[...] = jnp.zeros_like(small)
    for part in (0, 1):
        rows = slice(part * half, part * half + half)
        dh = keep[part] + from_core[0, rows].astype(F32)
        dh = dh + in_buf[part].astype(F32) + in_buf[2 + part].astype(F32) + in_buf[4 + part].astype(F32)
        back, dgain = norm_back(mid[rows, :], gain_two, dh)
        first = pl.multiple_of(own * ROWS + part * half, half)
        dm = g_s[pl.ds(first, half), :].astype(F32) + back
        dmid[rows, :] = dm
        hd[pl.ds(first, half), :] = dm.astype(BF16)
        small[1:2, :] += jnp.sum(dgain, axis=0, keepdims=True)
    gather_start(hd, ag_recv2, ag_core2)
    for k in range(6):
        await_bytes(out_buf.at[k], send.at[k])
    for b in range(4):
        vt[b] = k_s[b * QROWS : b * QROWS + QROWS, :].T

    def back_out(r, same):
        chunk = chunk_of(r, core if same else 1 - core)
        rows = pl.ds(pl.multiple_of(chunk * ROWS, ROWS), ROWS)
        put_two(mix_s, chunk, slice(512, 768), dot_nn(hd[rows, :], w2[...].reshape(1024, 256)).astype(BF16))

    back_out(0, True)
    gather_step(hd, ag_recv2, ag_core2, 1, 0)
    gather_step(hd, ag_recv2, ag_core2, 2, 1)
    gather_core(hd, ag_core2, 0)
    back_out(0, False)
    gather_step(hd, ag_recv2, ag_core2, 1, 1)
    gather_step(hd, ag_recv2, ag_core2, 2, 0)
    back_out(1, True)
    back_out(2, True)
    gather_core(hd, ag_core2, 1)
    back_out(1, False)
    gather_core(hd, ag_core2, 2)
    back_out(2, False)
    gather_step(hd, ag_recv2, ag_core2, 3, 0)
    gather_step(hd, ag_recv2, ag_core2, 3, 1)
    back_out(3, True)
    gather_core(hd, ag_core2, 3)
    back_out(3, False)

    def layer_to_chips():
        for r in (3, 1, 2):
            await_bytes(from_core2.at[r], core_recv2.at[r])
            lpart[r] = (lpart[r].astype(F32) + from_core2[r].astype(F32)).astype(BF16)
            y2, x2 = chip_peer(r)
            remote(
                lpart.at[r], in_buf2.at[r - 1], send2.at[1 + r], recv2.at[r - 1], y2 * 2 + core, z * 2 + x2
            ).start()

    def prepare(b, carry):
        rows = pl.ds(pl.multiple_of(b * QROWS, QROWS), QROWS)
        do = jnp.concatenate(
            [mix_s[perm_s[b * 4 + k], :, 512:768] for k in range(4)], axis=0
        )
        act_s[rows, 0:256] = do
        ones = jnp.ones((8, 128), BF16)
        for head in range(2):
            cols = slice(head * 128, head * 128 + 128)
            prod = do[:, cols].astype(F32) * o_s[pl.ds(b * 4, 4), :, cols].reshape(QROWS, 128).astype(F32)
            high = prod.astype(BF16)
            low = (prod - high.astype(F32)).astype(BF16)
            delta = dot_nt(ones, high) + dot_nt(ones, low)
            delta_s[b, :, head * QROWS : head * QROWS + QROWS] = delta[0:1]
        return carry

    lax.fori_loop(0, 4, prepare, 0)
    for b in range(16):
        mix_s[b, :, 0:256] = o_s[ids_s[b]]
    for b in range(4):
        scatter_rows(go, b, dot_tn(hd[:, b * 256 : b * 256 + 256], mix_s[:, :, 0:256].reshape(2048, 256)), 0, 256)
    across(go, ro, o_sem)
    dqt_s[...] = jnp.zeros_like(dqt_s)
    dk_s[...] = jnp.zeros_like(dk_s)
    dv_s[...] = jnp.zeros_like(dv_s)

    def key_tile(kt):
        krows = pl.ds(kt * QROWS, QROWS)

        def step(qt, diagonal):
            kb, vb, ktb = k_s[krows, :], v_s[krows, :], vt[kt]
            for g in range(4):
                head, part = g // 2, g % 2
                start = pl.multiple_of(qt * QROWS + part * 256, 256)
                cols = slice(head * 128, head * 128 + 128)
                lanes = slice(g * 256, g * 256 + 256)
                qb = q_s[pl.ds(start, 256), cols]
                dob = act_s[pl.ds(start, 256), cols]
                depth = 256 * (part + 1) if diagonal else QROWS
                s = dot_nt(kb[:depth], qb)
                p = jnp.exp2(s * (SCALE * LOG2E) - lse_s[qt, :, lanes])
                if diagonal:
                    ki = lax.broadcasted_iota(jnp.int32, (depth, 256), 0)
                    qi = lax.broadcasted_iota(jnp.int32, (depth, 256), 1) + part * 256
                    p = jnp.where(ki <= qi, p, 0.0)
                dp = dot_nt(vb[:depth], dob)
                ds = (p * (dp - delta_s[qt, :, lanes])).astype(BF16)
                out = pl.ds(kt * 4, depth // 128)
                dv_s[out] += dot_nn(p.astype(BF16), dob).reshape(depth // 128, 128, 128)
                dk_s[out] += dot_nn(ds, qb).reshape(depth // 128, 128, 128)
                dq = dot_nn(ktb[:, :depth], ds)
                dqt_s[qt * 4 + part * 2, cols, :] += dq[:, 0:128]
                dqt_s[qt * 4 + part * 2 + 1, cols, :] += dq[:, 128:256]

        step(kt, True)

        def off(qt, inner):
            step(qt, False)
            return inner

        lax.fori_loop(kt + 1, 4, off, 0)

    key_tile(0)
    layer_to_chips()
    across_relay(gf, rf, f_sem, f_came)
    key_tile(1)
    key_tile(2)
    key_tile(3)
    in_plane_near(gf, rf, sf, pf, f_came, fp_sem)

    home_f, home_c = plane_of(z), own
    stays = (home_f == f) & (home_c == c)

    def deliver(src, dst, k):
        @pl.when(jnp.logical_not(stays))
        def _():
            remote(src, dst, out_sem.at[k], out_sem.at[k + 1], home_f, home_c).start()

        @pl.when(stays)
        def _():
            pltpu.make_async_copy(src, dst, out_sem.at[k + 1]).start()

    await_bytes(from_core2.at[0], core_recv2.at[0])
    for r in (1, 2, 3):
        await_bytes(in_buf2.at[r - 1], recv2.at[r - 1])
    layer = mid[...] + lpart[0].astype(F32) + from_core2[0].astype(F32)
    layer = layer + in_buf2[0].astype(F32) + in_buf2[1].astype(F32) + in_buf2[2].astype(F32)
    in_buf2[0] = layer.astype(BF16)
    deliver(in_buf2.at[0], layer_out, 0)
    in_plane(ro, so, po, o_sem, op_sem)
    h_load.wait()

    def finish_chunk(chunk):
        rows = pl.ds(pl.multiple_of(chunk * ROWS, ROWS), ROWS)
        places = [ids_s[chunk * 2 + k] for k in range(2)]
        cos, sin = turns(jnp.concatenate([table_s[b] for b in places], axis=0))
        raw = dot_nn(xx[rows, :], w1[:, :, :, 0:384].reshape(1024, 384))
        for head in range(3):
            cols = slice(head * 128, head * 128 + 128)
            if head < 2:
                blocks = [dqt_s[b, cols, :].T for b in places]
                gain, lanes = gain_s[2:3, 0:128], slice(0, 128)
            else:
                blocks = [dk_s[b] for b in places]
                gain, lanes = gain_s[3:4, 0:128], slice(128, 256)
            d = jnp.concatenate(blocks, axis=0) * SCALE
            back, dgain = norm_back(raw[:, cols], gain, unturn(d, cos, sin))
            put_two(mix_s, chunk, cols, back.astype(BF16))
            small[2:3, lanes] += jnp.sum(dgain, axis=0, keepdims=True)
        for k in range(2):
            mix_s[chunk * 2 + k, :, 384:512] = dv_s[places[k]].astype(BF16)

    def partial(chunk):
        finish_chunk(chunk)
        return dot_nt(two_blocks(mix_s, chunk, slice(0, 512)), w1[...].reshape(1024, 512))

    gather_sent(hd)
    across_sent(gf, f_sem)
    await_bytes(rd, d_sem.at[1])
    for k in range(4):

        @pl.when(t * 4 + k != me)
        def _():
            await_bytes(core_out.at[k, pl.ds(0, 96)], d_sem.at[0])

    split_sum(partial, core_out, from_core, out_buf, in_buf, keep, send, core_recv, recv)
    for b in range(4):
        scatter_rows(gf, b, dot_tn(xx[:, b * 256 : b * 256 + 256], mix_s[:, :, 0:512].reshape(2048, 512)), 0, 512)
    ga = gf.at[:, :, pl.ds(0, 512)]
    across_near(ga, ra, a_sem, a_came)
    low, high = split_sum_end(in_buf, keep, recv)
    for part, dh in ((0, low), (1, high)):
        rows = slice(part * half, part * half + half)
        back, dgain = norm_back(x_keep[rows, :].astype(F32), gain_one, dh)
        in_buf2[1, rows, :] = (dmid[rows, :] + back).astype(BF16)
        small[0:1, :] += jnp.sum(dgain, axis=0, keepdims=True)
    deliver(in_buf2.at[1], grad_tokens, 2)
    across_relay(ga, ra, a_sem, a_came)

    s_in[t] = small[...]
    for j in range(1, 8):
        t2 = (t + j) % 8
        remote(small, s_in.at[t], s_sem.at[0], s_sem.at[1], t2 // 2, z * 2 + t2 % 2).start()

    await_bytes(pf, fp_sem.at[1])
    await_bytes(po, op_sem.at[1])
    await_bytes(s_in.at[pl.ds(0, 7)], s_sem.at[1])
    sbuf[...] = jnp.sum(s_in[...], axis=0)
    p_in[z] = sbuf[...]
    for j in range(1, 4):
        remote(sbuf, p_in.at[z], p_sem.at[0], p_sem.at[1], f, ((z + j) % 4) * 2 + x).start()
    in_plane_near(ga, ra, sa, pa, a_came, ap_sem)
    await_bytes(p_in.at[pl.ds(0, 3)], p_sem.at[1])
    small_out[...] = jnp.sum(p_in[...], axis=0)
    await_bytes(pa, ap_sem.at[1])

    await_bytes(layer_out, out_sem.at[1])
    await_bytes(grad_tokens, out_sem.at[3])

    @pl.when(jnp.logical_not(stays))
    def _():
        await_bytes(layer_out, out_sem.at[0])
        await_bytes(grad_tokens, out_sem.at[2])

    split_sum_sent(from_core, out_buf, send)
    for k in range(2):
        await_bytes(core_out2.at[k], send2.at[k])
    for r in (1, 2, 3):
        await_bytes(lpart.at[r], send2.at[1 + r])
    await_bytes(s_in.at[pl.ds(0, 7)], s_sem.at[0])
    await_bytes(p_in.at[pl.ds(0, 3)], p_sem.at[0])
    await_bytes(go.at[pl.ds(0, 3)], o_sem.at[0])
    await_bytes(ra.at[pl.ds(0, 3)], a_sem.at[0])
    await_bytes(pf.at[pl.ds(0, 7)], fp_sem.at[0])
    await_bytes(po.at[pl.ds(0, 7)], op_sem.at[0])
    await_bytes(pa.at[pl.ds(0, 7)], ap_sem.at[0])
    hop_done(0)
    hop_done(1)
    relay_done(g_s, g_send)

    @pl.when(f == seq)
    def _():
        for _ in range(3):
            await_bytes(pos_v, pos_sem.at[0])

    await_bytes(gains_all.at[pl.ds(0, 31)], gain_sem.at[0])
    for pack, w, sem in ((pack1, w1, w1_sem), (pack2, w2, w2_sem)):
        await_bytes(pack.at[pl.ds(0, 7)], sem.at[0])
        await_bytes(w.at[pl.ds(0, 3)], sem.at[2])
    await_bytes(pack3.at[pl.ds(0, 7)], w3_sem.at[0])
    weights_sent(w3, w3_sem)
    for k in range(4):

        @pl.when(jnp.logical_not(self_down & (z == k)))
        def _():
            await_bytes(wd_own, wd_sem.at[0])


def layer(*operands):
    any_spec, vmem = pl.BlockSpec(memory_space=pl.ANY), pl.BlockSpec(memory_space=pltpu.VMEM)
    half = ROWS // 2
    bf = lambda *shape: pltpu.VMEM(shape, BF16)
    fl = lambda *shape: pltpu.VMEM(shape, F32)
    out = lambda kind, *shape: jax.ShapeDtypeStruct(shape, kind)
    copies = (
        16, 16, 2, 6, 3, 3, 2, 2, 4, 4, 3, 4, 2,
        4, 3, 6, 8, 6, 8, 7, 4, 6, 6, 5, 4, 3,
        1, 4, 2, 1, 4, 2, 2, 2, 2, 4, 2, 2,
    )
    return pl.pallas_call(
        layer_kernel,
        out_shape=(
            out(BF16, ROWS, 1024), out(BF16, ROWS, 1024), out(BF16, 8, 32, 768), out(BF16, 8, 32, 256),
            out(BF16, 8, 32, 512), out(BF16, 4, 96, 1024), out(BF16, 2048, 1024), out(F32, 8, 1024),
        ),
        in_specs=[any_spec] * 3 + [vmem] * 6 + [any_spec] * 3,
        out_specs=(any_spec,) * 7 + (vmem,),
        scratch_shapes=[
            bf(2048, 1024), bf(2048, 1024), bf(2048, 1024), bf(4, 4, 64, 512), bf(4, 4, 64, 256), bf(4, 4, 64, 768),
            bf(384, 1024), bf(8, 32, 512), bf(8, 32, 256), bf(8, 32, 768), fl(32, 1, 128), fl(16, 128, 128),
            fl(8, 1024),
            bf(2048, 256), bf(2048, 128), bf(2048, 128), bf(16, 128, 256), bf(4, 128, QROWS), fl(128, 1024),
            fl(1, 1024), fl(4, 1, 1024), bf(ROWS, 1024), fl(ROWS, 1024),
            bf(16, 128, 768), bf(2048, 384), fl(4, 1, 1024), fl(16, 256, 128), fl(16, 128, 128), fl(16, 128, 128),
            fl(ROWS, 1024), fl(8, 1024),
            bf(4, ROWS, 1024), bf(4, ROWS, 1024), bf(6, half, 1024), bf(6, half, 1024), fl(2, half, 1024),
            bf(4, ROWS, 1024), bf(2, ROWS, 1024), bf(4, ROWS, 1024), bf(3, ROWS, 1024),
            bf(4, 256, 768), bf(4, 256, 256), bf(4, 256, 768), bf(4, 256, 256), bf(4, 256, 512),
            bf(256, 768), bf(256, 256), bf(256, 512), fl(8, 8, 1024), fl(8, 1024), fl(4, 8, 1024),
            bf(2, half, 1024), pltpu.VMEM((1, 2048), jnp.int32), pltpu.SMEM((1, 2048), jnp.int32),
            pltpu.SMEM((16,), jnp.int32), pltpu.SMEM((16,), jnp.int32),
        ]
        + [pltpu.SemaphoreType.DMA((count,)) for count in copies],
        compiler_params=pltpu.CompilerParams(collective_id=0, has_side_effects=True, vmem_limit_bytes=VMEM_LIMIT),
        name="layer",
    )(*operands)


def outputs_kernel(
    layer, tok, pf, po, pa, rd, small, o_l, o_t, o_q, o_k, o_v, o_o, o_g, o_u, o_d, o_first, o_second, o_head
):
    me = lax.axis_index("fsdp") * 8 + lax.axis_index("ctx")
    o_l[...] = layer[...]
    o_t[...] = tok[...]
    for k in range(8):
        wide, thin, third = (slice(k * w, k * w + w) for w in (256, 128, 384))
        o_g[:, third] = pf[k, :, 0:384].astype(F32)
        o_u[:, third] = pf[k, :, 384:768].astype(F32)
        o_o[:, wide] = po[k].astype(F32)
        o_q[:, wide] = pa[k, :, 0:256].astype(F32)
        o_k[:, thin] = pa[k, :, 256:384].astype(F32)
        o_v[:, thin] = pa[k, :, 384:512].astype(F32)
    o_d[...] = rd[0].astype(F32) + rd[1].astype(F32) + rd[2].astype(F32) + rd[3].astype(F32)
    turned = pltpu.roll(small[...], (1024 - 32 * me) % 1024, 1)
    o_first[...] = turned[0:1, 0:32]
    o_second[...] = turned[1:2, 0:32]
    turned = pltpu.roll(small[...], (1024 - 8 * me) % 1024, 1)
    o_head[...] = turned[2:3, 0:8]


def outputs(*came):
    vmem = pl.BlockSpec(memory_space=pltpu.VMEM)
    out = lambda kind, *shape: jax.ShapeDtypeStruct(shape, kind)
    return pl.pallas_call(
        outputs_kernel,
        out_shape=(
            out(BF16, ROWS, 1024), out(BF16, ROWS, 1024), out(F32, 32, 2048), out(F32, 32, 1024), out(F32, 32, 1024),
            out(F32, 32, 2048), out(F32, 32, 3072), out(F32, 32, 3072), out(F32, 96, 1024), out(F32, 1, 32),
            out(F32, 1, 32), out(F32, 1, 8),
        ),
        in_specs=[vmem] * 7,
        out_specs=(vmem,) * 12,
        compiler_params=pltpu.CompilerParams(vmem_limit_bytes=VMEM_LIMIT),
        name="outputs",
    )(*came)


def rope_table(length):
    inverse = 1000000.0 ** (-2.0 * np.arange(HEAD_DIM // 2, dtype=np.float64) / HEAD_DIM)
    angles = np.arange(length, dtype=np.float32)[:, None] * inverse.astype(np.float32)[None, :]
    angles = angles.astype(np.float64)
    return np.concatenate([np.cos(angles), np.sin(angles)], axis=1).astype(np.float32)


def per_device_planes(
    tokens, positions, w_query, w_key, w_value, w_output, w_gate, w_up, w_down, first_gain, second_gain, head_gain,
    cotangent,
):
    gains = jnp.concatenate([first_gain, second_gain, head_gain, jnp.zeros((56,), BF16)]).astype(F32)[None]
    table = jnp.asarray(rope_table(2048)).reshape(16, 128, HEAD_DIM)
    layer_out, grad_tokens, pf, po, pa, rd, _, small = layer(
        tokens[0], cotangent[0], positions, w_query, w_key, w_value, w_output.T, w_gate, w_up, w_down, gains, table
    )
    layer_out, grad_tokens, o_q, o_k, o_v, o_o, o_g, o_u, o_d, o_first, o_second, o_head = outputs(
        layer_out, grad_tokens, pf, po, pa, rd, small
    )
    return (
        layer_out[None],
        grad_tokens[None],
        o_q,
        o_k,
        o_v,
        o_o.T,
        o_g,
        o_u,
        o_d,
        o_first[0],
        o_second[0],
        o_head[0],
    )


def solution(mesh):
    planes = mesh.shape["fsdp"] == 4 and mesh.shape["ctx"] == 8
    body = per_device_planes if planes else per_device
    return jax.shard_map(
        body,
        mesh=mesh,
        in_specs=(
            P("fsdp", "ctx", None),
            P("fsdp", None),
            P(("fsdp", "ctx"), None),
            P(("fsdp", "ctx"), None),
            P(("fsdp", "ctx"), None),
            P(None, ("fsdp", "ctx")),
            P(("fsdp", "ctx"), None),
            P(("fsdp", "ctx"), None),
            P(("fsdp", "ctx"), None),
            P(("fsdp", "ctx")),
            P(("fsdp", "ctx")),
            P(("fsdp", "ctx")),
            P("fsdp", "ctx", None),
        ),
        out_specs=(
            P("fsdp", "ctx", None),
            P("fsdp", "ctx", None),
            P(("fsdp", "ctx"), None),
            P(("fsdp", "ctx"), None),
            P(("fsdp", "ctx"), None),
            P(None, ("fsdp", "ctx")),
            P(("fsdp", "ctx"), None),
            P(("fsdp", "ctx"), None),
            P(("fsdp", "ctx"), None),
            P(("fsdp", "ctx")),
            P(("fsdp", "ctx")),
            P(("fsdp", "ctx")),
        ),
        check_vma=False,
    )
```

```python
from functools import partial

import jax
import jax.numpy as jnp
import numpy as np
from jax import lax
from jax.experimental import pallas as pl
from jax.experimental.pallas import tpu as pltpu
from jax.sharding import PartitionSpec as P

MESH = pl.DeviceIdType.MESH

HEADS = 16
KV_HEADS = 8
HEAD_DIM = 128


def normed(operand, gain_in):
    return (
        operand * lax.rsqrt(jnp.mean(operand * operand, axis=-1, keepdims=True) + 1e-06) * gain_in
    )


def rotary(operand, places):
    head_width = operand.shape[-1]
    half_width = head_width // 2
    inverse = 1000000.0 ** (-2.0 * jnp.arange(half_width, dtype=jnp.float32) / head_width)
    angles = places.astype(jnp.float32)[:, None] * inverse[None, :]
    cosine = jnp.concatenate([jnp.cos(angles), jnp.cos(angles)], axis=-1)[:, None, :]
    sine_table = jnp.concatenate([jnp.sin(angles), jnp.sin(angles)], axis=-1)[:, None, :]
    turned = jnp.concatenate([-operand[..., half_width:], operand[..., :half_width]], axis=-1)
    return operand * cosine + turned * sine_table


def head_prep(raw_proj, gain_in, places, head_count):
    row_count = raw_proj.shape[0]
    shaped = raw_proj.reshape(row_count, head_count, HEAD_DIM)
    return rotary(normed(shaped, gain_in), places).reshape(row_count, head_count * HEAD_DIM)


def gated(gate_raw, up_raw):
    return jax.nn.silu(gate_raw) * up_raw


def project(left_side, right_side):
    return jnp.dot(left_side, right_side, preferred_element_type=jnp.float32)


def project_back(left_side, right_side):
    return lax.dot_general(
        left_side, right_side, (((1,), (1,)), ((), ())), preferred_element_type=jnp.float32
    )


def outer_sum(left_side, right_side):
    return lax.dot_general(
        left_side, right_side, (((0,), (0,)), ((), ())), preferred_element_type=jnp.float32
    )


def halves_apart(rows_in, shard_count):
    shape_in = rows_in.shape
    split = rows_in.reshape((shard_count, 2, shape_in[0] // (2 * shard_count)) + shape_in[1:])
    return jnp.swapaxes(split, 0, 1).reshape(shape_in)


def halves_back(rows_in, shard_count):
    shape_in = rows_in.shape
    split = rows_in.reshape((2, shard_count, shape_in[0] // (2 * shard_count)) + shape_in[1:])
    return jnp.swapaxes(split, 0, 1).reshape(shape_in)


def key_layout(key_rows, value_rows, place_all):
    key_count = key_rows.shape[0]
    key_block = min(512, key_count)
    block_count = key_count // key_block
    key_parts = key_rows.reshape(block_count, key_block, KV_HEADS, HEAD_DIM)
    value_parts = value_rows.reshape(block_count, key_block, KV_HEADS, HEAD_DIM)
    place_parts = place_all.reshape(block_count, key_block)
    return (key_parts, value_parts, place_parts)


def attend_forward(queries, key_rows, value_rows, place_here, place_all):
    row_count = queries.shape[0]
    group_size = HEADS // KV_HEADS
    score_scale = HEAD_DIM ** (-0.5)
    grouped = queries.reshape(row_count, KV_HEADS, group_size, HEAD_DIM)
    layout = key_layout(key_rows, value_rows, place_all)
    top_place = jnp.max(place_here)

    def attend_step(state_now, block_item):
        key_part, value_part, place_part = block_item

        def attend_compute(state_in):
            run_max, run_sum, run_out = state_in
            scores = (
                jnp.einsum("qhge,khe->hgqk", grouped, key_part, preferred_element_type=jnp.float32)
                * score_scale
            )
            visible = place_part[None, None, None, :] <= place_here[None, None, :, None]
            scores = jnp.where(visible, scores, -1e30)
            new_max = jnp.maximum(run_max, jnp.max(scores, axis=-1))
            weights = jnp.where(visible, jnp.exp(scores - new_max[..., None]), 0.0)
            rescale = jnp.exp(run_max - new_max)
            run_sum = run_sum * rescale + jnp.sum(weights, axis=-1)
            mixed = jnp.einsum(
                "hgqk,khe->hgqe",
                weights.astype(jnp.bfloat16),
                value_part,
                preferred_element_type=jnp.float32,
            )
            run_out = run_out * rescale[..., None] + mixed
            return (new_max, run_sum, run_out)

        state_next = lax.cond(
            jnp.min(place_part) > top_place, lambda state_in: state_in, attend_compute, state_now
        )
        return (state_next, None)

    start_state = (
        jnp.full((KV_HEADS, group_size, row_count), -1e30, jnp.float32),
        jnp.zeros((KV_HEADS, group_size, row_count), jnp.float32),
        jnp.zeros((KV_HEADS, group_size, row_count, HEAD_DIM), jnp.float32),
    )
    (run_max, run_sum, run_out), _ = lax.scan(attend_step, start_state, layout)
    attention = (
        (run_out / run_sum[..., None]).transpose(2, 0, 1, 3).reshape(row_count, HEADS * HEAD_DIM)
    )
    return (attention, run_max + jnp.log(run_sum))


def row_dot_table(grad_attn, attention):
    row_count = grad_attn.shape[0]
    group_size = HEADS // KV_HEADS
    grad_grouped = grad_attn.reshape(row_count, KV_HEADS, group_size, HEAD_DIM)
    return jnp.sum(
        grad_grouped.astype(jnp.float32)
        * attention.reshape(row_count, KV_HEADS, group_size, HEAD_DIM),
        axis=-1,
    ).transpose(1, 2, 0)


def attend_backward(
    queries, key_rows, value_rows, grad_attn, row_dots, log_total, place_here, place_all
):
    row_count = queries.shape[0]
    key_count = key_rows.shape[0]
    group_size = HEADS // KV_HEADS
    score_scale = HEAD_DIM ** (-0.5)
    grouped = queries.reshape(row_count, KV_HEADS, group_size, HEAD_DIM)
    grad_grouped = grad_attn.reshape(row_count, KV_HEADS, group_size, HEAD_DIM)
    layout = key_layout(key_rows, value_rows, place_all)
    top_place = jnp.max(place_here)

    def back_step(grad_query, block_item):
        key_part, value_part, place_part = block_item
        key_block = key_part.shape[0]

        def back_compute(grad_in):
            scores = (
                jnp.einsum("qhge,khe->hgqk", grouped, key_part, preferred_element_type=jnp.float32)
                * score_scale
            )
            visible = place_part[None, None, None, :] <= place_here[None, None, :, None]
            weights = jnp.where(
                visible, jnp.exp(jnp.where(visible, scores, -1e30) - log_total[..., None]), 0.0
            )
            grad_probs = jnp.einsum(
                "qhge,khe->hgqk", grad_grouped, value_part, preferred_element_type=jnp.float32
            )
            grad_scores = (weights * (grad_probs - row_dots[..., None])).astype(jnp.bfloat16)
            grad_out = (
                grad_in
                + jnp.einsum(
                    "hgqk,khe->qhge", grad_scores, key_part, preferred_element_type=jnp.float32
                )
                * score_scale
            )
            grad_keys = (
                jnp.einsum(
                    "hgqk,qhge->khe", grad_scores, grouped, preferred_element_type=jnp.float32
                )
                * score_scale
            )
            grad_values = jnp.einsum(
                "hgqk,qhge->khe",
                weights.astype(jnp.bfloat16),
                grad_grouped,
                preferred_element_type=jnp.float32,
            )
            return (
                grad_out,
                (
                    grad_keys.reshape(key_block, KV_HEADS * HEAD_DIM),
                    grad_values.reshape(key_block, KV_HEADS * HEAD_DIM),
                ),
            )

        def skipped(grad_in):
            empty_terms = jnp.zeros((key_block, KV_HEADS * HEAD_DIM), jnp.float32)
            return (grad_in, (empty_terms, empty_terms))

        return lax.cond(jnp.min(place_part) > top_place, skipped, back_compute, grad_query)

    start_grad = jnp.zeros((row_count, KV_HEADS, group_size, HEAD_DIM), jnp.float32)
    grad_query, key_terms = lax.scan(back_step, start_grad, layout)
    grad_query = grad_query.reshape(row_count, HEADS * HEAD_DIM)
    return (
        grad_query,
        key_terms[0].reshape(key_count, KV_HEADS * HEAD_DIM),
        key_terms[1].reshape(key_count, KV_HEADS * HEAD_DIM),
    )


def per_device(
    tokens,
    positions,
    w_query,
    w_key,
    w_value,
    w_output,
    w_gate,
    w_up,
    w_down,
    first_gain,
    second_gain,
    head_gain,
    cotangent,
):
    inputs = tokens[0].astype(jnp.float32)
    row_count = inputs.shape[0]
    shard_count = lax.axis_size("ctx")
    place_stored = positions[0]
    place_here = lax.dynamic_slice_in_dim(
        place_stored, lax.axis_index("ctx") * row_count, row_count
    )
    place_all = halves_apart(place_stored, shard_count)
    query_full, key_full, value_full, output_full, gain_first, gain_head = (
        lax.all_gather(w_query, ("fsdp", "ctx"), axis=0, tiled=True),
        lax.all_gather(w_key, ("fsdp", "ctx"), axis=0, tiled=True),
        lax.all_gather(w_value, ("fsdp", "ctx"), axis=0, tiled=True),
        lax.all_gather(w_output, ("fsdp", "ctx"), axis=1, tiled=True),
        lax.all_gather(first_gain, ("fsdp", "ctx"), axis=0, tiled=True),
        lax.all_gather(head_gain, ("fsdp", "ctx"), axis=0, tiled=True),
    )
    gain_one = gain_first.astype(jnp.float32)
    gain_query = gain_head[:HEAD_DIM].astype(jnp.float32)
    gain_key = gain_head[HEAD_DIM:].astype(jnp.float32)
    hidden_one = normed(inputs, gain_one).astype(jnp.bfloat16)
    query_raw = project(hidden_one, query_full)
    key_raw = project(hidden_one, key_full)
    value_rows = project(hidden_one, value_full).astype(jnp.bfloat16)
    query_prep = partial(head_prep, places=place_here, head_count=HEADS)
    key_prep = partial(head_prep, places=place_here, head_count=KV_HEADS)
    queries, query_back = jax.vjp(query_prep, query_raw, gain_query)
    key_local, key_back = jax.vjp(key_prep, key_raw, gain_key)
    queries = queries.astype(jnp.bfloat16)
    key_local = key_local.astype(jnp.bfloat16)
    key_stored, value_stored = (
        lax.all_gather(key_local, "ctx", axis=0, tiled=True),
        lax.all_gather(value_rows, "ctx", axis=0, tiled=True),
    )
    key_all = halves_apart(key_stored, shard_count)
    value_all = halves_apart(value_stored, shard_count)
    attention, log_total = attend_forward(queries, key_all, value_all, place_here, place_all)
    attn_low = attention.astype(jnp.bfloat16)
    middle = inputs + project(attn_low, output_full)
    gate_full, up_full, down_full, gain_second = (
        lax.all_gather(w_gate, ("fsdp", "ctx"), axis=0, tiled=True),
        lax.all_gather(w_up, ("fsdp", "ctx"), axis=0, tiled=True),
        lax.all_gather(w_down, ("fsdp", "ctx"), axis=0, tiled=True),
        lax.all_gather(second_gain, ("fsdp", "ctx"), axis=0, tiled=True),
    )
    gain_two = gain_second.astype(jnp.float32)
    hidden_two = normed(middle, gain_two).astype(jnp.bfloat16)
    gate_raw = project(hidden_two, gate_full)
    up_raw = project(hidden_two, up_full)
    activated, gated_back = jax.vjp(gated, gate_raw, up_raw)
    act_low = activated.astype(jnp.bfloat16)
    layer_out = (middle + project(act_low, down_full)).astype(jnp.bfloat16)
    grad_out = cotangent[0].astype(jnp.float32)
    gate_full, up_full, down_full, gain_second = (
        lax.all_gather(w_gate, ("fsdp", "ctx"), axis=0, tiled=True),
        lax.all_gather(w_up, ("fsdp", "ctx"), axis=0, tiled=True),
        lax.all_gather(w_down, ("fsdp", "ctx"), axis=0, tiled=True),
        lax.all_gather(second_gain, ("fsdp", "ctx"), axis=0, tiled=True),
    )
    gain_two = gain_second.astype(jnp.float32)
    out_low = grad_out.astype(jnp.bfloat16)
    down_terms = outer_sum(act_low, out_low)
    grad_act = project_back(out_low, down_full)
    grad_gate_raw, grad_up_raw = gated_back(grad_act)
    gate_low = grad_gate_raw.astype(jnp.bfloat16)
    up_low = grad_up_raw.astype(jnp.bfloat16)
    gate_terms = outer_sum(hidden_two, gate_low)
    up_terms = outer_sum(hidden_two, up_low)
    grad_hidden_two = project_back(gate_low, gate_full) + project_back(up_low, up_full)
    _, norm_two_back = jax.vjp(normed, middle, gain_two)
    middle_part, gain_two_terms = norm_two_back(grad_hidden_two)
    grad_gate, grad_up, grad_down, grad_second = (
        lax.psum_scatter(gate_terms, ("fsdp", "ctx"), scatter_dimension=0, tiled=True),
        lax.psum_scatter(up_terms, ("fsdp", "ctx"), scatter_dimension=0, tiled=True),
        lax.psum_scatter(down_terms, ("fsdp", "ctx"), scatter_dimension=0, tiled=True),
        lax.psum_scatter(gain_two_terms, ("fsdp", "ctx"), scatter_dimension=0, tiled=True),
    )
    grad_middle = grad_out + middle_part
    query_full, key_full, value_full, output_full, gain_first, gain_head = (
        lax.all_gather(w_query, ("fsdp", "ctx"), axis=0, tiled=True),
        lax.all_gather(w_key, ("fsdp", "ctx"), axis=0, tiled=True),
        lax.all_gather(w_value, ("fsdp", "ctx"), axis=0, tiled=True),
        lax.all_gather(w_output, ("fsdp", "ctx"), axis=1, tiled=True),
        lax.all_gather(first_gain, ("fsdp", "ctx"), axis=0, tiled=True),
        lax.all_gather(head_gain, ("fsdp", "ctx"), axis=0, tiled=True),
    )
    gain_one = gain_first.astype(jnp.float32)
    middle_low = grad_middle.astype(jnp.bfloat16)
    output_terms = outer_sum(attn_low, middle_low)
    grad_attn = project_back(middle_low, output_full).astype(jnp.bfloat16)
    row_dots = row_dot_table(grad_attn, attention)
    grad_queries, key_terms, value_terms = attend_backward(
        queries, key_all, value_all, grad_attn, row_dots, log_total, place_here, place_all
    )
    key_terms = halves_back(key_terms, shard_count)
    value_terms = halves_back(value_terms, shard_count)
    grad_key_local, grad_value_local = (
        lax.psum_scatter(
            key_terms.astype(jnp.bfloat16), "ctx", scatter_dimension=0, tiled=True
        ).astype(jnp.float32),
        lax.psum_scatter(
            value_terms.astype(jnp.bfloat16), "ctx", scatter_dimension=0, tiled=True
        ).astype(jnp.float32),
    )
    grad_query_raw, gain_query_terms = query_back(grad_queries)
    grad_key_raw, gain_key_terms = key_back(grad_key_local)
    query_low = grad_query_raw.astype(jnp.bfloat16)
    keyraw_low = grad_key_raw.astype(jnp.bfloat16)
    value_low = grad_value_local.astype(jnp.bfloat16)
    query_terms = outer_sum(hidden_one, query_low)
    key_weight_terms = outer_sum(hidden_one, keyraw_low)
    value_weight_terms = outer_sum(hidden_one, value_low)
    grad_hidden_one = (
        project_back(query_low, query_full)
        + project_back(keyraw_low, key_full)
        + project_back(value_low, value_full)
    )
    _, norm_one_back = jax.vjp(normed, inputs, gain_one)
    input_part, gain_one_terms = norm_one_back(grad_hidden_one)
    head_terms = jnp.concatenate([gain_query_terms, gain_key_terms])
    grad_query, grad_key, grad_value, grad_output, grad_first, grad_head = (
        lax.psum_scatter(query_terms, ("fsdp", "ctx"), scatter_dimension=0, tiled=True),
        lax.psum_scatter(key_weight_terms, ("fsdp", "ctx"), scatter_dimension=0, tiled=True),
        lax.psum_scatter(value_weight_terms, ("fsdp", "ctx"), scatter_dimension=0, tiled=True),
        lax.psum_scatter(output_terms, ("fsdp", "ctx"), scatter_dimension=1, tiled=True),
        lax.psum_scatter(gain_one_terms, ("fsdp", "ctx"), scatter_dimension=0, tiled=True),
        lax.psum_scatter(head_terms, ("fsdp", "ctx"), scatter_dimension=0, tiled=True),
    )
    grad_tokens = (grad_middle + input_part).astype(jnp.bfloat16)
    return (
        layer_out[None],
        grad_tokens[None],
        grad_query,
        grad_key,
        grad_value,
        grad_output,
        grad_gate,
        grad_up,
        grad_down,
        grad_first,
        grad_second,
        grad_head,
    )


ROWS = 256
QROWS = 512
EPS = 1e-06
LOG2E = 1.4426950408889634
SCALE = HEAD_DIM**-0.5
VMEM_LIMIT = 62 * 1024 * 1024
BF16 = jnp.bfloat16
F32 = jnp.float32


def dot_nn(a, b):
    return lax.dot_general(a, b, (((1,), (0,)), ((), ())), preferred_element_type=F32)


def dot_nt(a, b):
    return lax.dot_general(a, b, (((1,), (1,)), ((), ())), preferred_element_type=F32)


def dot_tn(a, b):
    return lax.dot_general(a, b, (((0,), (0,)), ((), ())), preferred_element_type=F32)


def whereabouts():
    f, c = lax.axis_index("fsdp"), lax.axis_index("ctx")
    return f, c, f // 2, f % 2, c // 2, c % 2


def plane_of(s):
    return (s % 2) * 2 + s // 2


def remote(src, dst, send, recv, fsdp, ctx):
    return pltpu.make_async_remote_copy(
        src_ref=src, dst_ref=dst, send_sem=send, recv_sem=recv, device_id=(fsdp, ctx), device_id_type=MESH
    )


def await_bytes(ref, sem):
    pltpu.make_async_copy(ref, ref, sem).wait()


def greet_all():
    f, c, y, core, z, x = whereabouts()
    barrier = pltpu.get_barrier_semaphore()
    me = f * 8 + c

    def greet(j, carry):
        dev = (me + j) % 32
        pl.semaphore_signal(barrier, inc=1, device_id=(dev // 8, dev % 8), device_id_type=MESH)
        return carry

    lax.fori_loop(1, 32, greet, 0)
    pl.semaphore_wait(barrier, 31)


def chip_peer(r):
    f, c, y, core, z, x = whereabouts()
    y2 = 1 - y if r & 2 else y
    x2 = 1 - x if r & 1 else x
    return y2, x2


def chunk_of(r, core):
    y2, x2 = chip_peer(r)
    return (core * 2 + y2) * 2 + x2


def rows_of(ref, chunk):
    return ref.at[pl.ds(pl.multiple_of(chunk * ROWS, ROWS), ROWS)]


def head_norm_rope(raw, gain, cos, sin):
    r = lax.rsqrt(jnp.mean(raw * raw, axis=-1, keepdims=True) + EPS)
    u = raw * r * gain
    return u * cos + pltpu.roll(u, HEAD_DIM // 2, 1) * sin


def norm_rows(values, gain):
    v = values.astype(F32)
    return v * lax.rsqrt(jnp.mean(v * v, axis=-1, keepdims=True) + EPS) * gain


def norm_back(values, gain, dy):
    r = lax.rsqrt(jnp.mean(values * values, axis=-1, keepdims=True) + EPS)
    cdy = gain * dy
    back = r * cdy - values * (r * r * r) * jnp.mean(cdy * values, axis=-1, keepdims=True)
    return back, dy * values * r


def unturn(d, cos, sin):
    return d * cos - pltpu.roll(d, HEAD_DIM // 2, 1) * sin


def order_z(n, z):
    upper = z // 2
    low = (z + upper) % 2
    base = (low, 1 - low, 2, 3)[n]
    return base + upper * (3 - 2 * base)


def split_sum(partial, core_out, from_core, out_buf, in_buf, keep, send, core_recv, recv):
    f, c, y, core, z, x = whereabouts()
    half = ROWS // 2

    def to_core(k, carry):
        r = 3 - k
        y2, x2 = (y + r // 2) % 2, (x + r % 2) % 2
        chunk = ((1 - core) * 2 + y2) * 2 + x2
        core_out[r] = partial(chunk).astype(BF16)
        remote(core_out.at[r], from_core.at[r], send.at[6], core_recv.at[r], y * 2 + 1 - core, c).start()
        return carry

    lax.fori_loop(0, 4, to_core, 0)

    def both(r):
        await_bytes(from_core.at[r], core_recv.at[r])
        return partial(chunk_of(r, core)) + from_core[r].astype(F32)

    def over_x(k):
        remote(out_buf.at[k], in_buf.at[k], send.at[k], recv.at[k], f, z * 2 + 1 - x).start()

    def over_y(k):
        remote(out_buf.at[k], in_buf.at[k], send.at[k], recv.at[k], (1 - y) * 2 + core, c).start()

    total = both(3)
    out_buf[0] = total[:half].astype(BF16)
    over_x(0)
    out_buf[1] = total[half:].astype(BF16)
    over_y(1)
    total = both(1)
    out_buf[2] = total[:half].astype(BF16)
    over_x(2)
    keep[0] = total[half:]
    total = both(2)
    out_buf[3] = total[half:].astype(BF16)
    over_y(3)
    keep[1] = total[:half]
    await_bytes(in_buf.at[0], recv.at[0])
    out_buf[5] = (keep[1] + in_buf[0].astype(F32)).astype(BF16)
    over_y(5)
    await_bytes(in_buf.at[1], recv.at[1])
    out_buf[4] = (keep[0] + in_buf[1].astype(F32)).astype(BF16)
    over_x(4)
    total = both(0)
    keep[0] = total[:half]
    keep[1] = total[half:]


def split_sum_end(in_buf, keep, recv):
    for k in (2, 3, 4, 5):
        await_bytes(in_buf.at[k], recv.at[k])
    return (
        keep[0] + in_buf[2].astype(F32) + in_buf[5].astype(F32),
        keep[1] + in_buf[3].astype(F32) + in_buf[4].astype(F32),
    )


def split_sum_sent(from_core, out_buf, send):
    await_bytes(from_core, send.at[6])
    for k in range(6):
        await_bytes(out_buf.at[k], send.at[k])


SPLIT_SUM_SCRATCH = [
    pltpu.VMEM((4, ROWS, 1024), BF16),
    pltpu.VMEM((4, ROWS, 1024), BF16),
    pltpu.VMEM((6, ROWS // 2, 1024), BF16),
    pltpu.VMEM((6, ROWS // 2, 1024), BF16),
    pltpu.VMEM((2, ROWS // 2, 1024), F32),
    pltpu.SemaphoreType.DMA((7,)),
    pltpu.SemaphoreType.DMA((4,)),
    pltpu.SemaphoreType.DMA((6,)),
]


def rows_in_order(pos_s, ids_s, perm_s):
    ids = [lax.div(pos_s[0, j * 128], jnp.int32(128)) for j in range(16)]
    for b in range(16):
        ids_s[b] = ids[b]
        place = jnp.int32(0)
        for j in range(16):
            place = place + j * (1 - lax.min(lax.abs(ids[j] - b), jnp.int32(1)))
        perm_s[b] = lax.min(place, jnp.int32(15))


def turns(table):
    cos, sin = table[:, 0 : HEAD_DIM // 2], table[:, HEAD_DIM // 2 :]
    return jnp.concatenate([cos, cos], axis=1), jnp.concatenate([-sin, sin], axis=1)


def two_blocks(ref, chunk, cols):
    return ref[pl.ds(chunk * 2, 2), :, cols].reshape(ROWS, -1)


def put_two(ref, chunk, cols, value):
    for k in range(2):
        ref[chunk * 2 + k, :, cols] = value[k * 128 : k * 128 + 128]


def gain_rows(gains_all):
    every = gains_all[...].reshape(32, 128)
    lane = lax.broadcasted_iota(jnp.int32, (32, 128), 1)

    def place(first, count, per_row):
        kept = jnp.where((lane >= first) & (lane < first + count), every, 0.0)
        turned = [pltpu.roll(kept, (count * seg - first) % 128, 1) for seg in range(per_row)]
        return [
            sum(turned[seg][m * per_row + seg : m * per_row + seg + 1] for seg in range(per_row))
            for m in range(32 // per_row)
        ]

    one, two = place(0, 32, 4), place(32, 32, 4)
    query, key = place(64, 8, 16)
    return jnp.concatenate(one, axis=1), jnp.concatenate(two, axis=1), query, key


PIECES = [
    ("o", 0), ("o", 1), ("x", 0), ("y", 0), ("o", 2), ("x", 1), ("y", 1), ("o", 3),
    ("x", 2), ("y", 2), ("d", 0), ("x", 3), ("y", 3), ("d", 1), ("d", 2), ("d", 3),
]


def layer_kernel(
    tok, cot, pos, wq, wk, wv, wo, wg, wu, wd_own, gains, table_h,
    layer_out, grad_tokens, pf, po, pa, rd, h_out, small_out,
    xx, hd, g_s, w1, w2, w3, wd, pack1, pack2, pack3, gains_all, table_s, gain_s,
    q_s, k_s, v_s, o_s, vt, acc, total, lse_s, x_keep, mid,
    mix_s, act_s, delta_s, dqt_s, dk_s, dv_s, dmid, small,
    core_out, from_core, out_buf, in_buf, keep, lpart, core_out2, from_core2, in_buf2,
    gf, go, ga, rdz, rf, ro, ra, sf, so, sa, s_in, sbuf, p_in, stage, pos_v, pos_s, ids_s, perm_s,
    x_recv, g_recv, stage_recv, hop_send, x_send, g_send, pos_sem, gain_sem, w1_sem, w2_sem, w3_sem, w3_came, wd_sem,
    load, ag_send, ag_recv, ag_core, ag_recv2, ag_core2, send, core_recv, recv, recv_d, send2, core_recv2, recv2,
    home_send, f_sem, f_came, o_sem, a_sem, a_came, dz_sem, dz_came, d_sem, fp_sem, op_sem, ap_sem, out_sem, s_sem, p_sem,
):
    f, c, y, core, z, x = whereabouts()
    me, t, own = f * 8 + c, f * 2 + x, (core * 2 + y) * 2 + x
    half = ROWS // 2
    upper = z // 2
    edge, inner, other_inner = 3 * upper, 1 + upper, 2 - upper
    table = pltpu.make_async_copy(table_h, table_s, load.at[0])
    table.start()
    for k in range(8):
        pack1[k, :, 0:256] = wq[:, k * 256 : k * 256 + 256]
        pack1[k, :, 256:384] = wk[:, k * 128 : k * 128 + 128]
        pack1[k, :, 384:512] = wv[:, k * 128 : k * 128 + 128]
    greet_all()

    home = plane_of(f)
    seq = plane_of(z)
    ys, cs = seq // 2, seq % 2
    side = (y + ys) % 2
    other_y = (1 - y) * 2 + core
    other_core = y * 2 + 1 - core
    other_x = z * 2 + 1 - x

    def piece(buf, chunk, part):
        return buf.at[pl.ds(pl.multiple_of(chunk * ROWS + part * half, half), half)]

    def hop_beyond(src, buf, recv_, k):
        high = src.at[pl.ds(half, half)]

        @pl.when(home != z)
        def _():
            remote(high, stage.at[k], hop_send.at[3 * k + 1], stage_recv.at[k], other_y, c).start()

        @pl.when(home == z)
        def _():
            remote(high, piece(buf, c, 1), hop_send.at[3 * k + 1], recv_.at[2 * c + 1], other_y, c).start()

    def hop(src, buf, recv_, k):
        low = src.at[pl.ds(0, half)]

        @pl.when(home != z)
        def _():
            remote(low, piece(buf, c, 0), hop_send.at[3 * k], recv_.at[2 * c], f, home * 2 + x).start()

        @pl.when(home == z)
        def _():
            pltpu.make_async_copy(low, piece(buf, c, 0), recv_.at[2 * c]).start()

    beyond = plane_of(other_y)

    def hop_on(buf, recv_, k):
        @pl.when(beyond != z)
        def _():
            await_bytes(stage.at[k], stage_recv.at[k])
            remote(stage.at[k], piece(buf, c, 1), hop_send.at[3 * k + 2], recv_.at[2 * c + 1], f, beyond * 2 + x).start()

    def hop_done(k):
        @pl.when(home != z)
        def _():
            await_bytes(stage.at[k], hop_send.at[3 * k])

        await_bytes(stage.at[k], hop_send.at[3 * k + 1])

        @pl.when(beyond != z)
        def _():
            await_bytes(stage.at[k], hop_send.at[3 * k + 2])

    def whereof(kind, n):
        chunk = order_z(n, z) * 2 + (x if kind in "oy" else 1 - x)
        return chunk, (side if kind in "ox" else 1 - side)

    def relay(buf, recv_, send_, kind, n):
        chunk, part = whereof(kind, n)
        rows = piece(buf, chunk, part)
        sem = recv_.at[2 * chunk + part]

        @pl.when(core == cs)
        def _():
            await_bytes(rows, sem)
            if kind == "o" or kind == "y" and n % 2 == 1:
                remote(rows, rows, send_.at[1], sem, f, other_x).start()
            if kind == "o" or kind == "x" and n % 2 == 0:
                remote(rows, rows, send_.at[2], sem, other_y, c).start()
            remote(rows, rows, send_.at[0], sem, other_core, c).start()

    def relay_wait(buf, recv_, kind, n):
        chunk, part = whereof(kind, n)

        @pl.when(core != cs)
        def _():
            await_bytes(piece(buf, chunk, part), recv_.at[2 * chunk + part])

    def relay_done(buf, send_):
        @pl.when(core == cs)
        def _():
            await_bytes(buf, send_.at[0])
            await_bytes(buf.at[pl.ds(0, 6 * half)], send_.at[1])
            await_bytes(buf.at[pl.ds(0, 6 * half)], send_.at[2])

    def my_rows(w):
        return w.at[f, z, pl.ds(pl.multiple_of(x * 32, 32), 32)]

    def weights_in_plane(pack, w, sem):
        pltpu.make_async_copy(pack.at[t], my_rows(w), sem.at[1]).start()
        for j in range(1, 8):
            t2 = (t + j) % 8
            remote(pack.at[t2], my_rows(w), sem.at[0], sem.at[1], t2 // 2, z * 2 + t2 % 2).start()

    def weights_across(w, sem):
        await_bytes(w.at[:, z], sem.at[1])
        for j in (1, 3, 2):
            remote(w.at[:, z], w.at[:, z], sem.at[2], sem.at[3], f, ((z + j) % 4) * 2 + x).start()

    def weights_near(w, sem, came):
        await_bytes(w.at[:, z], sem.at[1])
        for to_z in (inner + edge - z, other_inner):
            remote(w.at[:, z], w.at[:, z], sem.at[2], came.at[z], f, to_z * 2 + x).start()

    def weights_relay(w, sem, came):
        @pl.when(z == inner)
        def _():
            for from_z in (other_inner, 3 - edge):
                await_bytes(w.at[:, from_z], came.at[from_z])
                remote(w.at[:, from_z], w.at[:, from_z], sem.at[2], came.at[from_z], f, edge * 2 + x).start()

    def weights_done(w, came):
        @pl.when(z == inner)
        def _():
            await_bytes(w.at[:, edge], came.at[edge])

        @pl.when(z == edge)
        def _():
            for from_z in (inner, other_inner, 3 - edge):
                await_bytes(w.at[:, from_z], came.at[from_z])

    def weights_sent(w, sem):
        await_bytes(w.at[:, pl.ds(0, 2)], sem.at[2])

        @pl.when(z == inner)
        def _():
            await_bytes(w.at[:, pl.ds(0, 2)], sem.at[2])

    hop_beyond(tok, xx, x_recv, 0)
    hop(tok, xx, x_recv, 0)
    weights_in_plane(pack1, w1, w1_sem)

    @pl.when(f == seq)
    def _():
        pltpu.make_async_copy(pos, pos_v, pos_sem.at[1]).start()
        for j in range(1, 4):
            remote(pos, pos_v, pos_sem.at[0], pos_sem.at[1], (f + j) % 4, c).start()

    pltpu.make_async_copy(gains, gains_all.at[me], gain_sem.at[1]).start()

    def send_gains(j, carry):
        dev = (me + j) % 32
        remote(gains, gains_all.at[me], gain_sem.at[0], gain_sem.at[1], dev // 8, dev % 8).start()
        return carry

    lax.fori_loop(1, 32, send_gains, 0)
    relay(xx, x_recv, x_send, "o", 0)
    hop_on(xx, x_recv, 0)
    weights_across(w1, w1_sem)
    hop_beyond(cot, g_s, g_recv, 1)
    for k in range(8):
        pack2[k] = wo[:, k * 256 : k * 256 + 256]
        pack3[k, :, 0:384] = wg[:, k * 384 : k * 384 + 384]
        pack3[k, :, 384:768] = wu[:, k * 384 : k * 384 + 384]
    await_bytes(gains_all, gain_sem.at[1])
    one, two, gain_q, gain_k = gain_rows(gains_all)
    gain_s[...] = jnp.zeros_like(gain_s)
    gain_s[0:1, :] = one
    gain_s[1:2, :] = two
    gain_s[2:3, 0:128] = gain_q
    gain_s[3:4, 0:128] = gain_k
    await_bytes(pos_v, pos_sem.at[1])
    pos_copy = pltpu.make_async_copy(pos_v, pos_s, load.at[2])
    pos_copy.start()
    pos_copy.wait()
    rows_in_order(pos_s, ids_s, perm_s)

    def norm_piece(kind, n):
        chunk, part = whereof(kind, n)
        rows = pl.ds(pl.multiple_of(chunk * ROWS + part * half, half), half)
        hd[rows, :] = norm_rows(xx[rows, :], gain_s[0:1, :]).astype(BF16)

    for at, (kind, n) in enumerate(PIECES):
        if at:
            relay(xx, x_recv, x_send, kind, n)
        relay_wait(xx, x_recv, kind, n)
        norm_piece(kind, n)
        if at == 4:
            weights_in_plane(pack2, w2, w2_sem)
        if at == 8:
            weights_in_plane(pack3, w3, w3_sem)
        if at == 12:
            hop(cot, g_s, g_recv, 1)
            hop_on(g_s, g_recv, 1)
    h_copy = pltpu.make_async_copy(hd, h_out, load.at[1])
    h_copy.start()
    x_keep[...] = xx[pl.ds(pl.multiple_of(own * ROWS, ROWS), ROWS), :]

    t_down = me // 4
    down_rows = wd.at[pl.ds(pl.multiple_of((me % 4) * 96, 32), 96)]
    self_down = t_down == t
    table.wait()
    await_bytes(w1.at[pl.ds(0, 3)], w1_sem.at[3])

    def project(ch, carry):
        rows = pl.ds(pl.multiple_of(ch * ROWS, ROWS), ROWS)
        raw = dot_nn(hd[rows, :], w1[...].reshape(1024, 512))
        cos, sin = turns(jnp.concatenate([table_s[ids_s[ch * 2 + k]] for k in range(2)], axis=0))
        gq, gk = gain_s[2:3, 0:128], gain_s[3:4, 0:128]
        for k in range(2):
            cols = slice(k * 128, k * 128 + 128)
            put_two(mix_s, ch, cols, head_norm_rope(raw[:, cols], gq, cos, sin).astype(BF16))
        put_two(mix_s, ch, slice(256, 384), head_norm_rope(raw[:, 256:384], gk, cos, sin).astype(BF16))
        put_two(mix_s, ch, slice(384, 512), raw[:, 384:512].astype(BF16))
        return carry

    lax.fori_loop(0, 8, project, 0)
    weights_across(w2, w2_sem)
    weights_near(w3, w3_sem, w3_came)

    def arrange(b, carry):
        for k in range(4):
            rows = pl.ds(pl.multiple_of(b * QROWS + k * 128, 128), 128)
            stored = perm_s[b * 4 + k]
            q_s[rows, :] = mix_s[stored, :, 0:256]
            k_s[rows, :] = mix_s[stored, :, 256:384]
            v_s[rows, :] = mix_s[stored, :, 384:512]
        vt[b] = v_s[pl.ds(pl.multiple_of(b * QROWS, QROWS), QROWS), :].T
        return carry

    lax.fori_loop(0, 4, arrange, 0)
    def query_tile(qt):
        def step(kt, diagonal):
            kb = k_s[pl.ds(pl.multiple_of(kt * QROWS, QROWS), QROWS), :]
            vb = vt[kt]
            for g in range(4):
                head, part = g // 2, g % 2
                qb = q_s[pl.ds(qt * QROWS + part * 256, 256), head * 128 : head * 128 + 128]
                depth = 256 * (part + 1) if diagonal else QROWS
                s = dot_nt(kb[:depth], qb)
                p = jnp.exp2(s * (SCALE * LOG2E))
                if diagonal:
                    ki = lax.broadcasted_iota(jnp.int32, (depth, 256), 0)
                    qi = lax.broadcasted_iota(jnp.int32, (depth, 256), 1) + part * 256
                    p = jnp.where(ki <= qi, p, 0.0)
                cols = slice(g * 256, g * 256 + 256)
                total[:, cols] += jnp.sum(p, axis=0, keepdims=True)
                acc[:, cols] += dot_nn(vb[:, :depth], p.astype(BF16))

        total[...] = jnp.zeros_like(total)
        acc[...] = jnp.zeros_like(acc)

        def off(kt, inner):
            step(kt, False)
            return inner

        lax.fori_loop(0, qt, off, 0)
        step(qt, True)
        sums = total[...]
        lse_s[qt] = jnp.log2(sums)
        out = acc[...] * (1.0 / sums)
        for g in range(4):
            head, part = g // 2, g % 2
            value = out[:, g * 256 : g * 256 + 256].T.astype(BF16)
            put_two(o_s, qt * 2 + part, slice(head * 128, head * 128 + 128), value)

    for qt in range(4):
        query_tile(qt)
        if qt == 1:
            for n in range(4):
                relay(g_s, g_recv, g_send, "o", n)
    for k in range(4):
        here = self_down & (z == k)

        @pl.when(here)
        def _():
            pltpu.make_async_copy(wd_own, down_rows, wd_sem.at[1]).start()

        @pl.when(jnp.logical_not(here))
        def _():
            remote(wd_own, down_rows, wd_sem.at[0], wd_sem.at[1], t_down // 2, k * 2 + t_down % 2).start()

    await_bytes(w2.at[pl.ds(0, 3)], w2_sem.at[3])
    relay_done(xx, x_send)
    h_copy.wait()

    def attention_term(chunk):
        rows = jnp.concatenate([o_s[ids_s[chunk * 2 + k]] for k in range(2)], axis=0)
        return dot_nt(rows, w2[...].reshape(1024, 256))

    split_sum(attention_term, core_out, from_core, out_buf, in_buf, keep, send, core_recv, recv)
    for n in range(4):
        relay(g_s, g_recv, g_send, "x", n)
        relay(g_s, g_recv, g_send, "y", n)
    weights_relay(w3, w3_sem, w3_came)
    low, high = split_sum_end(in_buf, keep, recv)
    gain_one, gain_two = gain_s[0:1, :], gain_s[1:2, :]
    mid[0:half, :] = x_keep[0:half, :].astype(F32) + low
    mid[half:ROWS, :] = x_keep[half:ROWS, :].astype(F32) + high
    xx[pl.ds(pl.multiple_of(own * ROWS, ROWS), ROWS), :] = norm_rows(mid[...], gain_two).astype(BF16)

    def gather_start(every, sem, core_sem):
        for part in (0, 1):
            a, b = piece(every, own, part), piece(every, own, 1 - part)
            remote(a, a, ag_send.at[0], sem.at[part], f, z * 2 + 1 - x).start()
            remote(b, b, ag_send.at[1], sem.at[2 + 1 - part], (1 - y) * 2 + core, c).start()
        for part in (0, 1):
            a = piece(every, own, part)
            remote(a, a, ag_send.at[2], core_sem.at[part], y * 2 + 1 - core, c).start()

    def gather_step(every, sem, core_sem, r, part):
        a = piece(every, chunk_of(r, core), part)
        k = (r - 1) * 2 + part
        await_bytes(a, sem.at[k])
        if r == 1 and part == 0:
            remote(a, a, ag_send.at[1], sem.at[4], (1 - y) * 2 + core, c).start()
        if r == 2 and part == 1:
            remote(a, a, ag_send.at[0], sem.at[5], f, z * 2 + 1 - x).start()
        remote(a, a, ag_send.at[2], core_sem.at[2 * r + part], y * 2 + 1 - core, c).start()

    def gather_core(every, core_sem, r):
        for part in (0, 1):
            await_bytes(piece(every, chunk_of(r, 1 - core), part), core_sem.at[2 * r + part])

    def gather_sent(every):
        await_bytes(every.at[pl.ds(0, 3 * half)], ag_send.at[0])
        await_bytes(every.at[pl.ds(0, 3 * half)], ag_send.at[1])
        await_bytes(every.at[pl.ds(0, 8 * half)], ag_send.at[2])

    hop_done(0)
    hop_done(1)
    gather_start(xx, ag_recv, ag_core)
    split_sum_sent(from_core, out_buf, send)
    gather_step(xx, ag_recv, ag_core, 1, 0)
    gather_step(xx, ag_recv, ag_core, 2, 1)
    gather_step(xx, ag_recv, ag_core, 1, 1)
    gather_step(xx, ag_recv, ag_core, 2, 0)
    gather_step(xx, ag_recv, ag_core, 3, 0)
    gather_step(xx, ag_recv, ag_core, 3, 1)
    for n in range(4):
        relay(g_s, g_recv, g_send, "d", n)
    weights_done(w3, w3_came)

    def feed_forward(r, same):
        chunk = chunk_of(r, core if same else 1 - core)
        rows = pl.ds(pl.multiple_of(chunk * ROWS, ROWS), ROWS)
        gu = dot_nn(xx[rows, :], w3[...].reshape(1024, 768))
        gate, up = gu[:, 0:384], gu[:, 384:768]
        sig = 1.0 / (1.0 + jnp.exp(-gate))
        sil = gate * sig
        act_s[rows, :] = (sil * up).astype(BF16)
        put_two(mix_s, chunk, slice(0, 384), (up * sig * (1.0 + gate * (1.0 - sig))).astype(BF16))
        put_two(mix_s, chunk, slice(384, 768), sil.astype(BF16))

    def feed_back(r, same):
        chunk = chunk_of(r, core if same else 1 - core)
        rows = pl.ds(pl.multiple_of(chunk * ROWS, ROWS), ROWS)
        layer = dot_nn(act_s[rows, :], wd[...]).astype(BF16)
        if same:
            lpart[r] = layer
        else:
            slot = (3, 1, 2, 0).index(r) % 2
            if r in (2, 0):
                await_bytes(core_out2.at[slot], send2.at[slot])
            core_out2[slot] = layer
            remote(core_out2.at[slot], from_core2.at[r], send2.at[slot], core_recv2.at[r], other_core, c).start()
        dact = dot_nt(g_s[rows, :], wd[...])
        for cols in (slice(0, 384), slice(384, 768)):
            put_two(mix_s, chunk, cols, (dact * two_blocks(mix_s, chunk, cols).astype(F32)).astype(BF16))
        dh = dot_nt(two_blocks(mix_s, chunk, slice(0, 768)), w3[...].reshape(1024, 768))
        if not same:
            core_out[r] = dh.astype(BF16)
            remote(core_out.at[r], from_core.at[r], send.at[6], core_recv.at[r], other_core, c).start()
            return None
        return dh

    def dh_over_x(n):
        remote(out_buf.at[n], in_buf.at[n], send.at[n], recv_d.at[n], f, other_x).start()

    def dh_over_y(n):
        remote(out_buf.at[n], in_buf.at[n], send.at[n], recv_d.at[n], other_y, c).start()

    def dh_of_chip(r, low, high):
        feed_back(r, False)
        dh = feed_back(r, True)
        await_bytes(from_core.at[r], core_recv.at[r])
        total = dh + from_core[r].astype(F32)
        out_buf[low] = total[:half].astype(BF16)
        out_buf[high] = total[half:].astype(BF16)

    for r in range(4):
        feed_forward(r, True)
    for r in range(4):
        gather_core(xx, ag_core, r)
        feed_forward(r, False)
    for kind, n in PIECES:
        relay_wait(g_s, g_recv, kind, n)
    await_bytes(wd, wd_sem.at[1])
    dh_of_chip(3, 0, 1)
    dh_over_x(0)
    dh_over_y(1)
    dh_of_chip(1, 2, 4)
    dh_over_x(2)
    dh_of_chip(2, 5, 3)
    dh_over_y(3)
    await_bytes(in_buf.at[0], recv_d.at[0])
    out_buf[5] = (out_buf[5].astype(F32) + in_buf[0].astype(F32)).astype(BF16)
    dh_over_y(5)
    await_bytes(in_buf.at[1], recv_d.at[1])
    out_buf[4] = (out_buf[4].astype(F32) + in_buf[1].astype(F32)).astype(BF16)
    dh_over_x(4)
    feed_back(0, False)
    dh = feed_back(0, True)
    keep[0] = dh[:half]
    keep[1] = dh[half:]

    def scatter_rows(g, b, block, first, width):
        for k in range(4):
            g[k, b * 64 : b * 64 + 64, first : first + width] = block[k * 64 : k * 64 + 64].astype(BF16)

    def across(g, r_, sem):
        pltpu.make_async_copy(g.at[z], r_.at[z], sem.at[1]).start()
        for j in (2, 1, 3):
            z2 = (z + j) % 4
            remote(g.at[z2], r_.at[z], sem.at[0], sem.at[1], f, z2 * 2 + x).start()

    def across_near(g, r_, sem, came):
        @pl.when(z == edge)
        def _():
            for e in range(2):
                remote(
                    g.at[2 * (1 - upper) + e], r_.at[2 + e], sem.at[0], came.at[2 + e], f, inner * 2 + x
                ).start()

        remote(
            g.at[inner + edge - z], r_.at[upper], sem.at[0], came.at[upper], f, (inner + edge - z) * 2 + x
        ).start()

    def across_relay(g, r_, sem, came):
        @pl.when(z == inner)
        def _():
            for e in range(2):
                to_z = 2 * (1 - upper) + e
                await_bytes(r_.at[2 + e], came.at[2 + e])
                g[to_z] = (g[to_z].astype(F32) + r_[2 + e].astype(F32)).astype(BF16)
                remote(g.at[to_z], r_.at[upper], sem.at[0], came.at[upper], f, to_z * 2 + x).start()

    def across_sent(g, sem):
        await_bytes(g.at[pl.ds(0, 3)], sem.at[0])

    def to_plane(s_, p_, plane_sem):
        pltpu.make_async_copy(s_.at[pl.ds(pl.multiple_of(t * 32, 32), 32)], p_.at[t], plane_sem.at[1]).start()
        for j in range(1, 8):
            t2 = (t + j) % 8
            block = s_.at[pl.ds(pl.multiple_of(t2 * 32, 32), 32)]
            remote(block, p_.at[t], plane_sem.at[0], plane_sem.at[1], t2 // 2, z * 2 + t2 % 2).start()

    def in_plane(r_, s_, p_, sem, plane_sem):
        await_bytes(r_, sem.at[1])
        s_[...] = (r_[0].astype(F32) + r_[1].astype(F32) + r_[2].astype(F32) + r_[3].astype(F32)).astype(BF16)
        to_plane(s_, p_, plane_sem)

    def in_plane_near(g, r_, s_, p_, came, plane_sem):
        for k in range(2):
            await_bytes(r_.at[k], came.at[k])
        s_[...] = (g[z].astype(F32) + r_[0].astype(F32) + r_[1].astype(F32)).astype(BF16)
        to_plane(s_, p_, plane_sem)

    for b in range(4):
        scatter_rows(gf, b, dot_tn(xx[:, b * 256 : b * 256 + 256], mix_s[...].reshape(2048, 768)), 0, 768)
    across_near(gf, rf, f_sem, f_came)
    for k in range(2):
        await_bytes(core_out2.at[k], send2.at[k])
    for b in range(3):
        block = dot_tn(act_s[:, b * 128 : b * 128 + 128], g_s[...]).astype(BF16)
        for k in range(2):
            low, high = max(b * 128, k * 192), min(b * 128 + 128, k * 192 + 192)
            if low < high:
                core_out2[k, low - k * 192 : high - k * 192, :] = block[low - b * 128 : high - b * 128]
    await_bytes(from_core, send.at[6])
    gather_sent(xx)
    h_load = pltpu.make_async_copy(h_out, xx, load.at[3])
    h_load.start()

    await_bytes(from_core.at[0], core_recv.at[0])
    sums = split_sum_end(in_buf, keep, recv_d)
    small[...] = jnp.zeros_like(small)
    for part in (0, 1):
        rows = slice(part * half, part * half + half)
        dh = sums[part] + from_core[0, rows].astype(F32)
        back, dgain = norm_back(mid[rows, :], gain_two, dh)
        first = pl.multiple_of(own * ROWS + part * half, half)
        dm = g_s[pl.ds(first, half), :].astype(F32) + back
        dmid[rows, :] = dm
        hd[pl.ds(first, half), :] = dm.astype(BF16)
        small[1:2, :] += jnp.sum(dgain, axis=0, keepdims=True)
    gather_start(hd, ag_recv2, ag_core2)
    for k in range(6):
        await_bytes(out_buf.at[k], send.at[k])
    for b in range(4):
        vt[b] = k_s[b * QROWS : b * QROWS + QROWS, :].T

    def back_out(r, same):
        chunk = chunk_of(r, core if same else 1 - core)
        rows = pl.ds(pl.multiple_of(chunk * ROWS, ROWS), ROWS)
        put_two(mix_s, chunk, slice(512, 768), dot_nn(hd[rows, :], w2[...].reshape(1024, 256)).astype(BF16))

    back_out(0, True)
    gather_step(hd, ag_recv2, ag_core2, 1, 0)
    gather_step(hd, ag_recv2, ag_core2, 2, 1)
    gather_core(hd, ag_core2, 0)
    back_out(0, False)
    gather_step(hd, ag_recv2, ag_core2, 1, 1)
    gather_step(hd, ag_recv2, ag_core2, 2, 0)
    back_out(1, True)
    back_out(2, True)
    gather_core(hd, ag_core2, 1)
    back_out(1, False)
    gather_core(hd, ag_core2, 2)
    back_out(2, False)
    gather_step(hd, ag_recv2, ag_core2, 3, 0)
    gather_step(hd, ag_recv2, ag_core2, 3, 1)
    back_out(3, True)
    gather_core(hd, ag_core2, 3)
    back_out(3, False)

    in_half = upper == x

    def down_unit(e):
        return core_out2.at[e, pl.ds(0, 192)]

    def down_near():
        @pl.when(in_half)
        def _():
            to_z = inner + edge - z
            remote(down_unit(to_z % 2), rdz.at[0], dz_sem.at[0], dz_came.at[0], f, to_z * 2 + x).start()

        @pl.when(jnp.logical_not(in_half) & (z == edge))
        def _():
            for e in range(2):
                remote(down_unit(e), rdz.at[2 + e], dz_sem.at[0], dz_came.at[2 + e], f, inner * 2 + x).start()

    def down_relay():
        @pl.when(jnp.logical_not(in_half) & (z == inner))
        def _():
            for e in range(2):
                await_bytes(rdz.at[2 + e], dz_came.at[2 + e])
                core_out2[e, 0:192] = (core_out2[e, 0:192].astype(F32) + rdz[2 + e].astype(F32)).astype(BF16)
                remote(down_unit(e), rdz.at[1], dz_sem.at[0], dz_came.at[1], f, (2 * x + e) * 2 + x).start()

    def down_end():
        @pl.when(in_half)
        def _():
            for n in range(2):
                await_bytes(rdz.at[n], dz_came.at[n])
            mine = z % 2
            total = core_out2[mine, 0:192].astype(F32) + rdz[0].astype(F32) + rdz[1].astype(F32)
            core_out2[mine, 0:192] = total.astype(BF16)
            here = core_out2.at[mine, pl.ds(pl.multiple_of(x * 96, 32), 96)]
            there = core_out2.at[mine, pl.ds(pl.multiple_of((1 - x) * 96, 32), 96)]
            pltpu.make_async_copy(here, rd, d_sem.at[1]).start()
            remote(there, rd, d_sem.at[0], d_sem.at[1], f, other_x).start()

    def down_done():
        await_bytes(rd, d_sem.at[1])

        @pl.when(in_half)
        def _():
            await_bytes(rd, d_sem.at[0])
            await_bytes(rdz.at[0], dz_sem.at[0])

        @pl.when(jnp.logical_not(in_half))
        def _():
            await_bytes(rdz.at[pl.ds(0, 2)], dz_sem.at[0])

    down_near()
    home_f, home_c = plane_of(z), own
    stays = (home_f == f) & (home_c == c)

    beyond_c = (core * 2 + 1 - y) * 2 + x
    beyond_stays = (home_f == other_y) & (beyond_c == c)

    def deliver(low, high, dst, k):
        to_low, to_high = dst.at[pl.ds(0, half)], dst.at[pl.ds(half, half)]

        @pl.when(jnp.logical_not(stays))
        def _():
            remote(high, stage.at[k], out_sem.at[5 * k], out_sem.at[5 * k + 1], other_y, c).start()
            remote(low, to_low, out_sem.at[5 * k + 2], out_sem.at[5 * k + 3], home_f, home_c).start()

        @pl.when(stays)
        def _():
            pltpu.make_async_copy(low, to_low, out_sem.at[5 * k + 3]).start()
            pltpu.make_async_copy(high, to_high, out_sem.at[5 * k + 4]).start()

    def deliver_on(dst, k):
        @pl.when(jnp.logical_not(beyond_stays))
        def _():
            await_bytes(stage.at[k], out_sem.at[5 * k + 1])
            remote(
                stage.at[k], dst.at[pl.ds(half, half)], home_send.at[k], out_sem.at[5 * k + 4], home_f, beyond_c
            ).start()

    def deliver_done(dst, k):
        await_bytes(dst.at[pl.ds(0, half)], out_sem.at[5 * k + 3])
        await_bytes(dst.at[pl.ds(half, half)], out_sem.at[5 * k + 4])

        @pl.when(jnp.logical_not(stays))
        def _():
            await_bytes(stage.at[k], out_sem.at[5 * k])
            await_bytes(stage.at[k], out_sem.at[5 * k + 2])

        @pl.when(jnp.logical_not(beyond_stays))
        def _():
            await_bytes(stage.at[k], home_send.at[k])

    def layer_over_x(src, n):
        remote(src, in_buf2.at[n], send2.at[2 + n], recv2.at[n], f, other_x).start()

    def layer_over_y(src, n):
        remote(src, in_buf2.at[n], send2.at[2 + n], recv2.at[n], other_y, c).start()

    low_half, high_half = pl.ds(0, half), pl.ds(half, half)

    def layer_to_chips():
        for r in (3, 1, 2):
            await_bytes(from_core2.at[r], core_recv2.at[r])
            lpart[r] = (lpart[r].astype(F32) + from_core2[r].astype(F32)).astype(BF16)
            if r & 1:
                layer_over_x(lpart.at[r, low_half], 0 if r == 3 else 2)
            if r & 2:
                layer_over_y(lpart.at[r, high_half], 1 if r == 3 else 3)

    def layer_relay():
        await_bytes(in_buf2.at[0], recv2.at[0])
        lpart[2, 0:half] = (lpart[2, 0:half].astype(F32) + in_buf2[0].astype(F32)).astype(BF16)
        layer_over_y(lpart.at[2, low_half], 5)
        await_bytes(in_buf2.at[1], recv2.at[1])
        lpart[1, half:ROWS] = (lpart[1, half:ROWS].astype(F32) + in_buf2[1].astype(F32)).astype(BF16)
        layer_over_x(lpart.at[1, high_half], 4)

    def layer_end():
        await_bytes(from_core2.at[0], core_recv2.at[0])
        for n in (2, 3, 4, 5):
            await_bytes(in_buf2.at[n], recv2.at[n])
        for part in (0, 1):
            rows = slice(part * half, part * half + half)
            value = mid[rows, :] + lpart[0, rows].astype(F32) + from_core2[0, rows].astype(F32)
            value = value + in_buf2[2 + part].astype(F32) + in_buf2[5 - part].astype(F32)
            in_buf2[part] = value.astype(BF16)
        deliver(in_buf2.at[0], in_buf2.at[1], layer_out, 0)

    layer_to_chips()

    def prepare(b, carry):
        rows = pl.ds(pl.multiple_of(b * QROWS, QROWS), QROWS)
        do = jnp.concatenate(
            [mix_s[perm_s[b * 4 + k], :, 512:768] for k in range(4)], axis=0
        )
        act_s[rows, 0:256] = do
        ones = jnp.ones((8, 128), BF16)
        for head in range(2):
            cols = slice(head * 128, head * 128 + 128)
            prod = do[:, cols].astype(F32) * o_s[pl.ds(b * 4, 4), :, cols].reshape(QROWS, 128).astype(F32)
            high = prod.astype(BF16)
            low = (prod - high.astype(F32)).astype(BF16)
            delta = dot_nt(ones, high) + dot_nt(ones, low)
            delta_s[b, :, head * QROWS : head * QROWS + QROWS] = delta[0:1]
        return carry

    lax.fori_loop(0, 4, prepare, 0)
    for b in range(16):
        mix_s[b, :, 0:256] = o_s[ids_s[b]]
    for b in range(4):
        scatter_rows(go, b, dot_tn(hd[:, b * 256 : b * 256 + 256], mix_s[:, :, 0:256].reshape(2048, 256)), 0, 256)
    across(go, ro, o_sem)
    dqt_s[...] = jnp.zeros_like(dqt_s)
    dk_s[...] = jnp.zeros_like(dk_s)
    dv_s[...] = jnp.zeros_like(dv_s)

    def key_tile(kt):
        krows = pl.ds(kt * QROWS, QROWS)

        def step(qt, diagonal):
            kb, vb, ktb = k_s[krows, :], v_s[krows, :], vt[kt]
            for g in range(4):
                head, part = g // 2, g % 2
                start = pl.multiple_of(qt * QROWS + part * 256, 256)
                cols = slice(head * 128, head * 128 + 128)
                lanes = slice(g * 256, g * 256 + 256)
                qb = q_s[pl.ds(start, 256), cols]
                dob = act_s[pl.ds(start, 256), cols]
                depth = 256 * (part + 1) if diagonal else QROWS
                s = dot_nt(kb[:depth], qb)
                p = jnp.exp2(s * (SCALE * LOG2E) - lse_s[qt, :, lanes])
                if diagonal:
                    ki = lax.broadcasted_iota(jnp.int32, (depth, 256), 0)
                    qi = lax.broadcasted_iota(jnp.int32, (depth, 256), 1) + part * 256
                    p = jnp.where(ki <= qi, p, 0.0)
                dp = dot_nt(vb[:depth], dob)
                ds = (p * (dp - delta_s[qt, :, lanes])).astype(BF16)
                out = pl.ds(kt * 4, depth // 128)
                dv_s[out] += dot_nn(p.astype(BF16), dob).reshape(depth // 128, 128, 128)
                dk_s[out] += dot_nn(ds, qb).reshape(depth // 128, 128, 128)
                dq = dot_nn(ktb[:, :depth], ds)
                dqt_s[qt * 4 + part * 2, cols, :] += dq[:, 0:128]
                dqt_s[qt * 4 + part * 2 + 1, cols, :] += dq[:, 128:256]

        step(kt, True)

        def off(qt, inner):
            step(qt, False)
            return inner

        lax.fori_loop(kt + 1, 4, off, 0)

    key_tile(0)
    layer_relay()
    across_relay(gf, rf, f_sem, f_came)
    key_tile(1)
    key_tile(2)
    key_tile(3)

    h_load.wait()

    def finish_chunk(chunk):
        rows = pl.ds(pl.multiple_of(chunk * ROWS, ROWS), ROWS)
        places = [ids_s[chunk * 2 + k] for k in range(2)]
        cos, sin = turns(jnp.concatenate([table_s[b] for b in places], axis=0))
        raw = dot_nn(xx[rows, :], w1[:, :, :, 0:384].reshape(1024, 384))
        for head in range(3):
            cols = slice(head * 128, head * 128 + 128)
            if head < 2:
                blocks = [dqt_s[b, cols, :].T for b in places]
                gain, lanes = gain_s[2:3, 0:128], slice(0, 128)
            else:
                blocks = [dk_s[b] for b in places]
                gain, lanes = gain_s[3:4, 0:128], slice(128, 256)
            d = jnp.concatenate(blocks, axis=0) * SCALE
            back, dgain = norm_back(raw[:, cols], gain, unturn(d, cos, sin))
            put_two(mix_s, chunk, cols, back.astype(BF16))
            small[2:3, lanes] += jnp.sum(dgain, axis=0, keepdims=True)
        for k in range(2):
            mix_s[chunk * 2 + k, :, 384:512] = dv_s[places[k]].astype(BF16)

    def partial(chunk):
        return dot_nt(two_blocks(mix_s, chunk, slice(0, 512)), w1[...].reshape(1024, 512))

    gather_sent(hd)
    lax.fori_loop(0, 8, lambda chunk, carry: (finish_chunk(chunk), carry)[1], 0)
    for b in range(4):
        scatter_rows(ga, b, dot_tn(xx[:, b * 256 : b * 256 + 256], mix_s[:, :, 0:512].reshape(2048, 512)), 0, 512)
    across_near(ga, ra, a_sem, a_came)
    split_sum(partial, core_out, from_core, out_buf, in_buf, keep, send, core_recv, recv)
    layer_end()
    down_relay()
    in_plane_near(gf, rf, sf, pf, f_came, fp_sem)
    in_plane(ro, so, po, o_sem, op_sem)
    low, high = split_sum_end(in_buf, keep, recv)
    deliver_on(layer_out, 0)
    for part, dh in ((0, low), (1, high)):
        rows = slice(part * half, part * half + half)
        back, dgain = norm_back(x_keep[rows, :].astype(F32), gain_one, dh)
        in_buf2[2 + part] = (dmid[rows, :] + back).astype(BF16)
        small[0:1, :] += jnp.sum(dgain, axis=0, keepdims=True)
    deliver(in_buf2.at[2], in_buf2.at[3], grad_tokens, 1)
    across_relay(ga, ra, a_sem, a_came)

    s_in[t] = small[...]
    for j in range(1, 8):
        t2 = (t + j) % 8
        remote(small, s_in.at[t], s_sem.at[0], s_sem.at[1], t2 // 2, z * 2 + t2 % 2).start()

    deliver_on(grad_tokens, 1)
    down_end()
    await_bytes(pf, fp_sem.at[1])
    await_bytes(po, op_sem.at[1])
    await_bytes(s_in.at[pl.ds(0, 7)], s_sem.at[1])
    sbuf[...] = jnp.sum(s_in[...], axis=0)
    p_in[z] = sbuf[...]
    for j in range(1, 4):
        remote(sbuf, p_in.at[z], p_sem.at[0], p_sem.at[1], f, ((z + j) % 4) * 2 + x).start()
    in_plane_near(ga, ra, sa, pa, a_came, ap_sem)
    await_bytes(p_in.at[pl.ds(0, 3)], p_sem.at[1])
    small_out[...] = jnp.sum(p_in[...], axis=0)
    await_bytes(pa, ap_sem.at[1])

    deliver_done(layer_out, 0)
    deliver_done(grad_tokens, 1)
    split_sum_sent(from_core, out_buf, send)
    for n in range(6):
        await_bytes(in_buf2.at[n], send2.at[2 + n])
    await_bytes(s_in.at[pl.ds(0, 7)], s_sem.at[0])
    await_bytes(p_in.at[pl.ds(0, 3)], p_sem.at[0])
    down_done()
    across_sent(gf, f_sem)
    await_bytes(go.at[pl.ds(0, 3)], o_sem.at[0])
    await_bytes(ra.at[pl.ds(0, 3)], a_sem.at[0])
    await_bytes(pf.at[pl.ds(0, 7)], fp_sem.at[0])
    await_bytes(po.at[pl.ds(0, 7)], op_sem.at[0])
    await_bytes(pa.at[pl.ds(0, 7)], ap_sem.at[0])
    relay_done(g_s, g_send)

    @pl.when(f == seq)
    def _():
        for _ in range(3):
            await_bytes(pos_v, pos_sem.at[0])

    await_bytes(gains_all.at[pl.ds(0, 31)], gain_sem.at[0])
    for pack, sem in ((pack1, w1_sem), (pack2, w2_sem), (pack3, w3_sem)):
        await_bytes(pack.at[pl.ds(0, 7)], sem.at[0])
    await_bytes(w1.at[pl.ds(0, 3)], w1_sem.at[2])
    await_bytes(w2.at[pl.ds(0, 3)], w2_sem.at[2])
    weights_sent(w3, w3_sem)
    for k in range(4):

        @pl.when(jnp.logical_not(self_down & (z == k)))
        def _():
            await_bytes(wd_own, wd_sem.at[0])


def layer(*operands):
    any_spec, vmem = pl.BlockSpec(memory_space=pl.ANY), pl.BlockSpec(memory_space=pltpu.VMEM)
    half = ROWS // 2
    bf = lambda *shape: pltpu.VMEM(shape, BF16)
    fl = lambda *shape: pltpu.VMEM(shape, F32)
    out = lambda kind, *shape: jax.ShapeDtypeStruct(shape, kind)
    copies = (
        16, 16, 2, 6, 3, 3, 2, 2, 4, 4, 3, 4, 2,
        4, 3, 6, 8, 6, 8, 7, 4, 6, 6, 8, 4, 6,
        2, 1, 4, 2, 1, 4, 1, 4, 2, 2, 2, 2, 10, 2, 2,
    )
    return pl.pallas_call(
        layer_kernel,
        out_shape=(
            out(BF16, ROWS, 1024), out(BF16, ROWS, 1024), out(BF16, 8, 32, 768), out(BF16, 8, 32, 256),
            out(BF16, 8, 32, 512), out(BF16, 96, 1024), out(BF16, 2048, 1024), out(F32, 8, 1024),
        ),
        in_specs=[any_spec] * 3 + [vmem] * 6 + [any_spec] * 3,
        out_specs=(any_spec,) * 7 + (vmem,),
        scratch_shapes=[
            bf(2048, 1024), bf(2048, 1024), bf(2048, 1024), bf(4, 4, 64, 512), bf(4, 4, 64, 256), bf(4, 4, 64, 768),
            bf(384, 1024), bf(8, 32, 512), bf(8, 32, 256), bf(8, 32, 768), fl(32, 1, 128), fl(16, 128, 128),
            fl(8, 1024),
            bf(2048, 256), bf(2048, 128), bf(2048, 128), bf(16, 128, 256), bf(4, 128, QROWS), fl(128, 1024),
            fl(1, 1024), fl(4, 1, 1024), bf(ROWS, 1024), fl(ROWS, 1024),
            bf(16, 128, 768), bf(2048, 384), fl(4, 1, 1024), fl(16, 256, 128), fl(16, 128, 128), fl(16, 128, 128),
            fl(ROWS, 1024), fl(8, 1024),
            bf(4, ROWS, 1024), bf(4, ROWS, 1024), bf(6, half, 1024), bf(6, half, 1024), fl(2, half, 1024),
            bf(4, ROWS, 1024), bf(2, ROWS, 1024), bf(4, ROWS, 1024), bf(6, half, 1024),
            bf(4, 256, 768), bf(4, 256, 256), bf(4, 256, 512), bf(4, 192, 1024), bf(4, 256, 768), bf(4, 256, 256), bf(4, 256, 512),
            bf(256, 768), bf(256, 256), bf(256, 512), fl(8, 8, 1024), fl(8, 1024), fl(4, 8, 1024),
            bf(2, half, 1024), pltpu.VMEM((1, 2048), jnp.int32), pltpu.SMEM((1, 2048), jnp.int32),
            pltpu.SMEM((16,), jnp.int32), pltpu.SMEM((16,), jnp.int32),
        ]
        + [pltpu.SemaphoreType.DMA((count,)) for count in copies],
        compiler_params=pltpu.CompilerParams(collective_id=0, has_side_effects=True, vmem_limit_bytes=VMEM_LIMIT),
        name="layer",
    )(*operands)


def outputs_kernel(
    layer, tok, pf, po, pa, rd, small, o_l, o_t, o_q, o_k, o_v, o_o, o_g, o_u, o_d, o_first, o_second, o_head
):
    me = lax.axis_index("fsdp") * 8 + lax.axis_index("ctx")
    o_l[...] = layer[...]
    o_t[...] = tok[...]
    for k in range(8):
        wide, thin, third = (slice(k * w, k * w + w) for w in (256, 128, 384))
        o_g[:, third] = pf[k, :, 0:384].astype(F32)
        o_u[:, third] = pf[k, :, 384:768].astype(F32)
        o_o[:, wide] = po[k].astype(F32)
        o_q[:, wide] = pa[k, :, 0:256].astype(F32)
        o_k[:, thin] = pa[k, :, 256:384].astype(F32)
        o_v[:, thin] = pa[k, :, 384:512].astype(F32)
    o_d[...] = rd[...].astype(F32)
    turned = pltpu.roll(small[...], (1024 - 32 * me) % 1024, 1)
    o_first[...] = turned[0:1, 0:32]
    o_second[...] = turned[1:2, 0:32]
    turned = pltpu.roll(small[...], (1024 - 8 * me) % 1024, 1)
    o_head[...] = turned[2:3, 0:8]


def outputs(*came):
    vmem = pl.BlockSpec(memory_space=pltpu.VMEM)
    out = lambda kind, *shape: jax.ShapeDtypeStruct(shape, kind)
    return pl.pallas_call(
        outputs_kernel,
        out_shape=(
            out(BF16, ROWS, 1024), out(BF16, ROWS, 1024), out(F32, 32, 2048), out(F32, 32, 1024), out(F32, 32, 1024),
            out(F32, 32, 2048), out(F32, 32, 3072), out(F32, 32, 3072), out(F32, 96, 1024), out(F32, 1, 32),
            out(F32, 1, 32), out(F32, 1, 8),
        ),
        in_specs=[vmem] * 7,
        out_specs=(vmem,) * 12,
        compiler_params=pltpu.CompilerParams(vmem_limit_bytes=VMEM_LIMIT),
        name="outputs",
    )(*came)


def rope_table(length):
    inverse = 1000000.0 ** (-2.0 * np.arange(HEAD_DIM // 2, dtype=np.float64) / HEAD_DIM)
    angles = np.arange(length, dtype=np.float32)[:, None] * inverse.astype(np.float32)[None, :]
    angles = angles.astype(np.float64)
    return np.concatenate([np.cos(angles), np.sin(angles)], axis=1).astype(np.float32)


def per_device_planes(
    tokens, positions, w_query, w_key, w_value, w_output, w_gate, w_up, w_down, first_gain, second_gain, head_gain,
    cotangent,
):
    gains = jnp.concatenate([first_gain, second_gain, head_gain, jnp.zeros((56,), BF16)]).astype(F32)[None]
    table = jnp.asarray(rope_table(2048)).reshape(16, 128, HEAD_DIM)
    layer_out, grad_tokens, pf, po, pa, rd, _, small = layer(
        tokens[0], cotangent[0], positions, w_query, w_key, w_value, w_output.T, w_gate, w_up, w_down, gains, table
    )
    layer_out, grad_tokens, o_q, o_k, o_v, o_o, o_g, o_u, o_d, o_first, o_second, o_head = outputs(
        layer_out, grad_tokens, pf, po, pa, rd, small
    )
    return (
        layer_out[None],
        grad_tokens[None],
        o_q,
        o_k,
        o_v,
        o_o.T,
        o_g,
        o_u,
        o_d,
        o_first[0],
        o_second[0],
        o_head[0],
    )


def solution(mesh):
    planes = mesh.shape["fsdp"] == 4 and mesh.shape["ctx"] == 8
    body = per_device_planes if planes else per_device
    return jax.shard_map(
        body,
        mesh=mesh,
        in_specs=(
            P("fsdp", "ctx", None),
            P("fsdp", None),
            P(("fsdp", "ctx"), None),
            P(("fsdp", "ctx"), None),
            P(("fsdp", "ctx"), None),
            P(None, ("fsdp", "ctx")),
            P(("fsdp", "ctx"), None),
            P(("fsdp", "ctx"), None),
            P(("fsdp", "ctx"), None),
            P(("fsdp", "ctx")),
            P(("fsdp", "ctx")),
            P(("fsdp", "ctx")),
            P("fsdp", "ctx", None),
        ),
        out_specs=(
            P("fsdp", "ctx", None),
            P("fsdp", "ctx", None),
            P(("fsdp", "ctx"), None),
            P(("fsdp", "ctx"), None),
            P(("fsdp", "ctx"), None),
            P(None, ("fsdp", "ctx")),
            P(("fsdp", "ctx"), None),
            P(("fsdp", "ctx"), None),
            P(("fsdp", "ctx"), None),
            P(("fsdp", "ctx")),
            P(("fsdp", "ctx")),
            P(("fsdp", "ctx")),
        ),
        check_vma=False,
    )
```

```python
from functools import partial

import jax
import jax.numpy as jnp
import numpy as np
from jax import lax
from jax.experimental import pallas as pl
from jax.experimental.pallas import tpu as pltpu
from jax.sharding import PartitionSpec as P

MESH = pl.DeviceIdType.MESH

HEADS = 16
KV_HEADS = 8
HEAD_DIM = 128


def normed(operand, gain_in):
    return (
        operand * lax.rsqrt(jnp.mean(operand * operand, axis=-1, keepdims=True) + 1e-06) * gain_in
    )


def rotary(operand, places):
    head_width = operand.shape[-1]
    half_width = head_width // 2
    inverse = 1000000.0 ** (-2.0 * jnp.arange(half_width, dtype=jnp.float32) / head_width)
    angles = places.astype(jnp.float32)[:, None] * inverse[None, :]
    cosine = jnp.concatenate([jnp.cos(angles), jnp.cos(angles)], axis=-1)[:, None, :]
    sine_table = jnp.concatenate([jnp.sin(angles), jnp.sin(angles)], axis=-1)[:, None, :]
    turned = jnp.concatenate([-operand[..., half_width:], operand[..., :half_width]], axis=-1)
    return operand * cosine + turned * sine_table


def head_prep(raw_proj, gain_in, places, head_count):
    row_count = raw_proj.shape[0]
    shaped = raw_proj.reshape(row_count, head_count, HEAD_DIM)
    return rotary(normed(shaped, gain_in), places).reshape(row_count, head_count * HEAD_DIM)


def gated(gate_raw, up_raw):
    return jax.nn.silu(gate_raw) * up_raw


def project(left_side, right_side):
    return jnp.dot(left_side, right_side, preferred_element_type=jnp.float32)


def project_back(left_side, right_side):
    return lax.dot_general(
        left_side, right_side, (((1,), (1,)), ((), ())), preferred_element_type=jnp.float32
    )


def outer_sum(left_side, right_side):
    return lax.dot_general(
        left_side, right_side, (((0,), (0,)), ((), ())), preferred_element_type=jnp.float32
    )


def halves_apart(rows_in, shard_count):
    shape_in = rows_in.shape
    split = rows_in.reshape((shard_count, 2, shape_in[0] // (2 * shard_count)) + shape_in[1:])
    return jnp.swapaxes(split, 0, 1).reshape(shape_in)


def halves_back(rows_in, shard_count):
    shape_in = rows_in.shape
    split = rows_in.reshape((2, shard_count, shape_in[0] // (2 * shard_count)) + shape_in[1:])
    return jnp.swapaxes(split, 0, 1).reshape(shape_in)


def key_layout(key_rows, value_rows, place_all):
    key_count = key_rows.shape[0]
    key_block = min(512, key_count)
    block_count = key_count // key_block
    key_parts = key_rows.reshape(block_count, key_block, KV_HEADS, HEAD_DIM)
    value_parts = value_rows.reshape(block_count, key_block, KV_HEADS, HEAD_DIM)
    place_parts = place_all.reshape(block_count, key_block)
    return (key_parts, value_parts, place_parts)


def attend_forward(queries, key_rows, value_rows, place_here, place_all):
    row_count = queries.shape[0]
    group_size = HEADS // KV_HEADS
    score_scale = HEAD_DIM ** (-0.5)
    grouped = queries.reshape(row_count, KV_HEADS, group_size, HEAD_DIM)
    layout = key_layout(key_rows, value_rows, place_all)
    top_place = jnp.max(place_here)

    def attend_step(state_now, block_item):
        key_part, value_part, place_part = block_item

        def attend_compute(state_in):
            run_max, run_sum, run_out = state_in
            scores = (
                jnp.einsum("qhge,khe->hgqk", grouped, key_part, preferred_element_type=jnp.float32)
                * score_scale
            )
            visible = place_part[None, None, None, :] <= place_here[None, None, :, None]
            scores = jnp.where(visible, scores, -1e30)
            new_max = jnp.maximum(run_max, jnp.max(scores, axis=-1))
            weights = jnp.where(visible, jnp.exp(scores - new_max[..., None]), 0.0)
            rescale = jnp.exp(run_max - new_max)
            run_sum = run_sum * rescale + jnp.sum(weights, axis=-1)
            mixed = jnp.einsum(
                "hgqk,khe->hgqe",
                weights.astype(jnp.bfloat16),
                value_part,
                preferred_element_type=jnp.float32,
            )
            run_out = run_out * rescale[..., None] + mixed
            return (new_max, run_sum, run_out)

        state_next = lax.cond(
            jnp.min(place_part) > top_place, lambda state_in: state_in, attend_compute, state_now
        )
        return (state_next, None)

    start_state = (
        jnp.full((KV_HEADS, group_size, row_count), -1e30, jnp.float32),
        jnp.zeros((KV_HEADS, group_size, row_count), jnp.float32),
        jnp.zeros((KV_HEADS, group_size, row_count, HEAD_DIM), jnp.float32),
    )
    (run_max, run_sum, run_out), _ = lax.scan(attend_step, start_state, layout)
    attention = (
        (run_out / run_sum[..., None]).transpose(2, 0, 1, 3).reshape(row_count, HEADS * HEAD_DIM)
    )
    return (attention, run_max + jnp.log(run_sum))


def row_dot_table(grad_attn, attention):
    row_count = grad_attn.shape[0]
    group_size = HEADS // KV_HEADS
    grad_grouped = grad_attn.reshape(row_count, KV_HEADS, group_size, HEAD_DIM)
    return jnp.sum(
        grad_grouped.astype(jnp.float32)
        * attention.reshape(row_count, KV_HEADS, group_size, HEAD_DIM),
        axis=-1,
    ).transpose(1, 2, 0)


def attend_backward(
    queries, key_rows, value_rows, grad_attn, row_dots, log_total, place_here, place_all
):
    row_count = queries.shape[0]
    key_count = key_rows.shape[0]
    group_size = HEADS // KV_HEADS
    score_scale = HEAD_DIM ** (-0.5)
    grouped = queries.reshape(row_count, KV_HEADS, group_size, HEAD_DIM)
    grad_grouped = grad_attn.reshape(row_count, KV_HEADS, group_size, HEAD_DIM)
    layout = key_layout(key_rows, value_rows, place_all)
    top_place = jnp.max(place_here)

    def back_step(grad_query, block_item):
        key_part, value_part, place_part = block_item
        key_block = key_part.shape[0]

        def back_compute(grad_in):
            scores = (
                jnp.einsum("qhge,khe->hgqk", grouped, key_part, preferred_element_type=jnp.float32)
                * score_scale
            )
            visible = place_part[None, None, None, :] <= place_here[None, None, :, None]
            weights = jnp.where(
                visible, jnp.exp(jnp.where(visible, scores, -1e30) - log_total[..., None]), 0.0
            )
            grad_probs = jnp.einsum(
                "qhge,khe->hgqk", grad_grouped, value_part, preferred_element_type=jnp.float32
            )
            grad_scores = (weights * (grad_probs - row_dots[..., None])).astype(jnp.bfloat16)
            grad_out = (
                grad_in
                + jnp.einsum(
                    "hgqk,khe->qhge", grad_scores, key_part, preferred_element_type=jnp.float32
                )
                * score_scale
            )
            grad_keys = (
                jnp.einsum(
                    "hgqk,qhge->khe", grad_scores, grouped, preferred_element_type=jnp.float32
                )
                * score_scale
            )
            grad_values = jnp.einsum(
                "hgqk,qhge->khe",
                weights.astype(jnp.bfloat16),
                grad_grouped,
                preferred_element_type=jnp.float32,
            )
            return (
                grad_out,
                (
                    grad_keys.reshape(key_block, KV_HEADS * HEAD_DIM),
                    grad_values.reshape(key_block, KV_HEADS * HEAD_DIM),
                ),
            )

        def skipped(grad_in):
            empty_terms = jnp.zeros((key_block, KV_HEADS * HEAD_DIM), jnp.float32)
            return (grad_in, (empty_terms, empty_terms))

        return lax.cond(jnp.min(place_part) > top_place, skipped, back_compute, grad_query)

    start_grad = jnp.zeros((row_count, KV_HEADS, group_size, HEAD_DIM), jnp.float32)
    grad_query, key_terms = lax.scan(back_step, start_grad, layout)
    grad_query = grad_query.reshape(row_count, HEADS * HEAD_DIM)
    return (
        grad_query,
        key_terms[0].reshape(key_count, KV_HEADS * HEAD_DIM),
        key_terms[1].reshape(key_count, KV_HEADS * HEAD_DIM),
    )


def per_device(
    tokens,
    positions,
    w_query,
    w_key,
    w_value,
    w_output,
    w_gate,
    w_up,
    w_down,
    first_gain,
    second_gain,
    head_gain,
    cotangent,
):
    inputs = tokens[0].astype(jnp.float32)
    row_count = inputs.shape[0]
    shard_count = lax.axis_size("ctx")
    place_stored = positions[0]
    place_here = lax.dynamic_slice_in_dim(
        place_stored, lax.axis_index("ctx") * row_count, row_count
    )
    place_all = halves_apart(place_stored, shard_count)
    query_full, key_full, value_full, output_full, gain_first, gain_head = (
        lax.all_gather(w_query, ("fsdp", "ctx"), axis=0, tiled=True),
        lax.all_gather(w_key, ("fsdp", "ctx"), axis=0, tiled=True),
        lax.all_gather(w_value, ("fsdp", "ctx"), axis=0, tiled=True),
        lax.all_gather(w_output, ("fsdp", "ctx"), axis=1, tiled=True),
        lax.all_gather(first_gain, ("fsdp", "ctx"), axis=0, tiled=True),
        lax.all_gather(head_gain, ("fsdp", "ctx"), axis=0, tiled=True),
    )
    gain_one = gain_first.astype(jnp.float32)
    gain_query = gain_head[:HEAD_DIM].astype(jnp.float32)
    gain_key = gain_head[HEAD_DIM:].astype(jnp.float32)
    hidden_one = normed(inputs, gain_one).astype(jnp.bfloat16)
    query_raw = project(hidden_one, query_full)
    key_raw = project(hidden_one, key_full)
    value_rows = project(hidden_one, value_full).astype(jnp.bfloat16)
    query_prep = partial(head_prep, places=place_here, head_count=HEADS)
    key_prep = partial(head_prep, places=place_here, head_count=KV_HEADS)
    queries, query_back = jax.vjp(query_prep, query_raw, gain_query)
    key_local, key_back = jax.vjp(key_prep, key_raw, gain_key)
    queries = queries.astype(jnp.bfloat16)
    key_local = key_local.astype(jnp.bfloat16)
    key_stored, value_stored = (
        lax.all_gather(key_local, "ctx", axis=0, tiled=True),
        lax.all_gather(value_rows, "ctx", axis=0, tiled=True),
    )
    key_all = halves_apart(key_stored, shard_count)
    value_all = halves_apart(value_stored, shard_count)
    attention, log_total = attend_forward(queries, key_all, value_all, place_here, place_all)
    attn_low = attention.astype(jnp.bfloat16)
    middle = inputs + project(attn_low, output_full)
    gate_full, up_full, down_full, gain_second = (
        lax.all_gather(w_gate, ("fsdp", "ctx"), axis=0, tiled=True),
        lax.all_gather(w_up, ("fsdp", "ctx"), axis=0, tiled=True),
        lax.all_gather(w_down, ("fsdp", "ctx"), axis=0, tiled=True),
        lax.all_gather(second_gain, ("fsdp", "ctx"), axis=0, tiled=True),
    )
    gain_two = gain_second.astype(jnp.float32)
    hidden_two = normed(middle, gain_two).astype(jnp.bfloat16)
    gate_raw = project(hidden_two, gate_full)
    up_raw = project(hidden_two, up_full)
    activated, gated_back = jax.vjp(gated, gate_raw, up_raw)
    act_low = activated.astype(jnp.bfloat16)
    layer_out = (middle + project(act_low, down_full)).astype(jnp.bfloat16)
    grad_out = cotangent[0].astype(jnp.float32)
    gate_full, up_full, down_full, gain_second = (
        lax.all_gather(w_gate, ("fsdp", "ctx"), axis=0, tiled=True),
        lax.all_gather(w_up, ("fsdp", "ctx"), axis=0, tiled=True),
        lax.all_gather(w_down, ("fsdp", "ctx"), axis=0, tiled=True),
        lax.all_gather(second_gain, ("fsdp", "ctx"), axis=0, tiled=True),
    )
    gain_two = gain_second.astype(jnp.float32)
    out_low = grad_out.astype(jnp.bfloat16)
    down_terms = outer_sum(act_low, out_low)
    grad_act = project_back(out_low, down_full)
    grad_gate_raw, grad_up_raw = gated_back(grad_act)
    gate_low = grad_gate_raw.astype(jnp.bfloat16)
    up_low = grad_up_raw.astype(jnp.bfloat16)
    gate_terms = outer_sum(hidden_two, gate_low)
    up_terms = outer_sum(hidden_two, up_low)
    grad_hidden_two = project_back(gate_low, gate_full) + project_back(up_low, up_full)
    _, norm_two_back = jax.vjp(normed, middle, gain_two)
    middle_part, gain_two_terms = norm_two_back(grad_hidden_two)
    grad_gate, grad_up, grad_down, grad_second = (
        lax.psum_scatter(gate_terms, ("fsdp", "ctx"), scatter_dimension=0, tiled=True),
        lax.psum_scatter(up_terms, ("fsdp", "ctx"), scatter_dimension=0, tiled=True),
        lax.psum_scatter(down_terms, ("fsdp", "ctx"), scatter_dimension=0, tiled=True),
        lax.psum_scatter(gain_two_terms, ("fsdp", "ctx"), scatter_dimension=0, tiled=True),
    )
    grad_middle = grad_out + middle_part
    query_full, key_full, value_full, output_full, gain_first, gain_head = (
        lax.all_gather(w_query, ("fsdp", "ctx"), axis=0, tiled=True),
        lax.all_gather(w_key, ("fsdp", "ctx"), axis=0, tiled=True),
        lax.all_gather(w_value, ("fsdp", "ctx"), axis=0, tiled=True),
        lax.all_gather(w_output, ("fsdp", "ctx"), axis=1, tiled=True),
        lax.all_gather(first_gain, ("fsdp", "ctx"), axis=0, tiled=True),
        lax.all_gather(head_gain, ("fsdp", "ctx"), axis=0, tiled=True),
    )
    gain_one = gain_first.astype(jnp.float32)
    middle_low = grad_middle.astype(jnp.bfloat16)
    output_terms = outer_sum(attn_low, middle_low)
    grad_attn = project_back(middle_low, output_full).astype(jnp.bfloat16)
    row_dots = row_dot_table(grad_attn, attention)
    grad_queries, key_terms, value_terms = attend_backward(
        queries, key_all, value_all, grad_attn, row_dots, log_total, place_here, place_all
    )
    key_terms = halves_back(key_terms, shard_count)
    value_terms = halves_back(value_terms, shard_count)
    grad_key_local, grad_value_local = (
        lax.psum_scatter(
            key_terms.astype(jnp.bfloat16), "ctx", scatter_dimension=0, tiled=True
        ).astype(jnp.float32),
        lax.psum_scatter(
            value_terms.astype(jnp.bfloat16), "ctx", scatter_dimension=0, tiled=True
        ).astype(jnp.float32),
    )
    grad_query_raw, gain_query_terms = query_back(grad_queries)
    grad_key_raw, gain_key_terms = key_back(grad_key_local)
    query_low = grad_query_raw.astype(jnp.bfloat16)
    keyraw_low = grad_key_raw.astype(jnp.bfloat16)
    value_low = grad_value_local.astype(jnp.bfloat16)
    query_terms = outer_sum(hidden_one, query_low)
    key_weight_terms = outer_sum(hidden_one, keyraw_low)
    value_weight_terms = outer_sum(hidden_one, value_low)
    grad_hidden_one = (
        project_back(query_low, query_full)
        + project_back(keyraw_low, key_full)
        + project_back(value_low, value_full)
    )
    _, norm_one_back = jax.vjp(normed, inputs, gain_one)
    input_part, gain_one_terms = norm_one_back(grad_hidden_one)
    head_terms = jnp.concatenate([gain_query_terms, gain_key_terms])
    grad_query, grad_key, grad_value, grad_output, grad_first, grad_head = (
        lax.psum_scatter(query_terms, ("fsdp", "ctx"), scatter_dimension=0, tiled=True),
        lax.psum_scatter(key_weight_terms, ("fsdp", "ctx"), scatter_dimension=0, tiled=True),
        lax.psum_scatter(value_weight_terms, ("fsdp", "ctx"), scatter_dimension=0, tiled=True),
        lax.psum_scatter(output_terms, ("fsdp", "ctx"), scatter_dimension=1, tiled=True),
        lax.psum_scatter(gain_one_terms, ("fsdp", "ctx"), scatter_dimension=0, tiled=True),
        lax.psum_scatter(head_terms, ("fsdp", "ctx"), scatter_dimension=0, tiled=True),
    )
    grad_tokens = (grad_middle + input_part).astype(jnp.bfloat16)
    return (
        layer_out[None],
        grad_tokens[None],
        grad_query,
        grad_key,
        grad_value,
        grad_output,
        grad_gate,
        grad_up,
        grad_down,
        grad_first,
        grad_second,
        grad_head,
    )


ROWS = 256
QROWS = 512
EPS = 1e-06
LOG2E = 1.4426950408889634
SCALE = HEAD_DIM**-0.5
VMEM_LIMIT = 62 * 1024 * 1024
BF16 = jnp.bfloat16
F32 = jnp.float32


def dot_nn(a, b):
    return lax.dot_general(a, b, (((1,), (0,)), ((), ())), preferred_element_type=F32)


def dot_nt(a, b):
    return lax.dot_general(a, b, (((1,), (1,)), ((), ())), preferred_element_type=F32)


def dot_tn(a, b):
    return lax.dot_general(a, b, (((0,), (0,)), ((), ())), preferred_element_type=F32)


def whereabouts():
    f, c = lax.axis_index("fsdp"), lax.axis_index("ctx")
    return f, c, f // 2, f % 2, c // 2, c % 2


def plane_of(s):
    return (s % 2) * 2 + s // 2


def remote(src, dst, send, recv, fsdp, ctx):
    return pltpu.make_async_remote_copy(
        src_ref=src, dst_ref=dst, send_sem=send, recv_sem=recv, device_id=(fsdp, ctx), device_id_type=MESH
    )


def await_bytes(ref, sem):
    pltpu.make_async_copy(ref, ref, sem).wait()


def greet_all():
    f, c, y, core, z, x = whereabouts()
    barrier = pltpu.get_barrier_semaphore()
    me = f * 8 + c

    def greet(j, carry):
        dev = (me + j) % 32
        pl.semaphore_signal(barrier, inc=1, device_id=(dev // 8, dev % 8), device_id_type=MESH)
        return carry

    lax.fori_loop(1, 32, greet, 0)
    pl.semaphore_wait(barrier, 31)


def chip_peer(r):
    f, c, y, core, z, x = whereabouts()
    y2 = 1 - y if r & 2 else y
    x2 = 1 - x if r & 1 else x
    return y2, x2


def chunk_of(r, core):
    y2, x2 = chip_peer(r)
    return (core * 2 + y2) * 2 + x2


def rows_of(ref, chunk):
    return ref.at[pl.ds(pl.multiple_of(chunk * ROWS, ROWS), ROWS)]


def head_norm_rope(raw, gain, cos, sin):
    r = lax.rsqrt(jnp.mean(raw * raw, axis=-1, keepdims=True) + EPS)
    u = raw * r * gain
    return u * cos + pltpu.roll(u, HEAD_DIM // 2, 1) * sin


def norm_rows(values, gain):
    v = values.astype(F32)
    return v * lax.rsqrt(jnp.mean(v * v, axis=-1, keepdims=True) + EPS) * gain


def norm_back(values, gain, dy):
    r = lax.rsqrt(jnp.mean(values * values, axis=-1, keepdims=True) + EPS)
    cdy = gain * dy
    back = r * cdy - values * (r * r * r) * jnp.mean(cdy * values, axis=-1, keepdims=True)
    return back, dy * values * r


def unturn(d, cos, sin):
    return d * cos - pltpu.roll(d, HEAD_DIM // 2, 1) * sin


def order_z(n, z):
    upper = z // 2
    low = (z + upper) % 2
    far = n // 2
    base = far * n + (1 - far) * (low + n * (1 - 2 * low))
    return base + upper * (3 - 2 * base)


def turn_of(n):
    return 3 - 2 * n + 3 * (n // 2)


def chunk_at(r, core):
    f, c, y, _, z, x = whereabouts()
    return (core * 2 + (y + r // 2) % 2) * 2 + (x + r % 2) % 2


def split_step(n, total, out_buf, in_buf, keep, send, recv):
    f, c, y, core, z, x = whereabouts()
    half = ROWS // 2

    def over_x(k):
        remote(out_buf.at[k], in_buf.at[k], send.at[k], recv.at[k], f, z * 2 + 1 - x).start()

    def over_y(k):
        remote(out_buf.at[k], in_buf.at[k], send.at[k], recv.at[k], (1 - y) * 2 + core, c).start()

    def add(k, came):
        await_bytes(in_buf.at[came], recv.at[came])
        out_buf[k] = (out_buf[k].astype(F32) + in_buf[came].astype(F32)).astype(BF16)

    @pl.when(n < 3)
    def _():
        out_buf[2 * n + n // 2] = total[:half].astype(BF16)
        out_buf[1 + 3 * n - 4 * (n // 2)] = total[half:].astype(BF16)

    @pl.when(n == 0)
    def _():
        over_x(0)
        over_y(1)

    @pl.when(n == 1)
    def _():
        over_x(2)

    @pl.when(n == 2)
    def _():
        over_y(3)
        add(5, 0)
        over_y(5)
        add(4, 1)
        over_x(4)

    @pl.when(n == 3)
    def _():
        keep[0] = total[:half]
        keep[1] = total[half:]


def split_sum(partial, core_out, from_core, out_buf, in_buf, keep, send, core_recv, recv):
    f, c, y, core, z, x = whereabouts()

    def to_core(n, carry):
        r = turn_of(n)
        core_out[r] = partial(chunk_at(r, 1 - core)).astype(BF16)
        remote(core_out.at[r], from_core.at[r], send.at[6], core_recv.at[r], y * 2 + 1 - core, c).start()
        return carry

    lax.fori_loop(0, 4, to_core, 0)

    def to_chips(n, carry):
        r = turn_of(n)
        term = partial(chunk_at(r, core))
        await_bytes(from_core.at[r], core_recv.at[r])
        split_step(n, term + from_core[r].astype(F32), out_buf, in_buf, keep, send, recv)
        return carry

    lax.fori_loop(0, 4, to_chips, 0)


def split_sum_end(in_buf, keep, recv):
    for k in (2, 3, 4, 5):
        await_bytes(in_buf.at[k], recv.at[k])
    return (
        keep[0] + in_buf[2].astype(F32) + in_buf[5].astype(F32),
        keep[1] + in_buf[3].astype(F32) + in_buf[4].astype(F32),
    )


def split_sum_sent(from_core, out_buf, send):
    await_bytes(from_core, send.at[6])
    for k in range(6):
        await_bytes(out_buf.at[k], send.at[k])


SPLIT_SUM_SCRATCH = [
    pltpu.VMEM((4, ROWS, 1024), BF16),
    pltpu.VMEM((4, ROWS, 1024), BF16),
    pltpu.VMEM((6, ROWS // 2, 1024), BF16),
    pltpu.VMEM((6, ROWS // 2, 1024), BF16),
    pltpu.VMEM((2, ROWS // 2, 1024), F32),
    pltpu.SemaphoreType.DMA((7,)),
    pltpu.SemaphoreType.DMA((4,)),
    pltpu.SemaphoreType.DMA((6,)),
]


def rows_in_order(pos_s, ids_s, perm_s):
    ids = [lax.div(pos_s[0, j * 128], jnp.int32(128)) for j in range(16)]
    for b in range(16):
        ids_s[b] = ids[b]
        place = jnp.int32(0)
        for j in range(16):
            place = place + j * (1 - lax.min(lax.abs(ids[j] - b), jnp.int32(1)))
        perm_s[b] = lax.min(place, jnp.int32(15))


def turns(table):
    cos, sin = table[:, 0 : HEAD_DIM // 2], table[:, HEAD_DIM // 2 :]
    return jnp.concatenate([cos, cos], axis=1), jnp.concatenate([-sin, sin], axis=1)


def two_blocks(ref, chunk, cols):
    return ref[pl.ds(chunk * 2, 2), :, cols].reshape(ROWS, -1)


def put_two(ref, chunk, cols, value):
    for k in range(2):
        ref[chunk * 2 + k, :, cols] = value[k * 128 : k * 128 + 128]


def gain_rows(gains_all):
    every = gains_all[...].reshape(32, 128)
    lane = lax.broadcasted_iota(jnp.int32, (32, 128), 1)

    def place(first, count, per_row):
        kept = jnp.where((lane >= first) & (lane < first + count), every, 0.0)
        turned = [pltpu.roll(kept, (count * seg - first) % 128, 1) for seg in range(per_row)]
        return [
            sum(turned[seg][m * per_row + seg : m * per_row + seg + 1] for seg in range(per_row))
            for m in range(32 // per_row)
        ]

    one, two = place(0, 32, 4), place(32, 32, 4)
    query, key = place(64, 8, 16)
    return jnp.concatenate(one, axis=1), jnp.concatenate(two, axis=1), query, key


PIECES = [
    ("o", 0), ("o", 1), ("x", 0), ("y", 0), ("o", 2), ("x", 1), ("y", 1), ("o", 3),
    ("x", 2), ("y", 2), ("d", 0), ("x", 3), ("y", 3), ("d", 1), ("d", 2), ("d", 3),
]


def layer_kernel(
    tok, cot, pos, wq, wk, wv, wo, wg, wu, wd_own, gains, table_h,
    layer_out, grad_tokens, pf, po, pa, rd, h_out, small_out,
    xx, hd, g_s, w1, w2, w3, wd, pack1, pack2, pack3, gains_all, table_s, gain_s,
    q_s, k_s, v_s, o_s, vt, total, lse_s, x_keep, mid,
    mix_s, act_s, delta_s, dqt_s, dk_s, dv_s, small,
    core_out, from_core, out_buf, in_buf, keep, lpart, core_out2, from_core2, in_buf2,
    gf, go, ga, rdz, rf, ro, ra, sf, so, sa, s_in, sbuf, p_in, stage, pos_v, pos_s, ids_s, perm_s,
    x_recv, g_recv, stage_recv, hop_send, x_send, g_send, pos_sem, gain_sem, w1_sem, w2_sem, w3_sem, w3_came, wd_sem,
    load, ag_send, ag_recv, ag_core, ag_recv2, ag_core2, send, core_recv, recv, recv_d, send2, core_recv2, recv2,
    home_send, f_sem, f_came, o_sem, a_sem, a_came, dz_sem, dz_came, d_sem, fp_sem, op_sem, ap_sem, out_sem, s_sem, p_sem,
):
    f, c, y, core, z, x = whereabouts()
    me, t, own = f * 8 + c, f * 2 + x, (core * 2 + y) * 2 + x
    half = ROWS // 2
    upper = z // 2
    edge, inner, other_inner = 3 * upper, 1 + upper, 2 - upper
    table = pltpu.make_async_copy(table_h, table_s, load.at[0])
    table.start()
    for k in range(8):
        pack1[k, :, 0:256] = wq[:, k * 256 : k * 256 + 256]
        pack1[k, :, 256:384] = wk[:, k * 128 : k * 128 + 128]
        pack1[k, :, 384:512] = wv[:, k * 128 : k * 128 + 128]
    greet_all()

    home = plane_of(f)
    seq = plane_of(z)
    ys, cs = seq // 2, seq % 2
    side = (y + ys) % 2
    other_y = (1 - y) * 2 + core
    other_core = y * 2 + 1 - core
    other_x = z * 2 + 1 - x

    def piece(buf, chunk, part):
        return buf.at[pl.ds(pl.multiple_of(chunk * ROWS + part * half, half), half)]

    def hop_beyond(src, buf, recv_, k):
        high = src.at[pl.ds(half, half)]

        @pl.when(home != z)
        def _():
            remote(high, stage.at[k], hop_send.at[3 * k + 1], stage_recv.at[k], other_y, c).start()

        @pl.when(home == z)
        def _():
            remote(high, piece(buf, c, 1), hop_send.at[3 * k + 1], recv_.at[2 * c + 1], other_y, c).start()

    def hop(src, buf, recv_, k):
        low = src.at[pl.ds(0, half)]

        @pl.when(home != z)
        def _():
            remote(low, piece(buf, c, 0), hop_send.at[3 * k], recv_.at[2 * c], f, home * 2 + x).start()

        @pl.when(home == z)
        def _():
            pltpu.make_async_copy(low, piece(buf, c, 0), recv_.at[2 * c]).start()

    beyond = plane_of(other_y)

    def hop_on(buf, recv_, k):
        @pl.when(beyond != z)
        def _():
            await_bytes(stage.at[k], stage_recv.at[k])
            remote(stage.at[k], piece(buf, c, 1), hop_send.at[3 * k + 2], recv_.at[2 * c + 1], f, beyond * 2 + x).start()

    def hop_done(k):
        @pl.when(home != z)
        def _():
            await_bytes(stage.at[k], hop_send.at[3 * k])

        await_bytes(stage.at[k], hop_send.at[3 * k + 1])

        @pl.when(beyond != z)
        def _():
            await_bytes(stage.at[k], hop_send.at[3 * k + 2])

    def whereof(kind, n):
        chunk = order_z(n, z) * 2 + (x if kind in "oy" else 1 - x)
        return chunk, (side if kind in "ox" else 1 - side)

    def relay(buf, recv_, send_, kind, n):
        chunk, part = whereof(kind, n)
        rows = piece(buf, chunk, part)
        sem = recv_.at[2 * chunk + part]

        def over_x():
            remote(rows, rows, send_.at[1], sem, f, other_x).start()

        def over_y():
            remote(rows, rows, send_.at[2], sem, other_y, c).start()

        @pl.when(core == cs)
        def _():
            await_bytes(rows, sem)
            if kind == "o":
                over_x()
                over_y()
            if kind == "x":
                pl.when(n % 2 == 0)(over_y)
            if kind == "y":
                pl.when(n % 2 == 1)(over_x)
            remote(rows, rows, send_.at[0], sem, other_core, c).start()

    def relay_wait(buf, recv_, kind, n):
        chunk, part = whereof(kind, n)

        @pl.when(core != cs)
        def _():
            await_bytes(piece(buf, chunk, part), recv_.at[2 * chunk + part])

    def relay_done(buf, send_):
        @pl.when(core == cs)
        def _():
            await_bytes(buf, send_.at[0])
            await_bytes(buf.at[pl.ds(0, 6 * half)], send_.at[1])
            await_bytes(buf.at[pl.ds(0, 6 * half)], send_.at[2])

    def my_rows(w):
        return w.at[f, z, pl.ds(pl.multiple_of(x * 32, 32), 32)]

    def weights_in_plane(pack, w, sem):
        pltpu.make_async_copy(pack.at[t], my_rows(w), sem.at[1]).start()
        for j in range(1, 8):
            t2 = (t + j) % 8
            remote(pack.at[t2], my_rows(w), sem.at[0], sem.at[1], t2 // 2, z * 2 + t2 % 2).start()

    def weights_across(w, sem):
        await_bytes(w.at[:, z], sem.at[1])
        for n in (1, 2, 3):
            remote(w.at[:, z], w.at[:, z], sem.at[2], sem.at[3], f, order_z(n, z) * 2 + x).start()

    def weights_near(w, sem, came):
        await_bytes(w.at[:, z], sem.at[1])
        for to_z in (inner + edge - z, other_inner):
            remote(w.at[:, z], w.at[:, z], sem.at[2], came.at[z], f, to_z * 2 + x).start()

    def weights_relay(w, sem, came):
        @pl.when(z == inner)
        def _():
            for from_z in (other_inner, 3 - edge):
                await_bytes(w.at[:, from_z], came.at[from_z])
                remote(w.at[:, from_z], w.at[:, from_z], sem.at[2], came.at[from_z], f, edge * 2 + x).start()

    def weights_done(w, came):
        @pl.when(z == inner)
        def _():
            await_bytes(w.at[:, edge], came.at[edge])

        @pl.when(z == edge)
        def _():
            for from_z in (inner, other_inner, 3 - edge):
                await_bytes(w.at[:, from_z], came.at[from_z])

    def weights_sent(w, sem):
        await_bytes(w.at[:, pl.ds(0, 2)], sem.at[2])

        @pl.when(z == inner)
        def _():
            await_bytes(w.at[:, pl.ds(0, 2)], sem.at[2])

    hop_beyond(tok, xx, x_recv, 0)
    hop(tok, xx, x_recv, 0)
    weights_in_plane(pack1, w1, w1_sem)

    @pl.when(f == seq)
    def _():
        pltpu.make_async_copy(pos, pos_v, pos_sem.at[1]).start()
        for j in range(1, 4):
            remote(pos, pos_v, pos_sem.at[0], pos_sem.at[1], (f + j) % 4, c).start()

    pltpu.make_async_copy(gains, gains_all.at[me], gain_sem.at[1]).start()

    def send_gains(j, carry):
        dev = (me + j) % 32
        remote(gains, gains_all.at[me], gain_sem.at[0], gain_sem.at[1], dev // 8, dev % 8).start()
        return carry

    lax.fori_loop(1, 32, send_gains, 0)
    relay(xx, x_recv, x_send, "o", 0)
    hop_on(xx, x_recv, 0)
    for k in range(8):
        pack2[k] = wo[:, k * 256 : k * 256 + 256]
        pack3[k, :, 0:384] = wg[:, k * 384 : k * 384 + 384]
        pack3[k, :, 384:768] = wu[:, k * 384 : k * 384 + 384]
    await_bytes(gains_all, gain_sem.at[1])
    one, two, gain_q, gain_k = gain_rows(gains_all)
    gain_s[...] = jnp.zeros_like(gain_s)
    gain_s[0:1, :] = one
    gain_s[1:2, :] = two
    gain_s[2:3, 0:128] = gain_q
    gain_s[3:4, 0:128] = gain_k
    await_bytes(pos_v, pos_sem.at[1])
    pos_copy = pltpu.make_async_copy(pos_v, pos_s, load.at[2])
    pos_copy.start()
    pos_copy.wait()
    rows_in_order(pos_s, ids_s, perm_s)

    def norm_piece(kind, n):
        chunk, part = whereof(kind, n)
        rows = pl.ds(pl.multiple_of(chunk * ROWS + part * half, half), half)
        hd[rows, :] = norm_rows(xx[rows, :], gain_s[0:1, :]).astype(BF16)

    def pieces(n, carry):
        for kind, late, skip in (("o", 0, 1), ("x", 1, 0), ("y", 1, 0), ("d", 3, 0)):

            @pl.when((n >= late) & (n < late + 4))
            def _():
                pl.when(n >= skip)(lambda: relay(xx, x_recv, x_send, kind, n - late))
                relay_wait(xx, x_recv, kind, n - late)
                norm_piece(kind, n - late)

        @pl.when(n == 1)
        def _():
            weights_across(w1, w1_sem)

        @pl.when(n == 2)
        def _():
            weights_in_plane(pack2, w2, w2_sem)

        @pl.when(n == 3)
        def _():
            weights_in_plane(pack3, w3, w3_sem)
            hop_beyond(cot, g_s, g_recv, 1)

        @pl.when(n == 4)
        def _():
            hop(cot, g_s, g_recv, 1)

        return carry

    lax.fori_loop(0, 7, pieces, 0)
    hop_on(g_s, g_recv, 1)
    h_copy = pltpu.make_async_copy(hd, h_out, load.at[1])
    h_copy.start()
    x_keep[...] = xx[pl.ds(pl.multiple_of(own * ROWS, ROWS), ROWS), :]

    t_down = me // 4
    down_rows = wd.at[pl.ds(pl.multiple_of((me % 4) * 96, 32), 96)]
    self_down = t_down == t
    table.wait()
    await_bytes(w1.at[pl.ds(0, 3)], w1_sem.at[3])

    def project(ch, carry):
        rows = pl.ds(pl.multiple_of(ch * ROWS, ROWS), ROWS)
        raw = dot_nn(hd[rows, :], w1[...].reshape(1024, 512))
        cos, sin = turns(jnp.concatenate([table_s[ids_s[ch * 2 + k]] for k in range(2)], axis=0))
        gq, gk = gain_s[2:3, 0:128], gain_s[3:4, 0:128]
        for k in range(2):
            cols = slice(k * 128, k * 128 + 128)
            put_two(mix_s, ch, cols, head_norm_rope(raw[:, cols], gq, cos, sin).astype(BF16))
        put_two(mix_s, ch, slice(256, 384), head_norm_rope(raw[:, 256:384], gk, cos, sin).astype(BF16))
        put_two(mix_s, ch, slice(384, 512), raw[:, 384:512].astype(BF16))
        return carry

    lax.fori_loop(0, 8, project, 0, unroll=2)
    weights_across(w2, w2_sem)

    def arrange(b, carry):
        for k in range(4):
            rows = pl.ds(pl.multiple_of(b * QROWS + k * 128, 128), 128)
            stored = perm_s[b * 4 + k]
            q_s[rows, :] = mix_s[stored, :, 0:256]
            k_s[rows, :] = mix_s[stored, :, 256:384]
            v_s[rows, :] = mix_s[stored, :, 384:512]
        vt[b] = v_s[pl.ds(pl.multiple_of(b * QROWS, QROWS), QROWS), :].T
        return carry

    lax.fori_loop(0, 4, arrange, 0)
    acc = keep.at[0]

    def query_tile(qt):
        def step(kt, diagonal):
            kb = k_s[pl.ds(pl.multiple_of(kt * QROWS, QROWS), QROWS), :]
            vb = vt[kt]
            for g in range(4):
                head, part = g // 2, g % 2
                qb = q_s[pl.ds(pl.multiple_of(qt * QROWS + part * 256, 256), 256), head * 128 : head * 128 + 128]
                depth = 256 * (part + 1) if diagonal else QROWS
                s = dot_nt(kb[:depth], qb)
                p = jnp.exp2(s * (SCALE * LOG2E))
                if diagonal:
                    ki = lax.broadcasted_iota(jnp.int32, (depth, 256), 0)
                    qi = lax.broadcasted_iota(jnp.int32, (depth, 256), 1) + part * 256
                    p = jnp.where(ki <= qi, p, 0.0)
                cols = slice(g * 256, g * 256 + 256)
                total[:, cols] += jnp.sum(p, axis=0, keepdims=True)
                acc[:, cols] += dot_nn(vb[:, :depth], p.astype(BF16))

        total[...] = jnp.zeros_like(total)
        acc[...] = jnp.zeros_like(acc)

        def off(kt, inner):
            step(kt, False)
            return inner

        lax.fori_loop(0, qt, off, 0)
        step(qt, True)
        sums = total[...]
        lse_s[qt] = jnp.log2(sums)
        out = acc[...] * (1.0 / sums)
        for g in range(4):
            head, part = g // 2, g % 2
            value = out[:, g * 256 : g * 256 + 256].T.astype(BF16)
            put_two(o_s, qt * 2 + part, slice(head * 128, head * 128 + 128), value)

    def query_tiles(qt, carry):
        query_tile(qt)

        @pl.when(qt == 2)
        def _():
            for n in range(4):
                relay(g_s, g_recv, g_send, "o", n)
            weights_near(w3, w3_sem, w3_came)

        return carry

    lax.fori_loop(0, 4, query_tiles, 0)
    for k in range(4):
        here = self_down & (z == k)

        @pl.when(here)
        def _():
            pltpu.make_async_copy(wd_own, down_rows, wd_sem.at[1]).start()

        @pl.when(jnp.logical_not(here))
        def _():
            remote(wd_own, down_rows, wd_sem.at[0], wd_sem.at[1], t_down // 2, k * 2 + t_down % 2).start()

    await_bytes(w2.at[pl.ds(0, 3)], w2_sem.at[3])
    relay_done(xx, x_send)
    h_copy.wait()

    def attention_term(chunk):
        rows = jnp.concatenate([o_s[ids_s[chunk * 2 + k]] for k in range(2)], axis=0)
        return dot_nt(rows, w2[...].reshape(1024, 256))

    split_sum(attention_term, core_out, from_core, out_buf, in_buf, keep, send, core_recv, recv)
    for n in range(4):
        relay(g_s, g_recv, g_send, "x", n)
        relay(g_s, g_recv, g_send, "y", n)
    weights_relay(w3, w3_sem, w3_came)
    low, high = split_sum_end(in_buf, keep, recv)
    gain_one, gain_two = gain_s[0:1, :], gain_s[1:2, :]
    mid[0:half, :] = x_keep[0:half, :].astype(F32) + low
    mid[half:ROWS, :] = x_keep[half:ROWS, :].astype(F32) + high
    xx[pl.ds(pl.multiple_of(own * ROWS, ROWS), ROWS), :] = norm_rows(mid[...], gain_two).astype(BF16)

    def gather_start(every, sem, core_sem):
        for part in (0, 1):
            a, b = piece(every, own, part), piece(every, own, 1 - part)
            remote(a, a, ag_send.at[0], sem.at[part], f, z * 2 + 1 - x).start()
            remote(b, b, ag_send.at[1], sem.at[2 + 1 - part], (1 - y) * 2 + core, c).start()
        for part in (0, 1):
            a = piece(every, own, part)
            remote(a, a, ag_send.at[2], core_sem.at[part], y * 2 + 1 - core, c).start()

    def gather_step(every, sem, core_sem, r, part):
        a = piece(every, chunk_of(r, core), part)
        k = (r - 1) * 2 + part
        await_bytes(a, sem.at[k])
        if r == 1 and part == 0:
            remote(a, a, ag_send.at[1], sem.at[4], (1 - y) * 2 + core, c).start()
        if r == 2 and part == 1:
            remote(a, a, ag_send.at[0], sem.at[5], f, z * 2 + 1 - x).start()
        remote(a, a, ag_send.at[2], core_sem.at[2 * r + part], y * 2 + 1 - core, c).start()

    def gather_core(every, core_sem, r):
        for part in (0, 1):
            await_bytes(piece(every, chunk_of(r, 1 - core), part), core_sem.at[2 * r + part])

    def gather_sent(every):
        await_bytes(every.at[pl.ds(0, 3 * half)], ag_send.at[0])
        await_bytes(every.at[pl.ds(0, 3 * half)], ag_send.at[1])
        await_bytes(every.at[pl.ds(0, 8 * half)], ag_send.at[2])

    hop_done(0)
    hop_done(1)
    gather_start(xx, ag_recv, ag_core)
    split_sum_sent(from_core, out_buf, send)
    def feed_forward(chunk, carry):
        rows = pl.ds(pl.multiple_of(chunk * ROWS, ROWS), ROWS)
        gu = dot_nn(xx[rows, :], w3[...].reshape(1024, 768))
        gate, up = gu[:, 0:384], gu[:, 384:768]
        sig = 1.0 / (1.0 + jnp.exp(-gate))
        sil = gate * sig
        act_s[rows, :] = (sil * up).astype(BF16)
        put_two(mix_s, chunk, slice(0, 384), (up * sig * (1.0 + gate * (1.0 - sig))).astype(BF16))
        put_two(mix_s, chunk, slice(384, 768), sil.astype(BF16))
        return carry

    def feed_terms(chunk):
        rows = pl.ds(pl.multiple_of(chunk * ROWS, ROWS), ROWS)
        layer = dot_nn(act_s[rows, :], wd[...]).astype(BF16)
        dact = dot_nt(g_s[rows, :], wd[...])
        for cols in (slice(0, 384), slice(384, 768)):
            put_two(mix_s, chunk, cols, (dact * two_blocks(mix_s, chunk, cols).astype(F32)).astype(BF16))
        return layer, dot_nt(two_blocks(mix_s, chunk, slice(0, 768)), w3[...].reshape(1024, 768))

    def feed_back(n, carry):
        r = turn_of(n)
        slot = n % 2
        layer, dh = feed_terms(chunk_at(r, 1 - core))

        @pl.when(n >= 2)
        def _():
            await_bytes(core_out2.at[slot], send2.at[slot])

        core_out2[slot] = layer
        remote(core_out2.at[slot], from_core2.at[r], send2.at[slot], core_recv2.at[r], other_core, c).start()
        core_out[r] = dh.astype(BF16)
        remote(core_out.at[r], from_core.at[r], send.at[6], core_recv.at[r], other_core, c).start()
        layer, dh = feed_terms(chunk_at(r, core))
        lpart[r] = layer
        await_bytes(from_core.at[r], core_recv.at[r])
        split_step(n, dh + from_core[r].astype(F32), out_buf, in_buf, keep, send, recv_d)
        return carry

    gather_core(xx, ag_core, 0)
    weights_done(w3, w3_came)
    lax.fori_loop(0, 2, lambda n, carry: feed_forward(chunk_at(0, n), carry), 0)
    gather_step(xx, ag_recv, ag_core, 1, 0)
    gather_step(xx, ag_recv, ag_core, 2, 1)
    gather_step(xx, ag_recv, ag_core, 1, 1)
    gather_step(xx, ag_recv, ag_core, 2, 0)
    lax.fori_loop(1, 3, lambda r, carry: feed_forward(chunk_at(r, core), carry), 0)
    gather_core(xx, ag_core, 1)
    gather_core(xx, ag_core, 2)
    lax.fori_loop(1, 3, lambda r, carry: feed_forward(chunk_at(r, 1 - core), carry), 0)
    for n in range(4):
        relay(g_s, g_recv, g_send, "d", n)
    gather_step(xx, ag_recv, ag_core, 3, 0)
    gather_step(xx, ag_recv, ag_core, 3, 1)
    gather_core(xx, ag_core, 3)
    lax.fori_loop(0, 2, lambda n, carry: feed_forward(chunk_at(3, n), carry), 0)
    for kind, n in PIECES:
        relay_wait(g_s, g_recv, kind, n)
    in_half = upper == x
    held = 2 - 2 * ((upper + x) % 2)

    def down_unit(e):
        return rdz.at[held + e]

    def down_near():
        @pl.when(in_half)
        def _():
            to_z = inner + edge - z
            remote(down_unit(to_z % 2), rdz.at[0], dz_sem.at[0], dz_came.at[0], f, to_z * 2 + x).start()

        @pl.when(jnp.logical_not(in_half) & (z == edge))
        def _():
            for e in range(2):
                remote(down_unit(e), rdz.at[2 + e], dz_sem.at[0], dz_came.at[2 + e], f, inner * 2 + x).start()

    def down_relay():
        @pl.when(jnp.logical_not(in_half) & (z == inner))
        def _():
            for e in range(2):
                await_bytes(rdz.at[2 + e], dz_came.at[2 + e])
                rdz[e] = (rdz[e].astype(F32) + rdz[2 + e].astype(F32)).astype(BF16)
                remote(down_unit(e), rdz.at[1], dz_sem.at[0], dz_came.at[1], f, (2 * x + e) * 2 + x).start()

    def down_end():
        @pl.when(in_half)
        def _():
            for n in range(2):
                await_bytes(rdz.at[n], dz_came.at[n])
            mine = z % 2
            total = rdz[2 + mine].astype(F32) + rdz[0].astype(F32) + rdz[1].astype(F32)
            rdz[2 + mine] = total.astype(BF16)
            here = rdz.at[2 + mine, pl.ds(pl.multiple_of(x * 96, 32), 96)]
            there = rdz.at[2 + mine, pl.ds(pl.multiple_of((1 - x) * 96, 32), 96)]
            pltpu.make_async_copy(here, rd, d_sem.at[1]).start()
            remote(there, rd, d_sem.at[0], d_sem.at[1], f, other_x).start()

    def down_done():
        await_bytes(rd, d_sem.at[1])

        @pl.when(in_half)
        def _():
            await_bytes(rd, d_sem.at[0])
            await_bytes(rdz.at[0], dz_sem.at[0])

        @pl.when(jnp.logical_not(in_half))
        def _():
            await_bytes(rdz.at[pl.ds(0, 2)], dz_sem.at[0])

    for b in range(3):
        block = dot_tn(act_s[:, b * 128 : b * 128 + 128], g_s[...]).astype(BF16)
        for k in range(2):
            low, high = max(b * 128, k * 192), min(b * 128 + 128, k * 192 + 192)
            if low < high:
                rdz[held + k, low - k * 192 : high - k * 192, :] = block[low - b * 128 : high - b * 128]
    down_near()
    await_bytes(wd, wd_sem.at[1])
    lax.fori_loop(0, 4, feed_back, 0)

    def scatter_rows(g, b, block, first, width):
        for k in range(4):
            g[k, pl.ds(pl.multiple_of(b * 64, 64), 64), first : first + width] = block[k * 64 : k * 64 + 64].astype(BF16)

    def across(g, r_, sem):
        pltpu.make_async_copy(g.at[z], r_.at[z], sem.at[1]).start()
        for n in (3, 2, 1):
            z2 = order_z(n, z)
            remote(g.at[z2], r_.at[z], sem.at[0], sem.at[1], f, z2 * 2 + x).start()

    def across_near(g, r_, sem, came):
        @pl.when(z == edge)
        def _():
            for e in range(2):
                remote(
                    g.at[2 * (1 - upper) + e], r_.at[2 + e], sem.at[0], came.at[2 + e], f, inner * 2 + x
                ).start()

        remote(
            g.at[inner + edge - z], r_.at[upper], sem.at[0], came.at[upper], f, (inner + edge - z) * 2 + x
        ).start()

    def across_relay(g, r_, sem, came):
        @pl.when(z == inner)
        def _():
            for e in range(2):
                to_z = 2 * (1 - upper) + e
                await_bytes(r_.at[2 + e], came.at[2 + e])
                g[to_z] = (g[to_z].astype(F32) + r_[2 + e].astype(F32)).astype(BF16)
                remote(g.at[to_z], r_.at[upper], sem.at[0], came.at[upper], f, to_z * 2 + x).start()

    def across_sent(g, sem):
        await_bytes(g.at[pl.ds(0, 3)], sem.at[0])

    def to_plane(s_, p_, plane_sem):
        pltpu.make_async_copy(s_.at[pl.ds(pl.multiple_of(t * 32, 32), 32)], p_.at[t], plane_sem.at[1]).start()
        for j in range(1, 8):
            t2 = (t + j) % 8
            block = s_.at[pl.ds(pl.multiple_of(t2 * 32, 32), 32)]
            remote(block, p_.at[t], plane_sem.at[0], plane_sem.at[1], t2 // 2, z * 2 + t2 % 2).start()

    def in_plane(r_, s_, p_, sem, plane_sem):
        await_bytes(r_, sem.at[1])
        s_[...] = (r_[0].astype(F32) + r_[1].astype(F32) + r_[2].astype(F32) + r_[3].astype(F32)).astype(BF16)
        to_plane(s_, p_, plane_sem)

    def in_plane_near(g, r_, s_, p_, came, plane_sem):
        for k in range(2):
            await_bytes(r_.at[k], came.at[k])
        s_[...] = (g[z].astype(F32) + r_[0].astype(F32) + r_[1].astype(F32)).astype(BF16)
        to_plane(s_, p_, plane_sem)

    def columns(ref, b):
        return ref[:, pl.ds(pl.multiple_of(b * 256, 256), 256)]

    def grad_f(b, carry):
        scatter_rows(gf, b, dot_tn(columns(xx, b), mix_s[...].reshape(2048, 768)), 0, 768)
        return carry

    lax.fori_loop(0, 4, grad_f, 0)
    across_near(gf, rf, f_sem, f_came)
    await_bytes(from_core, send.at[6])
    gather_sent(xx)
    h_load = pltpu.make_async_copy(h_out, xx, load.at[3])
    h_load.start()

    sums = split_sum_end(in_buf, keep, recv_d)
    small[...] = jnp.zeros_like(small)
    for part in (0, 1):
        rows = slice(part * half, part * half + half)
        back, dgain = norm_back(mid[rows, :], gain_two, sums[part])
        first = pl.multiple_of(own * ROWS + part * half, half)
        dm = g_s[pl.ds(first, half), :].astype(F32) + back
        hd[pl.ds(first, half), :] = dm.astype(BF16)
        small[1:2, :] += jnp.sum(dgain, axis=0, keepdims=True)
    gather_start(hd, ag_recv2, ag_core2)
    down_relay()
    for k in range(6):
        await_bytes(out_buf.at[k], send.at[k])
    def key_columns(b, carry):
        vt[b] = k_s[pl.ds(pl.multiple_of(b * QROWS, QROWS), QROWS), :].T
        return carry

    lax.fori_loop(0, 4, key_columns, 0)

    def back_out(r, same):
        chunk = chunk_of(r, core if same else 1 - core)
        rows = pl.ds(pl.multiple_of(chunk * ROWS, ROWS), ROWS)
        put_two(mix_s, chunk, slice(512, 768), dot_nn(hd[rows, :], w2[...].reshape(1024, 256)).astype(BF16))

    back_out(0, True)
    gather_step(hd, ag_recv2, ag_core2, 1, 0)
    gather_step(hd, ag_recv2, ag_core2, 2, 1)
    gather_core(hd, ag_core2, 0)
    back_out(0, False)
    gather_step(hd, ag_recv2, ag_core2, 1, 1)
    gather_step(hd, ag_recv2, ag_core2, 2, 0)
    back_out(1, True)
    back_out(2, True)
    gather_core(hd, ag_core2, 1)
    back_out(1, False)
    gather_core(hd, ag_core2, 2)
    back_out(2, False)
    gather_step(hd, ag_recv2, ag_core2, 3, 0)
    gather_step(hd, ag_recv2, ag_core2, 3, 1)
    back_out(3, True)
    gather_core(hd, ag_core2, 3)
    back_out(3, False)

    home_f, home_c = plane_of(z), own
    stays = (home_f == f) & (home_c == c)

    beyond_c = (core * 2 + 1 - y) * 2 + x
    beyond_stays = (home_f == other_y) & (beyond_c == c)

    def deliver(low, high, dst, k):
        to_low, to_high = dst.at[pl.ds(0, half)], dst.at[pl.ds(half, half)]

        @pl.when(jnp.logical_not(stays))
        def _():
            remote(high, stage.at[k], out_sem.at[5 * k], out_sem.at[5 * k + 1], other_y, c).start()
            remote(low, to_low, out_sem.at[5 * k + 2], out_sem.at[5 * k + 3], home_f, home_c).start()

        @pl.when(stays)
        def _():
            pltpu.make_async_copy(low, to_low, out_sem.at[5 * k + 3]).start()
            pltpu.make_async_copy(high, to_high, out_sem.at[5 * k + 4]).start()

    def deliver_whole(low, high, dst):
        for part, src in ((0, low), (1, high)):
            to = dst.at[pl.ds(part * half, half)]

            @pl.when(jnp.logical_not(stays))
            def _():
                remote(src, to, out_sem.at[5 + part], out_sem.at[7 + part], home_f, home_c).start()

            @pl.when(stays)
            def _():
                pltpu.make_async_copy(src, to, out_sem.at[7 + part]).start()

    def deliver_whole_done(dst):
        for part in (0, 1):
            await_bytes(dst.at[pl.ds(part * half, half)], out_sem.at[7 + part])

            @pl.when(jnp.logical_not(stays))
            def _():
                await_bytes(stage.at[0], out_sem.at[5 + part])

    def deliver_on(dst, k):
        @pl.when(jnp.logical_not(beyond_stays))
        def _():
            await_bytes(stage.at[k], out_sem.at[5 * k + 1])
            remote(
                stage.at[k], dst.at[pl.ds(half, half)], home_send.at[k], out_sem.at[5 * k + 4], home_f, beyond_c
            ).start()

    def deliver_done(dst, k):
        await_bytes(dst.at[pl.ds(0, half)], out_sem.at[5 * k + 3])
        await_bytes(dst.at[pl.ds(half, half)], out_sem.at[5 * k + 4])

        @pl.when(jnp.logical_not(stays))
        def _():
            await_bytes(stage.at[k], out_sem.at[5 * k])
            await_bytes(stage.at[k], out_sem.at[5 * k + 2])

        @pl.when(jnp.logical_not(beyond_stays))
        def _():
            await_bytes(stage.at[k], home_send.at[k])

    def layer_over_x(src, n):
        remote(src, in_buf2.at[n], send2.at[2 + n], recv2.at[n], f, other_x).start()

    def layer_over_y(src, n):
        remote(src, in_buf2.at[n], send2.at[2 + n], recv2.at[n], other_y, c).start()

    low_half, high_half = pl.ds(0, half), pl.ds(half, half)

    def layer_to_chips():
        for r in (3, 1, 2):
            await_bytes(from_core2.at[r], core_recv2.at[r])
            lpart[r] = (lpart[r].astype(F32) + from_core2[r].astype(F32)).astype(BF16)
            if r & 1:
                layer_over_x(lpart.at[r, low_half], 0 if r == 3 else 2)
            if r & 2:
                layer_over_y(lpart.at[r, high_half], 1 if r == 3 else 3)

    def layer_relay():
        await_bytes(in_buf2.at[0], recv2.at[0])
        lpart[2, 0:half] = (lpart[2, 0:half].astype(F32) + in_buf2[0].astype(F32)).astype(BF16)
        layer_over_y(lpart.at[2, low_half], 5)
        await_bytes(in_buf2.at[1], recv2.at[1])
        lpart[1, half:ROWS] = (lpart[1, half:ROWS].astype(F32) + in_buf2[1].astype(F32)).astype(BF16)
        layer_over_x(lpart.at[1, high_half], 4)

    def layer_end():
        await_bytes(from_core2.at[0], core_recv2.at[0])
        for n in (2, 3, 4, 5):
            await_bytes(in_buf2.at[n], recv2.at[n])
        for part in (0, 1):
            rows = slice(part * half, part * half + half)
            value = mid[rows, :] + lpart[0, rows].astype(F32) + from_core2[0, rows].astype(F32)
            value = value + in_buf2[2 + part].astype(F32) + in_buf2[5 - part].astype(F32)
            in_buf2[part] = value.astype(BF16)
        deliver(in_buf2.at[0], in_buf2.at[1], layer_out, 0)

    layer_to_chips()
    across_relay(gf, rf, f_sem, f_came)

    def prepare(b, carry):
        rows = pl.ds(pl.multiple_of(b * QROWS, QROWS), QROWS)
        do = jnp.concatenate(
            [mix_s[perm_s[b * 4 + k], :, 512:768] for k in range(4)], axis=0
        )
        act_s[rows, 0:256] = do
        ones = jnp.ones((8, 128), BF16)
        for head in range(2):
            cols = slice(head * 128, head * 128 + 128)
            prod = do[:, cols].astype(F32) * o_s[pl.ds(b * 4, 4), :, cols].reshape(QROWS, 128).astype(F32)
            high = prod.astype(BF16)
            low = (prod - high.astype(F32)).astype(BF16)
            delta = dot_nt(ones, high) + dot_nt(ones, low)
            delta_s[b, :, head * QROWS : head * QROWS + QROWS] = delta[0:1]
        return carry

    lax.fori_loop(0, 4, prepare, 0)
    def stored(b, carry):
        mix_s[b, :, 0:256] = o_s[ids_s[b]]
        return carry

    lax.fori_loop(0, 16, stored, 0)

    def grad_o(b, carry):
        scatter_rows(go, b, dot_tn(columns(hd, b), mix_s[:, :, 0:256].reshape(2048, 256)), 0, 256)
        return carry

    lax.fori_loop(0, 4, grad_o, 0)
    across(go, ro, o_sem)
    dqt_s[...] = jnp.zeros_like(dqt_s)
    dk_s[...] = jnp.zeros_like(dk_s)
    dv_s[...] = jnp.zeros_like(dv_s)

    def key_tile(kt):
        krows = pl.ds(pl.multiple_of(kt * QROWS, QROWS), QROWS)

        def step(qt, diagonal):
            kb, vb, ktb = k_s[krows, :], v_s[krows, :], vt[kt]
            for g in range(4):
                head, part = g // 2, g % 2
                start = pl.multiple_of(qt * QROWS + part * 256, 256)
                cols = slice(head * 128, head * 128 + 128)
                lanes = slice(g * 256, g * 256 + 256)
                qb = q_s[pl.ds(start, 256), cols]
                dob = act_s[pl.ds(start, 256), cols]
                depth = 256 * (part + 1) if diagonal else QROWS
                s = dot_nt(kb[:depth], qb)
                p = jnp.exp2(s * (SCALE * LOG2E) - lse_s[qt, :, lanes])
                if diagonal:
                    ki = lax.broadcasted_iota(jnp.int32, (depth, 256), 0)
                    qi = lax.broadcasted_iota(jnp.int32, (depth, 256), 1) + part * 256
                    p = jnp.where(ki <= qi, p, 0.0)
                dp = dot_nt(vb[:depth], dob)
                ds = (p * (dp - delta_s[qt, :, lanes])).astype(BF16)
                out = pl.ds(kt * 4, depth // 128)
                dv_s[out] += dot_nn(p.astype(BF16), dob).reshape(depth // 128, 128, 128)
                dk_s[out] += dot_nn(ds, qb).reshape(depth // 128, 128, 128)
                dq = dot_nn(ktb[:, :depth], ds)
                dqt_s[qt * 4 + part * 2, cols, :] += dq[:, 0:128]
                dqt_s[qt * 4 + part * 2 + 1, cols, :] += dq[:, 128:256]

        step(kt, True)

        def off(qt, inner):
            step(qt, False)
            return inner

        lax.fori_loop(kt + 1, 4, off, 0)

    def key_tiles(kt, carry):
        key_tile(kt)

        @pl.when(kt == 0)
        def _():
            layer_relay()

        return carry

    lax.fori_loop(0, 4, key_tiles, 0)
    layer_end()
    h_load.wait()

    def finish_chunk(chunk, carry):
        rows = pl.ds(pl.multiple_of(chunk * ROWS, ROWS), ROWS)
        places = [ids_s[chunk * 2 + k] for k in range(2)]
        cos, sin = turns(jnp.concatenate([table_s[b] for b in places], axis=0))
        raw = dot_nn(xx[rows, :], w1[:, :, :, 0:384].reshape(1024, 384))
        for head in range(3):
            cols = slice(head * 128, head * 128 + 128)
            if head < 2:
                blocks = [dqt_s[b, cols, :].T for b in places]
                gain, lanes = gain_s[2:3, 0:128], slice(0, 128)
            else:
                blocks = [dk_s[b] for b in places]
                gain, lanes = gain_s[3:4, 0:128], slice(128, 256)
            d = jnp.concatenate(blocks, axis=0) * SCALE
            back, dgain = norm_back(raw[:, cols], gain, unturn(d, cos, sin))
            put_two(mix_s, chunk, cols, back.astype(BF16))
            small[2:3, lanes] += jnp.sum(dgain, axis=0, keepdims=True)
        for k in range(2):
            mix_s[chunk * 2 + k, :, 384:512] = dv_s[places[k]].astype(BF16)
        return carry

    def partial(chunk):
        return dot_nt(two_blocks(mix_s, chunk, slice(0, 512)), w1[...].reshape(1024, 512))

    gather_sent(hd)
    lax.fori_loop(0, 8, finish_chunk, 0)
    def grad_a(b, carry):
        scatter_rows(ga, b, dot_tn(columns(xx, b), mix_s[:, :, 0:512].reshape(2048, 512)), 0, 512)
        return carry

    lax.fori_loop(0, 4, grad_a, 0)
    across_near(ga, ra, a_sem, a_came)
    in_plane_near(gf, rf, sf, pf, f_came, fp_sem)
    down_end()
    in_plane(ro, so, po, o_sem, op_sem)
    split_sum(partial, core_out, from_core, out_buf, in_buf, keep, send, core_recv, recv)
    deliver_on(layer_out, 0)
    across_relay(ga, ra, a_sem, a_came)
    low, high = split_sum_end(in_buf, keep, recv)
    for part, dh in ((0, low), (1, high)):
        rows = slice(part * half, part * half + half)
        back, dgain = norm_back(x_keep[rows, :].astype(F32), gain_one, dh)
        dm = hd[pl.ds(pl.multiple_of(own * ROWS + part * half, half), half), :].astype(F32)
        in_buf2[2 + part] = (dm + back).astype(BF16)
        small[0:1, :] += jnp.sum(dgain, axis=0, keepdims=True)
    s_in[t] = small[...]
    for j in range(1, 8):
        t2 = (t + j) % 8
        remote(small, s_in.at[t], s_sem.at[0], s_sem.at[1], t2 // 2, z * 2 + t2 % 2).start()
    deliver_whole(in_buf2.at[2], in_buf2.at[3], grad_tokens)

    await_bytes(pf, fp_sem.at[1])
    await_bytes(po, op_sem.at[1])
    await_bytes(s_in.at[pl.ds(0, 7)], s_sem.at[1])
    sbuf[...] = jnp.sum(s_in[...], axis=0)
    p_in[z] = sbuf[...]
    for j in range(1, 4):
        remote(sbuf, p_in.at[z], p_sem.at[0], p_sem.at[1], f, ((z + j) % 4) * 2 + x).start()
    in_plane_near(ga, ra, sa, pa, a_came, ap_sem)
    await_bytes(p_in.at[pl.ds(0, 3)], p_sem.at[1])
    small_out[...] = jnp.sum(p_in[...], axis=0)
    await_bytes(pa, ap_sem.at[1])

    deliver_done(layer_out, 0)
    deliver_whole_done(grad_tokens)
    split_sum_sent(from_core, out_buf, send)
    for k in range(2):
        await_bytes(core_out2.at[k], send2.at[k])
    for n in range(6):
        await_bytes(in_buf2.at[n], send2.at[2 + n])
    await_bytes(s_in.at[pl.ds(0, 7)], s_sem.at[0])
    await_bytes(p_in.at[pl.ds(0, 3)], p_sem.at[0])
    down_done()
    across_sent(gf, f_sem)
    await_bytes(go.at[pl.ds(0, 3)], o_sem.at[0])
    await_bytes(ra.at[pl.ds(0, 3)], a_sem.at[0])
    await_bytes(pf.at[pl.ds(0, 7)], fp_sem.at[0])
    await_bytes(po.at[pl.ds(0, 7)], op_sem.at[0])
    await_bytes(pa.at[pl.ds(0, 7)], ap_sem.at[0])
    relay_done(g_s, g_send)

    @pl.when(f == seq)
    def _():
        for _ in range(3):
            await_bytes(pos_v, pos_sem.at[0])

    await_bytes(gains_all.at[pl.ds(0, 31)], gain_sem.at[0])
    for pack, sem in ((pack1, w1_sem), (pack2, w2_sem), (pack3, w3_sem)):
        await_bytes(pack.at[pl.ds(0, 7)], sem.at[0])
    await_bytes(w1.at[pl.ds(0, 3)], w1_sem.at[2])
    await_bytes(w2.at[pl.ds(0, 3)], w2_sem.at[2])
    weights_sent(w3, w3_sem)
    for k in range(4):

        @pl.when(jnp.logical_not(self_down & (z == k)))
        def _():
            await_bytes(wd_own, wd_sem.at[0])


def layer(*operands):
    any_spec, vmem = pl.BlockSpec(memory_space=pl.ANY), pl.BlockSpec(memory_space=pltpu.VMEM)
    half = ROWS // 2
    bf = lambda *shape: pltpu.VMEM(shape, BF16)
    fl = lambda *shape: pltpu.VMEM(shape, F32)
    out = lambda kind, *shape: jax.ShapeDtypeStruct(shape, kind)
    copies = (
        16, 16, 2, 6, 3, 3, 2, 2, 4, 4, 3, 4, 2,
        4, 3, 6, 8, 6, 8, 7, 4, 6, 6, 8, 4, 6,
        2, 1, 4, 2, 1, 4, 1, 4, 2, 2, 2, 2, 10, 2, 2,
    )
    return pl.pallas_call(
        layer_kernel,
        out_shape=(
            out(BF16, ROWS, 1024), out(BF16, ROWS, 1024), out(BF16, 8, 32, 768), out(BF16, 8, 32, 256),
            out(BF16, 8, 32, 512), out(BF16, 96, 1024), out(BF16, 2048, 1024), out(F32, 8, 1024),
        ),
        in_specs=[any_spec] * 3 + [vmem] * 6 + [any_spec] * 3,
        out_specs=(any_spec,) * 7 + (vmem,),
        scratch_shapes=[
            bf(2048, 1024), bf(2048, 1024), bf(2048, 1024), bf(4, 4, 64, 512), bf(4, 4, 64, 256), bf(4, 4, 64, 768),
            bf(384, 1024), bf(8, 32, 512), bf(8, 32, 256), bf(8, 32, 768), fl(32, 1, 128), fl(16, 128, 128),
            fl(8, 1024),
            bf(2048, 256), bf(2048, 128), bf(2048, 128), bf(16, 128, 256), bf(4, 128, QROWS),
            fl(1, 1024), fl(4, 1, 1024), bf(ROWS, 1024), fl(ROWS, 1024),
            bf(16, 128, 768), bf(2048, 384), fl(4, 1, 1024), fl(16, 256, 128), fl(16, 128, 128), fl(16, 128, 128),
            fl(8, 1024),
            bf(4, ROWS, 1024), bf(4, ROWS, 1024), bf(6, half, 1024), bf(6, half, 1024), fl(2, half, 1024),
            bf(4, ROWS, 1024), bf(2, ROWS, 1024), bf(4, ROWS, 1024), bf(6, half, 1024),
            bf(4, 256, 768), bf(4, 256, 256), bf(4, 256, 512), bf(4, 192, 1024), bf(4, 256, 768), bf(4, 256, 256), bf(4, 256, 512),
            bf(256, 768), bf(256, 256), bf(256, 512), fl(8, 8, 1024), fl(8, 1024), fl(4, 8, 1024),
            bf(2, half, 1024), pltpu.VMEM((1, 2048), jnp.int32), pltpu.SMEM((1, 2048), jnp.int32),
            pltpu.SMEM((16,), jnp.int32), pltpu.SMEM((16,), jnp.int32),
        ]
        + [pltpu.SemaphoreType.DMA((count,)) for count in copies],
        compiler_params=pltpu.CompilerParams(collective_id=0, has_side_effects=True, vmem_limit_bytes=VMEM_LIMIT),
        name="layer",
    )(*operands)


def outputs_kernel(
    layer, tok, pf, po, pa, rd, small, o_l, o_t, o_q, o_k, o_v, o_o, o_g, o_u, o_d, o_first, o_second, o_head
):
    me = lax.axis_index("fsdp") * 8 + lax.axis_index("ctx")
    o_l[...] = layer[...]
    o_t[...] = tok[...]
    for k in range(8):
        wide, thin, third = (slice(k * w, k * w + w) for w in (256, 128, 384))
        o_g[:, third] = pf[k, :, 0:384].astype(F32)
        o_u[:, third] = pf[k, :, 384:768].astype(F32)
        o_o[:, wide] = po[k].astype(F32)
        o_q[:, wide] = pa[k, :, 0:256].astype(F32)
        o_k[:, thin] = pa[k, :, 256:384].astype(F32)
        o_v[:, thin] = pa[k, :, 384:512].astype(F32)
    o_d[...] = rd[...].astype(F32)
    turned = pltpu.roll(small[...], (1024 - 32 * me) % 1024, 1)
    o_first[...] = turned[0:1, 0:32]
    o_second[...] = turned[1:2, 0:32]
    turned = pltpu.roll(small[...], (1024 - 8 * me) % 1024, 1)
    o_head[...] = turned[2:3, 0:8]


def outputs(*came):
    vmem = pl.BlockSpec(memory_space=pltpu.VMEM)
    out = lambda kind, *shape: jax.ShapeDtypeStruct(shape, kind)
    return pl.pallas_call(
        outputs_kernel,
        out_shape=(
            out(BF16, ROWS, 1024), out(BF16, ROWS, 1024), out(F32, 32, 2048), out(F32, 32, 1024), out(F32, 32, 1024),
            out(F32, 32, 2048), out(F32, 32, 3072), out(F32, 32, 3072), out(F32, 96, 1024), out(F32, 1, 32),
            out(F32, 1, 32), out(F32, 1, 8),
        ),
        in_specs=[vmem] * 7,
        out_specs=(vmem,) * 12,
        compiler_params=pltpu.CompilerParams(vmem_limit_bytes=VMEM_LIMIT),
        name="outputs",
    )(*came)


def rope_table(length):
    inverse = 1000000.0 ** (-2.0 * np.arange(HEAD_DIM // 2, dtype=np.float64) / HEAD_DIM)
    angles = np.arange(length, dtype=np.float32)[:, None] * inverse.astype(np.float32)[None, :]
    angles = angles.astype(np.float64)
    return np.concatenate([np.cos(angles), np.sin(angles)], axis=1).astype(np.float32)


def per_device_planes(
    tokens, positions, w_query, w_key, w_value, w_output, w_gate, w_up, w_down, first_gain, second_gain, head_gain,
    cotangent,
):
    gains = jnp.concatenate([first_gain, second_gain, head_gain, jnp.zeros((56,), BF16)]).astype(F32)[None]
    table = jnp.asarray(rope_table(2048)).reshape(16, 128, HEAD_DIM)
    layer_out, grad_tokens, pf, po, pa, rd, _, small = layer(
        tokens[0], cotangent[0], positions, w_query, w_key, w_value, w_output.T, w_gate, w_up, w_down, gains, table
    )
    layer_out, grad_tokens, o_q, o_k, o_v, o_o, o_g, o_u, o_d, o_first, o_second, o_head = outputs(
        layer_out, grad_tokens, pf, po, pa, rd, small
    )
    return (
        layer_out[None],
        grad_tokens[None],
        o_q,
        o_k,
        o_v,
        o_o.T,
        o_g,
        o_u,
        o_d,
        o_first[0],
        o_second[0],
        o_head[0],
    )


def solution(mesh):
    planes = mesh.shape["fsdp"] == 4 and mesh.shape["ctx"] == 8
    body = per_device_planes if planes else per_device
    return jax.shard_map(
        body,
        mesh=mesh,
        in_specs=(
            P("fsdp", "ctx", None),
            P("fsdp", None),
            P(("fsdp", "ctx"), None),
            P(("fsdp", "ctx"), None),
            P(("fsdp", "ctx"), None),
            P(None, ("fsdp", "ctx")),
            P(("fsdp", "ctx"), None),
            P(("fsdp", "ctx"), None),
            P(("fsdp", "ctx"), None),
            P(("fsdp", "ctx")),
            P(("fsdp", "ctx")),
            P(("fsdp", "ctx")),
            P("fsdp", "ctx", None),
        ),
        out_specs=(
            P("fsdp", "ctx", None),
            P("fsdp", "ctx", None),
            P(("fsdp", "ctx"), None),
            P(("fsdp", "ctx"), None),
            P(("fsdp", "ctx"), None),
            P(None, ("fsdp", "ctx")),
            P(("fsdp", "ctx"), None),
            P(("fsdp", "ctx"), None),
            P(("fsdp", "ctx"), None),
            P(("fsdp", "ctx")),
            P(("fsdp", "ctx")),
            P(("fsdp", "ctx")),
        ),
        check_vma=False,
    )
```

```python
from functools import partial

import jax
import jax.numpy as jnp
import numpy as np
from jax import lax
from jax.experimental import pallas as pl
from jax.experimental.pallas import tpu as pltpu
from jax.sharding import PartitionSpec as P

MESH = pl.DeviceIdType.MESH

HEADS = 16
KV_HEADS = 8
HEAD_DIM = 128


def normed(operand, gain_in):
    return (
        operand * lax.rsqrt(jnp.mean(operand * operand, axis=-1, keepdims=True) + 1e-06) * gain_in
    )


def rotary(operand, places):
    head_width = operand.shape[-1]
    half_width = head_width // 2
    inverse = 1000000.0 ** (-2.0 * jnp.arange(half_width, dtype=jnp.float32) / head_width)
    angles = places.astype(jnp.float32)[:, None] * inverse[None, :]
    cosine = jnp.concatenate([jnp.cos(angles), jnp.cos(angles)], axis=-1)[:, None, :]
    sine_table = jnp.concatenate([jnp.sin(angles), jnp.sin(angles)], axis=-1)[:, None, :]
    turned = jnp.concatenate([-operand[..., half_width:], operand[..., :half_width]], axis=-1)
    return operand * cosine + turned * sine_table


def head_prep(raw_proj, gain_in, places, head_count):
    row_count = raw_proj.shape[0]
    shaped = raw_proj.reshape(row_count, head_count, HEAD_DIM)
    return rotary(normed(shaped, gain_in), places).reshape(row_count, head_count * HEAD_DIM)


def gated(gate_raw, up_raw):
    return jax.nn.silu(gate_raw) * up_raw


def project(left_side, right_side):
    return jnp.dot(left_side, right_side, preferred_element_type=jnp.float32)


def project_back(left_side, right_side):
    return lax.dot_general(
        left_side, right_side, (((1,), (1,)), ((), ())), preferred_element_type=jnp.float32
    )


def outer_sum(left_side, right_side):
    return lax.dot_general(
        left_side, right_side, (((0,), (0,)), ((), ())), preferred_element_type=jnp.float32
    )


def halves_apart(rows_in, shard_count):
    shape_in = rows_in.shape
    split = rows_in.reshape((shard_count, 2, shape_in[0] // (2 * shard_count)) + shape_in[1:])
    return jnp.swapaxes(split, 0, 1).reshape(shape_in)


def halves_back(rows_in, shard_count):
    shape_in = rows_in.shape
    split = rows_in.reshape((2, shard_count, shape_in[0] // (2 * shard_count)) + shape_in[1:])
    return jnp.swapaxes(split, 0, 1).reshape(shape_in)


def key_layout(key_rows, value_rows, place_all):
    key_count = key_rows.shape[0]
    key_block = min(512, key_count)
    block_count = key_count // key_block
    key_parts = key_rows.reshape(block_count, key_block, KV_HEADS, HEAD_DIM)
    value_parts = value_rows.reshape(block_count, key_block, KV_HEADS, HEAD_DIM)
    place_parts = place_all.reshape(block_count, key_block)
    return (key_parts, value_parts, place_parts)


def attend_forward(queries, key_rows, value_rows, place_here, place_all):
    row_count = queries.shape[0]
    group_size = HEADS // KV_HEADS
    score_scale = HEAD_DIM ** (-0.5)
    grouped = queries.reshape(row_count, KV_HEADS, group_size, HEAD_DIM)
    layout = key_layout(key_rows, value_rows, place_all)
    top_place = jnp.max(place_here)

    def attend_step(state_now, block_item):
        key_part, value_part, place_part = block_item

        def attend_compute(state_in):
            run_max, run_sum, run_out = state_in
            scores = (
                jnp.einsum("qhge,khe->hgqk", grouped, key_part, preferred_element_type=jnp.float32)
                * score_scale
            )
            visible = place_part[None, None, None, :] <= place_here[None, None, :, None]
            scores = jnp.where(visible, scores, -1e30)
            new_max = jnp.maximum(run_max, jnp.max(scores, axis=-1))
            weights = jnp.where(visible, jnp.exp(scores - new_max[..., None]), 0.0)
            rescale = jnp.exp(run_max - new_max)
            run_sum = run_sum * rescale + jnp.sum(weights, axis=-1)
            mixed = jnp.einsum(
                "hgqk,khe->hgqe",
                weights.astype(jnp.bfloat16),
                value_part,
                preferred_element_type=jnp.float32,
            )
            run_out = run_out * rescale[..., None] + mixed
            return (new_max, run_sum, run_out)

        state_next = lax.cond(
            jnp.min(place_part) > top_place, lambda state_in: state_in, attend_compute, state_now
        )
        return (state_next, None)

    start_state = (
        jnp.full((KV_HEADS, group_size, row_count), -1e30, jnp.float32),
        jnp.zeros((KV_HEADS, group_size, row_count), jnp.float32),
        jnp.zeros((KV_HEADS, group_size, row_count, HEAD_DIM), jnp.float32),
    )
    (run_max, run_sum, run_out), _ = lax.scan(attend_step, start_state, layout)
    attention = (
        (run_out / run_sum[..., None]).transpose(2, 0, 1, 3).reshape(row_count, HEADS * HEAD_DIM)
    )
    return (attention, run_max + jnp.log(run_sum))


def row_dot_table(grad_attn, attention):
    row_count = grad_attn.shape[0]
    group_size = HEADS // KV_HEADS
    grad_grouped = grad_attn.reshape(row_count, KV_HEADS, group_size, HEAD_DIM)
    return jnp.sum(
        grad_grouped.astype(jnp.float32)
        * attention.reshape(row_count, KV_HEADS, group_size, HEAD_DIM),
        axis=-1,
    ).transpose(1, 2, 0)


def attend_backward(
    queries, key_rows, value_rows, grad_attn, row_dots, log_total, place_here, place_all
):
    row_count = queries.shape[0]
    key_count = key_rows.shape[0]
    group_size = HEADS // KV_HEADS
    score_scale = HEAD_DIM ** (-0.5)
    grouped = queries.reshape(row_count, KV_HEADS, group_size, HEAD_DIM)
    grad_grouped = grad_attn.reshape(row_count, KV_HEADS, group_size, HEAD_DIM)
    layout = key_layout(key_rows, value_rows, place_all)
    top_place = jnp.max(place_here)

    def back_step(grad_query, block_item):
        key_part, value_part, place_part = block_item
        key_block = key_part.shape[0]

        def back_compute(grad_in):
            scores = (
                jnp.einsum("qhge,khe->hgqk", grouped, key_part, preferred_element_type=jnp.float32)
                * score_scale
            )
            visible = place_part[None, None, None, :] <= place_here[None, None, :, None]
            weights = jnp.where(
                visible, jnp.exp(jnp.where(visible, scores, -1e30) - log_total[..., None]), 0.0
            )
            grad_probs = jnp.einsum(
                "qhge,khe->hgqk", grad_grouped, value_part, preferred_element_type=jnp.float32
            )
            grad_scores = (weights * (grad_probs - row_dots[..., None])).astype(jnp.bfloat16)
            grad_out = (
                grad_in
                + jnp.einsum(
                    "hgqk,khe->qhge", grad_scores, key_part, preferred_element_type=jnp.float32
                )
                * score_scale
            )
            grad_keys = (
                jnp.einsum(
                    "hgqk,qhge->khe", grad_scores, grouped, preferred_element_type=jnp.float32
                )
                * score_scale
            )
            grad_values = jnp.einsum(
                "hgqk,qhge->khe",
                weights.astype(jnp.bfloat16),
                grad_grouped,
                preferred_element_type=jnp.float32,
            )
            return (
                grad_out,
                (
                    grad_keys.reshape(key_block, KV_HEADS * HEAD_DIM),
                    grad_values.reshape(key_block, KV_HEADS * HEAD_DIM),
                ),
            )

        def skipped(grad_in):
            empty_terms = jnp.zeros((key_block, KV_HEADS * HEAD_DIM), jnp.float32)
            return (grad_in, (empty_terms, empty_terms))

        return lax.cond(jnp.min(place_part) > top_place, skipped, back_compute, grad_query)

    start_grad = jnp.zeros((row_count, KV_HEADS, group_size, HEAD_DIM), jnp.float32)
    grad_query, key_terms = lax.scan(back_step, start_grad, layout)
    grad_query = grad_query.reshape(row_count, HEADS * HEAD_DIM)
    return (
        grad_query,
        key_terms[0].reshape(key_count, KV_HEADS * HEAD_DIM),
        key_terms[1].reshape(key_count, KV_HEADS * HEAD_DIM),
    )


def per_device(
    tokens,
    positions,
    w_query,
    w_key,
    w_value,
    w_output,
    w_gate,
    w_up,
    w_down,
    first_gain,
    second_gain,
    head_gain,
    cotangent,
):
    inputs = tokens[0].astype(jnp.float32)
    row_count = inputs.shape[0]
    shard_count = lax.axis_size("ctx")
    place_stored = positions[0]
    place_here = lax.dynamic_slice_in_dim(
        place_stored, lax.axis_index("ctx") * row_count, row_count
    )
    place_all = halves_apart(place_stored, shard_count)
    query_full, key_full, value_full, output_full, gain_first, gain_head = (
        lax.all_gather(w_query, ("fsdp", "ctx"), axis=0, tiled=True),
        lax.all_gather(w_key, ("fsdp", "ctx"), axis=0, tiled=True),
        lax.all_gather(w_value, ("fsdp", "ctx"), axis=0, tiled=True),
        lax.all_gather(w_output, ("fsdp", "ctx"), axis=1, tiled=True),
        lax.all_gather(first_gain, ("fsdp", "ctx"), axis=0, tiled=True),
        lax.all_gather(head_gain, ("fsdp", "ctx"), axis=0, tiled=True),
    )
    gain_one = gain_first.astype(jnp.float32)
    gain_query = gain_head[:HEAD_DIM].astype(jnp.float32)
    gain_key = gain_head[HEAD_DIM:].astype(jnp.float32)
    hidden_one = normed(inputs, gain_one).astype(jnp.bfloat16)
    query_raw = project(hidden_one, query_full)
    key_raw = project(hidden_one, key_full)
    value_rows = project(hidden_one, value_full).astype(jnp.bfloat16)
    query_prep = partial(head_prep, places=place_here, head_count=HEADS)
    key_prep = partial(head_prep, places=place_here, head_count=KV_HEADS)
    queries, query_back = jax.vjp(query_prep, query_raw, gain_query)
    key_local, key_back = jax.vjp(key_prep, key_raw, gain_key)
    queries = queries.astype(jnp.bfloat16)
    key_local = key_local.astype(jnp.bfloat16)
    key_stored, value_stored = (
        lax.all_gather(key_local, "ctx", axis=0, tiled=True),
        lax.all_gather(value_rows, "ctx", axis=0, tiled=True),
    )
    key_all = halves_apart(key_stored, shard_count)
    value_all = halves_apart(value_stored, shard_count)
    attention, log_total = attend_forward(queries, key_all, value_all, place_here, place_all)
    attn_low = attention.astype(jnp.bfloat16)
    middle = inputs + project(attn_low, output_full)
    gate_full, up_full, down_full, gain_second = (
        lax.all_gather(w_gate, ("fsdp", "ctx"), axis=0, tiled=True),
        lax.all_gather(w_up, ("fsdp", "ctx"), axis=0, tiled=True),
        lax.all_gather(w_down, ("fsdp", "ctx"), axis=0, tiled=True),
        lax.all_gather(second_gain, ("fsdp", "ctx"), axis=0, tiled=True),
    )
    gain_two = gain_second.astype(jnp.float32)
    hidden_two = normed(middle, gain_two).astype(jnp.bfloat16)
    gate_raw = project(hidden_two, gate_full)
    up_raw = project(hidden_two, up_full)
    activated, gated_back = jax.vjp(gated, gate_raw, up_raw)
    act_low = activated.astype(jnp.bfloat16)
    layer_out = (middle + project(act_low, down_full)).astype(jnp.bfloat16)
    grad_out = cotangent[0].astype(jnp.float32)
    gate_full, up_full, down_full, gain_second = (
        lax.all_gather(w_gate, ("fsdp", "ctx"), axis=0, tiled=True),
        lax.all_gather(w_up, ("fsdp", "ctx"), axis=0, tiled=True),
        lax.all_gather(w_down, ("fsdp", "ctx"), axis=0, tiled=True),
        lax.all_gather(second_gain, ("fsdp", "ctx"), axis=0, tiled=True),
    )
    gain_two = gain_second.astype(jnp.float32)
    out_low = grad_out.astype(jnp.bfloat16)
    down_terms = outer_sum(act_low, out_low)
    grad_act = project_back(out_low, down_full)
    grad_gate_raw, grad_up_raw = gated_back(grad_act)
    gate_low = grad_gate_raw.astype(jnp.bfloat16)
    up_low = grad_up_raw.astype(jnp.bfloat16)
    gate_terms = outer_sum(hidden_two, gate_low)
    up_terms = outer_sum(hidden_two, up_low)
    grad_hidden_two = project_back(gate_low, gate_full) + project_back(up_low, up_full)
    _, norm_two_back = jax.vjp(normed, middle, gain_two)
    middle_part, gain_two_terms = norm_two_back(grad_hidden_two)
    grad_gate, grad_up, grad_down, grad_second = (
        lax.psum_scatter(gate_terms, ("fsdp", "ctx"), scatter_dimension=0, tiled=True),
        lax.psum_scatter(up_terms, ("fsdp", "ctx"), scatter_dimension=0, tiled=True),
        lax.psum_scatter(down_terms, ("fsdp", "ctx"), scatter_dimension=0, tiled=True),
        lax.psum_scatter(gain_two_terms, ("fsdp", "ctx"), scatter_dimension=0, tiled=True),
    )
    grad_middle = grad_out + middle_part
    query_full, key_full, value_full, output_full, gain_first, gain_head = (
        lax.all_gather(w_query, ("fsdp", "ctx"), axis=0, tiled=True),
        lax.all_gather(w_key, ("fsdp", "ctx"), axis=0, tiled=True),
        lax.all_gather(w_value, ("fsdp", "ctx"), axis=0, tiled=True),
        lax.all_gather(w_output, ("fsdp", "ctx"), axis=1, tiled=True),
        lax.all_gather(first_gain, ("fsdp", "ctx"), axis=0, tiled=True),
        lax.all_gather(head_gain, ("fsdp", "ctx"), axis=0, tiled=True),
    )
    gain_one = gain_first.astype(jnp.float32)
    middle_low = grad_middle.astype(jnp.bfloat16)
    output_terms = outer_sum(attn_low, middle_low)
    grad_attn = project_back(middle_low, output_full).astype(jnp.bfloat16)
    row_dots = row_dot_table(grad_attn, attention)
    grad_queries, key_terms, value_terms = attend_backward(
        queries, key_all, value_all, grad_attn, row_dots, log_total, place_here, place_all
    )
    key_terms = halves_back(key_terms, shard_count)
    value_terms = halves_back(value_terms, shard_count)
    grad_key_local, grad_value_local = (
        lax.psum_scatter(
            key_terms.astype(jnp.bfloat16), "ctx", scatter_dimension=0, tiled=True
        ).astype(jnp.float32),
        lax.psum_scatter(
            value_terms.astype(jnp.bfloat16), "ctx", scatter_dimension=0, tiled=True
        ).astype(jnp.float32),
    )
    grad_query_raw, gain_query_terms = query_back(grad_queries)
    grad_key_raw, gain_key_terms = key_back(grad_key_local)
    query_low = grad_query_raw.astype(jnp.bfloat16)
    keyraw_low = grad_key_raw.astype(jnp.bfloat16)
    value_low = grad_value_local.astype(jnp.bfloat16)
    query_terms = outer_sum(hidden_one, query_low)
    key_weight_terms = outer_sum(hidden_one, keyraw_low)
    value_weight_terms = outer_sum(hidden_one, value_low)
    grad_hidden_one = (
        project_back(query_low, query_full)
        + project_back(keyraw_low, key_full)
        + project_back(value_low, value_full)
    )
    _, norm_one_back = jax.vjp(normed, inputs, gain_one)
    input_part, gain_one_terms = norm_one_back(grad_hidden_one)
    head_terms = jnp.concatenate([gain_query_terms, gain_key_terms])
    grad_query, grad_key, grad_value, grad_output, grad_first, grad_head = (
        lax.psum_scatter(query_terms, ("fsdp", "ctx"), scatter_dimension=0, tiled=True),
        lax.psum_scatter(key_weight_terms, ("fsdp", "ctx"), scatter_dimension=0, tiled=True),
        lax.psum_scatter(value_weight_terms, ("fsdp", "ctx"), scatter_dimension=0, tiled=True),
        lax.psum_scatter(output_terms, ("fsdp", "ctx"), scatter_dimension=1, tiled=True),
        lax.psum_scatter(gain_one_terms, ("fsdp", "ctx"), scatter_dimension=0, tiled=True),
        lax.psum_scatter(head_terms, ("fsdp", "ctx"), scatter_dimension=0, tiled=True),
    )
    grad_tokens = (grad_middle + input_part).astype(jnp.bfloat16)
    return (
        layer_out[None],
        grad_tokens[None],
        grad_query,
        grad_key,
        grad_value,
        grad_output,
        grad_gate,
        grad_up,
        grad_down,
        grad_first,
        grad_second,
        grad_head,
    )


ROWS = 256
QROWS = 512
EPS = 1e-06
LOG2E = 1.4426950408889634
SCALE = HEAD_DIM**-0.5
VMEM_LIMIT = 62 * 1024 * 1024
BF16 = jnp.bfloat16
F32 = jnp.float32


def dot_nn(a, b):
    return lax.dot_general(a, b, (((1,), (0,)), ((), ())), preferred_element_type=F32)


def dot_nt(a, b):
    return lax.dot_general(a, b, (((1,), (1,)), ((), ())), preferred_element_type=F32)


def dot_tn(a, b):
    return lax.dot_general(a, b, (((0,), (0,)), ((), ())), preferred_element_type=F32)


def whereabouts():
    f, c = lax.axis_index("fsdp"), lax.axis_index("ctx")
    return f, c, f // 2, f % 2, c // 2, c % 2


def plane_of(s):
    return (s % 2) * 2 + s // 2


def remote(src, dst, send, recv, fsdp, ctx):
    return pltpu.make_async_remote_copy(
        src_ref=src, dst_ref=dst, send_sem=send, recv_sem=recv, device_id=(fsdp, ctx), device_id_type=MESH
    )


def await_bytes(ref, sem):
    pltpu.make_async_copy(ref, ref, sem).wait()


def greet_all():
    f, c, y, core, z, x = whereabouts()
    barrier = pltpu.get_barrier_semaphore()
    me = f * 8 + c

    def greet(j, carry):
        dev = (me + j) % 32
        pl.semaphore_signal(barrier, inc=1, device_id=(dev // 8, dev % 8), device_id_type=MESH)
        return carry

    lax.fori_loop(1, 32, greet, 0)
    pl.semaphore_wait(barrier, 31)


def chip_peer(r):
    f, c, y, core, z, x = whereabouts()
    y2 = 1 - y if r & 2 else y
    x2 = 1 - x if r & 1 else x
    return y2, x2


def chunk_of(r, core):
    y2, x2 = chip_peer(r)
    return (core * 2 + y2) * 2 + x2


def rows_of(ref, chunk):
    return ref.at[pl.ds(pl.multiple_of(chunk * ROWS, ROWS), ROWS)]


def head_norm_rope(raw, gain, cos, sin):
    r = lax.rsqrt(jnp.mean(raw * raw, axis=-1, keepdims=True) + EPS)
    u = raw * r * gain
    return u * cos + pltpu.roll(u, HEAD_DIM // 2, 1) * sin


def norm_rows(values, gain):
    v = values.astype(F32)
    return v * lax.rsqrt(jnp.mean(v * v, axis=-1, keepdims=True) + EPS) * gain


def norm_back(values, gain, dy):
    r = lax.rsqrt(jnp.mean(values * values, axis=-1, keepdims=True) + EPS)
    cdy = gain * dy
    back = r * cdy - values * (r * r * r) * jnp.mean(cdy * values, axis=-1, keepdims=True)
    return back, dy * values * r


def unturn(d, cos, sin):
    return d * cos - pltpu.roll(d, HEAD_DIM // 2, 1) * sin


def order_z(n, z):
    upper = z // 2
    low = (z + upper) % 2
    far = n // 2
    base = far * n + (1 - far) * (low + n * (1 - 2 * low))
    return base + upper * (3 - 2 * base)


def turn_of(n):
    return 3 - 2 * n + 3 * (n // 2)


def chunk_at(r, core):
    f, c, y, _, z, x = whereabouts()
    return (core * 2 + (y + r // 2) % 2) * 2 + (x + r % 2) % 2


def split_step(n, total, out_buf, in_buf, keep, send, recv):
    f, c, y, core, z, x = whereabouts()
    half = ROWS // 2

    def over_x(k):
        remote(out_buf.at[k], in_buf.at[k], send.at[k], recv.at[k], f, z * 2 + 1 - x).start()

    def over_y(k):
        remote(out_buf.at[k], in_buf.at[k], send.at[k], recv.at[k], (1 - y) * 2 + core, c).start()

    def add(k, came):
        await_bytes(in_buf.at[came], recv.at[came])
        out_buf[k] = (out_buf[k].astype(F32) + in_buf[came].astype(F32)).astype(BF16)

    @pl.when(n < 3)
    def _():
        out_buf[2 * n + n // 2] = total[:half].astype(BF16)
        out_buf[1 + 3 * n - 4 * (n // 2)] = total[half:].astype(BF16)

    @pl.when(n == 0)
    def _():
        over_x(0)
        over_y(1)

    @pl.when(n == 1)
    def _():
        over_x(2)

    @pl.when(n == 2)
    def _():
        over_y(3)
        add(5, 0)
        over_y(5)
        add(4, 1)
        over_x(4)

    @pl.when(n == 3)
    def _():
        keep[0] = total[:half]
        keep[1] = total[half:]


def split_sum(partial, core_out, from_core, out_buf, in_buf, keep, send, core_recv, recv):
    f, c, y, core, z, x = whereabouts()

    def to_core(n, carry):
        r = turn_of(n)
        core_out[r] = partial(chunk_at(r, 1 - core)).astype(BF16)
        remote(core_out.at[r], from_core.at[r], send.at[6], core_recv.at[r], y * 2 + 1 - core, c).start()
        return carry

    lax.fori_loop(0, 4, to_core, 0)

    def to_chips(n, carry):
        r = turn_of(n)
        term = partial(chunk_at(r, core))
        await_bytes(from_core.at[r], core_recv.at[r])
        split_step(n, term + from_core[r].astype(F32), out_buf, in_buf, keep, send, recv)
        return carry

    lax.fori_loop(0, 4, to_chips, 0)


def split_sum_end(in_buf, keep, recv):
    for k in (2, 3, 4, 5):
        await_bytes(in_buf.at[k], recv.at[k])
    return (
        keep[0] + in_buf[2].astype(F32) + in_buf[5].astype(F32),
        keep[1] + in_buf[3].astype(F32) + in_buf[4].astype(F32),
    )


def split_sum_sent(from_core, out_buf, send):
    await_bytes(from_core, send.at[6])
    for k in range(6):
        await_bytes(out_buf.at[k], send.at[k])


SPLIT_SUM_SCRATCH = [
    pltpu.VMEM((4, ROWS, 1024), BF16),
    pltpu.VMEM((4, ROWS, 1024), BF16),
    pltpu.VMEM((6, ROWS // 2, 1024), BF16),
    pltpu.VMEM((6, ROWS // 2, 1024), BF16),
    pltpu.VMEM((2, ROWS // 2, 1024), F32),
    pltpu.SemaphoreType.DMA((7,)),
    pltpu.SemaphoreType.DMA((4,)),
    pltpu.SemaphoreType.DMA((6,)),
]


def rows_in_order(pos_s, ids_s, perm_s):
    ids = [lax.div(pos_s[0, j * 128], jnp.int32(128)) for j in range(16)]
    for b in range(16):
        ids_s[b] = ids[b]
        place = jnp.int32(0)
        for j in range(16):
            place = place + j * (1 - lax.min(lax.abs(ids[j] - b), jnp.int32(1)))
        perm_s[b] = lax.min(place, jnp.int32(15))


def turns(table):
    cos, sin = table[:, 0 : HEAD_DIM // 2], table[:, HEAD_DIM // 2 :]
    return jnp.concatenate([cos, cos], axis=1), jnp.concatenate([-sin, sin], axis=1)


def two_blocks(ref, chunk, cols):
    return ref[pl.ds(chunk * 2, 2), :, cols].reshape(ROWS, -1)


def put_two(ref, chunk, cols, value):
    for k in range(2):
        ref[chunk * 2 + k, :, cols] = value[k * 128 : k * 128 + 128]


def gain_rows(gains_all):
    every = gains_all[...].reshape(32, 128)
    lane = lax.broadcasted_iota(jnp.int32, (32, 128), 1)

    def place(first, count, per_row):
        kept = jnp.where((lane >= first) & (lane < first + count), every, 0.0)
        turned = [pltpu.roll(kept, (count * seg - first) % 128, 1) for seg in range(per_row)]
        return [
            sum(turned[seg][m * per_row + seg : m * per_row + seg + 1] for seg in range(per_row))
            for m in range(32 // per_row)
        ]

    one, two = place(0, 32, 4), place(32, 32, 4)
    query, key = place(64, 8, 16)
    return jnp.concatenate(one, axis=1), jnp.concatenate(two, axis=1), query, key


PIECES = [
    ("o", 0), ("o", 1), ("x", 0), ("y", 0), ("o", 2), ("x", 1), ("y", 1), ("o", 3),
    ("x", 2), ("y", 2), ("d", 0), ("x", 3), ("y", 3), ("d", 1), ("d", 2), ("d", 3),
]


def layer_kernel(
    tok, cot, pos, wq, wk, wv, wo, wg, wu, wd_own, gains, table_h,
    layer_out, grad_tokens, pf, po, pa, rd, h_out, small_out,
    xx, hd, g_s, w1, w2, w3, wd, pack1, pack2, pack3, gains_all, table_s, gain_s,
    q_s, k_s, v_s, o_s, vt, total, lse_s, x_keep, mid,
    mix_s, act_s, delta_s, dqt_s, dk_s, dv_s, small,
    core_out, from_core, out_buf, in_buf, keep, lpart, core_out2, from_core2, in_buf2,
    gf, go, ga, rdz, rf, ro, ra, sf, so, sa, s_in, sbuf, p_in, stage, pos_v, pos_s, ids_s, perm_s,
    x_recv, g_recv, stage_recv, hop_send, x_send, g_send, pos_sem, gain_sem, w1_sem, w2_sem, w3_sem, w3_came, wd_sem,
    load, ag_send, ag_recv, ag_core, ag_recv2, ag_core2, send, core_recv, recv, recv_d, send2, core_recv2, recv2,
    home_send, f_sem, f_came, o_sem, a_sem, a_came, dz_sem, dz_came, d_sem, fp_sem, op_sem, ap_sem, out_sem, s_sem, p_sem,
):
    f, c, y, core, z, x = whereabouts()
    me, t, own = f * 8 + c, f * 2 + x, (core * 2 + y) * 2 + x
    half = ROWS // 2
    upper = z // 2
    edge, inner, other_inner = 3 * upper, 1 + upper, 2 - upper
    table = pltpu.make_async_copy(table_h, table_s, load.at[0])
    table.start()
    for k in range(8):
        pack1[k, :, 0:256] = wq[:, k * 256 : k * 256 + 256]
        pack1[k, :, 256:384] = wk[:, k * 128 : k * 128 + 128]
        pack1[k, :, 384:512] = wv[:, k * 128 : k * 128 + 128]
    greet_all()

    home = plane_of(f)
    seq = plane_of(z)
    ys, cs = seq // 2, seq % 2
    side = (y + ys) % 2
    other_y = (1 - y) * 2 + core
    other_core = y * 2 + 1 - core
    other_x = z * 2 + 1 - x

    def piece(buf, chunk, part):
        return buf.at[pl.ds(pl.multiple_of(chunk * ROWS + part * half, half), half)]

    def relays(k, from_z):
        return core == (cs + from_z) % 2 if k else core == cs

    def hop_beyond(src, buf, recv_, k):
        high = src.at[pl.ds(half, half)]
        to_f = (1 - y) * 2 + ((core + z) % 2 if k else core)

        @pl.when(home != z)
        def _():
            remote(high, stage.at[k], hop_send.at[3 * k + 1], stage_recv.at[k], other_y, c).start()

        @pl.when(home == z)
        def _():
            remote(high, piece(buf, c, 1), hop_send.at[3 * k + 1], recv_.at[2 * c + 1], to_f, c).start()

    def stays_low(k):
        return (home == z) & ((core + z) % 2 == core) if k else home == z

    def hop(src, buf, recv_, k):
        low = src.at[pl.ds(0, half)]
        to_f = y * 2 + ((core + z) % 2 if k else core)

        @pl.when(jnp.logical_not(stays_low(k)))
        def _():
            remote(low, piece(buf, c, 0), hop_send.at[3 * k], recv_.at[2 * c], to_f, home * 2 + x).start()

        @pl.when(stays_low(k))
        def _():
            pltpu.make_async_copy(low, piece(buf, c, 0), recv_.at[2 * c]).start()

    beyond = plane_of(other_y)

    def hop_on(buf, recv_, k):
        to_f = y * 2 + ((core + z) % 2 if k else core)

        @pl.when(beyond != z)
        def _():
            await_bytes(stage.at[k], stage_recv.at[k])
            remote(
                stage.at[k], piece(buf, c, 1), hop_send.at[3 * k + 2], recv_.at[2 * c + 1], to_f, beyond * 2 + x
            ).start()

    def hop_done(k):
        @pl.when(jnp.logical_not(stays_low(k)))
        def _():
            await_bytes(stage.at[k], hop_send.at[3 * k])

        await_bytes(stage.at[k], hop_send.at[3 * k + 1])

        @pl.when(beyond != z)
        def _():
            await_bytes(stage.at[k], hop_send.at[3 * k + 2])

    def whereof(kind, n):
        chunk = order_z(n, z) * 2 + (x if kind in "oy" else 1 - x)
        return chunk, (side if kind in "ox" else 1 - side)

    def relay(buf, recv_, send_, k, kind, n):
        chunk, part = whereof(kind, n)
        rows = piece(buf, chunk, part)
        sem = recv_.at[2 * chunk + part]

        def over_x():
            remote(rows, rows, send_.at[1], sem, f, other_x).start()

        def over_y():
            remote(rows, rows, send_.at[2], sem, other_y, c).start()

        @pl.when(relays(k, order_z(n, z)))
        def _():
            await_bytes(rows, sem)
            if kind == "o":
                over_x()
                over_y()
            if kind == "x":
                pl.when(n % 2 == 0)(over_y)
            if kind == "y":
                pl.when(n % 2 == 1)(over_x)
            remote(rows, rows, send_.at[0], sem, other_core, c).start()

    def relay_wait(buf, recv_, k, kind, n):
        chunk, part = whereof(kind, n)

        @pl.when(jnp.logical_not(relays(k, order_z(n, z))))
        def _():
            await_bytes(piece(buf, chunk, part), recv_.at[2 * chunk + part])

    def relay_done(buf, send_, k):
        for n in range(4):

            @pl.when(relays(k, order_z(n, z)))
            def _():
                await_bytes(buf.at[pl.ds(0, 4 * half)], send_.at[0])
                await_bytes(buf.at[pl.ds(0, half * (1 + n % 2))], send_.at[1])
                await_bytes(buf.at[pl.ds(0, half * (2 - n % 2))], send_.at[2])

    def my_rows(w):
        return w.at[f, z, pl.ds(pl.multiple_of(x * 32, 32), 32)]

    def weights_in_plane(pack, w, sem):
        pltpu.make_async_copy(pack.at[t], my_rows(w), sem.at[1]).start()
        for j in range(1, 8):
            t2 = (t + j) % 8
            remote(pack.at[t2], my_rows(w), sem.at[0], sem.at[1], t2 // 2, z * 2 + t2 % 2).start()

    def weights_across(w, sem):
        await_bytes(w.at[:, z], sem.at[1])
        for n in (1, 2, 3):
            remote(w.at[:, z], w.at[:, z], sem.at[2], sem.at[3], f, order_z(n, z) * 2 + x).start()

    def weights_near(w, sem, came):
        await_bytes(w.at[:, z], sem.at[1])
        for to_z in (inner + edge - z, other_inner):
            remote(w.at[:, z], w.at[:, z], sem.at[2], came.at[z], f, to_z * 2 + x).start()

    def weights_relay(w, sem, came):
        @pl.when(z == inner)
        def _():
            for from_z in (other_inner, 3 - edge):
                await_bytes(w.at[:, from_z], came.at[from_z])
                remote(w.at[:, from_z], w.at[:, from_z], sem.at[2], came.at[from_z], f, edge * 2 + x).start()

    def weights_done(w, came):
        @pl.when(z == inner)
        def _():
            await_bytes(w.at[:, edge], came.at[edge])

        @pl.when(z == edge)
        def _():
            for from_z in (inner, other_inner, 3 - edge):
                await_bytes(w.at[:, from_z], came.at[from_z])

    def weights_sent(w, sem):
        await_bytes(w.at[:, pl.ds(0, 2)], sem.at[2])

        @pl.when(z == inner)
        def _():
            await_bytes(w.at[:, pl.ds(0, 2)], sem.at[2])

    hop_beyond(tok, xx, x_recv, 0)
    hop(tok, xx, x_recv, 0)
    weights_in_plane(pack1, w1, w1_sem)

    @pl.when(f == seq)
    def _():
        pltpu.make_async_copy(pos, pos_v, pos_sem.at[1]).start()
        for j in range(1, 4):
            remote(pos, pos_v, pos_sem.at[0], pos_sem.at[1], (f + j) % 4, c).start()

    pltpu.make_async_copy(gains, gains_all.at[me], gain_sem.at[1]).start()

    def send_gains(j, carry):
        dev = (me + j) % 32
        remote(gains, gains_all.at[me], gain_sem.at[0], gain_sem.at[1], dev // 8, dev % 8).start()
        return carry

    lax.fori_loop(1, 32, send_gains, 0)
    relay(xx, x_recv, x_send, 0, "o", 0)
    hop_on(xx, x_recv, 0)
    for k in range(8):
        pack2[k] = wo[:, k * 256 : k * 256 + 256]
        pack3[k, :, 0:384] = wg[:, k * 384 : k * 384 + 384]
        pack3[k, :, 384:768] = wu[:, k * 384 : k * 384 + 384]
    await_bytes(gains_all, gain_sem.at[1])
    one, two, gain_q, gain_k = gain_rows(gains_all)
    gain_s[...] = jnp.zeros_like(gain_s)
    gain_s[0:1, :] = one
    gain_s[1:2, :] = two
    gain_s[2:3, 0:128] = gain_q
    gain_s[3:4, 0:128] = gain_k
    await_bytes(pos_v, pos_sem.at[1])
    pos_copy = pltpu.make_async_copy(pos_v, pos_s, load.at[2])
    pos_copy.start()
    pos_copy.wait()
    rows_in_order(pos_s, ids_s, perm_s)

    def norm_piece(kind, n):
        chunk, part = whereof(kind, n)
        rows = pl.ds(pl.multiple_of(chunk * ROWS + part * half, half), half)
        hd[rows, :] = norm_rows(xx[rows, :], gain_s[0:1, :]).astype(BF16)

    def pieces(n, carry):
        for kind, late, skip in (("o", 0, 1), ("x", 1, 0), ("y", 1, 0), ("d", 3, 0)):

            @pl.when((n >= late) & (n < late + 4))
            def _():
                pl.when(n >= skip)(lambda: relay(xx, x_recv, x_send, 0, kind, n - late))
                relay_wait(xx, x_recv, 0, kind, n - late)
                norm_piece(kind, n - late)

        @pl.when(n == 1)
        def _():
            weights_across(w1, w1_sem)

        @pl.when(n == 2)
        def _():
            weights_in_plane(pack2, w2, w2_sem)

        @pl.when(n == 3)
        def _():
            weights_in_plane(pack3, w3, w3_sem)
            hop_beyond(cot, g_s, g_recv, 1)

        @pl.when(n == 4)
        def _():
            hop(cot, g_s, g_recv, 1)

        return carry

    lax.fori_loop(0, 7, pieces, 0)
    hop_on(g_s, g_recv, 1)
    h_copy = pltpu.make_async_copy(hd, h_out, load.at[1])
    h_copy.start()
    x_keep[...] = xx[pl.ds(pl.multiple_of(own * ROWS, ROWS), ROWS), :]

    t_down = me // 4
    down_rows = wd.at[pl.ds(pl.multiple_of((me % 4) * 96, 32), 96)]
    self_down = t_down == t
    table.wait()
    await_bytes(w1.at[pl.ds(0, 3)], w1_sem.at[3])

    def project(ch, carry):
        rows = pl.ds(pl.multiple_of(ch * ROWS, ROWS), ROWS)
        raw = dot_nn(hd[rows, :], w1[...].reshape(1024, 512))
        cos, sin = turns(jnp.concatenate([table_s[ids_s[ch * 2 + k]] for k in range(2)], axis=0))
        gq, gk = gain_s[2:3, 0:128], gain_s[3:4, 0:128]
        for k in range(2):
            cols = slice(k * 128, k * 128 + 128)
            put_two(mix_s, ch, cols, head_norm_rope(raw[:, cols], gq, cos, sin).astype(BF16))
        put_two(mix_s, ch, slice(256, 384), head_norm_rope(raw[:, 256:384], gk, cos, sin).astype(BF16))
        put_two(mix_s, ch, slice(384, 512), raw[:, 384:512].astype(BF16))
        return carry

    lax.fori_loop(0, 8, project, 0, unroll=2)
    weights_across(w2, w2_sem)

    def arrange(b, carry):
        for k in range(4):
            rows = pl.ds(pl.multiple_of(b * QROWS + k * 128, 128), 128)
            stored = perm_s[b * 4 + k]
            q_s[rows, :] = mix_s[stored, :, 0:256]
            k_s[rows, :] = mix_s[stored, :, 256:384]
            v_s[rows, :] = mix_s[stored, :, 384:512]
        vt[b] = v_s[pl.ds(pl.multiple_of(b * QROWS, QROWS), QROWS), :].T
        return carry

    lax.fori_loop(0, 4, arrange, 0)
    acc = keep.at[0]

    def query_tile(qt):
        def step(kt, diagonal):
            kb = k_s[pl.ds(pl.multiple_of(kt * QROWS, QROWS), QROWS), :]
            vb = vt[kt]
            for g in range(4):
                head, part = g // 2, g % 2
                qb = q_s[pl.ds(pl.multiple_of(qt * QROWS + part * 256, 256), 256), head * 128 : head * 128 + 128]
                depth = 256 * (part + 1) if diagonal else QROWS
                s = dot_nt(kb[:depth], qb)
                p = jnp.exp2(s * (SCALE * LOG2E))
                if diagonal:
                    ki = lax.broadcasted_iota(jnp.int32, (depth, 256), 0)
                    qi = lax.broadcasted_iota(jnp.int32, (depth, 256), 1) + part * 256
                    p = jnp.where(ki <= qi, p, 0.0)
                cols = slice(g * 256, g * 256 + 256)
                total[:, cols] += jnp.sum(p, axis=0, keepdims=True)
                acc[:, cols] += dot_nn(vb[:, :depth], p.astype(BF16))

        total[...] = jnp.zeros_like(total)
        acc[...] = jnp.zeros_like(acc)

        def off(kt, inner):
            step(kt, False)
            return inner

        lax.fori_loop(0, qt, off, 0)
        step(qt, True)
        sums = total[...]
        lse_s[qt] = jnp.log2(sums)
        out = acc[...] * (1.0 / sums)
        for g in range(4):
            head, part = g // 2, g % 2
            value = out[:, g * 256 : g * 256 + 256].T.astype(BF16)
            put_two(o_s, qt * 2 + part, slice(head * 128, head * 128 + 128), value)

    def query_tiles(qt, carry):
        query_tile(qt)

        @pl.when(qt == 2)
        def _():
            for n in range(4):
                relay(g_s, g_recv, g_send, 1, "o", n)
            weights_near(w3, w3_sem, w3_came)

        return carry

    lax.fori_loop(0, 4, query_tiles, 0)
    for k in range(4):
        here = self_down & (z == k)

        @pl.when(here)
        def _():
            pltpu.make_async_copy(wd_own, down_rows, wd_sem.at[1]).start()

        @pl.when(jnp.logical_not(here))
        def _():
            remote(wd_own, down_rows, wd_sem.at[0], wd_sem.at[1], t_down // 2, k * 2 + t_down % 2).start()

    await_bytes(w2.at[pl.ds(0, 3)], w2_sem.at[3])
    relay_done(xx, x_send, 0)
    h_copy.wait()

    def attention_term(chunk):
        rows = jnp.concatenate([o_s[ids_s[chunk * 2 + k]] for k in range(2)], axis=0)
        return dot_nt(rows, w2[...].reshape(1024, 256))

    split_sum(attention_term, core_out, from_core, out_buf, in_buf, keep, send, core_recv, recv)
    for n in range(4):
        relay(g_s, g_recv, g_send, 1, "x", n)
        relay(g_s, g_recv, g_send, 1, "y", n)
    weights_relay(w3, w3_sem, w3_came)
    low, high = split_sum_end(in_buf, keep, recv)
    gain_one, gain_two = gain_s[0:1, :], gain_s[1:2, :]
    mid[0:half, :] = x_keep[0:half, :].astype(F32) + low
    mid[half:ROWS, :] = x_keep[half:ROWS, :].astype(F32) + high
    xx[pl.ds(pl.multiple_of(own * ROWS, ROWS), ROWS), :] = norm_rows(mid[...], gain_two).astype(BF16)

    def gather_start(every, sem, core_sem):
        for part in (0, 1):
            a, b = piece(every, own, part), piece(every, own, 1 - part)
            remote(a, a, ag_send.at[0], sem.at[part], f, z * 2 + 1 - x).start()
            remote(b, b, ag_send.at[1], sem.at[2 + 1 - part], (1 - y) * 2 + core, c).start()
        for part in (0, 1):
            a = piece(every, own, part)
            remote(a, a, ag_send.at[2], core_sem.at[part], y * 2 + 1 - core, c).start()

    def gather_step(every, sem, core_sem, r, part):
        a = piece(every, chunk_of(r, core), part)
        k = (r - 1) * 2 + part
        await_bytes(a, sem.at[k])
        if r == 1 and part == 0:
            remote(a, a, ag_send.at[1], sem.at[4], (1 - y) * 2 + core, c).start()
        if r == 2 and part == 1:
            remote(a, a, ag_send.at[0], sem.at[5], f, z * 2 + 1 - x).start()
        remote(a, a, ag_send.at[2], core_sem.at[2 * r + part], y * 2 + 1 - core, c).start()

    def gather_core(every, core_sem, r):
        for part in (0, 1):
            await_bytes(piece(every, chunk_of(r, 1 - core), part), core_sem.at[2 * r + part])

    def gather_sent(every):
        await_bytes(every.at[pl.ds(0, 3 * half)], ag_send.at[0])
        await_bytes(every.at[pl.ds(0, 3 * half)], ag_send.at[1])
        await_bytes(every.at[pl.ds(0, 8 * half)], ag_send.at[2])

    hop_done(0)
    hop_done(1)
    gather_start(xx, ag_recv, ag_core)
    split_sum_sent(from_core, out_buf, send)
    def feed_forward(chunk, carry):
        rows = pl.ds(pl.multiple_of(chunk * ROWS, ROWS), ROWS)
        gu = dot_nn(xx[rows, :], w3[...].reshape(1024, 768))
        gate, up = gu[:, 0:384], gu[:, 384:768]
        sig = 1.0 / (1.0 + jnp.exp(-gate))
        sil = gate * sig
        act_s[rows, :] = (sil * up).astype(BF16)
        put_two(mix_s, chunk, slice(0, 384), (up * sig * (1.0 + gate * (1.0 - sig))).astype(BF16))
        put_two(mix_s, chunk, slice(384, 768), sil.astype(BF16))
        return carry

    def feed_terms(chunk):
        rows = pl.ds(pl.multiple_of(chunk * ROWS, ROWS), ROWS)
        dact = dot_nt(g_s[rows, :], wd[...])
        for cols in (slice(0, 384), slice(384, 768)):
            put_two(mix_s, chunk, cols, (dact * two_blocks(mix_s, chunk, cols).astype(F32)).astype(BF16))
        return dot_nt(two_blocks(mix_s, chunk, slice(0, 768)), w3[...].reshape(1024, 768))

    def layer_terms(n, carry):
        r, slot = turn_of(n), n % 2

        def term(chunk):
            rows = pl.ds(pl.multiple_of(chunk * ROWS, ROWS), ROWS)
            return dot_nn(act_s[rows, :], wd[...]).astype(BF16)

        @pl.when(n >= 2)
        def _():
            await_bytes(core_out2.at[slot], send2.at[slot])

        core_out2[slot] = term(chunk_at(r, 1 - core))
        remote(core_out2.at[slot], from_core2.at[r], send2.at[slot], core_recv2.at[r], other_core, c).start()
        lpart[r] = term(chunk_at(r, core))
        return carry

    def feed_back(n, carry):
        r = turn_of(n)
        core_out[r] = feed_terms(chunk_at(r, 1 - core)).astype(BF16)
        remote(core_out.at[r], from_core.at[r], send.at[6], core_recv.at[r], other_core, c).start()
        dh = feed_terms(chunk_at(r, core))
        await_bytes(from_core.at[r], core_recv.at[r])
        split_step(n, dh + from_core[r].astype(F32), out_buf, in_buf, keep, send, recv_d)
        return carry

    gather_step(xx, ag_recv, ag_core, 1, 0)
    gather_step(xx, ag_recv, ag_core, 2, 1)
    gather_core(xx, ag_core, 0)
    weights_done(w3, w3_came)
    lax.fori_loop(0, 2, lambda n, carry: feed_forward(chunk_at(0, n), carry), 0)
    gather_step(xx, ag_recv, ag_core, 1, 1)
    gather_step(xx, ag_recv, ag_core, 2, 0)
    lax.fori_loop(1, 3, lambda r, carry: feed_forward(chunk_at(r, core), carry), 0)
    gather_core(xx, ag_core, 1)
    gather_core(xx, ag_core, 2)
    lax.fori_loop(1, 3, lambda r, carry: feed_forward(chunk_at(r, 1 - core), carry), 0)
    for n in range(4):
        relay(g_s, g_recv, g_send, 1, "d", n)
    gather_step(xx, ag_recv, ag_core, 3, 0)
    gather_step(xx, ag_recv, ag_core, 3, 1)
    gather_core(xx, ag_core, 3)
    lax.fori_loop(0, 2, lambda n, carry: feed_forward(chunk_at(3, n), carry), 0)
    for kind, n in PIECES:
        relay_wait(g_s, g_recv, 1, kind, n)
    in_half = upper == x
    held = 2 - 2 * ((upper + x) % 2)

    def down_unit(e):
        return rdz.at[held + e]

    def down_near():
        @pl.when(in_half)
        def _():
            to_z = inner + edge - z
            remote(down_unit(to_z % 2), rdz.at[0], dz_sem.at[0], dz_came.at[0], f, to_z * 2 + x).start()

        @pl.when(jnp.logical_not(in_half) & (z == edge))
        def _():
            for e in range(2):
                remote(down_unit(e), rdz.at[2 + e], dz_sem.at[0], dz_came.at[2 + e], f, inner * 2 + x).start()

    def down_relay():
        @pl.when(jnp.logical_not(in_half) & (z == inner))
        def _():
            for e in range(2):
                await_bytes(rdz.at[2 + e], dz_came.at[2 + e])
                rdz[e] = (rdz[e].astype(F32) + rdz[2 + e].astype(F32)).astype(BF16)
                remote(down_unit(e), rdz.at[1], dz_sem.at[0], dz_came.at[1], f, (2 * x + e) * 2 + x).start()

    def down_end():
        @pl.when(in_half)
        def _():
            for n in range(2):
                await_bytes(rdz.at[n], dz_came.at[n])
            mine = z % 2
            total = rdz[2 + mine].astype(F32) + rdz[0].astype(F32) + rdz[1].astype(F32)
            rdz[2 + mine] = total.astype(BF16)
            here = rdz.at[2 + mine, pl.ds(pl.multiple_of(x * 96, 32), 96)]
            there = rdz.at[2 + mine, pl.ds(pl.multiple_of((1 - x) * 96, 32), 96)]
            pltpu.make_async_copy(here, rd, d_sem.at[1]).start()
            remote(there, rd, d_sem.at[0], d_sem.at[1], f, other_x).start()

    def down_done():
        await_bytes(rd, d_sem.at[1])

        @pl.when(in_half)
        def _():
            await_bytes(rd, d_sem.at[0])
            await_bytes(rdz.at[0], dz_sem.at[0])

        @pl.when(jnp.logical_not(in_half))
        def _():
            await_bytes(rdz.at[pl.ds(0, 2)], dz_sem.at[0])

    for b in range(3):
        block = dot_tn(act_s[:, b * 128 : b * 128 + 128], g_s[...]).astype(BF16)
        for k in range(2):
            low, high = max(b * 128, k * 192), min(b * 128 + 128, k * 192 + 192)
            if low < high:
                rdz[held + k, low - k * 192 : high - k * 192, :] = block[low - b * 128 : high - b * 128]
    down_near()
    await_bytes(wd, wd_sem.at[1])
    lax.fori_loop(0, 4, feed_back, 0)

    def scatter_rows(g, b, block, first, width):
        for k in range(4):
            g[k, pl.ds(pl.multiple_of(b * 64, 64), 64), first : first + width] = block[k * 64 : k * 64 + 64].astype(BF16)

    def across(g, r_, sem):
        pltpu.make_async_copy(g.at[z], r_.at[z], sem.at[1]).start()
        for n in (3, 2, 1):
            z2 = order_z(n, z)
            remote(g.at[z2], r_.at[z], sem.at[0], sem.at[1], f, z2 * 2 + x).start()

    def across_near(g, r_, sem, came):
        @pl.when(z == edge)
        def _():
            for e in range(2):
                remote(
                    g.at[2 * (1 - upper) + e], r_.at[2 + e], sem.at[0], came.at[2 + e], f, inner * 2 + x
                ).start()

        remote(
            g.at[inner + edge - z], r_.at[upper], sem.at[0], came.at[upper], f, (inner + edge - z) * 2 + x
        ).start()

    def across_relay(g, r_, sem, came):
        @pl.when(z == inner)
        def _():
            for e in range(2):
                to_z = 2 * (1 - upper) + e
                await_bytes(r_.at[2 + e], came.at[2 + e])
                g[to_z] = (g[to_z].astype(F32) + r_[2 + e].astype(F32)).astype(BF16)
                remote(g.at[to_z], r_.at[upper], sem.at[0], came.at[upper], f, to_z * 2 + x).start()

    def across_sent(g, sem):
        await_bytes(g.at[pl.ds(0, 3)], sem.at[0])

    def to_plane(s_, p_, plane_sem):
        pltpu.make_async_copy(s_.at[pl.ds(pl.multiple_of(t * 32, 32), 32)], p_.at[t], plane_sem.at[1]).start()
        for j in range(1, 8):
            t2 = (t + j) % 8
            block = s_.at[pl.ds(pl.multiple_of(t2 * 32, 32), 32)]
            remote(block, p_.at[t], plane_sem.at[0], plane_sem.at[1], t2 // 2, z * 2 + t2 % 2).start()

    def in_plane(r_, s_, p_, sem, plane_sem):
        await_bytes(r_, sem.at[1])
        s_[...] = (r_[0].astype(F32) + r_[1].astype(F32) + r_[2].astype(F32) + r_[3].astype(F32)).astype(BF16)
        to_plane(s_, p_, plane_sem)

    def in_plane_near(g, r_, s_, p_, came, plane_sem):
        for k in range(2):
            await_bytes(r_.at[k], came.at[k])
        s_[...] = (g[z].astype(F32) + r_[0].astype(F32) + r_[1].astype(F32)).astype(BF16)
        to_plane(s_, p_, plane_sem)

    def columns(ref, b):
        return ref[:, pl.ds(pl.multiple_of(b * 256, 256), 256)]

    def grad_f(b, carry):
        scatter_rows(gf, b, dot_tn(columns(xx, b), mix_s[...].reshape(2048, 768)), 0, 768)
        return carry

    lax.fori_loop(0, 4, grad_f, 0)
    across_near(gf, rf, f_sem, f_came)
    await_bytes(from_core, send.at[6])
    gather_sent(xx)
    h_load = pltpu.make_async_copy(h_out, xx, load.at[3])
    h_load.start()

    sums = split_sum_end(in_buf, keep, recv_d)
    small[...] = jnp.zeros_like(small)
    for part in (0, 1):
        rows = slice(part * half, part * half + half)
        back, dgain = norm_back(mid[rows, :], gain_two, sums[part])
        first = pl.multiple_of(own * ROWS + part * half, half)
        dm = g_s[pl.ds(first, half), :].astype(F32) + back
        hd[pl.ds(first, half), :] = dm.astype(BF16)
        small[:, 1024:2048] += jnp.sum(dgain, axis=0, keepdims=True)
    gather_start(hd, ag_recv2, ag_core2)
    lax.fori_loop(0, 4, layer_terms, 0)
    down_relay()
    for k in range(6):
        await_bytes(out_buf.at[k], send.at[k])
    def key_columns(b, carry):
        vt[b] = k_s[pl.ds(pl.multiple_of(b * QROWS, QROWS), QROWS), :].T
        return carry

    lax.fori_loop(0, 4, key_columns, 0)

    def back_out(r, same):
        chunk = chunk_of(r, core if same else 1 - core)
        rows = pl.ds(pl.multiple_of(chunk * ROWS, ROWS), ROWS)
        put_two(mix_s, chunk, slice(512, 768), dot_nn(hd[rows, :], w2[...].reshape(1024, 256)).astype(BF16))

    back_out(0, True)
    gather_step(hd, ag_recv2, ag_core2, 1, 0)
    gather_step(hd, ag_recv2, ag_core2, 2, 1)
    gather_core(hd, ag_core2, 0)
    back_out(0, False)
    gather_step(hd, ag_recv2, ag_core2, 1, 1)
    gather_step(hd, ag_recv2, ag_core2, 2, 0)
    back_out(1, True)
    back_out(2, True)
    gather_core(hd, ag_core2, 1)
    back_out(1, False)
    gather_core(hd, ag_core2, 2)
    back_out(2, False)
    gather_step(hd, ag_recv2, ag_core2, 3, 0)
    gather_step(hd, ag_recv2, ag_core2, 3, 1)
    back_out(3, True)
    gather_core(hd, ag_core2, 3)
    back_out(3, False)

    home_f, home_c = plane_of(z), own
    stays = (home_f == f) & (home_c == c)

    beyond_c = (core * 2 + 1 - y) * 2 + x
    beyond_stays = (home_f == other_y) & (beyond_c == c)

    def deliver(low, high, dst, k):
        to_low, to_high = dst.at[pl.ds(0, half)], dst.at[pl.ds(half, half)]

        @pl.when(jnp.logical_not(stays))
        def _():
            remote(high, stage.at[k], out_sem.at[5 * k], out_sem.at[5 * k + 1], other_y, c).start()
            remote(low, to_low, out_sem.at[5 * k + 2], out_sem.at[5 * k + 3], home_f, home_c).start()

        @pl.when(stays)
        def _():
            pltpu.make_async_copy(low, to_low, out_sem.at[5 * k + 3]).start()
            pltpu.make_async_copy(high, to_high, out_sem.at[5 * k + 4]).start()

    def deliver_parts(low, high, dst):
        kept, sent = high.at[pl.ds(0, 64)], high.at[pl.ds(64, 64)]
        to = [dst.at[pl.ds(first, count)] for first, count in ((0, half), (half, 64), (half + 64, 64))]

        @pl.when(jnp.logical_not(stays))
        def _():
            remote(sent, stage.at[1, pl.ds(0, 64)], out_sem.at[5], out_sem.at[6], other_y, c).start()
            remote(low, to[0], out_sem.at[7], out_sem.at[8], home_f, home_c).start()
            remote(kept, to[1], out_sem.at[9], out_sem.at[10], home_f, home_c).start()

        @pl.when(stays)
        def _():
            pltpu.make_async_copy(low, to[0], out_sem.at[8]).start()
            pltpu.make_async_copy(kept, to[1], out_sem.at[10]).start()
            pltpu.make_async_copy(sent, to[2], out_sem.at[11]).start()

    def deliver_parts_on(dst):
        @pl.when(jnp.logical_not(beyond_stays))
        def _():
            part = stage.at[1, pl.ds(0, 64)]
            await_bytes(part, out_sem.at[6])
            to = dst.at[pl.ds(half + 64, 64)]
            remote(part, to, home_send.at[1], out_sem.at[11], home_f, beyond_c).start()

    def deliver_parts_done(dst):
        counts = ((0, half), (half, 64), (half + 64, 64))
        for (first, count), sem in zip(counts, (8, 10, 11)):
            await_bytes(dst.at[pl.ds(first, count)], out_sem.at[sem])

        @pl.when(jnp.logical_not(stays))
        def _():
            for (first, count), sem in zip(counts, (7, 9, 5)):
                await_bytes(dst.at[pl.ds(first, count)], out_sem.at[sem])

        @pl.when(jnp.logical_not(beyond_stays))
        def _():
            await_bytes(stage.at[1, pl.ds(0, 64)], home_send.at[1])

    def deliver_on(dst, k):
        @pl.when(jnp.logical_not(beyond_stays))
        def _():
            await_bytes(stage.at[k], out_sem.at[5 * k + 1])
            remote(
                stage.at[k], dst.at[pl.ds(half, half)], home_send.at[k], out_sem.at[5 * k + 4], home_f, beyond_c
            ).start()

    def deliver_done(dst, k):
        await_bytes(dst.at[pl.ds(0, half)], out_sem.at[5 * k + 3])
        await_bytes(dst.at[pl.ds(half, half)], out_sem.at[5 * k + 4])

        @pl.when(jnp.logical_not(stays))
        def _():
            await_bytes(stage.at[k], out_sem.at[5 * k])
            await_bytes(stage.at[k], out_sem.at[5 * k + 2])

        @pl.when(jnp.logical_not(beyond_stays))
        def _():
            await_bytes(stage.at[k], home_send.at[k])

    def layer_over_x(src, n):
        remote(src, in_buf2.at[n], send2.at[2 + n], recv2.at[n], f, other_x).start()

    def layer_over_y(src, n):
        remote(src, in_buf2.at[n], send2.at[2 + n], recv2.at[n], other_y, c).start()

    low_half, high_half = pl.ds(0, half), pl.ds(half, half)

    def layer_to_chips():
        for r in (3, 1, 2):
            await_bytes(from_core2.at[r], core_recv2.at[r])
            lpart[r] = (lpart[r].astype(F32) + from_core2[r].astype(F32)).astype(BF16)
            if r & 1:
                layer_over_x(lpart.at[r, low_half], 0 if r == 3 else 2)
            if r & 2:
                layer_over_y(lpart.at[r, high_half], 1 if r == 3 else 3)

    def layer_relay():
        await_bytes(in_buf2.at[0], recv2.at[0])
        lpart[2, 0:half] = (lpart[2, 0:half].astype(F32) + in_buf2[0].astype(F32)).astype(BF16)
        layer_over_y(lpart.at[2, low_half], 5)
        await_bytes(in_buf2.at[1], recv2.at[1])
        lpart[1, half:ROWS] = (lpart[1, half:ROWS].astype(F32) + in_buf2[1].astype(F32)).astype(BF16)
        layer_over_x(lpart.at[1, high_half], 4)

    def layer_end():
        await_bytes(from_core2.at[0], core_recv2.at[0])
        for n in (2, 3, 4, 5):
            await_bytes(in_buf2.at[n], recv2.at[n])
        for part in (0, 1):
            rows = slice(part * half, part * half + half)
            value = mid[rows, :] + lpart[0, rows].astype(F32) + from_core2[0, rows].astype(F32)
            value = value + in_buf2[2 + part].astype(F32) + in_buf2[5 - part].astype(F32)
            in_buf2[part] = value.astype(BF16)
        deliver(in_buf2.at[0], in_buf2.at[1], layer_out, 0)

    layer_to_chips()
    across_relay(gf, rf, f_sem, f_came)

    def prepare(b, carry):
        rows = pl.ds(pl.multiple_of(b * QROWS, QROWS), QROWS)
        do = jnp.concatenate(
            [mix_s[perm_s[b * 4 + k], :, 512:768] for k in range(4)], axis=0
        )
        act_s[rows, 0:256] = do
        ones = jnp.ones((8, 128), BF16)
        for head in range(2):
            cols = slice(head * 128, head * 128 + 128)
            prod = do[:, cols].astype(F32) * o_s[pl.ds(b * 4, 4), :, cols].reshape(QROWS, 128).astype(F32)
            high = prod.astype(BF16)
            low = (prod - high.astype(F32)).astype(BF16)
            delta = dot_nt(ones, high) + dot_nt(ones, low)
            delta_s[b, :, head * QROWS : head * QROWS + QROWS] = delta[0:1]
        return carry

    lax.fori_loop(0, 4, prepare, 0)
    def stored(b, carry):
        mix_s[b, :, 0:256] = o_s[ids_s[b]]
        return carry

    lax.fori_loop(0, 16, stored, 0)

    def grad_o(b, carry):
        scatter_rows(go, b, dot_tn(columns(hd, b), mix_s[:, :, 0:256].reshape(2048, 256)), 0, 256)
        return carry

    lax.fori_loop(0, 4, grad_o, 0)
    across(go, ro, o_sem)
    dqt_s[...] = jnp.zeros_like(dqt_s)
    dk_s[...] = jnp.zeros_like(dk_s)
    dv_s[...] = jnp.zeros_like(dv_s)

    def key_tile(kt):
        krows = pl.ds(pl.multiple_of(kt * QROWS, QROWS), QROWS)

        def step(qt, diagonal):
            kb, vb, ktb = k_s[krows, :], v_s[krows, :], vt[kt]
            for g in range(4):
                head, part = g // 2, g % 2
                start = pl.multiple_of(qt * QROWS + part * 256, 256)
                cols = slice(head * 128, head * 128 + 128)
                lanes = slice(g * 256, g * 256 + 256)
                qb = q_s[pl.ds(start, 256), cols]
                dob = act_s[pl.ds(start, 256), cols]
                depth = 256 * (part + 1) if diagonal else QROWS
                s = dot_nt(kb[:depth], qb)
                p = jnp.exp2(s * (SCALE * LOG2E) - lse_s[qt, :, lanes])
                if diagonal:
                    ki = lax.broadcasted_iota(jnp.int32, (depth, 256), 0)
                    qi = lax.broadcasted_iota(jnp.int32, (depth, 256), 1) + part * 256
                    p = jnp.where(ki <= qi, p, 0.0)
                dp = dot_nt(vb[:depth], dob)
                ds = (p * (dp - delta_s[qt, :, lanes])).astype(BF16)
                out = pl.ds(kt * 4, depth // 128)
                dv_s[out] += dot_nn(p.astype(BF16), dob).reshape(depth // 128, 128, 128)
                dk_s[out] += dot_nn(ds, qb).reshape(depth // 128, 128, 128)
                dq = dot_nn(ktb[:, :depth], ds)
                dqt_s[qt * 4 + part * 2, cols, :] += dq[:, 0:128]
                dqt_s[qt * 4 + part * 2 + 1, cols, :] += dq[:, 128:256]

        step(kt, True)

        def off(qt, inner):
            step(qt, False)
            return inner

        lax.fori_loop(kt + 1, 4, off, 0)

    def key_tiles(kt, carry):
        key_tile(kt)

        @pl.when(kt == 0)
        def _():
            layer_relay()

        return carry

    lax.fori_loop(0, 4, key_tiles, 0)
    layer_end()
    h_load.wait()

    def finish_chunk(chunk, carry):
        rows = pl.ds(pl.multiple_of(chunk * ROWS, ROWS), ROWS)
        places = [ids_s[chunk * 2 + k] for k in range(2)]
        cos, sin = turns(jnp.concatenate([table_s[b] for b in places], axis=0))
        raw = dot_nn(xx[rows, :], w1[:, :, :, 0:384].reshape(1024, 384))
        for head in range(3):
            cols = slice(head * 128, head * 128 + 128)
            if head < 2:
                blocks = [dqt_s[b, cols, :].T for b in places]
                gain, lanes = gain_s[2:3, 0:128], slice(2048, 2176)
            else:
                blocks = [dk_s[b] for b in places]
                gain, lanes = gain_s[3:4, 0:128], slice(2176, 2304)
            d = jnp.concatenate(blocks, axis=0) * SCALE
            back, dgain = norm_back(raw[:, cols], gain, unturn(d, cos, sin))
            put_two(mix_s, chunk, cols, back.astype(BF16))
            small[:, lanes] += jnp.sum(dgain, axis=0, keepdims=True)
        for k in range(2):
            mix_s[chunk * 2 + k, :, 384:512] = dv_s[places[k]].astype(BF16)
        return carry

    def partial(chunk):
        return dot_nt(two_blocks(mix_s, chunk, slice(0, 512)), w1[...].reshape(1024, 512))

    gather_sent(hd)
    lax.fori_loop(0, 8, finish_chunk, 0, unroll=2)
    def grad_a(b, carry):
        scatter_rows(ga, b, dot_tn(columns(xx, b), mix_s[:, :, 0:512].reshape(2048, 512)), 0, 512)
        return carry

    lax.fori_loop(0, 4, grad_a, 0)
    across_near(ga, ra, a_sem, a_came)
    in_plane_near(gf, rf, sf, pf, f_came, fp_sem)
    deliver_on(layer_out, 0)
    split_sum(partial, core_out, from_core, out_buf, in_buf, keep, send, core_recv, recv)
    across_relay(ga, ra, a_sem, a_came)
    low, high = split_sum_end(in_buf, keep, recv)
    for part, dh in ((0, low), (1, high)):
        rows = slice(part * half, part * half + half)
        back, dgain = norm_back(x_keep[rows, :].astype(F32), gain_one, dh)
        dm = hd[pl.ds(pl.multiple_of(own * ROWS + part * half, half), half), :].astype(F32)
        in_buf2[2 + part] = (dm + back).astype(BF16)
        small[:, 0:1024] += jnp.sum(dgain, axis=0, keepdims=True)
    s_in[t] = small[...]
    for j in range(1, 8):
        t2 = (t + j) % 8
        remote(small, s_in.at[t], s_sem.at[0], s_sem.at[1], t2 // 2, z * 2 + t2 % 2).start()
    deliver_parts(in_buf2.at[2], in_buf2.at[3], grad_tokens)
    down_end()
    in_plane(ro, so, po, o_sem, op_sem)
    deliver_parts_on(grad_tokens)
    await_bytes(s_in.at[pl.ds(0, 7)], s_sem.at[1])
    sbuf[...] = jnp.sum(s_in[...], axis=0)
    p_in[z] = sbuf[...]
    for j in range(1, 4):
        remote(sbuf, p_in.at[z], p_sem.at[0], p_sem.at[1], f, ((z + j) % 4) * 2 + x).start()
    in_plane_near(ga, ra, sa, pa, a_came, ap_sem)

    await_bytes(pf, fp_sem.at[1])
    await_bytes(p_in.at[pl.ds(0, 3)], p_sem.at[1])
    small_out[...] = jnp.sum(p_in[...], axis=0)
    await_bytes(pa, ap_sem.at[1])
    await_bytes(po, op_sem.at[1])

    deliver_done(layer_out, 0)
    deliver_parts_done(grad_tokens)
    split_sum_sent(from_core, out_buf, send)
    for k in range(2):
        await_bytes(core_out2.at[k], send2.at[k])
    for n in range(6):
        await_bytes(in_buf2.at[n], send2.at[2 + n])
    await_bytes(s_in.at[pl.ds(0, 7)], s_sem.at[0])
    await_bytes(p_in.at[pl.ds(0, 3)], p_sem.at[0])
    down_done()
    across_sent(gf, f_sem)
    await_bytes(go.at[pl.ds(0, 3)], o_sem.at[0])
    await_bytes(ra.at[pl.ds(0, 3)], a_sem.at[0])
    await_bytes(pf.at[pl.ds(0, 7)], fp_sem.at[0])
    await_bytes(po.at[pl.ds(0, 7)], op_sem.at[0])
    await_bytes(pa.at[pl.ds(0, 7)], ap_sem.at[0])
    relay_done(g_s, g_send, 1)

    @pl.when(f == seq)
    def _():
        for _ in range(3):
            await_bytes(pos_v, pos_sem.at[0])

    await_bytes(gains_all.at[pl.ds(0, 31)], gain_sem.at[0])
    for pack, sem in ((pack1, w1_sem), (pack2, w2_sem), (pack3, w3_sem)):
        await_bytes(pack.at[pl.ds(0, 7)], sem.at[0])
    await_bytes(w1.at[pl.ds(0, 3)], w1_sem.at[2])
    await_bytes(w2.at[pl.ds(0, 3)], w2_sem.at[2])
    weights_sent(w3, w3_sem)
    for k in range(4):

        @pl.when(jnp.logical_not(self_down & (z == k)))
        def _():
            await_bytes(wd_own, wd_sem.at[0])


def layer(*operands):
    any_spec, vmem = pl.BlockSpec(memory_space=pl.ANY), pl.BlockSpec(memory_space=pltpu.VMEM)
    half = ROWS // 2
    bf = lambda *shape: pltpu.VMEM(shape, BF16)
    fl = lambda *shape: pltpu.VMEM(shape, F32)
    out = lambda kind, *shape: jax.ShapeDtypeStruct(shape, kind)
    copies = (
        16, 16, 2, 6, 3, 3, 2, 2, 4, 4, 3, 4, 2,
        4, 3, 6, 8, 6, 8, 7, 4, 6, 6, 8, 4, 6,
        2, 1, 4, 2, 1, 4, 1, 4, 2, 2, 2, 2, 12, 2, 2,
    )
    return pl.pallas_call(
        layer_kernel,
        out_shape=(
            out(BF16, ROWS, 1024), out(BF16, ROWS, 1024), out(BF16, 8, 32, 768), out(BF16, 8, 32, 256),
            out(BF16, 8, 32, 512), out(BF16, 96, 1024), out(BF16, 2048, 1024), out(F32, 1, 2304),
        ),
        in_specs=[any_spec] * 3 + [vmem] * 6 + [any_spec] * 3,
        out_specs=(any_spec,) * 7 + (vmem,),
        scratch_shapes=[
            bf(2048, 1024), bf(2048, 1024), bf(2048, 1024), bf(4, 4, 64, 512), bf(4, 4, 64, 256), bf(4, 4, 64, 768),
            bf(384, 1024), bf(8, 32, 512), bf(8, 32, 256), bf(8, 32, 768), fl(32, 1, 128), fl(16, 128, 128),
            fl(8, 1024),
            bf(2048, 256), bf(2048, 128), bf(2048, 128), bf(16, 128, 256), bf(4, 128, QROWS),
            fl(1, 1024), fl(4, 1, 1024), bf(ROWS, 1024), fl(ROWS, 1024),
            bf(16, 128, 768), bf(2048, 384), fl(4, 1, 1024), fl(16, 256, 128), fl(16, 128, 128), fl(16, 128, 128),
            fl(1, 2304),
            bf(4, ROWS, 1024), bf(4, ROWS, 1024), bf(6, half, 1024), bf(6, half, 1024), fl(2, half, 1024),
            bf(4, ROWS, 1024), bf(2, ROWS, 1024), bf(4, ROWS, 1024), bf(6, half, 1024),
            bf(4, 256, 768), bf(4, 256, 256), bf(4, 256, 512), bf(4, 192, 1024), bf(4, 256, 768), bf(4, 256, 256), bf(4, 256, 512),
            bf(256, 768), bf(256, 256), bf(256, 512), fl(8, 1, 2304), fl(1, 2304), fl(4, 1, 2304),
            bf(2, half, 1024), pltpu.VMEM((1, 2048), jnp.int32), pltpu.SMEM((1, 2048), jnp.int32),
            pltpu.SMEM((16,), jnp.int32), pltpu.SMEM((16,), jnp.int32),
        ]
        + [pltpu.SemaphoreType.DMA((count,)) for count in copies],
        compiler_params=pltpu.CompilerParams(collective_id=0, has_side_effects=True, vmem_limit_bytes=VMEM_LIMIT),
        name="layer",
    )(*operands)


def outputs_kernel(
    layer, tok, pf, po, pa, rd, small, o_l, o_t, o_q, o_k, o_v, o_o, o_g, o_u, o_d, o_first, o_second, o_head
):
    me = lax.axis_index("fsdp") * 8 + lax.axis_index("ctx")
    o_l[...] = layer[...]
    o_t[...] = tok[...]
    for k in range(8):
        wide, thin, third = (slice(k * w, k * w + w) for w in (256, 128, 384))
        o_g[:, third] = pf[k, :, 0:384].astype(F32)
        o_u[:, third] = pf[k, :, 384:768].astype(F32)
        o_o[:, wide] = po[k].astype(F32)
        o_q[:, wide] = pa[k, :, 0:256].astype(F32)
        o_k[:, thin] = pa[k, :, 256:384].astype(F32)
        o_v[:, thin] = pa[k, :, 384:512].astype(F32)
    o_d[...] = rd[...].astype(F32)
    for o_ref, first, count, width in ((o_first, 0, 1024, 32), (o_second, 1024, 1024, 32), (o_head, 2048, 256, 8)):
        every = jnp.broadcast_to(small[:, first : first + count], (8, count))
        o_ref[...] = pltpu.roll(every, (count - width * me) % count, 1)[0:1, 0:width]


def outputs(*came):
    vmem = pl.BlockSpec(memory_space=pltpu.VMEM)
    out = lambda kind, *shape: jax.ShapeDtypeStruct(shape, kind)
    return pl.pallas_call(
        outputs_kernel,
        out_shape=(
            out(BF16, ROWS, 1024), out(BF16, ROWS, 1024), out(F32, 32, 2048), out(F32, 32, 1024), out(F32, 32, 1024),
            out(F32, 32, 2048), out(F32, 32, 3072), out(F32, 32, 3072), out(F32, 96, 1024), out(F32, 1, 32),
            out(F32, 1, 32), out(F32, 1, 8),
        ),
        in_specs=[vmem] * 7,
        out_specs=(vmem,) * 12,
        compiler_params=pltpu.CompilerParams(vmem_limit_bytes=VMEM_LIMIT),
        name="outputs",
    )(*came)


def rope_table(length):
    inverse = 1000000.0 ** (-2.0 * np.arange(HEAD_DIM // 2, dtype=np.float64) / HEAD_DIM)
    angles = np.arange(length, dtype=np.float32)[:, None] * inverse.astype(np.float32)[None, :]
    angles = angles.astype(np.float64)
    return np.concatenate([np.cos(angles), np.sin(angles)], axis=1).astype(np.float32)


def per_device_planes(
    tokens, positions, w_query, w_key, w_value, w_output, w_gate, w_up, w_down, first_gain, second_gain, head_gain,
    cotangent,
):
    gains = jnp.concatenate([first_gain, second_gain, head_gain, jnp.zeros((56,), BF16)]).astype(F32)[None]
    table = jnp.asarray(rope_table(2048)).reshape(16, 128, HEAD_DIM)
    layer_out, grad_tokens, pf, po, pa, rd, _, small = layer(
        tokens[0], cotangent[0], positions, w_query, w_key, w_value, w_output.T, w_gate, w_up, w_down, gains, table
    )
    layer_out, grad_tokens, o_q, o_k, o_v, o_o, o_g, o_u, o_d, o_first, o_second, o_head = outputs(
        layer_out, grad_tokens, pf, po, pa, rd, small
    )
    return (
        layer_out[None],
        grad_tokens[None],
        o_q,
        o_k,
        o_v,
        o_o.T,
        o_g,
        o_u,
        o_d,
        o_first[0],
        o_second[0],
        o_head[0],
    )


def solution(mesh):
    planes = mesh.shape["fsdp"] == 4 and mesh.shape["ctx"] == 8
    body = per_device_planes if planes else per_device
    return jax.shard_map(
        body,
        mesh=mesh,
        in_specs=(
            P("fsdp", "ctx", None),
            P("fsdp", None),
            P(("fsdp", "ctx"), None),
            P(("fsdp", "ctx"), None),
            P(("fsdp", "ctx"), None),
            P(None, ("fsdp", "ctx")),
            P(("fsdp", "ctx"), None),
            P(("fsdp", "ctx"), None),
            P(("fsdp", "ctx"), None),
            P(("fsdp", "ctx")),
            P(("fsdp", "ctx")),
            P(("fsdp", "ctx")),
            P("fsdp", "ctx", None),
        ),
        out_specs=(
            P("fsdp", "ctx", None),
            P("fsdp", "ctx", None),
            P(("fsdp", "ctx"), None),
            P(("fsdp", "ctx"), None),
            P(("fsdp", "ctx"), None),
            P(None, ("fsdp", "ctx")),
            P(("fsdp", "ctx"), None),
            P(("fsdp", "ctx"), None),
            P(("fsdp", "ctx"), None),
            P(("fsdp", "ctx")),
            P(("fsdp", "ctx")),
            P(("fsdp", "ctx")),
        ),
        check_vma=False,
    )
```

```python
from functools import partial

import jax
import jax.numpy as jnp
import numpy as np
from jax import lax
from jax.experimental import pallas as pl
from jax.experimental.pallas import tpu as pltpu
from jax.sharding import PartitionSpec as P

MESH = pl.DeviceIdType.MESH

HEADS = 16
KV_HEADS = 8
HEAD_DIM = 128


def normed(operand, gain_in):
    return (
        operand * lax.rsqrt(jnp.mean(operand * operand, axis=-1, keepdims=True) + 1e-06) * gain_in
    )


def rotary(operand, places):
    head_width = operand.shape[-1]
    half_width = head_width // 2
    inverse = 1000000.0 ** (-2.0 * jnp.arange(half_width, dtype=jnp.float32) / head_width)
    angles = places.astype(jnp.float32)[:, None] * inverse[None, :]
    cosine = jnp.concatenate([jnp.cos(angles), jnp.cos(angles)], axis=-1)[:, None, :]
    sine_table = jnp.concatenate([jnp.sin(angles), jnp.sin(angles)], axis=-1)[:, None, :]
    turned = jnp.concatenate([-operand[..., half_width:], operand[..., :half_width]], axis=-1)
    return operand * cosine + turned * sine_table


def head_prep(raw_proj, gain_in, places, head_count):
    row_count = raw_proj.shape[0]
    shaped = raw_proj.reshape(row_count, head_count, HEAD_DIM)
    return rotary(normed(shaped, gain_in), places).reshape(row_count, head_count * HEAD_DIM)


def gated(gate_raw, up_raw):
    return jax.nn.silu(gate_raw) * up_raw


def project(left_side, right_side):
    return jnp.dot(left_side, right_side, preferred_element_type=jnp.float32)


def project_back(left_side, right_side):
    return lax.dot_general(
        left_side, right_side, (((1,), (1,)), ((), ())), preferred_element_type=jnp.float32
    )


def outer_sum(left_side, right_side):
    return lax.dot_general(
        left_side, right_side, (((0,), (0,)), ((), ())), preferred_element_type=jnp.float32
    )


def halves_apart(rows_in, shard_count):
    shape_in = rows_in.shape
    split = rows_in.reshape((shard_count, 2, shape_in[0] // (2 * shard_count)) + shape_in[1:])
    return jnp.swapaxes(split, 0, 1).reshape(shape_in)


def halves_back(rows_in, shard_count):
    shape_in = rows_in.shape
    split = rows_in.reshape((2, shard_count, shape_in[0] // (2 * shard_count)) + shape_in[1:])
    return jnp.swapaxes(split, 0, 1).reshape(shape_in)


def key_layout(key_rows, value_rows, place_all):
    key_count = key_rows.shape[0]
    key_block = min(512, key_count)
    block_count = key_count // key_block
    key_parts = key_rows.reshape(block_count, key_block, KV_HEADS, HEAD_DIM)
    value_parts = value_rows.reshape(block_count, key_block, KV_HEADS, HEAD_DIM)
    place_parts = place_all.reshape(block_count, key_block)
    return (key_parts, value_parts, place_parts)


def attend_forward(queries, key_rows, value_rows, place_here, place_all):
    row_count = queries.shape[0]
    group_size = HEADS // KV_HEADS
    score_scale = HEAD_DIM ** (-0.5)
    grouped = queries.reshape(row_count, KV_HEADS, group_size, HEAD_DIM)
    layout = key_layout(key_rows, value_rows, place_all)
    top_place = jnp.max(place_here)

    def attend_step(state_now, block_item):
        key_part, value_part, place_part = block_item

        def attend_compute(state_in):
            run_max, run_sum, run_out = state_in
            scores = (
                jnp.einsum("qhge,khe->hgqk", grouped, key_part, preferred_element_type=jnp.float32)
                * score_scale
            )
            visible = place_part[None, None, None, :] <= place_here[None, None, :, None]
            scores = jnp.where(visible, scores, -1e30)
            new_max = jnp.maximum(run_max, jnp.max(scores, axis=-1))
            weights = jnp.where(visible, jnp.exp(scores - new_max[..., None]), 0.0)
            rescale = jnp.exp(run_max - new_max)
            run_sum = run_sum * rescale + jnp.sum(weights, axis=-1)
            mixed = jnp.einsum(
                "hgqk,khe->hgqe",
                weights.astype(jnp.bfloat16),
                value_part,
                preferred_element_type=jnp.float32,
            )
            run_out = run_out * rescale[..., None] + mixed
            return (new_max, run_sum, run_out)

        state_next = lax.cond(
            jnp.min(place_part) > top_place, lambda state_in: state_in, attend_compute, state_now
        )
        return (state_next, None)

    start_state = (
        jnp.full((KV_HEADS, group_size, row_count), -1e30, jnp.float32),
        jnp.zeros((KV_HEADS, group_size, row_count), jnp.float32),
        jnp.zeros((KV_HEADS, group_size, row_count, HEAD_DIM), jnp.float32),
    )
    (run_max, run_sum, run_out), _ = lax.scan(attend_step, start_state, layout)
    attention = (
        (run_out / run_sum[..., None]).transpose(2, 0, 1, 3).reshape(row_count, HEADS * HEAD_DIM)
    )
    return (attention, run_max + jnp.log(run_sum))


def row_dot_table(grad_attn, attention):
    row_count = grad_attn.shape[0]
    group_size = HEADS // KV_HEADS
    grad_grouped = grad_attn.reshape(row_count, KV_HEADS, group_size, HEAD_DIM)
    return jnp.sum(
        grad_grouped.astype(jnp.float32)
        * attention.reshape(row_count, KV_HEADS, group_size, HEAD_DIM),
        axis=-1,
    ).transpose(1, 2, 0)


def attend_backward(
    queries, key_rows, value_rows, grad_attn, row_dots, log_total, place_here, place_all
):
    row_count = queries.shape[0]
    key_count = key_rows.shape[0]
    group_size = HEADS // KV_HEADS
    score_scale = HEAD_DIM ** (-0.5)
    grouped = queries.reshape(row_count, KV_HEADS, group_size, HEAD_DIM)
    grad_grouped = grad_attn.reshape(row_count, KV_HEADS, group_size, HEAD_DIM)
    layout = key_layout(key_rows, value_rows, place_all)
    top_place = jnp.max(place_here)

    def back_step(grad_query, block_item):
        key_part, value_part, place_part = block_item
        key_block = key_part.shape[0]

        def back_compute(grad_in):
            scores = (
                jnp.einsum("qhge,khe->hgqk", grouped, key_part, preferred_element_type=jnp.float32)
                * score_scale
            )
            visible = place_part[None, None, None, :] <= place_here[None, None, :, None]
            weights = jnp.where(
                visible, jnp.exp(jnp.where(visible, scores, -1e30) - log_total[..., None]), 0.0
            )
            grad_probs = jnp.einsum(
                "qhge,khe->hgqk", grad_grouped, value_part, preferred_element_type=jnp.float32
            )
            grad_scores = (weights * (grad_probs - row_dots[..., None])).astype(jnp.bfloat16)
            grad_out = (
                grad_in
                + jnp.einsum(
                    "hgqk,khe->qhge", grad_scores, key_part, preferred_element_type=jnp.float32
                )
                * score_scale
            )
            grad_keys = (
                jnp.einsum(
                    "hgqk,qhge->khe", grad_scores, grouped, preferred_element_type=jnp.float32
                )
                * score_scale
            )
            grad_values = jnp.einsum(
                "hgqk,qhge->khe",
                weights.astype(jnp.bfloat16),
                grad_grouped,
                preferred_element_type=jnp.float32,
            )
            return (
                grad_out,
                (
                    grad_keys.reshape(key_block, KV_HEADS * HEAD_DIM),
                    grad_values.reshape(key_block, KV_HEADS * HEAD_DIM),
                ),
            )

        def skipped(grad_in):
            empty_terms = jnp.zeros((key_block, KV_HEADS * HEAD_DIM), jnp.float32)
            return (grad_in, (empty_terms, empty_terms))

        return lax.cond(jnp.min(place_part) > top_place, skipped, back_compute, grad_query)

    start_grad = jnp.zeros((row_count, KV_HEADS, group_size, HEAD_DIM), jnp.float32)
    grad_query, key_terms = lax.scan(back_step, start_grad, layout)
    grad_query = grad_query.reshape(row_count, HEADS * HEAD_DIM)
    return (
        grad_query,
        key_terms[0].reshape(key_count, KV_HEADS * HEAD_DIM),
        key_terms[1].reshape(key_count, KV_HEADS * HEAD_DIM),
    )


def per_device(
    tokens,
    positions,
    w_query,
    w_key,
    w_value,
    w_output,
    w_gate,
    w_up,
    w_down,
    first_gain,
    second_gain,
    head_gain,
    cotangent,
):
    inputs = tokens[0].astype(jnp.float32)
    row_count = inputs.shape[0]
    shard_count = lax.axis_size("ctx")
    place_stored = positions[0]
    place_here = lax.dynamic_slice_in_dim(
        place_stored, lax.axis_index("ctx") * row_count, row_count
    )
    place_all = halves_apart(place_stored, shard_count)
    query_full, key_full, value_full, output_full, gain_first, gain_head = (
        lax.all_gather(w_query, ("fsdp", "ctx"), axis=0, tiled=True),
        lax.all_gather(w_key, ("fsdp", "ctx"), axis=0, tiled=True),
        lax.all_gather(w_value, ("fsdp", "ctx"), axis=0, tiled=True),
        lax.all_gather(w_output, ("fsdp", "ctx"), axis=1, tiled=True),
        lax.all_gather(first_gain, ("fsdp", "ctx"), axis=0, tiled=True),
        lax.all_gather(head_gain, ("fsdp", "ctx"), axis=0, tiled=True),
    )
    gain_one = gain_first.astype(jnp.float32)
    gain_query = gain_head[:HEAD_DIM].astype(jnp.float32)
    gain_key = gain_head[HEAD_DIM:].astype(jnp.float32)
    hidden_one = normed(inputs, gain_one).astype(jnp.bfloat16)
    query_raw = project(hidden_one, query_full)
    key_raw = project(hidden_one, key_full)
    value_rows = project(hidden_one, value_full).astype(jnp.bfloat16)
    query_prep = partial(head_prep, places=place_here, head_count=HEADS)
    key_prep = partial(head_prep, places=place_here, head_count=KV_HEADS)
    queries, query_back = jax.vjp(query_prep, query_raw, gain_query)
    key_local, key_back = jax.vjp(key_prep, key_raw, gain_key)
    queries = queries.astype(jnp.bfloat16)
    key_local = key_local.astype(jnp.bfloat16)
    key_stored, value_stored = (
        lax.all_gather(key_local, "ctx", axis=0, tiled=True),
        lax.all_gather(value_rows, "ctx", axis=0, tiled=True),
    )
    key_all = halves_apart(key_stored, shard_count)
    value_all = halves_apart(value_stored, shard_count)
    attention, log_total = attend_forward(queries, key_all, value_all, place_here, place_all)
    attn_low = attention.astype(jnp.bfloat16)
    middle = inputs + project(attn_low, output_full)
    gate_full, up_full, down_full, gain_second = (
        lax.all_gather(w_gate, ("fsdp", "ctx"), axis=0, tiled=True),
        lax.all_gather(w_up, ("fsdp", "ctx"), axis=0, tiled=True),
        lax.all_gather(w_down, ("fsdp", "ctx"), axis=0, tiled=True),
        lax.all_gather(second_gain, ("fsdp", "ctx"), axis=0, tiled=True),
    )
    gain_two = gain_second.astype(jnp.float32)
    hidden_two = normed(middle, gain_two).astype(jnp.bfloat16)
    gate_raw = project(hidden_two, gate_full)
    up_raw = project(hidden_two, up_full)
    activated, gated_back = jax.vjp(gated, gate_raw, up_raw)
    act_low = activated.astype(jnp.bfloat16)
    layer_out = (middle + project(act_low, down_full)).astype(jnp.bfloat16)
    grad_out = cotangent[0].astype(jnp.float32)
    gate_full, up_full, down_full, gain_second = (
        lax.all_gather(w_gate, ("fsdp", "ctx"), axis=0, tiled=True),
        lax.all_gather(w_up, ("fsdp", "ctx"), axis=0, tiled=True),
        lax.all_gather(w_down, ("fsdp", "ctx"), axis=0, tiled=True),
        lax.all_gather(second_gain, ("fsdp", "ctx"), axis=0, tiled=True),
    )
    gain_two = gain_second.astype(jnp.float32)
    out_low = grad_out.astype(jnp.bfloat16)
    down_terms = outer_sum(act_low, out_low)
    grad_act = project_back(out_low, down_full)
    grad_gate_raw, grad_up_raw = gated_back(grad_act)
    gate_low = grad_gate_raw.astype(jnp.bfloat16)
    up_low = grad_up_raw.astype(jnp.bfloat16)
    gate_terms = outer_sum(hidden_two, gate_low)
    up_terms = outer_sum(hidden_two, up_low)
    grad_hidden_two = project_back(gate_low, gate_full) + project_back(up_low, up_full)
    _, norm_two_back = jax.vjp(normed, middle, gain_two)
    middle_part, gain_two_terms = norm_two_back(grad_hidden_two)
    grad_gate, grad_up, grad_down, grad_second = (
        lax.psum_scatter(gate_terms, ("fsdp", "ctx"), scatter_dimension=0, tiled=True),
        lax.psum_scatter(up_terms, ("fsdp", "ctx"), scatter_dimension=0, tiled=True),
        lax.psum_scatter(down_terms, ("fsdp", "ctx"), scatter_dimension=0, tiled=True),
        lax.psum_scatter(gain_two_terms, ("fsdp", "ctx"), scatter_dimension=0, tiled=True),
    )
    grad_middle = grad_out + middle_part
    query_full, key_full, value_full, output_full, gain_first, gain_head = (
        lax.all_gather(w_query, ("fsdp", "ctx"), axis=0, tiled=True),
        lax.all_gather(w_key, ("fsdp", "ctx"), axis=0, tiled=True),
        lax.all_gather(w_value, ("fsdp", "ctx"), axis=0, tiled=True),
        lax.all_gather(w_output, ("fsdp", "ctx"), axis=1, tiled=True),
        lax.all_gather(first_gain, ("fsdp", "ctx"), axis=0, tiled=True),
        lax.all_gather(head_gain, ("fsdp", "ctx"), axis=0, tiled=True),
    )
    gain_one = gain_first.astype(jnp.float32)
    middle_low = grad_middle.astype(jnp.bfloat16)
    output_terms = outer_sum(attn_low, middle_low)
    grad_attn = project_back(middle_low, output_full).astype(jnp.bfloat16)
    row_dots = row_dot_table(grad_attn, attention)
    grad_queries, key_terms, value_terms = attend_backward(
        queries, key_all, value_all, grad_attn, row_dots, log_total, place_here, place_all
    )
    key_terms = halves_back(key_terms, shard_count)
    value_terms = halves_back(value_terms, shard_count)
    grad_key_local, grad_value_local = (
        lax.psum_scatter(
            key_terms.astype(jnp.bfloat16), "ctx", scatter_dimension=0, tiled=True
        ).astype(jnp.float32),
        lax.psum_scatter(
            value_terms.astype(jnp.bfloat16), "ctx", scatter_dimension=0, tiled=True
        ).astype(jnp.float32),
    )
    grad_query_raw, gain_query_terms = query_back(grad_queries)
    grad_key_raw, gain_key_terms = key_back(grad_key_local)
    query_low = grad_query_raw.astype(jnp.bfloat16)
    keyraw_low = grad_key_raw.astype(jnp.bfloat16)
    value_low = grad_value_local.astype(jnp.bfloat16)
    query_terms = outer_sum(hidden_one, query_low)
    key_weight_terms = outer_sum(hidden_one, keyraw_low)
    value_weight_terms = outer_sum(hidden_one, value_low)
    grad_hidden_one = (
        project_back(query_low, query_full)
        + project_back(keyraw_low, key_full)
        + project_back(value_low, value_full)
    )
    _, norm_one_back = jax.vjp(normed, inputs, gain_one)
    input_part, gain_one_terms = norm_one_back(grad_hidden_one)
    head_terms = jnp.concatenate([gain_query_terms, gain_key_terms])
    grad_query, grad_key, grad_value, grad_output, grad_first, grad_head = (
        lax.psum_scatter(query_terms, ("fsdp", "ctx"), scatter_dimension=0, tiled=True),
        lax.psum_scatter(key_weight_terms, ("fsdp", "ctx"), scatter_dimension=0, tiled=True),
        lax.psum_scatter(value_weight_terms, ("fsdp", "ctx"), scatter_dimension=0, tiled=True),
        lax.psum_scatter(output_terms, ("fsdp", "ctx"), scatter_dimension=1, tiled=True),
        lax.psum_scatter(gain_one_terms, ("fsdp", "ctx"), scatter_dimension=0, tiled=True),
        lax.psum_scatter(head_terms, ("fsdp", "ctx"), scatter_dimension=0, tiled=True),
    )
    grad_tokens = (grad_middle + input_part).astype(jnp.bfloat16)
    return (
        layer_out[None],
        grad_tokens[None],
        grad_query,
        grad_key,
        grad_value,
        grad_output,
        grad_gate,
        grad_up,
        grad_down,
        grad_first,
        grad_second,
        grad_head,
    )


ROWS = 256
QROWS = 512
EPS = 1e-06
LOG2E = 1.4426950408889634
SCALE = HEAD_DIM**-0.5
VMEM_LIMIT = 62 * 1024 * 1024
BF16 = jnp.bfloat16
F32 = jnp.float32


def dot_nn(a, b):
    return lax.dot_general(a, b, (((1,), (0,)), ((), ())), preferred_element_type=F32)


def dot_nt(a, b):
    return lax.dot_general(a, b, (((1,), (1,)), ((), ())), preferred_element_type=F32)


def dot_tn(a, b):
    return lax.dot_general(a, b, (((0,), (0,)), ((), ())), preferred_element_type=F32)


def whereabouts():
    f, c = lax.axis_index("fsdp"), lax.axis_index("ctx")
    return f, c, f // 2, f % 2, c // 2, c % 2


def plane_of(s):
    return (s % 2) * 2 + s // 2


def remote(src, dst, send, recv, fsdp, ctx):
    return pltpu.make_async_remote_copy(
        src_ref=src, dst_ref=dst, send_sem=send, recv_sem=recv, device_id=(fsdp, ctx), device_id_type=MESH
    )


def await_bytes(ref, sem):
    pltpu.make_async_copy(ref, ref, sem).wait()


def greet_all():
    f, c, y, core, z, x = whereabouts()
    barrier = pltpu.get_barrier_semaphore()
    me = f * 8 + c

    def greet(j, carry):
        dev = (me + j) % 32
        pl.semaphore_signal(barrier, inc=1, device_id=(dev // 8, dev % 8), device_id_type=MESH)
        return carry

    lax.fori_loop(1, 32, greet, 0)
    pl.semaphore_wait(barrier, 31)


def chip_peer(r):
    f, c, y, core, z, x = whereabouts()
    y2 = 1 - y if r & 2 else y
    x2 = 1 - x if r & 1 else x
    return y2, x2


def chunk_of(r, core):
    y2, x2 = chip_peer(r)
    return (core * 2 + y2) * 2 + x2


def rows_of(ref, chunk):
    return ref.at[pl.ds(pl.multiple_of(chunk * ROWS, ROWS), ROWS)]


def head_norm_rope(raw, gain, cos, sin):
    r = lax.rsqrt(jnp.mean(raw * raw, axis=-1, keepdims=True) + EPS)
    u = raw * r * gain
    return u * cos + pltpu.roll(u, HEAD_DIM // 2, 1) * sin


def norm_rows(values, gain):
    v = values.astype(F32)
    return v * lax.rsqrt(jnp.mean(v * v, axis=-1, keepdims=True) + EPS) * gain


def norm_back(values, gain, dy):
    r = lax.rsqrt(jnp.mean(values * values, axis=-1, keepdims=True) + EPS)
    cdy = gain * dy
    back = r * cdy - values * (r * r * r) * jnp.mean(cdy * values, axis=-1, keepdims=True)
    return back, dy * values * r


def unturn(d, cos, sin):
    return d * cos - pltpu.roll(d, HEAD_DIM // 2, 1) * sin


def order_z(n, z):
    upper = z // 2
    low = (z + upper) % 2
    far = n // 2
    base = far * n + (1 - far) * (low + n * (1 - 2 * low))
    return base + upper * (3 - 2 * base)


def turn_of(n):
    return 3 - 2 * n + 3 * (n // 2)


def chunk_at(r, core):
    f, c, y, _, z, x = whereabouts()
    return (core * 2 + (y + r // 2) % 2) * 2 + (x + r % 2) % 2


def split_step(n, total, out_buf, in_buf, keep, send, recv):
    f, c, y, core, z, x = whereabouts()
    half = ROWS // 2

    def over_x(k):
        remote(out_buf.at[k], in_buf.at[k], send.at[k], recv.at[k], f, z * 2 + 1 - x).start()

    def over_y(k):
        remote(out_buf.at[k], in_buf.at[k], send.at[k], recv.at[k], (1 - y) * 2 + core, c).start()

    def add(k, came):
        await_bytes(in_buf.at[came], recv.at[came])
        out_buf[k] = (out_buf[k].astype(F32) + in_buf[came].astype(F32)).astype(BF16)

    @pl.when(n < 3)
    def _():
        out_buf[2 * n + n // 2] = total[:half].astype(BF16)
        out_buf[1 + 3 * n - 4 * (n // 2)] = total[half:].astype(BF16)

    @pl.when(n == 0)
    def _():
        over_x(0)
        over_y(1)

    @pl.when(n == 1)
    def _():
        over_x(2)

    @pl.when(n == 2)
    def _():
        over_y(3)
        add(5, 0)
        over_y(5)
        add(4, 1)
        over_x(4)

    @pl.when(n == 3)
    def _():
        keep[0] = total[:half]
        keep[1] = total[half:]


def split_sum(partial, core_out, from_core, out_buf, in_buf, keep, send, core_recv, recv):
    f, c, y, core, z, x = whereabouts()

    def to_core(n, carry):
        r = turn_of(n)
        core_out[r] = partial(chunk_at(r, 1 - core)).astype(BF16)
        remote(core_out.at[r], from_core.at[r], send.at[6], core_recv.at[r], y * 2 + 1 - core, c).start()
        return carry

    lax.fori_loop(0, 4, to_core, 0)

    def to_chips(n, carry):
        r = turn_of(n)
        term = partial(chunk_at(r, core))
        await_bytes(from_core.at[r], core_recv.at[r])
        split_step(n, term + from_core[r].astype(F32), out_buf, in_buf, keep, send, recv)
        return carry

    lax.fori_loop(0, 4, to_chips, 0)


def split_sum_end(in_buf, keep, recv):
    for k in (2, 3, 4, 5):
        await_bytes(in_buf.at[k], recv.at[k])
    return (
        keep[0] + in_buf[2].astype(F32) + in_buf[5].astype(F32),
        keep[1] + in_buf[3].astype(F32) + in_buf[4].astype(F32),
    )


def split_sum_sent(from_core, out_buf, send):
    await_bytes(from_core, send.at[6])
    for k in range(6):
        await_bytes(out_buf.at[k], send.at[k])


SPLIT_SUM_SCRATCH = [
    pltpu.VMEM((4, ROWS, 1024), BF16),
    pltpu.VMEM((4, ROWS, 1024), BF16),
    pltpu.VMEM((6, ROWS // 2, 1024), BF16),
    pltpu.VMEM((6, ROWS // 2, 1024), BF16),
    pltpu.VMEM((2, ROWS // 2, 1024), F32),
    pltpu.SemaphoreType.DMA((7,)),
    pltpu.SemaphoreType.DMA((4,)),
    pltpu.SemaphoreType.DMA((6,)),
]


def rows_in_order(pos_s, ids_s, perm_s):
    ids = [lax.div(pos_s[0, j * 128], jnp.int32(128)) for j in range(16)]
    for b in range(16):
        ids_s[b] = ids[b]
        place = jnp.int32(0)
        for j in range(16):
            place = place + j * (1 - lax.min(lax.abs(ids[j] - b), jnp.int32(1)))
        perm_s[b] = lax.min(place, jnp.int32(15))


def turns(table):
    cos, sin = table[:, 0 : HEAD_DIM // 2], table[:, HEAD_DIM // 2 :]
    return jnp.concatenate([cos, cos], axis=1), jnp.concatenate([-sin, sin], axis=1)


def two_blocks(ref, chunk, cols):
    return ref[pl.ds(chunk * 2, 2), :, cols].reshape(ROWS, -1)


def put_two(ref, chunk, cols, value):
    for k in range(2):
        ref[chunk * 2 + k, :, cols] = value[k * 128 : k * 128 + 128]


def gain_rows(gains_all):
    every = gains_all[...].reshape(32, 128)
    lane = lax.broadcasted_iota(jnp.int32, (32, 128), 1)

    def place(first, count, per_row):
        kept = jnp.where((lane >= first) & (lane < first + count), every, 0.0)
        turned = [pltpu.roll(kept, (count * seg - first) % 128, 1) for seg in range(per_row)]
        return [
            sum(turned[seg][m * per_row + seg : m * per_row + seg + 1] for seg in range(per_row))
            for m in range(32 // per_row)
        ]

    one, two = place(0, 32, 4), place(32, 32, 4)
    query, key = place(64, 8, 16)
    return jnp.concatenate(one, axis=1), jnp.concatenate(two, axis=1), query, key


PIECES = [
    ("o", 0), ("o", 1), ("x", 0), ("y", 0), ("o", 2), ("x", 1), ("y", 1), ("o", 3),
    ("x", 2), ("y", 2), ("d", 0), ("x", 3), ("y", 3), ("d", 1), ("d", 2), ("d", 3),
]


def layer_kernel(
    tok, cot, pos, wq, wk, wv, wo, wg, wu, wd_own, gains, table_h,
    layer_out, grad_tokens, pf, po, pa, rd, h_out, small_out,
    xx, hd, g_s, w1, w2, w3, wd, pack1, pack2, pack3, gains_all, table_s, gain_s,
    q_s, k_s, v_s, o_s, vt, total, lse_s, x_keep, mid,
    mix_s, act_s, delta_s, dqt_s, dk_s, dv_s, small,
    core_out, from_core, out_buf, in_buf, keep, lpart, core_out2, from_core2, in_buf2,
    gf, go, ga, rdz, rf, ro, ra, sf, so, sa, s_in, sbuf, p_in, stage, pos_v, pos_s, ids_s, perm_s,
    x_recv, g_recv, stage_recv, hop_send, x_send, g_send, pos_sem, gain_sem, w1_sem, w2_sem, w3_sem, w3_came, wd_sem,
    load, ag_send, ag_recv, ag_core, ag_recv2, ag_core2, send, core_recv, recv, recv_d, send2, core_recv2, recv2,
    home_send, f_sem, f_came, o_sem, a_sem, a_came, dz_sem, dz_came, d_sem, fp_sem, op_sem, ap_sem, out_sem, s_sem, p_sem,
):
    f, c, y, core, z, x = whereabouts()
    me, t, own = f * 8 + c, f * 2 + x, (core * 2 + y) * 2 + x
    half = ROWS // 2
    upper = z // 2
    edge, inner, other_inner = 3 * upper, 1 + upper, 2 - upper
    table = pltpu.make_async_copy(table_h, table_s, load.at[0])
    table.start()
    for k in range(8):
        pack1[k, :, 0:256] = wq[:, k * 256 : k * 256 + 256]
        pack1[k, :, 256:384] = wk[:, k * 128 : k * 128 + 128]
        pack1[k, :, 384:512] = wv[:, k * 128 : k * 128 + 128]
    greet_all()

    home = plane_of(f)
    seq = plane_of(z)
    ys, cs = seq // 2, seq % 2
    side = (y + ys) % 2
    other_y = (1 - y) * 2 + core
    other_core = y * 2 + 1 - core
    other_x = z * 2 + 1 - x

    def piece(buf, chunk, part):
        return buf.at[pl.ds(pl.multiple_of(chunk * ROWS + part * half, half), half)]

    def relays(k, from_z):
        return core == (cs + from_z) % 2 if k else core == cs

    def hop_beyond(src, buf, recv_, k):
        high = src.at[pl.ds(half, half)]
        to_f = (1 - y) * 2 + ((core + z) % 2 if k else core)

        @pl.when(home != z)
        def _():
            remote(high, stage.at[k], hop_send.at[3 * k + 1], stage_recv.at[k], other_y, c).start()

        @pl.when(home == z)
        def _():
            remote(high, piece(buf, c, 1), hop_send.at[3 * k + 1], recv_.at[2 * c + 1], to_f, c).start()

    def stays_low(k):
        return (home == z) & ((core + z) % 2 == core) if k else home == z

    def hop(src, buf, recv_, k):
        low = src.at[pl.ds(0, half)]
        to_f = y * 2 + ((core + z) % 2 if k else core)

        @pl.when(jnp.logical_not(stays_low(k)))
        def _():
            remote(low, piece(buf, c, 0), hop_send.at[3 * k], recv_.at[2 * c], to_f, home * 2 + x).start()

        @pl.when(stays_low(k))
        def _():
            pltpu.make_async_copy(low, piece(buf, c, 0), recv_.at[2 * c]).start()

    beyond = plane_of(other_y)

    def hop_on(buf, recv_, k):
        to_f = y * 2 + ((core + z) % 2 if k else core)

        @pl.when(beyond != z)
        def _():
            await_bytes(stage.at[k], stage_recv.at[k])
            remote(
                stage.at[k], piece(buf, c, 1), hop_send.at[3 * k + 2], recv_.at[2 * c + 1], to_f, beyond * 2 + x
            ).start()

    def hop_done(k):
        @pl.when(jnp.logical_not(stays_low(k)))
        def _():
            await_bytes(stage.at[k], hop_send.at[3 * k])

        await_bytes(stage.at[k], hop_send.at[3 * k + 1])

        @pl.when(beyond != z)
        def _():
            await_bytes(stage.at[k], hop_send.at[3 * k + 2])

    def whereof(kind, n):
        chunk = order_z(n, z) * 2 + (x if kind in "oy" else 1 - x)
        return chunk, (side if kind in "ox" else 1 - side)

    def relay(buf, recv_, send_, k, kind, n):
        chunk, part = whereof(kind, n)
        rows = piece(buf, chunk, part)
        sem = recv_.at[2 * chunk + part]

        def over_x():
            remote(rows, rows, send_.at[1], sem, f, other_x).start()

        def over_y():
            remote(rows, rows, send_.at[2], sem, other_y, c).start()

        @pl.when(relays(k, order_z(n, z)))
        def _():
            await_bytes(rows, sem)
            if kind == "o":
                over_x()
                over_y()
            if kind == "x":
                pl.when(n % 2 == 0)(over_y)
            if kind == "y":
                pl.when(n % 2 == 1)(over_x)
            remote(rows, rows, send_.at[0], sem, other_core, c).start()

    def relay_wait(buf, recv_, k, kind, n):
        chunk, part = whereof(kind, n)

        @pl.when(jnp.logical_not(relays(k, order_z(n, z))))
        def _():
            await_bytes(piece(buf, chunk, part), recv_.at[2 * chunk + part])

    def relay_done(buf, send_, k):
        for n in range(4):

            @pl.when(relays(k, order_z(n, z)))
            def _():
                await_bytes(buf.at[pl.ds(0, 4 * half)], send_.at[0])
                await_bytes(buf.at[pl.ds(0, half * (1 + n % 2))], send_.at[1])
                await_bytes(buf.at[pl.ds(0, half * (2 - n % 2))], send_.at[2])

    def my_rows(w):
        return w.at[f, z, pl.ds(pl.multiple_of(x * 32, 32), 32)]

    def weights_in_plane(pack, w, sem):
        pltpu.make_async_copy(pack.at[t], my_rows(w), sem.at[1]).start()
        for j in range(1, 8):
            t2 = (t + j) % 8
            remote(pack.at[t2], my_rows(w), sem.at[0], sem.at[1], t2 // 2, z * 2 + t2 % 2).start()

    def weights_across(w, sem):
        await_bytes(w.at[:, z], sem.at[1])
        for n in (1, 2, 3):
            remote(w.at[:, z], w.at[:, z], sem.at[2], sem.at[3], f, order_z(n, z) * 2 + x).start()

    def weights_near(w, sem, came):
        await_bytes(w.at[:, z], sem.at[1])
        for to_z in (inner + edge - z, other_inner):
            remote(w.at[:, z], w.at[:, z], sem.at[2], came.at[z], f, to_z * 2 + x).start()

    def weights_relay(w, sem, came):
        @pl.when(z == inner)
        def _():
            for from_z in (other_inner, 3 - edge):
                await_bytes(w.at[:, from_z], came.at[from_z])
                remote(w.at[:, from_z], w.at[:, from_z], sem.at[2], came.at[from_z], f, edge * 2 + x).start()

    def weights_done(w, came):
        @pl.when(z == inner)
        def _():
            await_bytes(w.at[:, edge], came.at[edge])

        @pl.when(z == edge)
        def _():
            for from_z in (inner, other_inner, 3 - edge):
                await_bytes(w.at[:, from_z], came.at[from_z])

    def weights_sent(w, sem):
        await_bytes(w.at[:, pl.ds(0, 2)], sem.at[2])

        @pl.when(z == inner)
        def _():
            await_bytes(w.at[:, pl.ds(0, 2)], sem.at[2])

    hop_beyond(tok, xx, x_recv, 0)
    hop(tok, xx, x_recv, 0)
    weights_in_plane(pack1, w1, w1_sem)

    @pl.when(f == seq)
    def _():
        pltpu.make_async_copy(pos, pos_v, pos_sem.at[1]).start()
        for j in range(1, 4):
            remote(pos, pos_v, pos_sem.at[0], pos_sem.at[1], (f + j) % 4, c).start()

    pltpu.make_async_copy(gains, gains_all.at[me], gain_sem.at[1]).start()

    def send_gains(j, carry):
        dev = (me + j) % 32
        remote(gains, gains_all.at[me], gain_sem.at[0], gain_sem.at[1], dev // 8, dev % 8).start()
        return carry

    lax.fori_loop(1, 32, send_gains, 0)
    relay(xx, x_recv, x_send, 0, "o", 0)
    hop_on(xx, x_recv, 0)
    for kind, n in (("o", 1), ("x", 0), ("y", 0)):
        relay(xx, x_recv, x_send, 0, kind, n)
    for k in range(8):
        pack2[k] = wo[:, k * 256 : k * 256 + 256]
        pack3[k, :, 0:384] = wg[:, k * 384 : k * 384 + 384]
        pack3[k, :, 384:768] = wu[:, k * 384 : k * 384 + 384]
    await_bytes(gains_all, gain_sem.at[1])
    one, two, gain_q, gain_k = gain_rows(gains_all)
    gain_s[...] = jnp.zeros_like(gain_s)
    gain_s[0:1, :] = one
    gain_s[1:2, :] = two
    gain_s[2:3, 0:128] = gain_q
    gain_s[3:4, 0:128] = gain_k
    await_bytes(pos_v, pos_sem.at[1])
    pos_copy = pltpu.make_async_copy(pos_v, pos_s, load.at[2])
    pos_copy.start()
    pos_copy.wait()
    rows_in_order(pos_s, ids_s, perm_s)

    def norm_piece(kind, n):
        chunk, part = whereof(kind, n)
        rows = pl.ds(pl.multiple_of(chunk * ROWS + part * half, half), half)
        hd[rows, :] = norm_rows(xx[rows, :], gain_s[0:1, :]).astype(BF16)

    def pieces(n, carry):
        for kind, late, skip in (("o", 0, 2), ("x", 1, 2), ("y", 1, 2), ("d", 3, 0)):

            @pl.when((n >= late) & (n < late + 4))
            def _():
                pl.when(n >= skip)(lambda: relay(xx, x_recv, x_send, 0, kind, n - late))
                relay_wait(xx, x_recv, 0, kind, n - late)
                norm_piece(kind, n - late)

        @pl.when(n == 1)
        def _():
            weights_across(w1, w1_sem)

        @pl.when(n == 2)
        def _():
            weights_in_plane(pack2, w2, w2_sem)

        @pl.when(n == 3)
        def _():
            weights_in_plane(pack3, w3, w3_sem)
            hop_beyond(cot, g_s, g_recv, 1)

        @pl.when(n == 4)
        def _():
            hop(cot, g_s, g_recv, 1)

        return carry

    lax.fori_loop(0, 7, pieces, 0)
    hop_on(g_s, g_recv, 1)
    h_copy = pltpu.make_async_copy(hd, h_out, load.at[1])
    h_copy.start()
    x_keep[...] = xx[pl.ds(pl.multiple_of(own * ROWS, ROWS), ROWS), :]

    t_down = me // 4
    down_rows = wd.at[pl.ds(pl.multiple_of((me % 4) * 96, 32), 96)]
    self_down = t_down == t
    table.wait()
    await_bytes(w1.at[pl.ds(0, 3)], w1_sem.at[3])

    def project(ch, carry):
        rows = pl.ds(pl.multiple_of(ch * ROWS, ROWS), ROWS)
        raw = dot_nn(hd[rows, :], w1[...].reshape(1024, 512))
        cos, sin = turns(jnp.concatenate([table_s[ids_s[ch * 2 + k]] for k in range(2)], axis=0))
        gq, gk = gain_s[2:3, 0:128], gain_s[3:4, 0:128]
        for k in range(2):
            cols = slice(k * 128, k * 128 + 128)
            put_two(mix_s, ch, cols, head_norm_rope(raw[:, cols], gq, cos, sin).astype(BF16))
        put_two(mix_s, ch, slice(256, 384), head_norm_rope(raw[:, 256:384], gk, cos, sin).astype(BF16))
        put_two(mix_s, ch, slice(384, 512), raw[:, 384:512].astype(BF16))
        return carry

    lax.fori_loop(0, 8, project, 0, unroll=2)
    weights_across(w2, w2_sem)

    def arrange(b, carry):
        for k in range(4):
            rows = pl.ds(pl.multiple_of(b * QROWS + k * 128, 128), 128)
            stored = perm_s[b * 4 + k]
            q_s[rows, :] = mix_s[stored, :, 0:256]
            k_s[rows, :] = mix_s[stored, :, 256:384]
            v_s[rows, :] = mix_s[stored, :, 384:512]
        vt[b] = v_s[pl.ds(pl.multiple_of(b * QROWS, QROWS), QROWS), :].T
        return carry

    lax.fori_loop(0, 4, arrange, 0)
    acc = keep.at[0]

    def query_tile(qt):
        def step(kt, diagonal):
            kb = k_s[pl.ds(pl.multiple_of(kt * QROWS, QROWS), QROWS), :]
            vb = vt[kt]
            for g in range(4):
                head, part = g // 2, g % 2
                qb = q_s[pl.ds(pl.multiple_of(qt * QROWS + part * 256, 256), 256), head * 128 : head * 128 + 128]
                depth = 256 * (part + 1) if diagonal else QROWS
                s = dot_nt(kb[:depth], qb)
                p = jnp.exp2(s * (SCALE * LOG2E))
                if diagonal:
                    ki = lax.broadcasted_iota(jnp.int32, (depth, 256), 0)
                    qi = lax.broadcasted_iota(jnp.int32, (depth, 256), 1) + part * 256
                    p = jnp.where(ki <= qi, p, 0.0)
                cols = slice(g * 256, g * 256 + 256)
                total[:, cols] += jnp.sum(p, axis=0, keepdims=True)
                acc[:, cols] += dot_nn(vb[:, :depth], p.astype(BF16))

        total[...] = jnp.zeros_like(total)
        acc[...] = jnp.zeros_like(acc)

        def off(kt, inner):
            step(kt, False)
            return inner

        lax.fori_loop(0, qt, off, 0)
        step(qt, True)
        sums = total[...]
        lse_s[qt] = jnp.log2(sums)
        out = acc[...] * (1.0 / sums)
        for g in range(4):
            head, part = g // 2, g % 2
            value = out[:, g * 256 : g * 256 + 256].T.astype(BF16)
            put_two(o_s, qt * 2 + part, slice(head * 128, head * 128 + 128), value)

    def query_tiles(qt, carry):
        query_tile(qt)

        @pl.when(qt == 1)
        def _():
            weights_near(w3, w3_sem, w3_came)

        @pl.when(qt == 2)
        def _():
            for n in range(4):
                relay(g_s, g_recv, g_send, 1, "o", n)

        return carry

    lax.fori_loop(0, 4, query_tiles, 0)
    for k in range(4):
        here = self_down & (z == k)

        @pl.when(here)
        def _():
            pltpu.make_async_copy(wd_own, down_rows, wd_sem.at[1]).start()

        @pl.when(jnp.logical_not(here))
        def _():
            remote(wd_own, down_rows, wd_sem.at[0], wd_sem.at[1], t_down // 2, k * 2 + t_down % 2).start()

    await_bytes(w2.at[pl.ds(0, 3)], w2_sem.at[3])
    relay_done(xx, x_send, 0)
    h_copy.wait()

    def attention_term(chunk):
        rows = jnp.concatenate([o_s[ids_s[chunk * 2 + k]] for k in range(2)], axis=0)
        return dot_nt(rows, w2[...].reshape(1024, 256))

    split_sum(attention_term, core_out, from_core, out_buf, in_buf, keep, send, core_recv, recv)
    for n in range(4):
        relay(g_s, g_recv, g_send, 1, "x", n)
        relay(g_s, g_recv, g_send, 1, "y", n)
    weights_relay(w3, w3_sem, w3_came)
    low, high = split_sum_end(in_buf, keep, recv)
    gain_one, gain_two = gain_s[0:1, :], gain_s[1:2, :]
    mid[0:half, :] = x_keep[0:half, :].astype(F32) + low
    mid[half:ROWS, :] = x_keep[half:ROWS, :].astype(F32) + high
    xx[pl.ds(pl.multiple_of(own * ROWS, ROWS), ROWS), :] = norm_rows(mid[...], gain_two).astype(BF16)

    def gather_start(every, sem, core_sem):
        for part in (0, 1):
            a, b = piece(every, own, part), piece(every, own, 1 - part)
            remote(a, a, ag_send.at[0], sem.at[part], f, z * 2 + 1 - x).start()
            remote(b, b, ag_send.at[1], sem.at[2 + 1 - part], (1 - y) * 2 + core, c).start()
        for part in (0, 1):
            a = piece(every, own, part)
            remote(a, a, ag_send.at[2], core_sem.at[part], y * 2 + 1 - core, c).start()

    def gather_step(every, sem, core_sem, r, part):
        a = piece(every, chunk_of(r, core), part)
        k = (r - 1) * 2 + part
        await_bytes(a, sem.at[k])
        if r == 1 and part == 0:
            remote(a, a, ag_send.at[1], sem.at[4], (1 - y) * 2 + core, c).start()
        if r == 2 and part == 1:
            remote(a, a, ag_send.at[0], sem.at[5], f, z * 2 + 1 - x).start()
        remote(a, a, ag_send.at[2], core_sem.at[2 * r + part], y * 2 + 1 - core, c).start()

    def gather_core(every, core_sem, r):
        for part in (0, 1):
            await_bytes(piece(every, chunk_of(r, 1 - core), part), core_sem.at[2 * r + part])

    def gather_sent(every):
        await_bytes(every.at[pl.ds(0, 3 * half)], ag_send.at[0])
        await_bytes(every.at[pl.ds(0, 3 * half)], ag_send.at[1])
        await_bytes(every.at[pl.ds(0, 8 * half)], ag_send.at[2])

    hop_done(0)
    hop_done(1)
    gather_start(xx, ag_recv, ag_core)
    split_sum_sent(from_core, out_buf, send)
    def feed_forward(chunk, carry):
        rows = pl.ds(pl.multiple_of(chunk * ROWS, ROWS), ROWS)
        gu = dot_nn(xx[rows, :], w3[...].reshape(1024, 768))
        gate, up = gu[:, 0:384], gu[:, 384:768]
        sig = 1.0 / (1.0 + jnp.exp(-gate))
        sil = gate * sig
        act_s[rows, :] = (sil * up).astype(BF16)
        put_two(mix_s, chunk, slice(0, 384), (up * sig * (1.0 + gate * (1.0 - sig))).astype(BF16))
        put_two(mix_s, chunk, slice(384, 768), sil.astype(BF16))
        return carry

    def feed_terms(chunk):
        rows = pl.ds(pl.multiple_of(chunk * ROWS, ROWS), ROWS)
        dact = dot_nt(g_s[rows, :], wd[...])
        for cols in (slice(0, 384), slice(384, 768)):
            put_two(mix_s, chunk, cols, (dact * two_blocks(mix_s, chunk, cols).astype(F32)).astype(BF16))
        return dot_nt(two_blocks(mix_s, chunk, slice(0, 768)), w3[...].reshape(1024, 768))

    def layer_terms(n, carry):
        r, slot = turn_of(n), n % 2

        def term(chunk):
            rows = pl.ds(pl.multiple_of(chunk * ROWS, ROWS), ROWS)
            return dot_nn(act_s[rows, :], wd[...]).astype(BF16)

        @pl.when(n >= 2)
        def _():
            await_bytes(core_out2.at[slot], send2.at[slot])

        core_out2[slot] = term(chunk_at(r, 1 - core))
        remote(core_out2.at[slot], from_core2.at[r], send2.at[slot], core_recv2.at[r], other_core, c).start()
        lpart[r] = term(chunk_at(r, core))
        return carry

    def feed_back(n, carry):
        r = turn_of(n)
        core_out[r] = feed_terms(chunk_at(r, 1 - core)).astype(BF16)
        remote(core_out.at[r], from_core.at[r], send.at[6], core_recv.at[r], other_core, c).start()
        dh = feed_terms(chunk_at(r, core))
        await_bytes(from_core.at[r], core_recv.at[r])
        split_step(n, dh + from_core[r].astype(F32), out_buf, in_buf, keep, send, recv_d)
        return carry

    gather_step(xx, ag_recv, ag_core, 1, 0)
    gather_step(xx, ag_recv, ag_core, 2, 1)
    gather_core(xx, ag_core, 0)
    weights_done(w3, w3_came)
    lax.fori_loop(0, 2, lambda n, carry: feed_forward(chunk_at(0, n), carry), 0)
    gather_step(xx, ag_recv, ag_core, 1, 1)
    gather_step(xx, ag_recv, ag_core, 2, 0)
    lax.fori_loop(1, 3, lambda r, carry: feed_forward(chunk_at(r, core), carry), 0)
    gather_core(xx, ag_core, 1)
    gather_core(xx, ag_core, 2)
    lax.fori_loop(1, 3, lambda r, carry: feed_forward(chunk_at(r, 1 - core), carry), 0)
    for n in range(4):
        relay(g_s, g_recv, g_send, 1, "d", n)
    gather_step(xx, ag_recv, ag_core, 3, 0)
    gather_step(xx, ag_recv, ag_core, 3, 1)
    gather_core(xx, ag_core, 3)
    lax.fori_loop(0, 2, lambda n, carry: feed_forward(chunk_at(3, n), carry), 0)
    for kind, n in PIECES:
        relay_wait(g_s, g_recv, 1, kind, n)
    in_half = upper == x
    held = 2 - 2 * ((upper + x) % 2)

    def down_unit(e):
        return rdz.at[held + e]

    def down_near():
        @pl.when(in_half)
        def _():
            to_z = inner + edge - z
            remote(down_unit(to_z % 2), rdz.at[0], dz_sem.at[0], dz_came.at[0], f, to_z * 2 + x).start()

        @pl.when(jnp.logical_not(in_half) & (z == edge))
        def _():
            for e in range(2):
                remote(down_unit(e), rdz.at[2 + e], dz_sem.at[0], dz_came.at[2 + e], f, inner * 2 + x).start()

    def down_relay():
        @pl.when(jnp.logical_not(in_half) & (z == inner))
        def _():
            for e in range(2):
                await_bytes(rdz.at[2 + e], dz_came.at[2 + e])
                rdz[e] = (rdz[e].astype(F32) + rdz[2 + e].astype(F32)).astype(BF16)
                remote(down_unit(e), rdz.at[1], dz_sem.at[0], dz_came.at[1], f, (2 * x + e) * 2 + x).start()

    def down_end():
        @pl.when(in_half)
        def _():
            for n in range(2):
                await_bytes(rdz.at[n], dz_came.at[n])
            mine = z % 2
            total = rdz[2 + mine].astype(F32) + rdz[0].astype(F32) + rdz[1].astype(F32)
            rdz[2 + mine] = total.astype(BF16)
            here = rdz.at[2 + mine, pl.ds(pl.multiple_of(x * 96, 32), 96)]
            there = rdz.at[2 + mine, pl.ds(pl.multiple_of((1 - x) * 96, 32), 96)]
            pltpu.make_async_copy(here, rd, d_sem.at[1]).start()
            remote(there, rd, d_sem.at[0], d_sem.at[1], f, other_x).start()

    def down_done():
        await_bytes(rd, d_sem.at[1])

        @pl.when(in_half)
        def _():
            await_bytes(rd, d_sem.at[0])
            await_bytes(rdz.at[0], dz_sem.at[0])

        @pl.when(jnp.logical_not(in_half))
        def _():
            await_bytes(rdz.at[pl.ds(0, 2)], dz_sem.at[0])

    for b in range(3):
        block = dot_tn(act_s[:, b * 128 : b * 128 + 128], g_s[...]).astype(BF16)
        for k in range(2):
            low, high = max(b * 128, k * 192), min(b * 128 + 128, k * 192 + 192)
            if low < high:
                rdz[held + k, low - k * 192 : high - k * 192, :] = block[low - b * 128 : high - b * 128]
    down_near()
    await_bytes(wd, wd_sem.at[1])
    lax.fori_loop(0, 4, feed_back, 0)

    def scatter_rows(g, b, block, first, width):
        for k in range(4):
            g[k, pl.ds(pl.multiple_of(b * 64, 64), 64), first : first + width] = block[k * 64 : k * 64 + 64].astype(BF16)

    def across(g, r_, sem):
        pltpu.make_async_copy(g.at[z], r_.at[z], sem.at[1]).start()
        for n in (3, 2, 1):
            z2 = order_z(n, z)
            remote(g.at[z2], r_.at[z], sem.at[0], sem.at[1], f, z2 * 2 + x).start()

    def across_near(g, r_, sem, came):
        @pl.when(z == edge)
        def _():
            for e in (1 - upper, upper):
                remote(
                    g.at[2 * (1 - upper) + e], r_.at[2 + e], sem.at[0], came.at[2 + e], f, inner * 2 + x
                ).start()

        remote(
            g.at[inner + edge - z], r_.at[upper], sem.at[0], came.at[upper], f, (inner + edge - z) * 2 + x
        ).start()

    def across_relay(g, r_, sem, came):
        @pl.when(z == inner)
        def _():
            for e in (1 - upper, upper):
                to_z = 2 * (1 - upper) + e
                await_bytes(r_.at[2 + e], came.at[2 + e])
                g[to_z] = (g[to_z].astype(F32) + r_[2 + e].astype(F32)).astype(BF16)
                remote(g.at[to_z], r_.at[upper], sem.at[0], came.at[upper], f, to_z * 2 + x).start()

    def across_sent(g, sem):
        await_bytes(g.at[pl.ds(0, 3)], sem.at[0])

    def to_plane(s_, p_, plane_sem):
        pltpu.make_async_copy(s_.at[pl.ds(pl.multiple_of(t * 32, 32), 32)], p_.at[t], plane_sem.at[1]).start()
        for j in range(1, 8):
            t2 = (t + j) % 8
            block = s_.at[pl.ds(pl.multiple_of(t2 * 32, 32), 32)]
            remote(block, p_.at[t], plane_sem.at[0], plane_sem.at[1], t2 // 2, z * 2 + t2 % 2).start()

    def in_plane(r_, s_, p_, sem, plane_sem):
        await_bytes(r_, sem.at[1])
        s_[...] = (r_[0].astype(F32) + r_[1].astype(F32) + r_[2].astype(F32) + r_[3].astype(F32)).astype(BF16)
        to_plane(s_, p_, plane_sem)

    def in_plane_near(g, r_, s_, p_, came, plane_sem):
        for k in range(2):
            await_bytes(r_.at[k], came.at[k])
        s_[...] = (g[z].astype(F32) + r_[0].astype(F32) + r_[1].astype(F32)).astype(BF16)
        to_plane(s_, p_, plane_sem)

    def columns(ref, b):
        return ref[:, pl.ds(pl.multiple_of(b * 256, 256), 256)]

    def grad_f(b, carry):
        scatter_rows(gf, b, dot_tn(columns(xx, b), mix_s[...].reshape(2048, 768)), 0, 768)
        return carry

    lax.fori_loop(0, 4, grad_f, 0)
    across_near(gf, rf, f_sem, f_came)
    await_bytes(from_core, send.at[6])
    gather_sent(xx)
    h_load = pltpu.make_async_copy(h_out, xx, load.at[3])
    h_load.start()

    sums = split_sum_end(in_buf, keep, recv_d)
    small[...] = jnp.zeros_like(small)
    for part in (0, 1):
        rows = slice(part * half, part * half + half)
        back, dgain = norm_back(mid[rows, :], gain_two, sums[part])
        first = pl.multiple_of(own * ROWS + part * half, half)
        dm = g_s[pl.ds(first, half), :].astype(F32) + back
        hd[pl.ds(first, half), :] = dm.astype(BF16)
        small[:, 1024:2048] += jnp.sum(dgain, axis=0, keepdims=True)
    gather_start(hd, ag_recv2, ag_core2)
    lax.fori_loop(0, 4, layer_terms, 0)
    down_relay()
    for k in range(6):
        await_bytes(out_buf.at[k], send.at[k])
    def key_columns(b, carry):
        vt[b] = k_s[pl.ds(pl.multiple_of(b * QROWS, QROWS), QROWS), :].T
        return carry

    lax.fori_loop(0, 4, key_columns, 0)

    def back_out(r, same):
        chunk = chunk_of(r, core if same else 1 - core)
        rows = pl.ds(pl.multiple_of(chunk * ROWS, ROWS), ROWS)
        put_two(mix_s, chunk, slice(512, 768), dot_nn(hd[rows, :], w2[...].reshape(1024, 256)).astype(BF16))

    back_out(0, True)
    gather_step(hd, ag_recv2, ag_core2, 1, 0)
    gather_step(hd, ag_recv2, ag_core2, 2, 1)
    gather_core(hd, ag_core2, 0)
    back_out(0, False)
    gather_step(hd, ag_recv2, ag_core2, 1, 1)
    gather_step(hd, ag_recv2, ag_core2, 2, 0)
    back_out(1, True)
    back_out(2, True)
    gather_core(hd, ag_core2, 1)
    back_out(1, False)
    gather_core(hd, ag_core2, 2)
    back_out(2, False)
    gather_step(hd, ag_recv2, ag_core2, 3, 0)
    gather_step(hd, ag_recv2, ag_core2, 3, 1)
    back_out(3, True)
    gather_core(hd, ag_core2, 3)
    back_out(3, False)

    home_f, home_c = plane_of(z), own
    stays = (home_f == f) & (home_c == c)

    beyond_c = (core * 2 + 1 - y) * 2 + x
    beyond_stays = (home_f == other_y) & (beyond_c == c)

    def deliver(low, high, dst, k):
        to_low, to_high = dst.at[pl.ds(0, half)], dst.at[pl.ds(half, half)]

        @pl.when(jnp.logical_not(stays))
        def _():
            remote(high, stage.at[k], out_sem.at[5 * k], out_sem.at[5 * k + 1], other_y, c).start()
            remote(low, to_low, out_sem.at[5 * k + 2], out_sem.at[5 * k + 3], home_f, home_c).start()

        @pl.when(stays)
        def _():
            pltpu.make_async_copy(low, to_low, out_sem.at[5 * k + 3]).start()
            pltpu.make_async_copy(high, to_high, out_sem.at[5 * k + 4]).start()

    def send_small():
        s_in[t] = small[...]
        for j in range(1, 8):
            t2 = (t + j) % 8
            remote(small, s_in.at[t], s_sem.at[0], s_sem.at[1], t2 // 2, z * 2 + t2 % 2).start()

    def deliver_part(part, src, dst):
        pieces_of = ((0, half, 0, 7),) if part == 0 else ((half, 64, 0, 9),)
        if part:
            sent = src.at[pl.ds(64, 64)]

            @pl.when(jnp.logical_not(stays))
            def _():
                remote(sent, stage.at[1, pl.ds(0, 64)], out_sem.at[5], out_sem.at[6], other_y, c).start()

            @pl.when(stays)
            def _():
                pltpu.make_async_copy(sent, dst.at[pl.ds(half + 64, 64)], out_sem.at[11]).start()

        for first, count, at, sem in pieces_of:
            rows, to = src.at[pl.ds(at, count)], dst.at[pl.ds(first, count)]

            @pl.when(jnp.logical_not(stays))
            def _():
                remote(rows, to, out_sem.at[sem], out_sem.at[sem + 1], home_f, home_c).start()

            @pl.when(stays)
            def _():
                pltpu.make_async_copy(rows, to, out_sem.at[sem + 1]).start()

    def deliver_parts_on(dst):
        @pl.when(jnp.logical_not(beyond_stays))
        def _():
            part = stage.at[1, pl.ds(0, 64)]
            await_bytes(part, out_sem.at[6])
            to = dst.at[pl.ds(half + 64, 64)]
            remote(part, to, home_send.at[1], out_sem.at[11], home_f, beyond_c).start()

    def deliver_parts_done(dst):
        counts = ((0, half), (half, 64), (half + 64, 64))
        for (first, count), sem in zip(counts, (8, 10, 11)):
            await_bytes(dst.at[pl.ds(first, count)], out_sem.at[sem])

        @pl.when(jnp.logical_not(stays))
        def _():
            for (first, count), sem in zip(counts, (7, 9, 5)):
                await_bytes(dst.at[pl.ds(first, count)], out_sem.at[sem])

        @pl.when(jnp.logical_not(beyond_stays))
        def _():
            await_bytes(stage.at[1, pl.ds(0, 64)], home_send.at[1])

    def deliver_on(dst, k):
        @pl.when(jnp.logical_not(beyond_stays))
        def _():
            await_bytes(stage.at[k], out_sem.at[5 * k + 1])
            remote(
                stage.at[k], dst.at[pl.ds(half, half)], home_send.at[k], out_sem.at[5 * k + 4], home_f, beyond_c
            ).start()

    def deliver_done(dst, k):
        await_bytes(dst.at[pl.ds(0, half)], out_sem.at[5 * k + 3])
        await_bytes(dst.at[pl.ds(half, half)], out_sem.at[5 * k + 4])

        @pl.when(jnp.logical_not(stays))
        def _():
            await_bytes(stage.at[k], out_sem.at[5 * k])
            await_bytes(stage.at[k], out_sem.at[5 * k + 2])

        @pl.when(jnp.logical_not(beyond_stays))
        def _():
            await_bytes(stage.at[k], home_send.at[k])

    def layer_over_x(src, n):
        remote(src, in_buf2.at[n], send2.at[2 + n], recv2.at[n], f, other_x).start()

    def layer_over_y(src, n):
        remote(src, in_buf2.at[n], send2.at[2 + n], recv2.at[n], other_y, c).start()

    low_half, high_half = pl.ds(0, half), pl.ds(half, half)

    def layer_to_chips():
        for r in (3, 1, 2):
            await_bytes(from_core2.at[r], core_recv2.at[r])
            lpart[r] = (lpart[r].astype(F32) + from_core2[r].astype(F32)).astype(BF16)
            if r & 1:
                layer_over_x(lpart.at[r, low_half], 0 if r == 3 else 2)
            if r & 2:
                layer_over_y(lpart.at[r, high_half], 1 if r == 3 else 3)

    def layer_relay():
        await_bytes(in_buf2.at[0], recv2.at[0])
        lpart[2, 0:half] = (lpart[2, 0:half].astype(F32) + in_buf2[0].astype(F32)).astype(BF16)
        layer_over_y(lpart.at[2, low_half], 5)
        await_bytes(in_buf2.at[1], recv2.at[1])
        lpart[1, half:ROWS] = (lpart[1, half:ROWS].astype(F32) + in_buf2[1].astype(F32)).astype(BF16)
        layer_over_x(lpart.at[1, high_half], 4)

    def layer_end():
        await_bytes(from_core2.at[0], core_recv2.at[0])
        for n in (2, 3, 4, 5):
            await_bytes(in_buf2.at[n], recv2.at[n])
        for part in (0, 1):
            rows = slice(part * half, part * half + half)
            value = mid[rows, :] + lpart[0, rows].astype(F32) + from_core2[0, rows].astype(F32)
            value = value + in_buf2[2 + part].astype(F32) + in_buf2[5 - part].astype(F32)
            in_buf2[part] = value.astype(BF16)
        deliver(in_buf2.at[0], in_buf2.at[1], layer_out, 0)

    layer_to_chips()
    across_relay(gf, rf, f_sem, f_came)

    def prepare(b, carry):
        rows = pl.ds(pl.multiple_of(b * QROWS, QROWS), QROWS)
        do = jnp.concatenate(
            [mix_s[perm_s[b * 4 + k], :, 512:768] for k in range(4)], axis=0
        )
        act_s[rows, 0:256] = do
        ones = jnp.ones((8, 128), BF16)
        for head in range(2):
            cols = slice(head * 128, head * 128 + 128)
            prod = do[:, cols].astype(F32) * o_s[pl.ds(b * 4, 4), :, cols].reshape(QROWS, 128).astype(F32)
            high = prod.astype(BF16)
            low = (prod - high.astype(F32)).astype(BF16)
            delta = dot_nt(ones, high) + dot_nt(ones, low)
            delta_s[b, :, head * QROWS : head * QROWS + QROWS] = delta[0:1]
        return carry

    lax.fori_loop(0, 4, prepare, 0)
    def stored(b, carry):
        mix_s[b, :, 0:256] = o_s[ids_s[b]]
        return carry

    lax.fori_loop(0, 16, stored, 0)

    def grad_o(b, carry):
        scatter_rows(go, b, dot_tn(columns(hd, b), mix_s[:, :, 0:256].reshape(2048, 256)), 0, 256)
        return carry

    lax.fori_loop(0, 4, grad_o, 0)
    across(go, ro, o_sem)
    dqt_s[...] = jnp.zeros_like(dqt_s)
    dk_s[...] = jnp.zeros_like(dk_s)
    dv_s[...] = jnp.zeros_like(dv_s)

    def key_tile(kt):
        krows = pl.ds(pl.multiple_of(kt * QROWS, QROWS), QROWS)

        def step(qt, diagonal):
            kb, vb, ktb = k_s[krows, :], v_s[krows, :], vt[kt]
            for g in range(4):
                head, part = g // 2, g % 2
                start = pl.multiple_of(qt * QROWS + part * 256, 256)
                cols = slice(head * 128, head * 128 + 128)
                lanes = slice(g * 256, g * 256 + 256)
                qb = q_s[pl.ds(start, 256), cols]
                dob = act_s[pl.ds(start, 256), cols]
                depth = 256 * (part + 1) if diagonal else QROWS
                s = dot_nt(kb[:depth], qb)
                p = jnp.exp2(s * (SCALE * LOG2E) - lse_s[qt, :, lanes])
                if diagonal:
                    ki = lax.broadcasted_iota(jnp.int32, (depth, 256), 0)
                    qi = lax.broadcasted_iota(jnp.int32, (depth, 256), 1) + part * 256
                    p = jnp.where(ki <= qi, p, 0.0)
                dp = dot_nt(vb[:depth], dob)
                ds = (p * (dp - delta_s[qt, :, lanes])).astype(BF16)
                out = pl.ds(kt * 4, depth // 128)
                dv_s[out] += dot_nn(p.astype(BF16), dob).reshape(depth // 128, 128, 128)
                dk_s[out] += dot_nn(ds, qb).reshape(depth // 128, 128, 128)
                dq = dot_nn(ktb[:, :depth], ds)
                dqt_s[qt * 4 + part * 2, cols, :] += dq[:, 0:128]
                dqt_s[qt * 4 + part * 2 + 1, cols, :] += dq[:, 128:256]

        step(kt, True)

        def off(qt, inner):
            step(qt, False)
            return inner

        lax.fori_loop(kt + 1, 4, off, 0)

    def key_tiles(kt, carry):
        key_tile(kt)

        @pl.when(kt == 0)
        def _():
            layer_relay()

        return carry

    lax.fori_loop(0, 4, key_tiles, 0)
    layer_end()
    h_load.wait()

    def finish_chunk(chunk, carry):
        rows = pl.ds(pl.multiple_of(chunk * ROWS, ROWS), ROWS)
        places = [ids_s[chunk * 2 + k] for k in range(2)]
        cos, sin = turns(jnp.concatenate([table_s[b] for b in places], axis=0))
        raw = dot_nn(xx[rows, :], w1[:, :, :, 0:384].reshape(1024, 384))
        for head in range(3):
            cols = slice(head * 128, head * 128 + 128)
            if head < 2:
                blocks = [dqt_s[b, cols, :].T for b in places]
                gain, lanes = gain_s[2:3, 0:128], slice(2048, 2176)
            else:
                blocks = [dk_s[b] for b in places]
                gain, lanes = gain_s[3:4, 0:128], slice(2176, 2304)
            d = jnp.concatenate(blocks, axis=0) * SCALE
            back, dgain = norm_back(raw[:, cols], gain, unturn(d, cos, sin))
            put_two(mix_s, chunk, cols, back.astype(BF16))
            small[:, lanes] += jnp.sum(dgain, axis=0, keepdims=True)
        for k in range(2):
            mix_s[chunk * 2 + k, :, 384:512] = dv_s[places[k]].astype(BF16)
        return carry

    def partial(chunk):
        return dot_nt(two_blocks(mix_s, chunk, slice(0, 512)), w1[...].reshape(1024, 512))

    gather_sent(hd)
    lax.fori_loop(0, 8, finish_chunk, 0, unroll=2)
    def grad_a(b, carry):
        scatter_rows(ga, b, dot_tn(columns(xx, b), mix_s[:, :, 0:512].reshape(2048, 512)), 0, 512)
        return carry

    lax.fori_loop(0, 4, grad_a, 0)
    across_near(ga, ra, a_sem, a_came)
    in_plane_near(gf, rf, sf, pf, f_came, fp_sem)
    deliver_on(layer_out, 0)
    split_sum(partial, core_out, from_core, out_buf, in_buf, keep, send, core_recv, recv)
    across_relay(ga, ra, a_sem, a_came)
    for part in (0, 1):
        for n in (2 + part, 5 - part):
            await_bytes(in_buf.at[n], recv.at[n])
        dh = keep[part] + in_buf[2 + part].astype(F32) + in_buf[5 - part].astype(F32)
        rows = slice(part * half, part * half + half)
        back, dgain = norm_back(x_keep[rows, :].astype(F32), gain_one, dh)
        dm = hd[pl.ds(pl.multiple_of(own * ROWS + part * half, half), half), :].astype(F32)
        in_buf2[2 + part] = (dm + back).astype(BF16)
        small[:, 0:1024] += jnp.sum(dgain, axis=0, keepdims=True)
        if part:
            send_small()
        deliver_part(part, in_buf2.at[2 + part], grad_tokens)
    down_end()
    in_plane(ro, so, po, o_sem, op_sem)
    deliver_parts_on(grad_tokens)
    await_bytes(s_in.at[pl.ds(0, 7)], s_sem.at[1])
    sbuf[...] = jnp.sum(s_in[...], axis=0)
    p_in[z] = sbuf[...]
    for j in range(1, 4):
        remote(sbuf, p_in.at[z], p_sem.at[0], p_sem.at[1], f, ((z + j) % 4) * 2 + x).start()
    in_plane_near(ga, ra, sa, pa, a_came, ap_sem)

    await_bytes(pf, fp_sem.at[1])
    await_bytes(p_in.at[pl.ds(0, 3)], p_sem.at[1])
    small_out[...] = jnp.sum(p_in[...], axis=0)
    await_bytes(pa, ap_sem.at[1])
    await_bytes(po, op_sem.at[1])

    deliver_done(layer_out, 0)
    deliver_parts_done(grad_tokens)
    split_sum_sent(from_core, out_buf, send)
    for k in range(2):
        await_bytes(core_out2.at[k], send2.at[k])
    for n in range(6):
        await_bytes(in_buf2.at[n], send2.at[2 + n])
    await_bytes(s_in.at[pl.ds(0, 7)], s_sem.at[0])
    await_bytes(p_in.at[pl.ds(0, 3)], p_sem.at[0])
    down_done()
    across_sent(gf, f_sem)
    await_bytes(go.at[pl.ds(0, 3)], o_sem.at[0])
    await_bytes(ra.at[pl.ds(0, 3)], a_sem.at[0])
    await_bytes(pf.at[pl.ds(0, 7)], fp_sem.at[0])
    await_bytes(po.at[pl.ds(0, 7)], op_sem.at[0])
    await_bytes(pa.at[pl.ds(0, 7)], ap_sem.at[0])
    relay_done(g_s, g_send, 1)

    @pl.when(f == seq)
    def _():
        for _ in range(3):
            await_bytes(pos_v, pos_sem.at[0])

    await_bytes(gains_all.at[pl.ds(0, 31)], gain_sem.at[0])
    for pack, sem in ((pack1, w1_sem), (pack2, w2_sem), (pack3, w3_sem)):
        await_bytes(pack.at[pl.ds(0, 7)], sem.at[0])
    await_bytes(w1.at[pl.ds(0, 3)], w1_sem.at[2])
    await_bytes(w2.at[pl.ds(0, 3)], w2_sem.at[2])
    weights_sent(w3, w3_sem)
    for k in range(4):

        @pl.when(jnp.logical_not(self_down & (z == k)))
        def _():
            await_bytes(wd_own, wd_sem.at[0])


def layer(*operands):
    any_spec, vmem = pl.BlockSpec(memory_space=pl.ANY), pl.BlockSpec(memory_space=pltpu.VMEM)
    half = ROWS // 2
    bf = lambda *shape: pltpu.VMEM(shape, BF16)
    fl = lambda *shape: pltpu.VMEM(shape, F32)
    out = lambda kind, *shape: jax.ShapeDtypeStruct(shape, kind)
    copies = (
        16, 16, 2, 6, 3, 3, 2, 2, 4, 4, 3, 4, 2,
        4, 3, 6, 8, 6, 8, 7, 4, 6, 6, 8, 4, 6,
        2, 1, 4, 2, 1, 4, 1, 4, 2, 2, 2, 2, 12, 2, 2,
    )
    return pl.pallas_call(
        layer_kernel,
        out_shape=(
            out(BF16, ROWS, 1024), out(BF16, ROWS, 1024), out(BF16, 8, 32, 768), out(BF16, 8, 32, 256),
            out(BF16, 8, 32, 512), out(BF16, 96, 1024), out(BF16, 2048, 1024), out(F32, 1, 2304),
        ),
        in_specs=[any_spec] * 3 + [vmem] * 6 + [any_spec] * 3,
        out_specs=(any_spec,) * 7 + (vmem,),
        scratch_shapes=[
            bf(2048, 1024), bf(2048, 1024), bf(2048, 1024), bf(4, 4, 64, 512), bf(4, 4, 64, 256), bf(4, 4, 64, 768),
            bf(384, 1024), bf(8, 32, 512), bf(8, 32, 256), bf(8, 32, 768), fl(32, 1, 128), fl(16, 128, 128),
            fl(8, 1024),
            bf(2048, 256), bf(2048, 128), bf(2048, 128), bf(16, 128, 256), bf(4, 128, QROWS),
            fl(1, 1024), fl(4, 1, 1024), bf(ROWS, 1024), fl(ROWS, 1024),
            bf(16, 128, 768), bf(2048, 384), fl(4, 1, 1024), fl(16, 256, 128), fl(16, 128, 128), fl(16, 128, 128),
            fl(1, 2304),
            bf(4, ROWS, 1024), bf(4, ROWS, 1024), bf(6, half, 1024), bf(6, half, 1024), fl(2, half, 1024),
            bf(4, ROWS, 1024), bf(2, ROWS, 1024), bf(4, ROWS, 1024), bf(6, half, 1024),
            bf(4, 256, 768), bf(4, 256, 256), bf(4, 256, 512), bf(4, 192, 1024), bf(4, 256, 768), bf(4, 256, 256), bf(4, 256, 512),
            bf(256, 768), bf(256, 256), bf(256, 512), fl(8, 1, 2304), fl(1, 2304), fl(4, 1, 2304),
            bf(2, half, 1024), pltpu.VMEM((1, 2048), jnp.int32), pltpu.SMEM((1, 2048), jnp.int32),
            pltpu.SMEM((16,), jnp.int32), pltpu.SMEM((16,), jnp.int32),
        ]
        + [pltpu.SemaphoreType.DMA((count,)) for count in copies],
        compiler_params=pltpu.CompilerParams(collective_id=0, has_side_effects=True, vmem_limit_bytes=VMEM_LIMIT),
        name="layer",
    )(*operands)


def outputs_kernel(
    layer, tok, pf, po, pa, rd, small, o_l, o_t, o_q, o_k, o_v, o_o, o_g, o_u, o_d, o_first, o_second, o_head
):
    me = lax.axis_index("fsdp") * 8 + lax.axis_index("ctx")
    o_l[...] = layer[...]
    o_t[...] = tok[...]
    for k in range(8):
        wide, thin, third = (slice(k * w, k * w + w) for w in (256, 128, 384))
        o_g[:, third] = pf[k, :, 0:384].astype(F32)
        o_u[:, third] = pf[k, :, 384:768].astype(F32)
        o_o[:, wide] = po[k].astype(F32)
        o_q[:, wide] = pa[k, :, 0:256].astype(F32)
        o_k[:, thin] = pa[k, :, 256:384].astype(F32)
        o_v[:, thin] = pa[k, :, 384:512].astype(F32)
    o_d[...] = rd[...].astype(F32)
    for o_ref, first, count, width in ((o_first, 0, 1024, 32), (o_second, 1024, 1024, 32), (o_head, 2048, 256, 8)):
        every = jnp.broadcast_to(small[:, first : first + count], (8, count))
        o_ref[...] = pltpu.roll(every, (count - width * me) % count, 1)[0:1, 0:width]


def outputs(*came):
    vmem = pl.BlockSpec(memory_space=pltpu.VMEM)
    out = lambda kind, *shape: jax.ShapeDtypeStruct(shape, kind)
    return pl.pallas_call(
        outputs_kernel,
        out_shape=(
            out(BF16, ROWS, 1024), out(BF16, ROWS, 1024), out(F32, 32, 2048), out(F32, 32, 1024), out(F32, 32, 1024),
            out(F32, 32, 2048), out(F32, 32, 3072), out(F32, 32, 3072), out(F32, 96, 1024), out(F32, 1, 32),
            out(F32, 1, 32), out(F32, 1, 8),
        ),
        in_specs=[vmem] * 7,
        out_specs=(vmem,) * 12,
        compiler_params=pltpu.CompilerParams(vmem_limit_bytes=VMEM_LIMIT),
        name="outputs",
    )(*came)


def rope_table(length):
    inverse = 1000000.0 ** (-2.0 * np.arange(HEAD_DIM // 2, dtype=np.float64) / HEAD_DIM)
    angles = np.arange(length, dtype=np.float32)[:, None] * inverse.astype(np.float32)[None, :]
    angles = angles.astype(np.float64)
    return np.concatenate([np.cos(angles), np.sin(angles)], axis=1).astype(np.float32)


def per_device_planes(
    tokens, positions, w_query, w_key, w_value, w_output, w_gate, w_up, w_down, first_gain, second_gain, head_gain,
    cotangent,
):
    gains = jnp.concatenate([first_gain, second_gain, head_gain, jnp.zeros((56,), BF16)]).astype(F32)[None]
    table = jnp.asarray(rope_table(2048)).reshape(16, 128, HEAD_DIM)
    layer_out, grad_tokens, pf, po, pa, rd, _, small = layer(
        tokens[0], cotangent[0], positions, w_query, w_key, w_value, w_output.T, w_gate, w_up, w_down, gains, table
    )
    layer_out, grad_tokens, o_q, o_k, o_v, o_o, o_g, o_u, o_d, o_first, o_second, o_head = outputs(
        layer_out, grad_tokens, pf, po, pa, rd, small
    )
    return (
        layer_out[None],
        grad_tokens[None],
        o_q,
        o_k,
        o_v,
        o_o.T,
        o_g,
        o_u,
        o_d,
        o_first[0],
        o_second[0],
        o_head[0],
    )


def solution(mesh):
    planes = mesh.shape["fsdp"] == 4 and mesh.shape["ctx"] == 8
    body = per_device_planes if planes else per_device
    return jax.shard_map(
        body,
        mesh=mesh,
        in_specs=(
            P("fsdp", "ctx", None),
            P("fsdp", None),
            P(("fsdp", "ctx"), None),
            P(("fsdp", "ctx"), None),
            P(("fsdp", "ctx"), None),
            P(None, ("fsdp", "ctx")),
            P(("fsdp", "ctx"), None),
            P(("fsdp", "ctx"), None),
            P(("fsdp", "ctx"), None),
            P(("fsdp", "ctx")),
            P(("fsdp", "ctx")),
            P(("fsdp", "ctx")),
            P("fsdp", "ctx", None),
        ),
        out_specs=(
            P("fsdp", "ctx", None),
            P("fsdp", "ctx", None),
            P(("fsdp", "ctx"), None),
            P(("fsdp", "ctx"), None),
            P(("fsdp", "ctx"), None),
            P(None, ("fsdp", "ctx")),
            P(("fsdp", "ctx"), None),
            P(("fsdp", "ctx"), None),
            P(("fsdp", "ctx"), None),
            P(("fsdp", "ctx")),
            P(("fsdp", "ctx")),
            P(("fsdp", "ctx")),
        ),
        check_vma=False,
    )
```

```python
from functools import partial

import jax
import jax.numpy as jnp
import numpy as np
from jax import lax
from jax.experimental import pallas as pl
from jax.experimental.pallas import tpu as pltpu
from jax.sharding import PartitionSpec as P

MESH = pl.DeviceIdType.MESH

HEADS = 16
KV_HEADS = 8
HEAD_DIM = 128


def normed(operand, gain_in):
    return (
        operand * lax.rsqrt(jnp.mean(operand * operand, axis=-1, keepdims=True) + 1e-06) * gain_in
    )


def rotary(operand, places):
    head_width = operand.shape[-1]
    half_width = head_width // 2
    inverse = 1000000.0 ** (-2.0 * jnp.arange(half_width, dtype=jnp.float32) / head_width)
    angles = places.astype(jnp.float32)[:, None] * inverse[None, :]
    cosine = jnp.concatenate([jnp.cos(angles), jnp.cos(angles)], axis=-1)[:, None, :]
    sine_table = jnp.concatenate([jnp.sin(angles), jnp.sin(angles)], axis=-1)[:, None, :]
    turned = jnp.concatenate([-operand[..., half_width:], operand[..., :half_width]], axis=-1)
    return operand * cosine + turned * sine_table


def head_prep(raw_proj, gain_in, places, head_count):
    row_count = raw_proj.shape[0]
    shaped = raw_proj.reshape(row_count, head_count, HEAD_DIM)
    return rotary(normed(shaped, gain_in), places).reshape(row_count, head_count * HEAD_DIM)


def gated(gate_raw, up_raw):
    return jax.nn.silu(gate_raw) * up_raw


def project(left_side, right_side):
    return jnp.dot(left_side, right_side, preferred_element_type=jnp.float32)


def project_back(left_side, right_side):
    return lax.dot_general(
        left_side, right_side, (((1,), (1,)), ((), ())), preferred_element_type=jnp.float32
    )


def outer_sum(left_side, right_side):
    return lax.dot_general(
        left_side, right_side, (((0,), (0,)), ((), ())), preferred_element_type=jnp.float32
    )


def halves_apart(rows_in, shard_count):
    shape_in = rows_in.shape
    split = rows_in.reshape((shard_count, 2, shape_in[0] // (2 * shard_count)) + shape_in[1:])
    return jnp.swapaxes(split, 0, 1).reshape(shape_in)


def halves_back(rows_in, shard_count):
    shape_in = rows_in.shape
    split = rows_in.reshape((2, shard_count, shape_in[0] // (2 * shard_count)) + shape_in[1:])
    return jnp.swapaxes(split, 0, 1).reshape(shape_in)


def key_layout(key_rows, value_rows, place_all):
    key_count = key_rows.shape[0]
    key_block = min(512, key_count)
    block_count = key_count // key_block
    key_parts = key_rows.reshape(block_count, key_block, KV_HEADS, HEAD_DIM)
    value_parts = value_rows.reshape(block_count, key_block, KV_HEADS, HEAD_DIM)
    place_parts = place_all.reshape(block_count, key_block)
    return (key_parts, value_parts, place_parts)


def attend_forward(queries, key_rows, value_rows, place_here, place_all):
    row_count = queries.shape[0]
    group_size = HEADS // KV_HEADS
    score_scale = HEAD_DIM ** (-0.5)
    grouped = queries.reshape(row_count, KV_HEADS, group_size, HEAD_DIM)
    layout = key_layout(key_rows, value_rows, place_all)
    top_place = jnp.max(place_here)

    def attend_step(state_now, block_item):
        key_part, value_part, place_part = block_item

        def attend_compute(state_in):
            run_max, run_sum, run_out = state_in
            scores = (
                jnp.einsum("qhge,khe->hgqk", grouped, key_part, preferred_element_type=jnp.float32)
                * score_scale
            )
            visible = place_part[None, None, None, :] <= place_here[None, None, :, None]
            scores = jnp.where(visible, scores, -1e30)
            new_max = jnp.maximum(run_max, jnp.max(scores, axis=-1))
            weights = jnp.where(visible, jnp.exp(scores - new_max[..., None]), 0.0)
            rescale = jnp.exp(run_max - new_max)
            run_sum = run_sum * rescale + jnp.sum(weights, axis=-1)
            mixed = jnp.einsum(
                "hgqk,khe->hgqe",
                weights.astype(jnp.bfloat16),
                value_part,
                preferred_element_type=jnp.float32,
            )
            run_out = run_out * rescale[..., None] + mixed
            return (new_max, run_sum, run_out)

        state_next = lax.cond(
            jnp.min(place_part) > top_place, lambda state_in: state_in, attend_compute, state_now
        )
        return (state_next, None)

    start_state = (
        jnp.full((KV_HEADS, group_size, row_count), -1e30, jnp.float32),
        jnp.zeros((KV_HEADS, group_size, row_count), jnp.float32),
        jnp.zeros((KV_HEADS, group_size, row_count, HEAD_DIM), jnp.float32),
    )
    (run_max, run_sum, run_out), _ = lax.scan(attend_step, start_state, layout)
    attention = (
        (run_out / run_sum[..., None]).transpose(2, 0, 1, 3).reshape(row_count, HEADS * HEAD_DIM)
    )
    return (attention, run_max + jnp.log(run_sum))


def row_dot_table(grad_attn, attention):
    row_count = grad_attn.shape[0]
    group_size = HEADS // KV_HEADS
    grad_grouped = grad_attn.reshape(row_count, KV_HEADS, group_size, HEAD_DIM)
    return jnp.sum(
        grad_grouped.astype(jnp.float32)
        * attention.reshape(row_count, KV_HEADS, group_size, HEAD_DIM),
        axis=-1,
    ).transpose(1, 2, 0)


def attend_backward(
    queries, key_rows, value_rows, grad_attn, row_dots, log_total, place_here, place_all
):
    row_count = queries.shape[0]
    key_count = key_rows.shape[0]
    group_size = HEADS // KV_HEADS
    score_scale = HEAD_DIM ** (-0.5)
    grouped = queries.reshape(row_count, KV_HEADS, group_size, HEAD_DIM)
    grad_grouped = grad_attn.reshape(row_count, KV_HEADS, group_size, HEAD_DIM)
    layout = key_layout(key_rows, value_rows, place_all)
    top_place = jnp.max(place_here)

    def back_step(grad_query, block_item):
        key_part, value_part, place_part = block_item
        key_block = key_part.shape[0]

        def back_compute(grad_in):
            scores = (
                jnp.einsum("qhge,khe->hgqk", grouped, key_part, preferred_element_type=jnp.float32)
                * score_scale
            )
            visible = place_part[None, None, None, :] <= place_here[None, None, :, None]
            weights = jnp.where(
                visible, jnp.exp(jnp.where(visible, scores, -1e30) - log_total[..., None]), 0.0
            )
            grad_probs = jnp.einsum(
                "qhge,khe->hgqk", grad_grouped, value_part, preferred_element_type=jnp.float32
            )
            grad_scores = (weights * (grad_probs - row_dots[..., None])).astype(jnp.bfloat16)
            grad_out = (
                grad_in
                + jnp.einsum(
                    "hgqk,khe->qhge", grad_scores, key_part, preferred_element_type=jnp.float32
                )
                * score_scale
            )
            grad_keys = (
                jnp.einsum(
                    "hgqk,qhge->khe", grad_scores, grouped, preferred_element_type=jnp.float32
                )
                * score_scale
            )
            grad_values = jnp.einsum(
                "hgqk,qhge->khe",
                weights.astype(jnp.bfloat16),
                grad_grouped,
                preferred_element_type=jnp.float32,
            )
            return (
                grad_out,
                (
                    grad_keys.reshape(key_block, KV_HEADS * HEAD_DIM),
                    grad_values.reshape(key_block, KV_HEADS * HEAD_DIM),
                ),
            )

        def skipped(grad_in):
            empty_terms = jnp.zeros((key_block, KV_HEADS * HEAD_DIM), jnp.float32)
            return (grad_in, (empty_terms, empty_terms))

        return lax.cond(jnp.min(place_part) > top_place, skipped, back_compute, grad_query)

    start_grad = jnp.zeros((row_count, KV_HEADS, group_size, HEAD_DIM), jnp.float32)
    grad_query, key_terms = lax.scan(back_step, start_grad, layout)
    grad_query = grad_query.reshape(row_count, HEADS * HEAD_DIM)
    return (
        grad_query,
        key_terms[0].reshape(key_count, KV_HEADS * HEAD_DIM),
        key_terms[1].reshape(key_count, KV_HEADS * HEAD_DIM),
    )


def per_device(
    tokens,
    positions,
    w_query,
    w_key,
    w_value,
    w_output,
    w_gate,
    w_up,
    w_down,
    first_gain,
    second_gain,
    head_gain,
    cotangent,
):
    inputs = tokens[0].astype(jnp.float32)
    row_count = inputs.shape[0]
    shard_count = lax.axis_size("ctx")
    place_stored = positions[0]
    place_here = lax.dynamic_slice_in_dim(
        place_stored, lax.axis_index("ctx") * row_count, row_count
    )
    place_all = halves_apart(place_stored, shard_count)
    query_full, key_full, value_full, output_full, gain_first, gain_head = (
        lax.all_gather(w_query, ("fsdp", "ctx"), axis=0, tiled=True),
        lax.all_gather(w_key, ("fsdp", "ctx"), axis=0, tiled=True),
        lax.all_gather(w_value, ("fsdp", "ctx"), axis=0, tiled=True),
        lax.all_gather(w_output, ("fsdp", "ctx"), axis=1, tiled=True),
        lax.all_gather(first_gain, ("fsdp", "ctx"), axis=0, tiled=True),
        lax.all_gather(head_gain, ("fsdp", "ctx"), axis=0, tiled=True),
    )
    gain_one = gain_first.astype(jnp.float32)
    gain_query = gain_head[:HEAD_DIM].astype(jnp.float32)
    gain_key = gain_head[HEAD_DIM:].astype(jnp.float32)
    hidden_one = normed(inputs, gain_one).astype(jnp.bfloat16)
    query_raw = project(hidden_one, query_full)
    key_raw = project(hidden_one, key_full)
    value_rows = project(hidden_one, value_full).astype(jnp.bfloat16)
    query_prep = partial(head_prep, places=place_here, head_count=HEADS)
    key_prep = partial(head_prep, places=place_here, head_count=KV_HEADS)
    queries, query_back = jax.vjp(query_prep, query_raw, gain_query)
    key_local, key_back = jax.vjp(key_prep, key_raw, gain_key)
    queries = queries.astype(jnp.bfloat16)
    key_local = key_local.astype(jnp.bfloat16)
    key_stored, value_stored = (
        lax.all_gather(key_local, "ctx", axis=0, tiled=True),
        lax.all_gather(value_rows, "ctx", axis=0, tiled=True),
    )
    key_all = halves_apart(key_stored, shard_count)
    value_all = halves_apart(value_stored, shard_count)
    attention, log_total = attend_forward(queries, key_all, value_all, place_here, place_all)
    attn_low = attention.astype(jnp.bfloat16)
    middle = inputs + project(attn_low, output_full)
    gate_full, up_full, down_full, gain_second = (
        lax.all_gather(w_gate, ("fsdp", "ctx"), axis=0, tiled=True),
        lax.all_gather(w_up, ("fsdp", "ctx"), axis=0, tiled=True),
        lax.all_gather(w_down, ("fsdp", "ctx"), axis=0, tiled=True),
        lax.all_gather(second_gain, ("fsdp", "ctx"), axis=0, tiled=True),
    )
    gain_two = gain_second.astype(jnp.float32)
    hidden_two = normed(middle, gain_two).astype(jnp.bfloat16)
    gate_raw = project(hidden_two, gate_full)
    up_raw = project(hidden_two, up_full)
    activated, gated_back = jax.vjp(gated, gate_raw, up_raw)
    act_low = activated.astype(jnp.bfloat16)
    layer_out = (middle + project(act_low, down_full)).astype(jnp.bfloat16)
    grad_out = cotangent[0].astype(jnp.float32)
    gate_full, up_full, down_full, gain_second = (
        lax.all_gather(w_gate, ("fsdp", "ctx"), axis=0, tiled=True),
        lax.all_gather(w_up, ("fsdp", "ctx"), axis=0, tiled=True),
        lax.all_gather(w_down, ("fsdp", "ctx"), axis=0, tiled=True),
        lax.all_gather(second_gain, ("fsdp", "ctx"), axis=0, tiled=True),
    )
    gain_two = gain_second.astype(jnp.float32)
    out_low = grad_out.astype(jnp.bfloat16)
    down_terms = outer_sum(act_low, out_low)
    grad_act = project_back(out_low, down_full)
    grad_gate_raw, grad_up_raw = gated_back(grad_act)
    gate_low = grad_gate_raw.astype(jnp.bfloat16)
    up_low = grad_up_raw.astype(jnp.bfloat16)
    gate_terms = outer_sum(hidden_two, gate_low)
    up_terms = outer_sum(hidden_two, up_low)
    grad_hidden_two = project_back(gate_low, gate_full) + project_back(up_low, up_full)
    _, norm_two_back = jax.vjp(normed, middle, gain_two)
    middle_part, gain_two_terms = norm_two_back(grad_hidden_two)
    grad_gate, grad_up, grad_down, grad_second = (
        lax.psum_scatter(gate_terms, ("fsdp", "ctx"), scatter_dimension=0, tiled=True),
        lax.psum_scatter(up_terms, ("fsdp", "ctx"), scatter_dimension=0, tiled=True),
        lax.psum_scatter(down_terms, ("fsdp", "ctx"), scatter_dimension=0, tiled=True),
        lax.psum_scatter(gain_two_terms, ("fsdp", "ctx"), scatter_dimension=0, tiled=True),
    )
    grad_middle = grad_out + middle_part
    query_full, key_full, value_full, output_full, gain_first, gain_head = (
        lax.all_gather(w_query, ("fsdp", "ctx"), axis=0, tiled=True),
        lax.all_gather(w_key, ("fsdp", "ctx"), axis=0, tiled=True),
        lax.all_gather(w_value, ("fsdp", "ctx"), axis=0, tiled=True),
        lax.all_gather(w_output, ("fsdp", "ctx"), axis=1, tiled=True),
        lax.all_gather(first_gain, ("fsdp", "ctx"), axis=0, tiled=True),
        lax.all_gather(head_gain, ("fsdp", "ctx"), axis=0, tiled=True),
    )
    gain_one = gain_first.astype(jnp.float32)
    middle_low = grad_middle.astype(jnp.bfloat16)
    output_terms = outer_sum(attn_low, middle_low)
    grad_attn = project_back(middle_low, output_full).astype(jnp.bfloat16)
    row_dots = row_dot_table(grad_attn, attention)
    grad_queries, key_terms, value_terms = attend_backward(
        queries, key_all, value_all, grad_attn, row_dots, log_total, place_here, place_all
    )
    key_terms = halves_back(key_terms, shard_count)
    value_terms = halves_back(value_terms, shard_count)
    grad_key_local, grad_value_local = (
        lax.psum_scatter(
            key_terms.astype(jnp.bfloat16), "ctx", scatter_dimension=0, tiled=True
        ).astype(jnp.float32),
        lax.psum_scatter(
            value_terms.astype(jnp.bfloat16), "ctx", scatter_dimension=0, tiled=True
        ).astype(jnp.float32),
    )
    grad_query_raw, gain_query_terms = query_back(grad_queries)
    grad_key_raw, gain_key_terms = key_back(grad_key_local)
    query_low = grad_query_raw.astype(jnp.bfloat16)
    keyraw_low = grad_key_raw.astype(jnp.bfloat16)
    value_low = grad_value_local.astype(jnp.bfloat16)
    query_terms = outer_sum(hidden_one, query_low)
    key_weight_terms = outer_sum(hidden_one, keyraw_low)
    value_weight_terms = outer_sum(hidden_one, value_low)
    grad_hidden_one = (
        project_back(query_low, query_full)
        + project_back(keyraw_low, key_full)
        + project_back(value_low, value_full)
    )
    _, norm_one_back = jax.vjp(normed, inputs, gain_one)
    input_part, gain_one_terms = norm_one_back(grad_hidden_one)
    head_terms = jnp.concatenate([gain_query_terms, gain_key_terms])
    grad_query, grad_key, grad_value, grad_output, grad_first, grad_head = (
        lax.psum_scatter(query_terms, ("fsdp", "ctx"), scatter_dimension=0, tiled=True),
        lax.psum_scatter(key_weight_terms, ("fsdp", "ctx"), scatter_dimension=0, tiled=True),
        lax.psum_scatter(value_weight_terms, ("fsdp", "ctx"), scatter_dimension=0, tiled=True),
        lax.psum_scatter(output_terms, ("fsdp", "ctx"), scatter_dimension=1, tiled=True),
        lax.psum_scatter(gain_one_terms, ("fsdp", "ctx"), scatter_dimension=0, tiled=True),
        lax.psum_scatter(head_terms, ("fsdp", "ctx"), scatter_dimension=0, tiled=True),
    )
    grad_tokens = (grad_middle + input_part).astype(jnp.bfloat16)
    return (
        layer_out[None],
        grad_tokens[None],
        grad_query,
        grad_key,
        grad_value,
        grad_output,
        grad_gate,
        grad_up,
        grad_down,
        grad_first,
        grad_second,
        grad_head,
    )


ROWS = 256
QROWS = 512
EPS = 1e-06
LOG2E = 1.4426950408889634
SCALE = HEAD_DIM**-0.5
VMEM_LIMIT = 62 * 1024 * 1024
BF16 = jnp.bfloat16
F32 = jnp.float32


def dot_nn(a, b):
    return lax.dot_general(a, b, (((1,), (0,)), ((), ())), preferred_element_type=F32)


def dot_nt(a, b):
    return lax.dot_general(a, b, (((1,), (1,)), ((), ())), preferred_element_type=F32)


def dot_tn(a, b):
    return lax.dot_general(a, b, (((0,), (0,)), ((), ())), preferred_element_type=F32)


def whereabouts():
    f, c = lax.axis_index("fsdp"), lax.axis_index("ctx")
    return f, c, f // 2, f % 2, c // 2, c % 2


def plane_of(s):
    return (s % 2) * 2 + s // 2


def remote(src, dst, send, recv, fsdp, ctx):
    return pltpu.make_async_remote_copy(
        src_ref=src, dst_ref=dst, send_sem=send, recv_sem=recv, device_id=(fsdp, ctx), device_id_type=MESH
    )


def await_bytes(ref, sem):
    pltpu.make_async_copy(ref, ref, sem).wait()


def greet_all():
    f, c, y, core, z, x = whereabouts()
    barrier = pltpu.get_barrier_semaphore()
    me = f * 8 + c

    def greet(j, carry):
        dev = (me + j) % 32
        pl.semaphore_signal(barrier, inc=1, device_id=(dev // 8, dev % 8), device_id_type=MESH)
        return carry

    lax.fori_loop(1, 32, greet, 0)
    pl.semaphore_wait(barrier, 31)


def chip_peer(r):
    f, c, y, core, z, x = whereabouts()
    y2 = 1 - y if r & 2 else y
    x2 = 1 - x if r & 1 else x
    return y2, x2


def chunk_of(r, core):
    y2, x2 = chip_peer(r)
    return (core * 2 + y2) * 2 + x2


def rows_of(ref, chunk):
    return ref.at[pl.ds(pl.multiple_of(chunk * ROWS, ROWS), ROWS)]


def head_norm_rope(raw, gain, cos, sin):
    r = lax.rsqrt(jnp.mean(raw * raw, axis=-1, keepdims=True) + EPS)
    u = raw * r * gain
    return u * cos + pltpu.roll(u, HEAD_DIM // 2, 1) * sin


def norm_rows(values, gain):
    v = values.astype(F32)
    return v * lax.rsqrt(jnp.mean(v * v, axis=-1, keepdims=True) + EPS) * gain


def norm_back(values, gain, dy):
    r = lax.rsqrt(jnp.mean(values * values, axis=-1, keepdims=True) + EPS)
    cdy = gain * dy
    back = r * cdy - values * (r * r * r) * jnp.mean(cdy * values, axis=-1, keepdims=True)
    return back, dy * values * r


def unturn(d, cos, sin):
    return d * cos - pltpu.roll(d, HEAD_DIM // 2, 1) * sin


def order_z(n, z):
    upper = z // 2
    low = (z + upper) % 2
    far = n // 2
    base = far * n + (1 - far) * (low + n * (1 - 2 * low))
    return base + upper * (3 - 2 * base)


def turn_of(n):
    return 3 - 2 * n + 3 * (n // 2)


def chunk_at(r, core):
    f, c, y, _, z, x = whereabouts()
    return (core * 2 + (y + r // 2) % 2) * 2 + (x + r % 2) % 2


def split_step(n, total, out_buf, in_buf, keep, send, recv):
    f, c, y, core, z, x = whereabouts()
    half = ROWS // 2

    def over_x(k):
        remote(out_buf.at[k], in_buf.at[k], send.at[k], recv.at[k], f, z * 2 + 1 - x).start()

    def over_y(k):
        remote(out_buf.at[k], in_buf.at[k], send.at[k], recv.at[k], (1 - y) * 2 + core, c).start()

    def add(k, came):
        await_bytes(in_buf.at[came], recv.at[came])
        out_buf[k] = (out_buf[k].astype(F32) + in_buf[came].astype(F32)).astype(BF16)

    @pl.when(n < 3)
    def _():
        out_buf[2 * n + n // 2] = total[:half].astype(BF16)
        out_buf[1 + 3 * n - 4 * (n // 2)] = total[half:].astype(BF16)

    @pl.when(n == 0)
    def _():
        over_x(0)
        over_y(1)

    @pl.when(n == 1)
    def _():
        over_x(2)

    @pl.when(n == 2)
    def _():
        over_y(3)
        add(5, 0)
        over_y(5)
        add(4, 1)
        over_x(4)

    @pl.when(n == 3)
    def _():
        keep[0] = total[:half]
        keep[1] = total[half:]


def split_sum(partial, core_out, from_core, out_buf, in_buf, keep, send, core_recv, recv):
    f, c, y, core, z, x = whereabouts()

    def to_core(n, carry):
        r = turn_of(n)
        core_out[r] = partial(chunk_at(r, 1 - core)).astype(BF16)
        remote(core_out.at[r], from_core.at[r], send.at[6], core_recv.at[r], y * 2 + 1 - core, c).start()
        return carry

    lax.fori_loop(0, 4, to_core, 0)

    def to_chips(n, carry):
        r = turn_of(n)
        term = partial(chunk_at(r, core))
        await_bytes(from_core.at[r], core_recv.at[r])
        split_step(n, term + from_core[r].astype(F32), out_buf, in_buf, keep, send, recv)
        return carry

    lax.fori_loop(0, 4, to_chips, 0)


def split_sum_end(in_buf, keep, recv):
    for k in (2, 3, 4, 5):
        await_bytes(in_buf.at[k], recv.at[k])
    return (
        keep[0] + in_buf[2].astype(F32) + in_buf[5].astype(F32),
        keep[1] + in_buf[3].astype(F32) + in_buf[4].astype(F32),
    )


def split_sum_sent(from_core, out_buf, send):
    await_bytes(from_core, send.at[6])
    for k in range(6):
        await_bytes(out_buf.at[k], send.at[k])


SPLIT_SUM_SCRATCH = [
    pltpu.VMEM((4, ROWS, 1024), BF16),
    pltpu.VMEM((4, ROWS, 1024), BF16),
    pltpu.VMEM((6, ROWS // 2, 1024), BF16),
    pltpu.VMEM((6, ROWS // 2, 1024), BF16),
    pltpu.VMEM((2, ROWS // 2, 1024), F32),
    pltpu.SemaphoreType.DMA((7,)),
    pltpu.SemaphoreType.DMA((4,)),
    pltpu.SemaphoreType.DMA((6,)),
]


def rows_in_order(pos_s, ids_s, perm_s):
    ids = [lax.div(pos_s[0, j * 128], jnp.int32(128)) for j in range(16)]
    for b in range(16):
        ids_s[b] = ids[b]
        place = jnp.int32(0)
        for j in range(16):
            place = place + j * (1 - lax.min(lax.abs(ids[j] - b), jnp.int32(1)))
        perm_s[b] = lax.min(place, jnp.int32(15))


def turns(table):
    cos, sin = table[:, 0 : HEAD_DIM // 2], table[:, HEAD_DIM // 2 :]
    return jnp.concatenate([cos, cos], axis=1), jnp.concatenate([-sin, sin], axis=1)


def two_blocks(ref, chunk, cols):
    return ref[pl.ds(chunk * 2, 2), :, cols].reshape(ROWS, -1)


def put_two(ref, chunk, cols, value):
    for k in range(2):
        ref[chunk * 2 + k, :, cols] = value[k * 128 : k * 128 + 128]


def gain_rows(gains_all):
    every = gains_all[...].reshape(32, 128)
    lane = lax.broadcasted_iota(jnp.int32, (32, 128), 1)

    def place(first, count, per_row):
        kept = jnp.where((lane >= first) & (lane < first + count), every, 0.0)
        turned = [pltpu.roll(kept, (count * seg - first) % 128, 1) for seg in range(per_row)]
        return [
            sum(turned[seg][m * per_row + seg : m * per_row + seg + 1] for seg in range(per_row))
            for m in range(32 // per_row)
        ]

    one, two = place(0, 32, 4), place(32, 32, 4)
    query, key = place(64, 8, 16)
    return jnp.concatenate(one, axis=1), jnp.concatenate(two, axis=1), query, key


PIECES = [
    ("o", 0), ("o", 1), ("x", 0), ("y", 0), ("o", 2), ("x", 1), ("y", 1), ("o", 3),
    ("x", 2), ("y", 2), ("d", 0), ("x", 3), ("y", 3), ("d", 1), ("d", 2), ("d", 3),
]


def layer_kernel(
    tok, cot, pos, wq, wk, wv, wo, wg, wu, wd_own, gains, table_h,
    layer_out, grad_tokens, pf, po, pa, rd, h_out, small_out,
    xx, hd, g_s, w1, w2, w3, wd, pack1, pack2, pack3, gains_all, table_s, gain_s,
    q_s, k_s, v_s, o_s, vt, total, lse_s, x_keep, mid,
    mix_s, act_s, delta_s, dqt_s, dk_s, dv_s, small,
    core_out, from_core, out_buf, in_buf, keep, lpart, core_out2, from_core2, in_buf2,
    gf, go, ga, rdz, rf, ro, ra, sf, so, sa, s_in, sbuf, p_in, stage, pos_v, pos_s, ids_s, perm_s,
    x_recv, g_recv, stage_recv, hop_send, x_send, g_send, pos_sem, gain_sem, w1_sem, w2_sem, w3_sem, w3_came, wd_sem,
    load, ag_send, ag_recv, ag_core, ag_recv2, ag_core2, send, core_recv, recv, recv_d, send2, core_recv2, recv2,
    home_send, f_sem, f_came, o_sem, o_came, a_sem, a_came, dz_sem, dz_came, d_sem, fp_sem, op_sem, ap_sem, out_sem, s_sem, p_sem,
):
    f, c, y, core, z, x = whereabouts()
    me, t, own = f * 8 + c, f * 2 + x, (core * 2 + y) * 2 + x
    half = ROWS // 2
    upper = z // 2
    edge, inner, other_inner = 3 * upper, 1 + upper, 2 - upper
    table = pltpu.make_async_copy(table_h, table_s, load.at[0])
    table.start()
    for k in range(8):
        pack1[k, :, 0:256] = wq[:, k * 256 : k * 256 + 256]
        pack1[k, :, 256:384] = wk[:, k * 128 : k * 128 + 128]
        pack1[k, :, 384:512] = wv[:, k * 128 : k * 128 + 128]
    greet_all()

    home = plane_of(f)
    seq = plane_of(z)
    ys, cs = seq // 2, seq % 2
    side = (y + ys) % 2
    other_y = (1 - y) * 2 + core
    other_core = y * 2 + 1 - core
    other_x = z * 2 + 1 - x

    def piece(buf, chunk, part):
        return buf.at[pl.ds(pl.multiple_of(chunk * ROWS + part * half, half), half)]

    def relays(k, from_z):
        return core == (cs + from_z) % 2 if k else core == cs

    def hop_beyond(src, buf, recv_, k):
        high = src.at[pl.ds(half, half)]
        to_f = (1 - y) * 2 + ((core + z) % 2 if k else core)

        @pl.when(home != z)
        def _():
            remote(high, stage.at[k], hop_send.at[3 * k + 1], stage_recv.at[k], other_y, c).start()

        @pl.when(home == z)
        def _():
            remote(high, piece(buf, c, 1), hop_send.at[3 * k + 1], recv_.at[2 * c + 1], to_f, c).start()

    def stays_low(k):
        return (home == z) & ((core + z) % 2 == core) if k else home == z

    def hop(src, buf, recv_, k):
        low = src.at[pl.ds(0, half)]
        to_f = y * 2 + ((core + z) % 2 if k else core)

        @pl.when(jnp.logical_not(stays_low(k)))
        def _():
            remote(low, piece(buf, c, 0), hop_send.at[3 * k], recv_.at[2 * c], to_f, home * 2 + x).start()

        @pl.when(stays_low(k))
        def _():
            pltpu.make_async_copy(low, piece(buf, c, 0), recv_.at[2 * c]).start()

    beyond = plane_of(other_y)

    def hop_on(buf, recv_, k):
        to_f = y * 2 + ((core + z) % 2 if k else core)

        @pl.when(beyond != z)
        def _():
            await_bytes(stage.at[k], stage_recv.at[k])
            remote(
                stage.at[k], piece(buf, c, 1), hop_send.at[3 * k + 2], recv_.at[2 * c + 1], to_f, beyond * 2 + x
            ).start()

    def hop_done(k):
        @pl.when(jnp.logical_not(stays_low(k)))
        def _():
            await_bytes(stage.at[k], hop_send.at[3 * k])

        await_bytes(stage.at[k], hop_send.at[3 * k + 1])

        @pl.when(beyond != z)
        def _():
            await_bytes(stage.at[k], hop_send.at[3 * k + 2])

    def whereof(kind, n):
        chunk = order_z(n, z) * 2 + (x if kind in "oy" else 1 - x)
        return chunk, (side if kind in "ox" else 1 - side)

    def relay(buf, recv_, send_, k, kind, n):
        chunk, part = whereof(kind, n)
        rows = piece(buf, chunk, part)
        sem = recv_.at[2 * chunk + part]

        def over_x():
            remote(rows, rows, send_.at[1], sem, f, other_x).start()

        def over_y():
            remote(rows, rows, send_.at[2], sem, other_y, c).start()

        @pl.when(relays(k, order_z(n, z)))
        def _():
            await_bytes(rows, sem)
            if kind == "o":
                over_x()
                over_y()
            if kind == "x":
                pl.when(n % 2 == 0)(over_y)
            if kind == "y":
                pl.when(n % 2 == 1)(over_x)
            remote(rows, rows, send_.at[0], sem, other_core, c).start()

    def relay_wait(buf, recv_, k, kind, n):
        chunk, part = whereof(kind, n)

        @pl.when(jnp.logical_not(relays(k, order_z(n, z))))
        def _():
            await_bytes(piece(buf, chunk, part), recv_.at[2 * chunk + part])

    def relay_done(buf, send_, k):
        for n in range(4):

            @pl.when(relays(k, order_z(n, z)))
            def _():
                await_bytes(buf.at[pl.ds(0, 4 * half)], send_.at[0])
                await_bytes(buf.at[pl.ds(0, half * (1 + n % 2))], send_.at[1])
                await_bytes(buf.at[pl.ds(0, half * (2 - n % 2))], send_.at[2])

    def my_rows(w):
        return w.at[f, z, pl.ds(pl.multiple_of(x * 32, 32), 32)]

    def weights_in_plane(pack, w, sem):
        pltpu.make_async_copy(pack.at[t], my_rows(w), sem.at[1]).start()
        for j in range(1, 8):
            t2 = (t + j) % 8
            remote(pack.at[t2], my_rows(w), sem.at[0], sem.at[1], t2 // 2, z * 2 + t2 % 2).start()

    def weights_across(w, sem):
        await_bytes(w.at[:, z], sem.at[1])
        for n in (1, 2, 3):
            remote(w.at[:, z], w.at[:, z], sem.at[2], sem.at[3], f, order_z(n, z) * 2 + x).start()

    def weights_near(w, sem, came):
        await_bytes(w.at[:, z], sem.at[1])
        for to_z in (inner + edge - z, other_inner):
            remote(w.at[:, z], w.at[:, z], sem.at[2], came.at[z], f, to_z * 2 + x).start()

    def weights_relay(w, sem, came):
        @pl.when(z == inner)
        def _():
            for from_z in (other_inner, 3 - edge):
                await_bytes(w.at[:, from_z], came.at[from_z])
                remote(w.at[:, from_z], w.at[:, from_z], sem.at[2], came.at[from_z], f, edge * 2 + x).start()

    def weights_done(w, came):
        @pl.when(z == inner)
        def _():
            await_bytes(w.at[:, edge], came.at[edge])

        @pl.when(z == edge)
        def _():
            for from_z in (inner, other_inner, 3 - edge):
                await_bytes(w.at[:, from_z], came.at[from_z])

    def weights_sent(w, sem):
        await_bytes(w.at[:, pl.ds(0, 2)], sem.at[2])

        @pl.when(z == inner)
        def _():
            await_bytes(w.at[:, pl.ds(0, 2)], sem.at[2])

    hop_beyond(tok, xx, x_recv, 0)
    hop(tok, xx, x_recv, 0)
    weights_in_plane(pack1, w1, w1_sem)

    @pl.when(f == seq)
    def _():
        pltpu.make_async_copy(pos, pos_v, pos_sem.at[1]).start()
        for j in range(1, 4):
            remote(pos, pos_v, pos_sem.at[0], pos_sem.at[1], (f + j) % 4, c).start()

    pltpu.make_async_copy(gains, gains_all.at[me], gain_sem.at[1]).start()

    def send_gains(j, carry):
        dev = (me + j) % 32
        remote(gains, gains_all.at[me], gain_sem.at[0], gain_sem.at[1], dev // 8, dev % 8).start()
        return carry

    lax.fori_loop(1, 32, send_gains, 0)
    relay(xx, x_recv, x_send, 0, "o", 0)
    hop_on(xx, x_recv, 0)
    for kind, n in (("o", 1), ("x", 0), ("y", 0)):
        relay(xx, x_recv, x_send, 0, kind, n)
    for k in range(8):
        pack2[k] = wo[:, k * 256 : k * 256 + 256]
        pack3[k, :, 0:384] = wg[:, k * 384 : k * 384 + 384]
        pack3[k, :, 384:768] = wu[:, k * 384 : k * 384 + 384]
    await_bytes(gains_all, gain_sem.at[1])
    one, two, gain_q, gain_k = gain_rows(gains_all)
    gain_s[...] = jnp.zeros_like(gain_s)
    gain_s[0:1, :] = one
    gain_s[1:2, :] = two
    gain_s[2:3, 0:128] = gain_q
    gain_s[3:4, 0:128] = gain_k
    await_bytes(pos_v, pos_sem.at[1])
    pos_copy = pltpu.make_async_copy(pos_v, pos_s, load.at[2])
    pos_copy.start()
    pos_copy.wait()
    rows_in_order(pos_s, ids_s, perm_s)

    def norm_piece(kind, n):
        chunk, part = whereof(kind, n)
        rows = pl.ds(pl.multiple_of(chunk * ROWS + part * half, half), half)
        hd[rows, :] = norm_rows(xx[rows, :], gain_s[0:1, :]).astype(BF16)

    def pieces(n, carry):
        for kind, late, skip in (("o", 0, 2), ("x", 1, 2), ("y", 1, 2), ("d", 3, 0)):

            @pl.when((n >= late) & (n < late + 4))
            def _():
                pl.when(n >= skip)(lambda: relay(xx, x_recv, x_send, 0, kind, n - late))
                relay_wait(xx, x_recv, 0, kind, n - late)
                norm_piece(kind, n - late)

        @pl.when(n == 1)
        def _():
            weights_across(w1, w1_sem)

        @pl.when(n == 2)
        def _():
            weights_in_plane(pack2, w2, w2_sem)

        @pl.when(n == 3)
        def _():
            weights_in_plane(pack3, w3, w3_sem)
            hop_beyond(cot, g_s, g_recv, 1)

        @pl.when(n == 4)
        def _():
            hop(cot, g_s, g_recv, 1)

        return carry

    lax.fori_loop(0, 7, pieces, 0)
    hop_on(g_s, g_recv, 1)
    h_copy = pltpu.make_async_copy(hd, h_out, load.at[1])
    h_copy.start()
    x_keep[...] = xx[pl.ds(pl.multiple_of(own * ROWS, ROWS), ROWS), :]

    t_down = me // 4
    down_rows = wd.at[pl.ds(pl.multiple_of((me % 4) * 96, 32), 96)]
    self_down = t_down == t
    table.wait()
    await_bytes(w1.at[pl.ds(0, 3)], w1_sem.at[3])

    def project(ch, carry):
        rows = pl.ds(pl.multiple_of(ch * ROWS, ROWS), ROWS)
        raw = dot_nn(hd[rows, :], w1[...].reshape(1024, 512))
        cos, sin = turns(jnp.concatenate([table_s[ids_s[ch * 2 + k]] for k in range(2)], axis=0))
        gq, gk = gain_s[2:3, 0:128], gain_s[3:4, 0:128]
        for k in range(2):
            cols = slice(k * 128, k * 128 + 128)
            put_two(mix_s, ch, cols, head_norm_rope(raw[:, cols], gq, cos, sin).astype(BF16))
        put_two(mix_s, ch, slice(256, 384), head_norm_rope(raw[:, 256:384], gk, cos, sin).astype(BF16))
        put_two(mix_s, ch, slice(384, 512), raw[:, 384:512].astype(BF16))
        return carry

    lax.fori_loop(0, 8, project, 0, unroll=2)
    weights_across(w2, w2_sem)

    def arrange(b, carry):
        for k in range(4):
            rows = pl.ds(pl.multiple_of(b * QROWS + k * 128, 128), 128)
            stored = perm_s[b * 4 + k]
            q_s[rows, :] = mix_s[stored, :, 0:256]
            k_s[rows, :] = mix_s[stored, :, 256:384]
            v_s[rows, :] = mix_s[stored, :, 384:512]
        vt[b] = v_s[pl.ds(pl.multiple_of(b * QROWS, QROWS), QROWS), :].T
        return carry

    lax.fori_loop(0, 4, arrange, 0)
    acc = keep.at[0]

    def query_tile(qt):
        def step(kt, diagonal):
            kb = k_s[pl.ds(pl.multiple_of(kt * QROWS, QROWS), QROWS), :]
            vb = vt[kt]
            for g in range(4):
                head, part = g // 2, g % 2
                qb = q_s[pl.ds(pl.multiple_of(qt * QROWS + part * 256, 256), 256), head * 128 : head * 128 + 128]
                depth = 256 * (part + 1) if diagonal else QROWS
                s = dot_nt(kb[:depth], qb)
                p = jnp.exp2(s * (SCALE * LOG2E))
                if diagonal:
                    ki = lax.broadcasted_iota(jnp.int32, (depth, 256), 0)
                    qi = lax.broadcasted_iota(jnp.int32, (depth, 256), 1) + part * 256
                    p = jnp.where(ki <= qi, p, 0.0)
                cols = slice(g * 256, g * 256 + 256)
                total[:, cols] += jnp.sum(p, axis=0, keepdims=True)
                acc[:, cols] += dot_nn(vb[:, :depth], p.astype(BF16))

        total[...] = jnp.zeros_like(total)
        acc[...] = jnp.zeros_like(acc)

        def off(kt, inner):
            step(kt, False)
            return inner

        lax.fori_loop(0, qt, off, 0)
        step(qt, True)
        sums = total[...]
        lse_s[qt] = jnp.log2(sums)
        out = acc[...] * (1.0 / sums)
        for g in range(4):
            head, part = g // 2, g % 2
            value = out[:, g * 256 : g * 256 + 256].T.astype(BF16)
            put_two(o_s, qt * 2 + part, slice(head * 128, head * 128 + 128), value)

    def query_tiles(qt, carry):
        query_tile(qt)

        @pl.when(qt == 1)
        def _():
            weights_near(w3, w3_sem, w3_came)

        @pl.when(qt == 2)
        def _():
            for n in range(4):
                relay(g_s, g_recv, g_send, 1, "o", n)

        return carry

    lax.fori_loop(0, 4, query_tiles, 0)
    for k in range(4):
        here = self_down & (z == k)

        @pl.when(here)
        def _():
            pltpu.make_async_copy(wd_own, down_rows, wd_sem.at[1]).start()

        @pl.when(jnp.logical_not(here))
        def _():
            remote(wd_own, down_rows, wd_sem.at[0], wd_sem.at[1], t_down // 2, k * 2 + t_down % 2).start()

    await_bytes(w2.at[pl.ds(0, 3)], w2_sem.at[3])
    relay_done(xx, x_send, 0)
    h_copy.wait()

    def attention_term(chunk):
        rows = jnp.concatenate([o_s[ids_s[chunk * 2 + k]] for k in range(2)], axis=0)
        return dot_nt(rows, w2[...].reshape(1024, 256))

    split_sum(attention_term, core_out, from_core, out_buf, in_buf, keep, send, core_recv, recv)
    for n in range(4):
        relay(g_s, g_recv, g_send, 1, "x", n)
        relay(g_s, g_recv, g_send, 1, "y", n)
    weights_relay(w3, w3_sem, w3_came)
    low, high = split_sum_end(in_buf, keep, recv)
    gain_one, gain_two = gain_s[0:1, :], gain_s[1:2, :]
    mid[0:half, :] = x_keep[0:half, :].astype(F32) + low
    mid[half:ROWS, :] = x_keep[half:ROWS, :].astype(F32) + high
    xx[pl.ds(pl.multiple_of(own * ROWS, ROWS), ROWS), :] = norm_rows(mid[...], gain_two).astype(BF16)

    def gather_start(every, sem, core_sem):
        for part in (0, 1):
            a, b = piece(every, own, part), piece(every, own, 1 - part)
            remote(a, a, ag_send.at[0], sem.at[part], f, z * 2 + 1 - x).start()
            remote(b, b, ag_send.at[1], sem.at[2 + 1 - part], (1 - y) * 2 + core, c).start()
        for part in (0, 1):
            a = piece(every, own, part)
            remote(a, a, ag_send.at[2], core_sem.at[part], y * 2 + 1 - core, c).start()

    def gather_step(every, sem, core_sem, r, part):
        a = piece(every, chunk_of(r, core), part)
        k = (r - 1) * 2 + part
        await_bytes(a, sem.at[k])
        if r == 1 and part == 0:
            remote(a, a, ag_send.at[1], sem.at[4], (1 - y) * 2 + core, c).start()
        if r == 2 and part == 1:
            remote(a, a, ag_send.at[0], sem.at[5], f, z * 2 + 1 - x).start()
        remote(a, a, ag_send.at[2], core_sem.at[2 * r + part], y * 2 + 1 - core, c).start()

    def gather_core(every, core_sem, r):
        for part in (0, 1):
            await_bytes(piece(every, chunk_of(r, 1 - core), part), core_sem.at[2 * r + part])

    def gather_sent(every):
        await_bytes(every.at[pl.ds(0, 3 * half)], ag_send.at[0])
        await_bytes(every.at[pl.ds(0, 3 * half)], ag_send.at[1])
        await_bytes(every.at[pl.ds(0, 8 * half)], ag_send.at[2])

    hop_done(0)
    hop_done(1)
    gather_start(xx, ag_recv, ag_core)
    split_sum_sent(from_core, out_buf, send)
    def feed_forward(chunk, carry):
        rows = pl.ds(pl.multiple_of(chunk * ROWS, ROWS), ROWS)
        gu = dot_nn(xx[rows, :], w3[...].reshape(1024, 768))
        gate, up = gu[:, 0:384], gu[:, 384:768]
        sig = 1.0 / (1.0 + jnp.exp(-gate))
        sil = gate * sig
        act_s[rows, :] = (sil * up).astype(BF16)
        put_two(mix_s, chunk, slice(0, 384), (up * sig * (1.0 + gate * (1.0 - sig))).astype(BF16))
        put_two(mix_s, chunk, slice(384, 768), sil.astype(BF16))
        return carry

    def feed_terms(chunk):
        rows = pl.ds(pl.multiple_of(chunk * ROWS, ROWS), ROWS)
        dact = dot_nt(g_s[rows, :], wd[...])
        for cols in (slice(0, 384), slice(384, 768)):
            put_two(mix_s, chunk, cols, (dact * two_blocks(mix_s, chunk, cols).astype(F32)).astype(BF16))
        return dot_nt(two_blocks(mix_s, chunk, slice(0, 768)), w3[...].reshape(1024, 768))

    def layer_terms(n, carry):
        r, slot = turn_of(n), n % 2

        def term(chunk):
            rows = pl.ds(pl.multiple_of(chunk * ROWS, ROWS), ROWS)
            return dot_nn(act_s[rows, :], wd[...]).astype(BF16)

        @pl.when(n >= 2)
        def _():
            await_bytes(core_out2.at[slot], send2.at[slot])

        core_out2[slot] = term(chunk_at(r, 1 - core))
        remote(core_out2.at[slot], from_core2.at[r], send2.at[slot], core_recv2.at[r], other_core, c).start()
        lpart[r] = term(chunk_at(r, core))
        return carry

    def feed_back(n, carry):
        r = turn_of(n)
        core_out[r] = feed_terms(chunk_at(r, 1 - core)).astype(BF16)
        remote(core_out.at[r], from_core.at[r], send.at[6], core_recv.at[r], other_core, c).start()
        dh = feed_terms(chunk_at(r, core))
        await_bytes(from_core.at[r], core_recv.at[r])
        split_step(n, dh + from_core[r].astype(F32), out_buf, in_buf, keep, send, recv_d)
        return carry

    gather_step(xx, ag_recv, ag_core, 1, 0)
    gather_step(xx, ag_recv, ag_core, 2, 1)
    gather_core(xx, ag_core, 0)
    weights_done(w3, w3_came)
    lax.fori_loop(0, 2, lambda n, carry: feed_forward(chunk_at(0, n), carry), 0)
    gather_step(xx, ag_recv, ag_core, 1, 1)
    gather_step(xx, ag_recv, ag_core, 2, 0)
    lax.fori_loop(1, 3, lambda r, carry: feed_forward(chunk_at(r, core), carry), 0)
    gather_core(xx, ag_core, 1)
    gather_core(xx, ag_core, 2)
    lax.fori_loop(1, 3, lambda r, carry: feed_forward(chunk_at(r, 1 - core), carry), 0)
    for n in range(4):
        relay(g_s, g_recv, g_send, 1, "d", n)
    gather_step(xx, ag_recv, ag_core, 3, 0)
    gather_step(xx, ag_recv, ag_core, 3, 1)
    gather_core(xx, ag_core, 3)
    lax.fori_loop(0, 2, lambda n, carry: feed_forward(chunk_at(3, n), carry), 0)
    for kind, n in PIECES:
        relay_wait(g_s, g_recv, 1, kind, n)
    in_half = upper == x
    held = 2 - 2 * ((upper + x) % 2)

    def down_unit(e):
        return rdz.at[held + e]

    def down_near():
        @pl.when(in_half)
        def _():
            to_z = inner + edge - z
            remote(down_unit(to_z % 2), rdz.at[0], dz_sem.at[0], dz_came.at[0], f, to_z * 2 + x).start()

        @pl.when(jnp.logical_not(in_half) & (z == edge))
        def _():
            for e in range(2):
                remote(down_unit(e), rdz.at[2 + e], dz_sem.at[0], dz_came.at[2 + e], f, inner * 2 + x).start()

    def down_relay():
        @pl.when(jnp.logical_not(in_half) & (z == inner))
        def _():
            for e in range(2):
                await_bytes(rdz.at[2 + e], dz_came.at[2 + e])
                rdz[e] = (rdz[e].astype(F32) + rdz[2 + e].astype(F32)).astype(BF16)
                remote(down_unit(e), rdz.at[1], dz_sem.at[0], dz_came.at[1], f, (2 * x + e) * 2 + x).start()

    def down_end():
        @pl.when(in_half)
        def _():
            for n in range(2):
                await_bytes(rdz.at[n], dz_came.at[n])
            mine = z % 2
            total = rdz[2 + mine].astype(F32) + rdz[0].astype(F32) + rdz[1].astype(F32)
            rdz[2 + mine] = total.astype(BF16)
            here = rdz.at[2 + mine, pl.ds(pl.multiple_of(x * 96, 32), 96)]
            there = rdz.at[2 + mine, pl.ds(pl.multiple_of((1 - x) * 96, 32), 96)]
            pltpu.make_async_copy(here, rd, d_sem.at[1]).start()
            remote(there, rd, d_sem.at[0], d_sem.at[1], f, other_x).start()

    def down_done():
        await_bytes(rd, d_sem.at[1])

        @pl.when(in_half)
        def _():
            await_bytes(rd, d_sem.at[0])
            await_bytes(rdz.at[0], dz_sem.at[0])

        @pl.when(jnp.logical_not(in_half))
        def _():
            await_bytes(rdz.at[pl.ds(0, 2)], dz_sem.at[0])

    for b in range(3):
        block = dot_tn(act_s[:, b * 128 : b * 128 + 128], g_s[...]).astype(BF16)
        for k in range(2):
            low, high = max(b * 128, k * 192), min(b * 128 + 128, k * 192 + 192)
            if low < high:
                rdz[held + k, low - k * 192 : high - k * 192, :] = block[low - b * 128 : high - b * 128]
    down_near()
    await_bytes(wd, wd_sem.at[1])
    lax.fori_loop(0, 4, feed_back, 0)

    def scatter_rows(g, b, block, first, width):
        for k in range(4):
            g[k, pl.ds(pl.multiple_of(b * 64, 64), 64), first : first + width] = block[k * 64 : k * 64 + 64].astype(BF16)

    def across_near(g, r_, sem, came):
        @pl.when(z == edge)
        def _():
            for e in (1 - upper, upper):
                remote(
                    g.at[2 * (1 - upper) + e], r_.at[2 + e], sem.at[0], came.at[2 + e], f, inner * 2 + x
                ).start()

        remote(
            g.at[inner + edge - z], r_.at[upper], sem.at[0], came.at[upper], f, (inner + edge - z) * 2 + x
        ).start()

    def across_relay(g, r_, sem, came):
        @pl.when(z == inner)
        def _():
            for e in (1 - upper, upper):
                to_z = 2 * (1 - upper) + e
                await_bytes(r_.at[2 + e], came.at[2 + e])
                g[to_z] = (g[to_z].astype(F32) + r_[2 + e].astype(F32)).astype(BF16)
                remote(g.at[to_z], r_.at[upper], sem.at[0], came.at[upper], f, to_z * 2 + x).start()

    def across_sent(g, sem):
        await_bytes(g.at[pl.ds(0, 3)], sem.at[0])

    def to_plane(s_, p_, plane_sem):
        pltpu.make_async_copy(s_.at[pl.ds(pl.multiple_of(t * 32, 32), 32)], p_.at[t], plane_sem.at[1]).start()
        for j in range(1, 8):
            t2 = (t + j) % 8
            block = s_.at[pl.ds(pl.multiple_of(t2 * 32, 32), 32)]
            remote(block, p_.at[t], plane_sem.at[0], plane_sem.at[1], t2 // 2, z * 2 + t2 % 2).start()

    def in_plane_near(g, r_, s_, p_, came, plane_sem):
        for k in range(2):
            await_bytes(r_.at[k], came.at[k])
        s_[...] = (g[z].astype(F32) + r_[0].astype(F32) + r_[1].astype(F32)).astype(BF16)
        to_plane(s_, p_, plane_sem)

    def columns(ref, b):
        return ref[:, pl.ds(pl.multiple_of(b * 256, 256), 256)]

    def grad_f(b, carry):
        scatter_rows(gf, b, dot_tn(columns(xx, b), mix_s[...].reshape(2048, 768)), 0, 768)
        return carry

    lax.fori_loop(0, 4, grad_f, 0)
    across_near(gf, rf, f_sem, f_came)
    await_bytes(from_core, send.at[6])
    gather_sent(xx)
    h_load = pltpu.make_async_copy(h_out, xx, load.at[3])
    h_load.start()

    sums = split_sum_end(in_buf, keep, recv_d)
    small[...] = jnp.zeros_like(small)
    for part in (0, 1):
        rows = slice(part * half, part * half + half)
        back, dgain = norm_back(mid[rows, :], gain_two, sums[part])
        first = pl.multiple_of(own * ROWS + part * half, half)
        dm = g_s[pl.ds(first, half), :].astype(F32) + back
        hd[pl.ds(first, half), :] = dm.astype(BF16)
        small[:, 1024:2048] += jnp.sum(dgain, axis=0, keepdims=True)
    gather_start(hd, ag_recv2, ag_core2)
    lax.fori_loop(0, 4, layer_terms, 0)
    down_relay()
    for k in range(6):
        await_bytes(out_buf.at[k], send.at[k])
    def key_columns(b, carry):
        vt[b] = k_s[pl.ds(pl.multiple_of(b * QROWS, QROWS), QROWS), :].T
        return carry

    lax.fori_loop(0, 4, key_columns, 0)

    def back_out(r, same):
        chunk = chunk_of(r, core if same else 1 - core)
        rows = pl.ds(pl.multiple_of(chunk * ROWS, ROWS), ROWS)
        put_two(mix_s, chunk, slice(512, 768), dot_nn(hd[rows, :], w2[...].reshape(1024, 256)).astype(BF16))

    back_out(0, True)
    gather_step(hd, ag_recv2, ag_core2, 1, 0)
    gather_step(hd, ag_recv2, ag_core2, 2, 1)
    gather_core(hd, ag_core2, 0)
    back_out(0, False)
    gather_step(hd, ag_recv2, ag_core2, 1, 1)
    gather_step(hd, ag_recv2, ag_core2, 2, 0)
    back_out(1, True)
    back_out(2, True)
    gather_core(hd, ag_core2, 1)
    back_out(1, False)
    gather_core(hd, ag_core2, 2)
    back_out(2, False)
    gather_step(hd, ag_recv2, ag_core2, 3, 0)
    gather_step(hd, ag_recv2, ag_core2, 3, 1)
    back_out(3, True)
    gather_core(hd, ag_core2, 3)
    back_out(3, False)

    home_f, home_c = plane_of(z), own
    stays = (home_f == f) & (home_c == c)

    beyond_c = (core * 2 + 1 - y) * 2 + x
    beyond_stays = (home_f == other_y) & (beyond_c == c)

    def deliver(low, high, dst, k):
        to_low, to_high = dst.at[pl.ds(0, half)], dst.at[pl.ds(half, half)]

        @pl.when(jnp.logical_not(stays))
        def _():
            remote(high, stage.at[k], out_sem.at[5 * k], out_sem.at[5 * k + 1], other_y, c).start()
            remote(low, to_low, out_sem.at[5 * k + 2], out_sem.at[5 * k + 3], home_f, home_c).start()

        @pl.when(stays)
        def _():
            pltpu.make_async_copy(low, to_low, out_sem.at[5 * k + 3]).start()
            pltpu.make_async_copy(high, to_high, out_sem.at[5 * k + 4]).start()

    def send_small():
        s_in[t] = small[...]
        for j in range(1, 8):
            t2 = (t + j) % 8
            remote(small, s_in.at[t], s_sem.at[0], s_sem.at[1], t2 // 2, z * 2 + t2 % 2).start()

    def deliver_part(part, src, dst):
        pieces_of = ((0, half, 0, 7),) if part == 0 else ((half, 64, 0, 9),)
        if part:
            sent = src.at[pl.ds(64, 64)]

            @pl.when(jnp.logical_not(stays))
            def _():
                remote(sent, stage.at[1, pl.ds(0, 64)], out_sem.at[5], out_sem.at[6], other_y, c).start()

            @pl.when(stays)
            def _():
                pltpu.make_async_copy(sent, dst.at[pl.ds(half + 64, 64)], out_sem.at[11]).start()

        for first, count, at, sem in pieces_of:
            rows, to = src.at[pl.ds(at, count)], dst.at[pl.ds(first, count)]

            @pl.when(jnp.logical_not(stays))
            def _():
                remote(rows, to, out_sem.at[sem], out_sem.at[sem + 1], home_f, home_c).start()

            @pl.when(stays)
            def _():
                pltpu.make_async_copy(rows, to, out_sem.at[sem + 1]).start()

    def deliver_parts_on(dst):
        @pl.when(jnp.logical_not(beyond_stays))
        def _():
            part = stage.at[1, pl.ds(0, 64)]
            await_bytes(part, out_sem.at[6])
            to = dst.at[pl.ds(half + 64, 64)]
            remote(part, to, home_send.at[1], out_sem.at[11], home_f, beyond_c).start()

    def deliver_parts_done(dst):
        counts = ((0, half), (half, 64), (half + 64, 64))
        for (first, count), sem in zip(counts, (8, 10, 11)):
            await_bytes(dst.at[pl.ds(first, count)], out_sem.at[sem])

        @pl.when(jnp.logical_not(stays))
        def _():
            for (first, count), sem in zip(counts, (7, 9, 5)):
                await_bytes(dst.at[pl.ds(first, count)], out_sem.at[sem])

        @pl.when(jnp.logical_not(beyond_stays))
        def _():
            await_bytes(stage.at[1, pl.ds(0, 64)], home_send.at[1])

    def deliver_on(dst, k):
        @pl.when(jnp.logical_not(beyond_stays))
        def _():
            await_bytes(stage.at[k], out_sem.at[5 * k + 1])
            remote(
                stage.at[k], dst.at[pl.ds(half, half)], home_send.at[k], out_sem.at[5 * k + 4], home_f, beyond_c
            ).start()

    def deliver_done(dst, k):
        await_bytes(dst.at[pl.ds(0, half)], out_sem.at[5 * k + 3])
        await_bytes(dst.at[pl.ds(half, half)], out_sem.at[5 * k + 4])

        @pl.when(jnp.logical_not(stays))
        def _():
            await_bytes(stage.at[k], out_sem.at[5 * k])
            await_bytes(stage.at[k], out_sem.at[5 * k + 2])

        @pl.when(jnp.logical_not(beyond_stays))
        def _():
            await_bytes(stage.at[k], home_send.at[k])

    def layer_over_x(src, n):
        remote(src, in_buf2.at[n], send2.at[2 + n], recv2.at[n], f, other_x).start()

    def layer_over_y(src, n):
        remote(src, in_buf2.at[n], send2.at[2 + n], recv2.at[n], other_y, c).start()

    low_half, high_half = pl.ds(0, half), pl.ds(half, half)

    def layer_to_chips():
        for r in (3, 1, 2):
            await_bytes(from_core2.at[r], core_recv2.at[r])
            lpart[r] = (lpart[r].astype(F32) + from_core2[r].astype(F32)).astype(BF16)
            if r & 1:
                layer_over_x(lpart.at[r, low_half], 0 if r == 3 else 2)
            if r & 2:
                layer_over_y(lpart.at[r, high_half], 1 if r == 3 else 3)

    def layer_relay():
        await_bytes(in_buf2.at[0], recv2.at[0])
        lpart[2, 0:half] = (lpart[2, 0:half].astype(F32) + in_buf2[0].astype(F32)).astype(BF16)
        layer_over_y(lpart.at[2, low_half], 5)
        await_bytes(in_buf2.at[1], recv2.at[1])
        lpart[1, half:ROWS] = (lpart[1, half:ROWS].astype(F32) + in_buf2[1].astype(F32)).astype(BF16)
        layer_over_x(lpart.at[1, high_half], 4)

    def layer_end():
        await_bytes(from_core2.at[0], core_recv2.at[0])
        for n in (2, 3, 4, 5):
            await_bytes(in_buf2.at[n], recv2.at[n])
        for part in (0, 1):
            rows = slice(part * half, part * half + half)
            value = mid[rows, :] + lpart[0, rows].astype(F32) + from_core2[0, rows].astype(F32)
            value = value + in_buf2[2 + part].astype(F32) + in_buf2[5 - part].astype(F32)
            in_buf2[part] = value.astype(BF16)
        deliver(in_buf2.at[0], in_buf2.at[1], layer_out, 0)

    layer_to_chips()
    across_relay(gf, rf, f_sem, f_came)

    def prepare(b, carry):
        rows = pl.ds(pl.multiple_of(b * QROWS, QROWS), QROWS)
        do = jnp.concatenate(
            [mix_s[perm_s[b * 4 + k], :, 512:768] for k in range(4)], axis=0
        )
        act_s[rows, 0:256] = do
        ones = jnp.ones((8, 128), BF16)
        for head in range(2):
            cols = slice(head * 128, head * 128 + 128)
            prod = do[:, cols].astype(F32) * o_s[pl.ds(b * 4, 4), :, cols].reshape(QROWS, 128).astype(F32)
            high = prod.astype(BF16)
            low = (prod - high.astype(F32)).astype(BF16)
            delta = dot_nt(ones, high) + dot_nt(ones, low)
            delta_s[b, :, head * QROWS : head * QROWS + QROWS] = delta[0:1]
        return carry

    lax.fori_loop(0, 4, prepare, 0)
    def stored(b, carry):
        mix_s[b, :, 0:256] = o_s[ids_s[b]]
        return carry

    lax.fori_loop(0, 16, stored, 0)

    def grad_o(b, carry):
        scatter_rows(go, b, dot_tn(columns(hd, b), mix_s[:, :, 0:256].reshape(2048, 256)), 0, 256)
        return carry

    lax.fori_loop(0, 4, grad_o, 0)
    across_near(go, ro, o_sem, o_came)
    dqt_s[...] = jnp.zeros_like(dqt_s)
    dk_s[...] = jnp.zeros_like(dk_s)
    dv_s[...] = jnp.zeros_like(dv_s)

    def key_tile(kt):
        krows = pl.ds(pl.multiple_of(kt * QROWS, QROWS), QROWS)

        def step(qt, diagonal):
            kb, vb, ktb = k_s[krows, :], v_s[krows, :], vt[kt]
            for g in range(4):
                head, part = g // 2, g % 2
                start = pl.multiple_of(qt * QROWS + part * 256, 256)
                cols = slice(head * 128, head * 128 + 128)
                lanes = slice(g * 256, g * 256 + 256)
                qb = q_s[pl.ds(start, 256), cols]
                dob = act_s[pl.ds(start, 256), cols]
                depth = 256 * (part + 1) if diagonal else QROWS
                s = dot_nt(kb[:depth], qb)
                p = jnp.exp2(s * (SCALE * LOG2E) - lse_s[qt, :, lanes])
                if diagonal:
                    ki = lax.broadcasted_iota(jnp.int32, (depth, 256), 0)
                    qi = lax.broadcasted_iota(jnp.int32, (depth, 256), 1) + part * 256
                    p = jnp.where(ki <= qi, p, 0.0)
                dp = dot_nt(vb[:depth], dob)
                ds = (p * (dp - delta_s[qt, :, lanes])).astype(BF16)
                out = pl.ds(kt * 4, depth // 128)
                dv_s[out] += dot_nn(p.astype(BF16), dob).reshape(depth // 128, 128, 128)
                dk_s[out] += dot_nn(ds, qb).reshape(depth // 128, 128, 128)
                dq = dot_nn(ktb[:, :depth], ds)
                dqt_s[qt * 4 + part * 2, cols, :] += dq[:, 0:128]
                dqt_s[qt * 4 + part * 2 + 1, cols, :] += dq[:, 128:256]

        step(kt, True)

        def off(qt, inner):
            step(qt, False)
            return inner

        lax.fori_loop(kt + 1, 4, off, 0)

    def key_tiles(kt, carry):
        key_tile(kt)

        @pl.when(kt == 0)
        def _():
            layer_relay()

        return carry

    lax.fori_loop(0, 4, key_tiles, 0)
    layer_end()
    across_relay(go, ro, o_sem, o_came)
    h_load.wait()

    def finish_chunk(chunk, carry):
        rows = pl.ds(pl.multiple_of(chunk * ROWS, ROWS), ROWS)
        places = [ids_s[chunk * 2 + k] for k in range(2)]
        cos, sin = turns(jnp.concatenate([table_s[b] for b in places], axis=0))
        raw = dot_nn(xx[rows, :], w1[:, :, :, 0:384].reshape(1024, 384))
        for head in range(3):
            cols = slice(head * 128, head * 128 + 128)
            if head < 2:
                blocks = [dqt_s[b, cols, :].T for b in places]
                gain, lanes = gain_s[2:3, 0:128], slice(2048, 2176)
            else:
                blocks = [dk_s[b] for b in places]
                gain, lanes = gain_s[3:4, 0:128], slice(2176, 2304)
            d = jnp.concatenate(blocks, axis=0) * SCALE
            back, dgain = norm_back(raw[:, cols], gain, unturn(d, cos, sin))
            put_two(mix_s, chunk, cols, back.astype(BF16))
            small[:, lanes] += jnp.sum(dgain, axis=0, keepdims=True)
        for k in range(2):
            mix_s[chunk * 2 + k, :, 384:512] = dv_s[places[k]].astype(BF16)
        return carry

    def partial(chunk):
        return dot_nt(two_blocks(mix_s, chunk, slice(0, 512)), w1[...].reshape(1024, 512))

    gather_sent(hd)
    lax.fori_loop(0, 8, finish_chunk, 0, unroll=2)
    def grad_a(b, carry):
        scatter_rows(ga, b, dot_tn(columns(xx, b), mix_s[:, :, 0:512].reshape(2048, 512)), 0, 512)
        return carry

    lax.fori_loop(0, 4, grad_a, 0)
    across_near(ga, ra, a_sem, a_came)
    in_plane_near(gf, rf, sf, pf, f_came, fp_sem)
    split_sum(partial, core_out, from_core, out_buf, in_buf, keep, send, core_recv, recv)
    across_relay(ga, ra, a_sem, a_came)
    deliver_on(layer_out, 0)
    for part in (0, 1):
        for n in (2 + part, 5 - part):
            await_bytes(in_buf.at[n], recv.at[n])
        dh = keep[part] + in_buf[2 + part].astype(F32) + in_buf[5 - part].astype(F32)
        rows = slice(part * half, part * half + half)
        back, dgain = norm_back(x_keep[rows, :].astype(F32), gain_one, dh)
        dm = hd[pl.ds(pl.multiple_of(own * ROWS + part * half, half), half), :].astype(F32)
        in_buf2[2 + part] = (dm + back).astype(BF16)
        small[:, 0:1024] += jnp.sum(dgain, axis=0, keepdims=True)
        if part:
            send_small()
        deliver_part(part, in_buf2.at[2 + part], grad_tokens)
    down_end()
    in_plane_near(go, ro, so, po, o_came, op_sem)
    deliver_parts_on(grad_tokens)
    await_bytes(s_in.at[pl.ds(0, 7)], s_sem.at[1])
    sbuf[...] = jnp.sum(s_in[...], axis=0)
    p_in[z] = sbuf[...]
    for j in range(1, 4):
        remote(sbuf, p_in.at[z], p_sem.at[0], p_sem.at[1], f, ((z + j) % 4) * 2 + x).start()
    in_plane_near(ga, ra, sa, pa, a_came, ap_sem)

    await_bytes(pf, fp_sem.at[1])
    await_bytes(p_in.at[pl.ds(0, 3)], p_sem.at[1])
    small_out[...] = jnp.sum(p_in[...], axis=0)
    await_bytes(pa, ap_sem.at[1])
    await_bytes(po, op_sem.at[1])

    deliver_done(layer_out, 0)
    deliver_parts_done(grad_tokens)
    split_sum_sent(from_core, out_buf, send)
    for k in range(2):
        await_bytes(core_out2.at[k], send2.at[k])
    for n in range(6):
        await_bytes(in_buf2.at[n], send2.at[2 + n])
    await_bytes(s_in.at[pl.ds(0, 7)], s_sem.at[0])
    await_bytes(p_in.at[pl.ds(0, 3)], p_sem.at[0])
    down_done()
    across_sent(gf, f_sem)
    await_bytes(go.at[pl.ds(0, 3)], o_sem.at[0])
    await_bytes(ra.at[pl.ds(0, 3)], a_sem.at[0])
    await_bytes(pf.at[pl.ds(0, 7)], fp_sem.at[0])
    await_bytes(po.at[pl.ds(0, 7)], op_sem.at[0])
    await_bytes(pa.at[pl.ds(0, 7)], ap_sem.at[0])
    relay_done(g_s, g_send, 1)

    @pl.when(f == seq)
    def _():
        for _ in range(3):
            await_bytes(pos_v, pos_sem.at[0])

    await_bytes(gains_all.at[pl.ds(0, 31)], gain_sem.at[0])
    for pack, sem in ((pack1, w1_sem), (pack2, w2_sem), (pack3, w3_sem)):
        await_bytes(pack.at[pl.ds(0, 7)], sem.at[0])
    await_bytes(w1.at[pl.ds(0, 3)], w1_sem.at[2])
    await_bytes(w2.at[pl.ds(0, 3)], w2_sem.at[2])
    weights_sent(w3, w3_sem)
    for k in range(4):

        @pl.when(jnp.logical_not(self_down & (z == k)))
        def _():
            await_bytes(wd_own, wd_sem.at[0])


def layer(*operands):
    any_spec, vmem = pl.BlockSpec(memory_space=pl.ANY), pl.BlockSpec(memory_space=pltpu.VMEM)
    half = ROWS // 2
    bf = lambda *shape: pltpu.VMEM(shape, BF16)
    fl = lambda *shape: pltpu.VMEM(shape, F32)
    out = lambda kind, *shape: jax.ShapeDtypeStruct(shape, kind)
    copies = (
        16, 16, 2, 6, 3, 3, 2, 2, 4, 4, 3, 4, 2,
        4, 3, 6, 8, 6, 8, 7, 4, 6, 6, 8, 4, 6,
        2, 1, 4, 1, 4, 1, 4, 1, 4, 2, 2, 2, 2, 12, 2, 2,
    )
    return pl.pallas_call(
        layer_kernel,
        out_shape=(
            out(BF16, ROWS, 1024), out(BF16, ROWS, 1024), out(BF16, 8, 32, 768), out(BF16, 8, 32, 256),
            out(BF16, 8, 32, 512), out(BF16, 96, 1024), out(BF16, 2048, 1024), out(F32, 1, 2304),
        ),
        in_specs=[any_spec] * 3 + [vmem] * 6 + [any_spec] * 3,
        out_specs=(any_spec,) * 7 + (vmem,),
        scratch_shapes=[
            bf(2048, 1024), bf(2048, 1024), bf(2048, 1024), bf(4, 4, 64, 512), bf(4, 4, 64, 256), bf(4, 4, 64, 768),
            bf(384, 1024), bf(8, 32, 512), bf(8, 32, 256), bf(8, 32, 768), fl(32, 1, 128), fl(16, 128, 128),
            fl(8, 1024),
            bf(2048, 256), bf(2048, 128), bf(2048, 128), bf(16, 128, 256), bf(4, 128, QROWS),
            fl(1, 1024), fl(4, 1, 1024), bf(ROWS, 1024), fl(ROWS, 1024),
            bf(16, 128, 768), bf(2048, 384), fl(4, 1, 1024), fl(16, 256, 128), fl(16, 128, 128), fl(16, 128, 128),
            fl(1, 2304),
            bf(4, ROWS, 1024), bf(4, ROWS, 1024), bf(6, half, 1024), bf(6, half, 1024), fl(2, half, 1024),
            bf(4, ROWS, 1024), bf(2, ROWS, 1024), bf(4, ROWS, 1024), bf(6, half, 1024),
            bf(4, 256, 768), bf(4, 256, 256), bf(4, 256, 512), bf(4, 192, 1024), bf(4, 256, 768), bf(4, 256, 256), bf(4, 256, 512),
            bf(256, 768), bf(256, 256), bf(256, 512), fl(8, 1, 2304), fl(1, 2304), fl(4, 1, 2304),
            bf(2, half, 1024), pltpu.VMEM((1, 2048), jnp.int32), pltpu.SMEM((1, 2048), jnp.int32),
            pltpu.SMEM((16,), jnp.int32), pltpu.SMEM((16,), jnp.int32),
        ]
        + [pltpu.SemaphoreType.DMA((count,)) for count in copies],
        compiler_params=pltpu.CompilerParams(collective_id=0, has_side_effects=True, vmem_limit_bytes=VMEM_LIMIT),
        name="layer",
    )(*operands)


def outputs_kernel(
    layer, tok, pf, po, pa, rd, small, o_l, o_t, o_q, o_k, o_v, o_o, o_g, o_u, o_d, o_first, o_second, o_head
):
    me = lax.axis_index("fsdp") * 8 + lax.axis_index("ctx")
    o_l[...] = layer[...]
    o_t[...] = tok[...]
    for k in range(8):
        wide, thin, third = (slice(k * w, k * w + w) for w in (256, 128, 384))
        o_g[:, third] = pf[k, :, 0:384].astype(F32)
        o_u[:, third] = pf[k, :, 384:768].astype(F32)
        o_o[:, wide] = po[k].astype(F32)
        o_q[:, wide] = pa[k, :, 0:256].astype(F32)
        o_k[:, thin] = pa[k, :, 256:384].astype(F32)
        o_v[:, thin] = pa[k, :, 384:512].astype(F32)
    o_d[...] = rd[...].astype(F32)
    for o_ref, first, count, width in ((o_first, 0, 1024, 32), (o_second, 1024, 1024, 32), (o_head, 2048, 256, 8)):
        every = jnp.broadcast_to(small[:, first : first + count], (8, count))
        o_ref[...] = pltpu.roll(every, (count - width * me) % count, 1)[0:1, 0:width]


def outputs(*came):
    vmem = pl.BlockSpec(memory_space=pltpu.VMEM)
    out = lambda kind, *shape: jax.ShapeDtypeStruct(shape, kind)
    return pl.pallas_call(
        outputs_kernel,
        out_shape=(
            out(BF16, ROWS, 1024), out(BF16, ROWS, 1024), out(F32, 32, 2048), out(F32, 32, 1024), out(F32, 32, 1024),
            out(F32, 32, 2048), out(F32, 32, 3072), out(F32, 32, 3072), out(F32, 96, 1024), out(F32, 1, 32),
            out(F32, 1, 32), out(F32, 1, 8),
        ),
        in_specs=[vmem] * 7,
        out_specs=(vmem,) * 12,
        compiler_params=pltpu.CompilerParams(vmem_limit_bytes=VMEM_LIMIT),
        name="outputs",
    )(*came)


def rope_table(length):
    inverse = 1000000.0 ** (-2.0 * np.arange(HEAD_DIM // 2, dtype=np.float64) / HEAD_DIM)
    angles = np.arange(length, dtype=np.float32)[:, None] * inverse.astype(np.float32)[None, :]
    angles = angles.astype(np.float64)
    return np.concatenate([np.cos(angles), np.sin(angles)], axis=1).astype(np.float32)


def per_device_planes(
    tokens, positions, w_query, w_key, w_value, w_output, w_gate, w_up, w_down, first_gain, second_gain, head_gain,
    cotangent,
):
    gains = jnp.concatenate([first_gain, second_gain, head_gain, jnp.zeros((56,), BF16)]).astype(F32)[None]
    table = jnp.asarray(rope_table(2048)).reshape(16, 128, HEAD_DIM)
    layer_out, grad_tokens, pf, po, pa, rd, _, small = layer(
        tokens[0], cotangent[0], positions, w_query, w_key, w_value, w_output.T, w_gate, w_up, w_down, gains, table
    )
    layer_out, grad_tokens, o_q, o_k, o_v, o_o, o_g, o_u, o_d, o_first, o_second, o_head = outputs(
        layer_out, grad_tokens, pf, po, pa, rd, small
    )
    return (
        layer_out[None],
        grad_tokens[None],
        o_q,
        o_k,
        o_v,
        o_o.T,
        o_g,
        o_u,
        o_d,
        o_first[0],
        o_second[0],
        o_head[0],
    )


def solution(mesh):
    planes = mesh.shape["fsdp"] == 4 and mesh.shape["ctx"] == 8
    body = per_device_planes if planes else per_device
    return jax.shard_map(
        body,
        mesh=mesh,
        in_specs=(
            P("fsdp", "ctx", None),
            P("fsdp", None),
            P(("fsdp", "ctx"), None),
            P(("fsdp", "ctx"), None),
            P(("fsdp", "ctx"), None),
            P(None, ("fsdp", "ctx")),
            P(("fsdp", "ctx"), None),
            P(("fsdp", "ctx"), None),
            P(("fsdp", "ctx"), None),
            P(("fsdp", "ctx")),
            P(("fsdp", "ctx")),
            P(("fsdp", "ctx")),
            P("fsdp", "ctx", None),
        ),
        out_specs=(
            P("fsdp", "ctx", None),
            P("fsdp", "ctx", None),
            P(("fsdp", "ctx"), None),
            P(("fsdp", "ctx"), None),
            P(("fsdp", "ctx"), None),
            P(None, ("fsdp", "ctx")),
            P(("fsdp", "ctx"), None),
            P(("fsdp", "ctx"), None),
            P(("fsdp", "ctx"), None),
            P(("fsdp", "ctx")),
            P(("fsdp", "ctx")),
            P(("fsdp", "ctx")),
        ),
        check_vma=False,
    )
```
